32 devices in a mesh: rows: 8 (over z, y), strip: 4 (over x, core).
Axes of the slice: x: 2, y: 2, z: 4, core: 2. Of those that a mesh axis runs over, the one named last changes fastest.
Arguments:
- frames: bfloat16 [2048, 3, 64, 64], P('rows', None, 'strip'), may hold values from -4 to 4
- segment_ids: int32 [32, 64], P('rows'), may hold values from 0 to 3, never falling along the last dimension, each value on 1 to 32 neighbouring positions
- encode_one: bfloat16 [32, 3, 4, 4], replicated, may hold values from -1.25 to 1.25
- encode_two: bfloat16 [64, 32, 4, 4], replicated, may hold values from -0.375 to 0.375
- encode_three: bfloat16 [128, 64, 4, 4], replicated, may hold values from -0.25 to 0.25
- encode_four: bfloat16 [256, 128, 4, 4], replicated, may hold values from -0.1875 to 0.1875
- latent_head: bfloat16 [4096, 1024], P(None, 'strip'), may hold values from -0.1875 to 0.1875
- token_embed: bfloat16 [1024, 512], P('strip'), may hold values from -6 to 6
- positions: bfloat16 [64, 512], replicated, may hold values from -3 to 3
- norm_gains: float32 [2, 2, 512], replicated, may hold values from 0.5 to 1.5
- qkv_weight: bfloat16 [2, 512, 3, 512], P(None, None, None, 'strip'), may hold values from -0.25 to 0.25
- out_weight: bfloat16 [2, 512, 512], P(None, 'strip'), may hold values from -0.75 to 0.75
- up_weight: bfloat16 [2, 512, 2048], P(None, None, 'strip'), may hold values from -0.375 to 0.375
- down_weight: bfloat16 [2, 2048, 512], P(None, 'strip'), may hold values from -0.125 to 0.125
- decode_head: bfloat16 [1024, 4096], P('strip'), may hold values from -4 to 4
- decode_one: bfloat16 [128, 256, 4, 4], replicated, may hold values from -0.25 to 0.25
- decode_two: bfloat16 [64, 128, 4, 4], replicated, may hold values from -0.375 to 0.375
- decode_three: bfloat16 [32, 64, 4, 4], replicated, may hold values from -0.5 to 0.5
- decode_four: bfloat16 [3, 32, 4, 4], replicated, may hold values from -0.5 to 0.5
- token_cotangent: bfloat16 [2048, 512], P('rows'), may hold values from -6 to 6
- frame_cotangent: bfloat16 [2048, 3, 64, 64], P('rows', None, 'strip'), may hold values from -6 to 6
Outputs:
- tokens_out: bfloat16 [2048, 512], P('rows')
- recon_frames: bfloat16 [2048, 3, 64, 64], P('rows', None, 'strip')
- frames_grad: float32 [2048, 3, 64, 64], P('rows', None, 'strip')
- encode_one_grad: float32 [32, 3, 4, 4], replicated
- encode_two_grad: float32 [64, 32, 4, 4], replicated
- encode_three_grad: float32 [128, 64, 4, 4], replicated
- encode_four_grad: float32 [256, 128, 4, 4], replicated
- latent_head_grad: float32 [4096, 1024], P(None, 'strip')
- token_embed_grad: float32 [1024, 512], P('strip')
- positions_grad: float32 [64, 512], replicated
- norm_gains_grad: float32 [2, 2, 512], replicated
- qkv_weight_grad: float32 [2, 512, 3, 512], P(None, None, None, 'strip')
- out_weight_grad: float32 [2, 512, 512], P(None, 'strip')
- up_weight_grad: float32 [2, 512, 2048], P(None, None, 'strip')
- down_weight_grad: float32 [2, 2048, 512], P(None, 'strip')
- decode_head_grad: float32 [1024, 4096], P('strip')
- decode_one_grad: float32 [128, 256, 4, 4], replicated
- decode_two_grad: float32 [64, 128, 4, 4], replicated
- decode_three_grad: float32 [32, 64, 4, 4], replicated
- decode_four_grad: float32 [3, 32, 4, 4], replicated
The draws below stay inside these ranges and needn't reach their ends.
Inputs may be any that keep to these rules, and one draw needn't show every extreme that they name: `segment_ids`: along a sequence of 64 steps the episode numbers never fall, and one episode spans at most 32 steps of a sequence.
All inputs are finite; a program needn't handle non-finite values.
Results may differ from the reference program's by a relative error of at most 0.035.
Values may be sent and summed in bfloat16 or wider, within the bound.
A program may use at most 320 MiB of HBM per device.

```python
import math
import jax
import jax.numpy as jnp
import numpy as np
from jax import lax

D = 512
HEADS = 8
HEAD_DIM = 64
FF = 2048
LAYERS = 2
C1 = 32
C2 = 64
C3 = 128
C4 = 256
LGROUPS = 32
LCLASS = 32
IMG = 64
STEPS = 64
SEQ_DEV = 4
SEQS = 32
FRAMES = 2048
FEAT = 4096
LATENT = 1024


def block_scale(rng, dims, cuts, smallest, high):
    loudness = 1.0
    for position, parts in cuts:
        heights = jax.random.uniform(jax.random.fold_in(jax.random.fold_in(rng, 6), position), (parts,), jnp.float32, smallest / len(cuts), high / len(cuts))
        loudness = loudness * jnp.repeat(jnp.exp(heights), dims[position] // parts).reshape((-1,) + (1,) * (len(dims) - 1 - position))
    return loudness


def length_profile(amount, total, bound, skew):
    portions = [(1 << 20) // math.isqrt(grade ** skew) + 1 for grade in range(2, amount + 1)]
    spare, given = total - bound - (amount - 1), [1] * (amount - 1)
    while spare > 0:
        movable = [i for i in range(amount - 1) if given[i] < bound]
        whole, budget = sum([portions[i] for i in movable]), spare
        for i in movable:
            extra = min(bound - given[i], max(1, budget * portions[i] // whole), spare)
            given[i] = given[i] + extra
            spare = spare - extra
    return np.array([bound] + given)


def ragged_sizes(key, number_of, total, bound, lean):
    if number_of == 2:
        one = jax.random.randint(key, (), max(1, total - bound), min(bound, total - 1) + 1)
        return jnp.stack([one, total - one])
    tallies = jnp.asarray(length_profile(number_of, total, bound, lean), jnp.int32)
    pairs = (number_of - 1) // 2
    source_of, taker = tallies[1:1 + 2 * pairs:2], tallies[2:2 + 2 * pairs:2]
    margin = jnp.minimum(source_of - 1, bound - taker)
    moved = jax.random.randint(jax.random.fold_in(key, 1), (pairs,), 0, 1 << 20) % (margin + 1)
    tallies = tallies.at[1:1 + 2 * pairs:2].set(source_of - moved).at[2:2 + 2 * pairs:2].set(taker + moved)
    return tallies[jax.random.permutation(jax.random.fold_in(key, 2), number_of)]


def gaussian(key, shape, deviation, limit, shards=(), held_as=jnp.bfloat16):
    drawn = jax.random.normal(key, shape, jnp.float32) * deviation
    if len(shards) > 0:
        drawn = block_scale(key, shape, shards, -0.22, 0.18) * drawn
    return jnp.clip(drawn, min=-limit, max=limit).astype(held_as)


def setup_inputs(seed: int = 0) -> dict:
    streams_of = jax.random.split(jax.random.key(seed), 22)
    return {
        "frames": gaussian(streams_of[0], (FRAMES, 3, IMG, IMG), 1.0, 4.0, ((0, 8), (2, 4))),
        "segment_ids": jax.vmap(lambda own: jnp.searchsorted(jnp.cumsum(ragged_sizes(own, 4, STEPS, STEPS // 2, 0)), jnp.arange(STEPS), side="right"))(jax.random.split(streams_of[1], SEQS)).reshape((SEQS, STEPS)).astype(jnp.int32),
        "encode_one": gaussian(streams_of[2], (C1, 3, 4, 4), 24 ** -0.5, 1.25),
        "encode_two": gaussian(streams_of[3], (C2, C1, 4, 4), (C1 * 8) ** -0.5, 0.375),
        "encode_three": gaussian(streams_of[4], (C3, C2, 4, 4), (C2 * 8) ** -0.5, 0.25),
        "encode_four": gaussian(streams_of[5], (C4, C3, 4, 4), (C3 * 8) ** -0.5, 0.1875),
        "latent_head": gaussian(streams_of[6], (FEAT, LATENT), (FEAT // 4) ** -0.5, 0.1875, ((1, 4),)),
        "token_embed": gaussian(streams_of[7], (LATENT, D), 1.0, 6.0, ((0, 4),)),
        "positions": gaussian(streams_of[8], (STEPS, D), 0.5, 3.0),
        "norm_gains": jnp.clip(1.0 + 0.1 * jax.random.normal(streams_of[9], (LAYERS, 2, D), jnp.float32), 0.5, 1.5),
        "qkv_weight": gaussian(streams_of[10], (LAYERS, D, 3, D), D ** -0.5, 0.25, ((3, 4),)),
        "out_weight": gaussian(streams_of[11], (LAYERS, D, D), (D // 8) ** -0.5, 0.75, ((1, 4),)),
        "up_weight": gaussian(streams_of[12], (LAYERS, D, FF), (D // 2) ** -0.5, 0.375, ((2, 4),)),
        "down_weight": gaussian(streams_of[13], (LAYERS, FF, D), FF ** -0.5, 0.125, ((1, 4),)),
        "decode_head": gaussian(streams_of[14], (LATENT, FEAT), 0.7, 4.0, ((0, 4),)),
        "decode_one": gaussian(streams_of[15], (C3, C4, 4, 4), (C4 * 2) ** -0.5, 0.25),
        "decode_two": gaussian(streams_of[16], (C2, C3, 4, 4), (C3 * 2) ** -0.5, 0.375),
        "decode_three": gaussian(streams_of[17], (C1, C2, 4, 4), (C2 * 2) ** -0.5, 0.5),
        "decode_four": gaussian(streams_of[18], (3, C1, 4, 4), (C1 * 4) ** -0.5, 0.5),
        "token_cotangent": gaussian(streams_of[19], (FRAMES, D), 1.0, 6.0, ((0, 8),)),
        "frame_cotangent": gaussian(streams_of[20], (FRAMES, 3, IMG, IMG), 1.0, 6.0, ((0, 8), (2, 4))),
    }


@jax.custom_vjp
def low(v):
    return lax.optimization_barrier(v.astype(jnp.bfloat16)).astype(jnp.float32)

@jax.custom_vjp
def low_back(v):
    return v

def low_keep(v):
    return (low(v), None)

def low_pass(kept, grad):
    return (grad,)

def back_keep(v):
    return (v, None)

def back_low(kept, grad):
    return (low(grad),)
low.defvjp(low_keep, low_pass)
low_back.defvjp(back_keep, back_low)
EPS = 1e-05
SCALE = 0.125
NEG = -1e+30
HIGH = lax.Precision.HIGHEST
LAYOUT = ('NCHW', 'OIHW', 'NCHW')

def pad_rows(values):
    return jnp.pad(values, ((0, 0), (0, 0), (1, 1), (0, 0)))

def encode_conv(values, weight):
    return lax.conv_general_dilated(pad_rows(values), weight, (2, 2), ((0, 0), (1, 1)), dimension_numbers=LAYOUT, precision=HIGH)

def decode_conv(values, weight):
    return lax.conv_general_dilated(pad_rows(values), weight, (1, 1), ((0, 0), (2, 2)), lhs_dilation=(2, 2), dimension_numbers=LAYOUT, precision=HIGH)

def smooth_unit(values):
    return values * jax.nn.sigmoid(values)

def softened(scores):
    shifted = scores - lax.optimization_barrier(jnp.max(scores, -1, keepdims=True))
    raised = jnp.exp(shifted)
    return raised / lax.optimization_barrier(jnp.sum(raised, -1, keepdims=True))

def normalize(values, gain):
    centred = values - lax.optimization_barrier(jnp.mean(values, -1, keepdims=True))
    spread = lax.optimization_barrier(jnp.mean(centred * centred, -1, keepdims=True))
    return centred * lax.rsqrt(spread + EPS) * gain

def attention_block(hidden, allowed, gain_pair, qkv_layer, out_layer, up_layer, down_layer):
    head_shape = hidden.shape[:2] + (HEADS, HEAD_DIM)
    normed = low(normalize(hidden, gain_pair[0]))
    mixed = jnp.einsum('gsd,dkh->gskh', normed, qkv_layer, precision=HIGH)
    queries = low(low_back(mixed[:, :, 0])).reshape(head_shape)
    keys_all = low(low_back(mixed[:, :, 1])).reshape(head_shape)
    values_all = low(low_back(mixed[:, :, 2])).reshape(head_shape)
    scores = jnp.einsum('gqhe,gkhe->ghqk', queries, keys_all, precision=HIGH)
    scores = jnp.where(allowed[:, None], low_back(scores * SCALE), NEG)
    chances = softened(scores)
    attended = jnp.einsum('ghqk,gkhe->gqhe', low(chances), values_all, precision=HIGH)
    attended = low(low_back(attended)).reshape(hidden.shape)
    middle = hidden + low_back(jnp.einsum('gsd,de->gse', attended, out_layer, precision=HIGH))
    normed_ffn = low(normalize(middle, gain_pair[1]))
    before = low_back(jnp.einsum('gsd,df->gsf', normed_ffn, up_layer, precision=HIGH))
    inner_act = low(smooth_unit(before))
    return middle + low_back(jnp.einsum('gsf,fd->gsd', inner_act, down_layer, precision=HIGH))

def forward(params, frames, segments):
    encoders = params[0:4]
    latent_head, token_embed, positions, norm_gains = params[4:8]
    qkv_weight, out_weight, up_weight, down_weight, decode_head = params[8:13]
    decoders = params[13:17]
    maps = frames
    for weight in encoders:
        maps = low(smooth_unit(low_back(encode_conv(maps, weight))))
    frame_count = maps.shape[0]
    features = maps.reshape(frame_count, -1)
    logits = low_back(jnp.dot(features, latent_head, precision=HIGH))
    chances = softened(logits.reshape(frame_count, LGROUPS, LCLASS)).reshape(frame_count, LATENT)
    latent = low(chances)
    embedded = low_back(jnp.dot(latent, token_embed, precision=HIGH))
    hidden = embedded.reshape(-1, STEPS, D) + positions[None]
    places = jnp.arange(STEPS)
    causal = places[:, None] >= places[None, :]
    allowed = causal[None] & (segments[:, :, None] == segments[:, None, :])
    for layer_index in range(LAYERS):
        hidden = attention_block(hidden, allowed, norm_gains[layer_index], qkv_weight[layer_index], out_weight[layer_index], up_weight[layer_index], down_weight[layer_index])
    decoded = low_back(jnp.dot(latent, decode_head, precision=HIGH)).reshape(maps.shape)
    dmaps = low(smooth_unit(decoded))
    for weight in decoders[:3]:
        dmaps = low(smooth_unit(low_back(decode_conv(dmaps, weight))))
    recon = decode_conv(dmaps, decoders[3])
    return (hidden.reshape(frame_count, D), recon)

def reference(frames, segment_ids, encode_one, encode_two, encode_three, encode_four, latent_head, token_embed, positions, norm_gains, qkv_weight, out_weight, up_weight, down_weight, decode_head, decode_one, decode_two, decode_three, decode_four, token_cotangent, frame_cotangent):
    params = tuple((weight.astype(jnp.float32) for weight in (encode_one, encode_two, encode_three, encode_four, latent_head, token_embed, positions, norm_gains, qkv_weight, out_weight, up_weight, down_weight, decode_head, decode_one, decode_two, decode_three, decode_four)))
    groups = SEQS // SEQ_DEV
    per_group = SEQ_DEV * STEPS
    frame_groups = frames.reshape((groups, per_group) + frames.shape[1:])
    segment_groups = segment_ids.reshape(groups, SEQ_DEV, STEPS)
    token_groups = token_cotangent.reshape(groups, per_group, D)
    recon_groups = frame_cotangent.reshape(frame_groups.shape)

    def one_group(totals, group_items):
        pixels, segments, token_cot, frame_cot = group_items

        def run_group(weights, images):
            return forward(weights, images, segments)
        outputs, pullback = jax.vjp(run_group, params, pixels.astype(jnp.float32))
        weight_grads, image_grads = pullback((token_cot.astype(jnp.float32), frame_cot.astype(jnp.float32)))
        totals = jax.tree.map(jnp.add, totals, weight_grads)
        return (totals, (outputs[0].astype(jnp.bfloat16), outputs[1].astype(jnp.bfloat16), image_grads))
    zero_grads = jax.tree.map(jnp.zeros_like, params)
    totals, results = lax.scan(one_group, zero_grads, (frame_groups, segment_groups, token_groups, recon_groups))
    tokens_out = results[0].reshape(FRAMES, D)
    recon_frames = results[1].reshape(frames.shape)
    frames_grad = results[2].reshape(frames.shape)
    return (tokens_out, recon_frames, frames_grad, totals[0], totals[1], totals[2], totals[3], totals[4], totals[5], totals[6], totals[7], totals[8], totals[9], totals[10], totals[11], totals[12], totals[13], totals[14], totals[15], totals[16])
```

```python
import functools

import jax
import jax.numpy as jnp
from jax import lax
from jax.experimental import pallas as pl
from jax.experimental.pallas import tpu as pltpu
from jax.sharding import PartitionSpec as P

HEAD_DIM = 64
LCLASS = 32
EPS = 1e-05
SCALE = 0.125
NEG = -1e30
F32 = jnp.float32
BF = jnp.bfloat16
NF = 64
MIB = 1 << 20
MESH = pl.DeviceIdType.MESH


def canon_T(we, a):
    _,_,c,o=we.shape
    flat=we.reshape(4,4*c,o)
    cols=[]
    for j in range(a):
        top=(a+2*j-1)*c
        cols.append(jnp.pad(flat,((0,0),(top,512-top-4*c),(0,0))))
    return jnp.concatenate(cols,axis=2)

def canon_U(T, a):
    Tt=jnp.swapaxes(T,1,2)
    z=jnp.zeros_like(Tt[:,:,:128])
    left=jnp.concatenate([Tt[:,:,384:512],z],axis=2)
    mid=Tt[:,:,128:384]
    right=jnp.concatenate([z,Tt[:,:,0:128]],axis=2)
    if a>1:
        left=left[:,128:]; right=right[:,:128]
    U=jnp.concatenate([left,mid,right],axis=1)
    return jnp.stack([jnp.concatenate([U[1],U[3]]),jnp.concatenate([U[0],U[2]])])

def outer_A(we):
    w=jnp.arange(64)[:,None]; j=jnp.arange(32)[None,:]
    kw=w-2*j+1
    hot=(kw[None]==jnp.arange(4)[:,None,None]).astype(we.dtype)
    full=jnp.einsum("kwj,hkco->hcwjo",hot,we,preferred_element_type=F32).astype(we.dtype)
    full=full.reshape(4,192,1024)
    z=jnp.zeros_like(full[0])
    return jnp.stack([jnp.concatenate([z,full[0]]),jnp.concatenate([full[1],full[2]]),jnp.concatenate([full[3],z])])

def outer_B(A):
    return jnp.swapaxes(A,1,2).reshape(3072,384)

def gt_to_we(GT, a, c, o):
    tot=0
    for j in range(a):
        s=(a+2*j-1)*c
        tot=tot+GT[:,j*o:(j+1)*o,s:s+4*c]
    return tot

def red_to_we(red):
    r=red.reshape(3,32,2,3,64)[...,:4]
    r=r.transpose(0,2,3,4,1)
    return jnp.stack([r[0,1],r[1,0],r[1,1],r[2,0]])

def sig(z): return 1.0/(1.0+jnp.exp(-z))

def zero_big(ref,rows):
    z=jnp.zeros((NF,1280),BF)
    ref[0,0]=z; ref[rows//2,1]=z
    e=jnp.zeros((rows//2+1,2,NF,128),BF)
    ref[:,:,:,0:128]=e; ref[:,:,:,1152:1280]=e

def zero_small(ref,rows,pad):
    z=jnp.zeros((NF,1024+2*pad),BF)
    ref[0]=z; ref[rows+1]=z
    if pad:
        e=jnp.zeros((rows+2,NF,pad),BF)
        ref[:,:,0:pad]=e; ref[:,:,1024+pad:]=e

def put_big(ref,half0,rows,q,val):
    v=val.reshape(rows,NF,256)
    for t in range(rows):
        ref[half0+(t+1)//2,(t+1)%2,:,128+256*q:384+256*q]=v[t]

def loop(n,body):
    if n==1: body(0)
    else:
        def step(g,c):
            body(g); return c
        lax.fori_loop(0,n,step,0)

def down(src,t_ref,rows,per,emit):
    def body(g):
        i0=g*per
        for q in range(4):
            lhs=jnp.concatenate([src[pl.ds(i0+kh//2,per),kh%2,:,256*q:256*q+512].reshape(per*NF,512) for kh in range(4)],axis=1)
            emit(i0,g*(per//2),q,jnp.dot(lhs,t_ref[...],preferred_element_type=F32))
    loop(rows//per,body)

def up(src,u_ref,rows,per,emit):
    k=u_ref.shape[1]//2
    def body(g):
        m0=g*per
        for q in range(4):
            for odd in range(2):
                lhs=jnp.concatenate([src[pl.ds(m0+1+odd-s,per),:,256*q:256*q+k].reshape(per*NF,k) for s in range(2)],axis=1)
                emit(m0,odd,q,jnp.dot(lhs,u_ref[odd],preferred_element_type=F32).reshape(per,NF,256))
    loop(rows//per,body)

def turn(src,dst,rows,pad):
    for q in range(4):
        dst[256*q:256*q+256,:]=src[1:rows+1,:,pad+256*q:pad+256*q+256].reshape(rows*NF,256).T

def grad_w(big,yt,rows,out):
    def body(kh,half):
        acc=jnp.zeros((256,512),F32)
        for q in range(4):
            win=big[pl.ds(half,rows),kh-2*half,:,256*q:256*q+512].reshape(rows*NF,512)
            acc=acc+jnp.dot(yt[256*q:256*q+256,:],win,preferred_element_type=F32)
        out[kh]=acc
    for kh in range(4): body(kh,kh//2)

def outer_down(xp,a_ref,emit,per=4):
    def body(g):
        i0=g*per
        lhs=jnp.concatenate([xp[pl.ds(i0+d,per)].reshape(per*NF,384) for d in range(3)],axis=1)
        for q in range(4):
            emit(i0,g*(per//2),q,jnp.dot(lhs,a_ref[:,256*q:256*q+256],preferred_element_type=F32))
    loop(32//per,body)

def outer_up(yp,b_ref,emit,per=4):
    def body(g):
        i0=g*per
        lhs=jnp.concatenate([yp[pl.ds(i0+2-d,per)].reshape(per*NF,1024) for d in range(3)],axis=1)
        emit(i0,jnp.dot(lhs,b_ref[...],preferred_element_type=F32).reshape(per,NF,384))
    loop(32//per,body)

def outer_grad(xp,yt,red):
    lane=lax.broadcasted_iota(jnp.int32,(32,384),1)%64
    for d in range(3):
        x=xp[d:d+32].reshape(32*NF,384)
        tot=jnp.zeros((32,384),F32)
        for jb in range(4):
            g=jnp.dot(yt[256*jb:256*jb+256,:],x,preferred_element_type=F32)
            for jj in range(8):
                j=8*jb+jj
                v=pltpu.roll(g[32*jj:32*jj+32],(385-2*j)%384,1)
                if j==0: v=jnp.where(lane==0,0.0,v)
                if j==31: v=jnp.where(lane==3,0.0,v)
                tot=tot+v
        red[d]=tot

def enc_fwd_kernel(xp,a,t2,t3,t4,z1,z2,z3,z4,feat,m1,m2,m3):
    zero_big(m1,32); zero_big(m2,16); zero_big(m3,8)
    def keep(z,m):
        def emit(i0,half0,q,acc):
            rows=acc.shape[0]//NF
            z[pl.ds(i0,rows),:,256*q:256*q+256]=acc.astype(BF).reshape(rows,NF,256)
            val=(acc*sig(acc)).astype(BF)
            if m is None: feat[pl.ds(i0,rows),:,256*q:256*q+256]=val.reshape(rows,NF,256)
            else: put_big(m,half0,rows,q,val)
        return emit
    outer_down(xp,a,keep(z1,m1))
    down(m1,t2,16,4,keep(z2,m2))
    down(m2,t3,8,4,keep(z3,m3))
    down(m3,t4,4,4,keep(z4,None))

def enc_bwd_kernel(xp,z1,z2,z3,z4,df,u2,u3,u4,b,dx,g2,g3,g4,red,m1,m2,m3,s1,s2,s3,s4,yt1,yt2,yt3,yt4):
    zero_big(m1,32); zero_big(m2,16); zero_big(m3,8)
    zero_small(s1,32,0); zero_small(s2,16,128); zero_small(s3,8,128); zero_small(s4,4,256)
    z=z4[...].astype(F32); s=sig(z)
    s4[1:5,:,256:1280]=(df[...].astype(F32)*(s*(1.0+z*(1.0-s)))).astype(BF)
    def back(z_ref,m,dst,pad):
        def emit(m0,odd,q,acc):
            per=acc.shape[0]
            for t in range(per):
                h=2*(m0+t)+odd
                zz=z_ref[h,:,256*q:256*q+256].astype(F32)
                ss=sig(zz); mm=zz*ss
                dst[h+1,:,pad+256*q:pad+256*q+256]=(acc[t]*(ss+mm*(1.0-ss))).astype(BF)
                m[m0+t+odd,1-odd,:,128+256*q:384+256*q]=mm.astype(BF)
        return emit
    up(s4,u4,4,4,back(z3,m3,s3,128))
    turn(s4,yt4,4,256); grad_w(m3,yt4,4,g4)
    up(s3,u3,8,4,back(z2,m2,s2,128))
    turn(s3,yt3,8,128); grad_w(m2,yt3,8,g3)
    up(s2,u2,16,4,back(z1,m1,s1,0))
    turn(s2,yt2,16,128); grad_w(m1,yt2,16,g2)
    def put(i0,acc): dx[pl.ds(i0,acc.shape[0])]=acc.astype(BF)
    outer_up(s1,b,put)
    turn(s1,yt1,32,0); outer_grad(xp,yt1,red)

def dec_fwd_kernel(dec,u4,u3,u2,b,recon,p3,p2,p1,s4,s3,s2,s1):
    zero_small(s1,32,0); zero_small(s2,16,128); zero_small(s3,8,128); zero_small(s4,4,256)
    z=dec[...].astype(F32)
    s4[1:5,:,256:1280]=(z*sig(z)).astype(BF)
    def fwd(p,dst,pad):
        def emit(m0,odd,q,acc):
            for t in range(acc.shape[0]):
                h=2*(m0+t)+odd
                v=acc[t]
                p[h,:,256*q:256*q+256]=v.astype(BF)
                dst[h+1,:,pad+256*q:pad+256*q+256]=(v*sig(v)).astype(BF)
        return emit
    up(s4,u4,4,4,fwd(p3,s3,128))
    up(s3,u3,8,4,fwd(p2,s2,128))
    up(s2,u2,16,4,fwd(p1,s1,0))
    def put(i0,acc): recon[pl.ds(i0,acc.shape[0])]=acc.astype(BF)
    outer_up(s1,b,put)

def dec_bwd_kernel(cp,dec,p3,p2,p1,a,t2,t3,t4,gdec,g2,g3,g4,red,d1,d2,d3,s,yt1,yt2,yt3,yt4):
    zero_big(d1,32); zero_big(d2,16); zero_big(d3,8)
    def maps(p,rows,yt):
        for q in range(4):
            zz=p[:,:,256*q:256*q+256].reshape(rows*NF,256).astype(F32)
            yt[256*q:256*q+256,:]=(zz*sig(zz)).astype(BF).T
    def back(p,dst):
        def emit(i0,half0,q,acc):
            rows=acc.shape[0]//NF
            zz=p[pl.ds(i0,rows),:,256*q:256*q+256].astype(F32).reshape(rows*NF,256)
            ss=sig(zz)
            val=(acc*(ss*(1.0+zz*(1.0-ss)))).astype(BF)
            if dst is None: gdec[pl.ds(i0,rows),:,256*q:256*q+256]=val.reshape(rows,NF,256)
            else: put_big(dst,half0,rows,q,val)
        return emit
    maps(p1,32,yt1); outer_grad(cp,yt1,red)
    outer_down(cp,a,back(p1,d1))
    maps(p2,16,yt2); grad_w(d1,yt2,16,g2)
    down(d1,t2,16,4,back(p2,d2))
    maps(p3,8,yt3); grad_w(d2,yt3,8,g3)
    down(d2,t3,8,4,back(p3,d3))
    maps(dec,4,yt4); grad_w(d3,yt4,4,g4)
    down(d3,t4,4,4,back(dec,None))

def S(shape,dt=BF): return jax.ShapeDtypeStruct(shape,dt)
def V(shape,dt=BF): return pltpu.VMEM(shape,dt)
VM=lambda n:[pl.BlockSpec(memory_space=pltpu.VMEM)]*n
def run(kernel,outs,scratch,args,name,lim=60,flops=10**10):
    return pl.pallas_call(kernel,out_shape=outs,in_specs=VM(len(args)),out_specs=tuple(VM(len(outs))),
        scratch_shapes=scratch,compiler_params=pltpu.CompilerParams(vmem_limit_bytes=lim*MIB),
        cost_estimate=pl.CostEstimate(flops=flops,bytes_accessed=20*MIB,transcendentals=0),name=name)(*args)
big=lambda h:V((h//2+1,2,NF,1280))
def enc_fwd(xp,a,t2,t3,t4):
    return run(enc_fwd_kernel,(S((32,NF,1024)),S((16,NF,1024)),S((8,NF,1024)),S((4,NF,1024)),S((4,NF,1024))),
      [big(32),big(16),big(8)],(xp,a,t2,t3,t4),"encode")
GS=tuple([S((4,256,512),F32)]*3+[S((3,32,384),F32)])
small=lambda h,p:V((h+2,NF,1024+2*p))
yts=[V((1024,32*NF)),V((1024,16*NF)),V((1024,8*NF)),V((1024,4*NF))]
def enc_bwd(xp,z1,z2,z3,z4,df,u2,u3,u4,b):
    return run(enc_bwd_kernel,(S((32,NF,384)),)+GS,[big(32),big(16),big(8),small(32,0),small(16,128),small(8,128),small(4,256)]+yts,
      (xp,z1,z2,z3,z4,df,u2,u3,u4,b),"encode_back")
def dec_fwd(dec,u4,u3,u2,b):
    return run(dec_fwd_kernel,(S((32,NF,384)),S((8,NF,1024)),S((16,NF,1024)),S((32,NF,1024))),
      [small(4,256),small(8,128),small(16,128),small(32,0)],(dec,u4,u3,u2,b),"decode")
def dec_bwd(cp,dec,p3,p2,p1,a,t2,t3,t4):
    return run(dec_bwd_kernel,(S((4,NF,1024)),)+GS,[big(32),big(16),big(8),V((8,128))]+yts,
      (cp,dec,p3,p2,p1,a,t2,t3,t4),"decode_back")


def greet(me):
    barrier = pltpu.get_barrier_semaphore()
    row = lax.axis_index("rows")
    for k in range(1, 4):
        pl.semaphore_signal(
            barrier, inc=1, device_id=(row, lax.rem(me + k, 4)), device_id_type=MESH
        )
    pl.semaphore_wait(barrier, 3)


def frames_in_kernel(x, out, stage, send_sem, recv_sem):
    me = lax.axis_index("strip")
    row = lax.axis_index("rows")
    out[0] = jnp.zeros((NF, 384), BF)
    out[33] = jnp.zeros((NF, 384), BF)

    def turn_rows(i, carry):
        block = jnp.concatenate(
            [x[c, 2 * i + p] for p in range(2) for c in range(3)], axis=0
        )
        flat = block.T
        for k in range(4):
            first = NF * ((k % 2) * 2 + k // 2)
            stage[k, i] = flat[first : first + NF]
        return carry

    lax.fori_loop(0, 8, turn_rows, 0)
    greet(me)
    copies = []
    for k in range(1, 4):
        to = lax.rem(me + k, 4)
        copies.append(
            pltpu.make_async_remote_copy(
                src_ref=stage.at[to],
                dst_ref=out.at[pl.ds(1 + 8 * me, 8)],
                send_sem=send_sem.at[k - 1],
                recv_sem=recv_sem.at[k - 1],
                device_id=(row, to),
                device_id_type=MESH,
            )
        )
    for copy in copies:
        copy.start()
    out[pl.ds(1 + 8 * me, 8)] = stage[me]
    for copy in copies:
        copy.wait()


def frames_out_kernel(y, out, got, send_sem, recv_sem):
    me = lax.axis_index("strip")
    row = lax.axis_index("rows")
    greet(me)
    copies = []
    for k in range(1, 4):
        to = lax.rem(me + k, 4)
        copies.append(
            pltpu.make_async_remote_copy(
                src_ref=y.at[pl.ds(8 * to, 8)],
                dst_ref=got.at[me],
                send_sem=send_sem.at[k - 1],
                recv_sem=recv_sem.at[k - 1],
                device_id=(row, to),
                device_id_type=MESH,
            )
        )
    for copy in copies:
        copy.start()
    got[me] = y[pl.ds(8 * me, 8)]
    for copy in copies:
        copy.wait()

    def turn_rows(i, carry):
        block = jnp.concatenate([got[(b % 2) * 2 + b // 2, i] for b in range(4)], axis=0)
        flat = block.T.astype(out.dtype)
        for p in range(2):
            for c in range(3):
                first = 64 * (3 * p + c)
                out[c, 2 * i + p] = flat[first : first + 64]
        return carry

    lax.fori_loop(0, 8, turn_rows, 0)


def frames_in(block, ident):
    return pl.pallas_call(
        frames_in_kernel,
        out_shape=jax.ShapeDtypeStruct((34, NF, 384), BF),
        in_specs=VM(1),
        out_specs=VM(1)[0],
        scratch_shapes=[
            pltpu.VMEM((4, 8, NF, 384), BF),
            pltpu.SemaphoreType.DMA((3,)),
            pltpu.SemaphoreType.DMA((3,)),
        ],
        compiler_params=pltpu.CompilerParams(
            collective_id=ident, has_side_effects=True, vmem_limit_bytes=32 * MIB
        ),
        name="frames_in",
    )(jnp.transpose(block, (1, 2, 3, 0)))


def frames_out(pairs, dtype, ident):
    flat = pl.pallas_call(
        frames_out_kernel,
        out_shape=jax.ShapeDtypeStruct((3, 16, 64, 256), dtype),
        in_specs=VM(1),
        out_specs=VM(1)[0],
        scratch_shapes=[
            pltpu.VMEM((4, 8, NF, 384), BF),
            pltpu.SemaphoreType.DMA((3,)),
            pltpu.SemaphoreType.DMA((3,)),
        ],
        compiler_params=pltpu.CompilerParams(
            collective_id=ident, has_side_effects=True, vmem_limit_bytes=32 * MIB
        ),
        name="frames_out",
    )(pairs)
    return jnp.transpose(flat, (3, 0, 1, 2))


def across(value):
    return lax.ppermute(value, "strip", [(0, 2), (2, 0), (1, 3), (3, 1)])


def beside(value):
    return lax.ppermute(value, "strip", [(0, 1), (1, 0), (2, 3), (3, 2)])


def pair_total(partial_value):
    low = partial_value.astype(BF)
    got = across(low)
    half = low.shape[0] // 2
    got = jnp.concatenate([got[half:], got[:half]], axis=0)
    return low.astype(F32) + got.astype(F32)


def fold(full, axis):
    half = full.shape[axis] // 2
    own = lax.slice_in_dim(full, 0, half, axis=axis)
    other = lax.slice_in_dim(full, half, 2 * half, axis=axis)
    return own + beside(other.astype(BF)).astype(F32)


def with_sibling(shard, axis):
    return jnp.concatenate([shard, beside(shard)], axis=axis)


def normalize(hidden):
    centred = hidden - jnp.mean(hidden, -1, keepdims=True)
    scale_inv = lax.rsqrt(jnp.mean(centred * centred, -1, keepdims=True) + EPS)
    return (centred * scale_inv, scale_inv)


def normalize_back(grad_normed, unit_rows, scale_inv, gain):
    grad_unit = grad_normed * gain
    grad_gain = jnp.sum(grad_normed * unit_rows, 0)
    grad_rows = scale_inv * (
        grad_unit
        - jnp.mean(grad_unit, -1, keepdims=True)
        - unit_rows * jnp.mean(grad_unit * unit_rows, -1, keepdims=True)
    )
    return (grad_gain, grad_rows)


def grouped_softmax(logits):
    frame_count = logits.shape[0]
    grouped = logits.reshape(frame_count, -1, LCLASS)
    shifted = grouped - jnp.max(grouped, -1, keepdims=True)
    raised = jnp.exp(shifted)
    return (raised / jnp.sum(raised, -1, keepdims=True)).reshape(frame_count, -1)


def make_mask(segment_ids):
    places = jnp.arange(segment_ids.shape[1])
    causal = places[:, None] >= places[None, :]
    return causal[None] & (segment_ids[:, :, None] == segment_ids[:, None, :])


def split_heads(flat_rows, sequences):
    return flat_rows.reshape(sequences, -1, flat_rows.shape[-1] // HEAD_DIM, HEAD_DIM)


def score_block(queries, keys_part, allowed):
    scores = (
        jnp.einsum("bqhe,bkhe->bhqk", queries, keys_part, preferred_element_type=F32) * SCALE
    )
    return jnp.where(allowed[:, None], scores, NEG)


def mm(a, b):
    return jnp.dot(a, b, preferred_element_type=F32)


def mm_t(a, b):
    return lax.dot_general(a, b, (((1,), (1,)), ((), ())), preferred_element_type=F32)


def t_mm(a, b):
    return lax.dot_general(a, b, (((0,), (0,)), ((), ())), preferred_element_type=F32)


def layer_forward(hidden, allowed, gain_pair, qkv_layer, out_layer, up_layer, down_layer):
    sequences = allowed.shape[0]
    unit_attn, inv_attn = normalize(hidden)
    normed_attn = (unit_attn * gain_pair[0]).astype(BF)
    mixed = [mm(normed_attn, qkv_layer[:, k]).astype(BF) for k in range(3)]
    queries, keys_part, vals_part = [split_heads(part, sequences) for part in mixed]
    scores = score_block(queries, keys_part, allowed)
    top_score = jnp.max(scores, -1, keepdims=True)
    raised = jnp.exp(scores - top_score)
    chances = raised / jnp.sum(raised, -1, keepdims=True)
    attended = jnp.einsum(
        "bhqk,bkhe->bqhe", chances.astype(BF), vals_part, preferred_element_type=F32
    )
    attended = attended.astype(BF).reshape(hidden.shape[0], -1)
    middle = hidden + pair_total(mm(attended, out_layer))
    unit_ffn, inv_ffn = normalize(middle)
    normed_ffn = (unit_ffn * gain_pair[1]).astype(BF)
    before = mm(normed_ffn, up_layer)
    inner_act = (before * sig(before)).astype(BF)
    result = middle + pair_total(mm(inner_act, down_layer))
    kept = (
        unit_attn,
        inv_attn,
        normed_attn,
        (queries, keys_part, vals_part),
        chances,
        attended,
        unit_ffn,
        inv_ffn,
        normed_ffn,
        before,
        inner_act,
    )
    return (result, kept)


def layer_backward(
    grad_hidden, allowed, gain_pair, qkv_layer, out_layer, up_layer, down_layer, kept
):
    (
        unit_attn,
        inv_attn,
        normed_attn,
        mixed,
        chances,
        attended,
        unit_ffn,
        inv_ffn,
        normed_ffn,
        before,
        inner_act,
    ) = kept
    token_count = grad_hidden.shape[0]
    grad_low = grad_hidden.astype(BF)
    grad_down = t_mm(inner_act, grad_low)
    grad_inner = mm_t(grad_low, down_layer)
    squash = sig(before)
    grad_before = (grad_inner * (squash * (1.0 + before * (1.0 - squash)))).astype(BF)
    grad_up = t_mm(normed_ffn, grad_before)
    grad_normed = pair_total(mm_t(grad_before, up_layer))
    gain_ffn, grad_mid = normalize_back(grad_normed, unit_ffn, inv_ffn, gain_pair[1])
    grad_middle = grad_hidden + grad_mid
    middle_low = grad_middle.astype(BF)
    grad_project = t_mm(attended, middle_low)
    sequences = allowed.shape[0]
    grad_attended = split_heads(mm_t(middle_low, out_layer).astype(BF), sequences)
    queries, keys_part, vals_part = mixed
    grad_vals = jnp.einsum(
        "bhqk,bqhe->bkhe", chances.astype(BF), grad_attended, preferred_element_type=F32
    )
    grad_chances = jnp.einsum(
        "bqhe,bkhe->bhqk", grad_attended, vals_part, preferred_element_type=F32
    )
    weighted_total = jnp.sum(chances * grad_chances, -1, keepdims=True)
    grad_scores = (chances * (grad_chances - weighted_total)).astype(BF)
    grad_queries = SCALE * jnp.einsum(
        "bhqk,bkhe->bqhe", grad_scores, keys_part, preferred_element_type=F32
    )
    grad_keys = SCALE * jnp.einsum(
        "bhqk,bqhe->bkhe", grad_scores, queries, preferred_element_type=F32
    )
    grad_mixed = [
        part.reshape(token_count, -1).astype(BF) for part in (grad_queries, grad_keys, grad_vals)
    ]
    grad_qkv = jnp.stack([t_mm(normed_attn, part) for part in grad_mixed])
    grad_normed_attn = pair_total(
        sum(mm_t(part, qkv_layer[:, k]) for k, part in enumerate(grad_mixed))
    )
    gain_attn, grad_first = normalize_back(grad_normed_attn, unit_attn, inv_attn, gain_pair[0])
    return (
        grad_middle + grad_first,
        jnp.stack([gain_attn, gain_ffn]),
        grad_qkv,
        grad_project,
        grad_up,
        grad_down,
    )


def rows_total(parts):
    count = lax.axis_size("rows")
    flat = jnp.concatenate([part.astype(BF) for part in parts], axis=0)
    total = flat.shape[0]
    flat = jnp.pad(flat, ((0, -total % (16 * count)), (0, 0)))
    share = lax.psum_scatter(flat, "rows", scatter_dimension=0, tiled=True)
    whole = lax.all_gather(share, "rows", axis=0, tiled=True)
    pieces = []
    offset = 0
    for part in parts:
        pieces.append(whole[offset : offset + part.shape[0]])
        offset = offset + part.shape[0]
    return pieces


def pack_kernels(outer, first, second, third):
    parts = [
        jnp.concatenate([third[:, :, :256], third[:, :, 256:]], axis=1).reshape(2048, 256),
        second.reshape(512, 256),
        jnp.concatenate([first[:2], first[2:]], axis=2).reshape(128, 256),
        jnp.pad(outer.reshape(6, 256), ((0, 122), (0, 0))),
    ]
    return jnp.concatenate(parts, axis=0)


def unpack_kernels(flat):
    third = flat[:2048].reshape(4, 512, 256)
    third = jnp.concatenate([third[:, :256], third[:, 256:]], axis=2)
    second = flat[2048:2560].reshape(4, 128, 256)
    first = flat[2560:2688].reshape(2, 64, 256)
    first = jnp.concatenate([first[:, :, :128], first[:, :, 128:]], axis=0)
    outer = flat[2688:2694].reshape(4, 3, 4, 32)
    return (outer, first, second, third)


def strip_share(flat, x, core):
    half = flat.shape[0] // 2
    low = flat.astype(BF)
    mine = lax.dynamic_slice_in_dim(low, core * half, half)
    theirs = lax.dynamic_slice_in_dim(low, (1 - core) * half, half)
    summed = mine.astype(F32) + beside(theirs).astype(F32)
    low = summed.astype(BF)
    half = half // 2
    mine = lax.dynamic_slice_in_dim(low, x * half, half)
    theirs = lax.dynamic_slice_in_dim(low, (1 - x) * half, half)
    return mine.astype(F32) + across(theirs).astype(F32)


def strip_whole(share, x, core):
    got = across(share)
    half = jnp.where(
        x == 0, jnp.concatenate([share, got]), jnp.concatenate([got, share])
    )
    got = beside(half)
    return jnp.where(
        core == 0, jnp.concatenate([half, got]), jnp.concatenate([got, half])
    )


def features_first(weight):
    return weight.reshape(256, 16, -1).transpose(1, 0, 2).reshape(weight.shape)


def channels_first(weight):
    return weight.reshape(16, 256, -1).transpose(1, 0, 2).reshape(weight.shape)


def shards(
    frames,
    segment_ids,
    encode_one,
    encode_two,
    encode_three,
    encode_four,
    latent_head,
    token_embed,
    positions,
    norm_gains,
    qkv_weight,
    out_weight,
    up_weight,
    down_weight,
    decode_head,
    decode_one,
    decode_two,
    decode_three,
    decode_four,
    token_cotangent,
    frame_cotangent,
):
    strip = lax.axis_index("strip")
    x, core = strip // 2, strip % 2
    layers = qkv_weight.shape[0]

    enc = [w.transpose(2, 3, 1, 0) for w in (encode_one, encode_two, encode_three, encode_four)]
    dec = [
        jnp.flip(w, (2, 3)).transpose(2, 3, 0, 1)
        for w in (decode_four, decode_three, decode_two, decode_one)
    ]
    folds = (4, 2, 1)
    enc_a = outer_A(enc[0])
    dec_a = outer_A(dec[0])
    enc_b, dec_b = outer_B(enc_a), outer_B(dec_a)
    enc_a, dec_a = enc_a.reshape(1152, 1024), dec_a.reshape(1152, 1024)
    enc_t = [canon_T(w, a) for w, a in zip(enc[1:], folds)]
    dec_t = [canon_T(w, a) for w, a in zip(dec[1:], folds)]
    enc_u = [canon_U(t, a) for t, a in zip(enc_t, folds)]
    dec_u = [canon_U(t, a) for t, a in zip(dec_t, folds)]
    enc_t = [t.reshape(2048, 256) for t in enc_t]
    dec_t = [t.reshape(2048, 256) for t in dec_t]

    head_in = with_sibling(features_first(latent_head), 1)
    head_out = with_sibling(features_first(decode_head.T), 1)
    embed = with_sibling(token_embed, 0)
    qkv = with_sibling(qkv_weight, 3)
    project = with_sibling(out_weight, 1)
    widen = with_sibling(up_weight, 2)
    narrow = with_sibling(down_weight, 1)

    pixels = frames_in(frames, 1)
    z1, z2, z3, z4, feat = enc_fwd(pixels, enc_a, *enc_t)
    feat = jnp.concatenate([feat, across(feat)], axis=1)
    head_in4 = head_in.reshape(4, 1024, 512)
    logits = sum(mm(feat[h], head_in4[h]) for h in range(4))
    chances = grouped_softmax(logits)
    latent = chances.astype(BF)

    head_out4 = head_out.reshape(4, 1024, 512)
    spread = jnp.stack([mm_t(latent, head_out4[h]) for h in range(4)]).astype(BF)
    decoded = (
        spread[:, :NF].astype(F32) + across(spread[:, NF:]).astype(F32)
    ).astype(BF)
    recon_pairs, p3, p2, p1 = dec_fwd(decoded, dec_u[2], dec_u[1], dec_u[0], dec_b)
    recon = frames_out(recon_pairs, BF, 3)

    first = 2 * core
    def mine(array, size):
        own = lax.dynamic_slice_in_dim(array, (first + x) * size, size)
        other = lax.dynamic_slice_in_dim(array, (first + 1 - x) * size, size)
        return jnp.concatenate([own, other], axis=0)
    segments = mine(segment_ids, 1)
    allowed = make_mask(segments)
    embedded = pair_total(mm(latent, embed))
    hidden = embedded.reshape(2, NF, -1) + positions.astype(F32)[None]
    hidden = hidden.reshape(2 * NF, -1)
    kept_layers = []
    for k in range(layers):
        hidden, kept = layer_forward(
            hidden, allowed, norm_gains[k], qkv[k], project[k], widen[k], narrow[k]
        )
        kept_layers.append(kept)
    tokens = hidden.astype(BF)
    tokens = jnp.where(
        x == 0, tokens, jnp.concatenate([tokens[NF:], tokens[:NF]], axis=0)
    )
    other_tokens = beside(tokens)
    tokens_out = jnp.where(
        core == 0,
        jnp.concatenate([tokens, other_tokens]),
        jnp.concatenate([other_tokens, tokens]),
    )
    grad_hidden = mine(token_cotangent, NF).astype(F32)
    layer_grads = [None] * layers
    for k in reversed(range(layers)):
        grad_hidden, *layer_grads[k] = layer_backward(
            grad_hidden,
            allowed,
            norm_gains[k],
            qkv[k],
            project[k],
            widen[k],
            narrow[k],
            kept_layers[k],
        )
    gains, g_qkv, g_project, g_widen, g_narrow = [
        jnp.stack([entry[slot] for entry in layer_grads]) for slot in range(5)
    ]
    g_positions = grad_hidden[:NF] + grad_hidden[NF:]
    embed_low = grad_hidden.astype(BF)
    g_embed = fold(t_mm(latent, embed_low), 0)
    grad_latent = mm_t(embed_low, embed)
    g_qkv = fold(g_qkv, 3)
    g_project = fold(g_project, 1)
    g_widen = fold(g_widen, 2)
    g_narrow = fold(g_narrow, 1)
    small = jnp.concatenate([g_positions, gains.reshape(-1, 512)], axis=0)
    small = small + beside(small.astype(BF)).astype(F32)

    hints = frames_in(frame_cotangent, 2)
    g_decoded, h2, h3, h4, h_outer = dec_bwd(hints, decoded, p3, p2, p1, dec_a, *dec_t)
    g_spread = jnp.concatenate([g_decoded, across(g_decoded)], axis=1)
    g_head_out = fold(jnp.concatenate([t_mm(g_spread[h], latent) for h in range(4)]), 1)
    grad_latent = grad_latent + sum(mm(g_spread[h], head_out4[h]) for h in range(4))
    dec_flat = pack_kernels(
        red_to_we(h_outer),
        gt_to_we(h2, 4, 32, 64),
        gt_to_we(h3, 2, 64, 128),
        gt_to_we(h4, 1, 128, 256),
    )
    dec_share = strip_share(dec_flat, x, core)

    early_wide = rows_total(
        [
            g_widen.reshape(-1, 512),
            g_narrow.reshape(-1, 512),
            g_project.reshape(-1, 512),
            g_embed,
            small,
        ]
    )
    qkv_rows = jnp.concatenate([g_qkv[0], g_qkv[1]], axis=-1).reshape(-1, 256)
    early = rows_total([g_head_out, qkv_rows, dec_share])

    grouped = chances.reshape(2 * NF, -1, LCLASS)
    grad_grouped = grad_latent.reshape(grouped.shape)
    grad_logits = grouped * (grad_grouped - jnp.sum(grouped * grad_grouped, -1, keepdims=True))
    grad_logits = grad_logits.reshape(2 * NF, -1).astype(BF)
    g_head_in = fold(jnp.concatenate([t_mm(feat[h], grad_logits) for h in range(4)]), 1)
    g_feat = jnp.stack([mm_t(grad_logits, head_in4[h]) for h in range(4)]).astype(BF)
    g_feat = (g_feat[:, :NF].astype(F32) + across(g_feat[:, NF:]).astype(F32)).astype(BF)
    d_pairs, e2, e3, e4, e_outer = enc_bwd(pixels, z1, z2, z3, z4, g_feat, *enc_u, enc_b)
    frames_grad = frames_out(d_pairs, F32, 4)
    enc_flat = pack_kernels(
        red_to_we(e_outer),
        gt_to_we(e2, 4, 32, 64),
        gt_to_we(e3, 2, 64, 128),
        gt_to_we(e4, 1, 128, 256),
    )
    enc_share = strip_share(enc_flat, x, core)
    late = rows_total([g_head_in, enc_share])

    def of_encoder(part, c, o):
        return part.astype(F32).reshape(4, o, 4, c).transpose(1, 3, 0, 2)

    def of_decoder(part, c, o):
        return jnp.flip(part.astype(F32).reshape(4, o, 4, c), (0, 2)).transpose(3, 1, 0, 2)

    k1, k2, k3, k4 = unpack_kernels(strip_whole(late[1], x, core))
    j1, j2, j3, j4 = unpack_kernels(strip_whole(early[2], x, core))
    r_qkv = early[1].astype(F32).reshape(3, 512, 2, 128).transpose(2, 1, 0, 3)
    return (
        tokens_out,
        recon,
        frames_grad,
        k1.astype(F32).transpose(3, 1, 0, 2),
        of_encoder(k2, 32, 64),
        of_encoder(k3, 64, 128),
        of_encoder(k4, 128, 256),
        channels_first(late[0].astype(F32)),
        early_wide[3].astype(F32),
        early_wide[4][:NF].astype(F32),
        early_wide[4][NF:].astype(F32).reshape(norm_gains.shape),
        r_qkv,
        early_wide[2].astype(F32).reshape(out_weight.shape),
        early_wide[0].astype(F32).reshape(up_weight.shape),
        early_wide[1].astype(F32).reshape(down_weight.shape),
        channels_first(early[0].astype(F32)).T,
        of_decoder(j4, 128, 256),
        of_decoder(j3, 64, 128),
        of_decoder(j2, 32, 64),
        jnp.flip(j1.astype(F32), (0, 2)).transpose(1, 3, 0, 2),
    )


def solution(mesh):
    placed = (
        P("rows", None, "strip", None),
        P("rows", None),
        P(),
        P(),
        P(),
        P(),
        P(None, "strip"),
        P("strip", None),
        P(),
        P(),
        P(None, None, None, "strip"),
        P(None, "strip", None),
        P(None, None, "strip"),
        P(None, "strip", None),
        P("strip", None),
        P(),
        P(),
        P(),
        P(),
        P("rows", None),
        P("rows", None, "strip", None),
    )
    return jax.shard_map(
        shards,
        mesh=mesh,
        in_specs=placed,
        out_specs=(
            P("rows", None),
            P("rows", None, "strip", None),
            P("rows", None, "strip", None),
            P(),
            P(),
            P(),
            P(),
            P(None, "strip"),
            P("strip", None),
            P(),
            P(),
            P(None, None, None, "strip"),
            P(None, "strip", None),
            P(None, None, "strip"),
            P(None, "strip", None),
            P("strip", None),
            P(),
            P(),
            P(),
            P(),
        ),
        check_vma=False,
    )
```

```python
import functools

import jax
import jax.numpy as jnp
from jax import lax
from jax.experimental import pallas as pl
from jax.experimental.pallas import tpu as pltpu
from jax.sharding import PartitionSpec as P

HEAD_DIM = 64
LCLASS = 32
EPS = 1e-05
SCALE = 0.125
NEG = -1e30
F32 = jnp.float32
BF = jnp.bfloat16
NF = 64
MIB = 1 << 20
MESH = pl.DeviceIdType.MESH


def canon_T(we, a):
    _,_,c,o=we.shape
    flat=we.reshape(4,4*c,o)
    cols=[]
    for j in range(a):
        top=(a+2*j-1)*c
        cols.append(jnp.pad(flat,((0,0),(top,512-top-4*c),(0,0))))
    return jnp.concatenate(cols,axis=2)

def canon_U(T, a):
    Tt=jnp.swapaxes(T,1,2)
    z=jnp.zeros_like(Tt[:,:,:128])
    left=jnp.concatenate([Tt[:,:,384:512],z],axis=2)
    mid=Tt[:,:,128:384]
    right=jnp.concatenate([z,Tt[:,:,0:128]],axis=2)
    if a>1:
        left=left[:,128:]; right=right[:,:128]
    U=jnp.concatenate([left,mid,right],axis=1)
    return jnp.stack([jnp.concatenate([U[1],U[3]]),jnp.concatenate([U[0],U[2]])])

def outer_A(we):
    w=jnp.arange(64)[:,None]; j=jnp.arange(32)[None,:]
    kw=w-2*j+1
    hot=(kw[None]==jnp.arange(4)[:,None,None]).astype(we.dtype)
    full=jnp.einsum("kwj,hkco->hcwjo",hot,we,preferred_element_type=F32).astype(we.dtype)
    full=full.reshape(4,192,1024)
    z=jnp.zeros_like(full[0])
    return jnp.stack([jnp.concatenate([z,full[0]]),jnp.concatenate([full[1],full[2]]),jnp.concatenate([full[3],z])])

def outer_B(A):
    return jnp.swapaxes(A,1,2).reshape(3072,384)

def gt_to_we(GT, a, c, o):
    tot=0
    for j in range(a):
        s=(a+2*j-1)*c
        tot=tot+GT[:,j*o:(j+1)*o,s:s+4*c]
    return tot

def red_to_we(red):
    r=red.reshape(3,32,2,3,64)[...,:4]
    r=r.transpose(0,2,3,4,1)
    return jnp.stack([r[0,1],r[1,0],r[1,1],r[2,0]])

def sig(z): return 1.0/(1.0+jnp.exp(-z))

def zero_big(ref,rows):
    z=jnp.zeros((NF,1280),BF)
    ref[0,0]=z; ref[rows//2,1]=z
    e=jnp.zeros((rows//2+1,2,NF,128),BF)
    ref[:,:,:,0:128]=e; ref[:,:,:,1152:1280]=e

def zero_small(ref,rows,pad):
    z=jnp.zeros((NF,1024+2*pad),BF)
    ref[0]=z; ref[rows+1]=z
    if pad:
        e=jnp.zeros((rows+2,NF,pad),BF)
        ref[:,:,0:pad]=e; ref[:,:,1024+pad:]=e

def put_big(ref,half0,rows,q,val):
    v=val.reshape(rows,NF,256)
    for t in range(rows):
        ref[half0+(t+1)//2,(t+1)%2,:,128+256*q:384+256*q]=v[t]

def loop(n,body):
    if n==1: body(0)
    else:
        def step(g,c):
            body(g); return c
        lax.fori_loop(0,n,step,0)

def down(src,t_ref,rows,per,emit):
    def body(g):
        i0=g*per
        for q in range(4):
            lhs=jnp.concatenate([src[pl.ds(i0+kh//2,per),kh%2,:,256*q:256*q+512].reshape(per*NF,512) for kh in range(4)],axis=1)
            emit(i0,g*(per//2),q,jnp.dot(lhs,t_ref[...],preferred_element_type=F32))
    loop(rows//per,body)

def up(src,u_ref,rows,per,emit):
    k=u_ref.shape[1]//2
    def body(g):
        m0=g*per
        for q in range(4):
            for odd in range(2):
                lhs=jnp.concatenate([src[pl.ds(m0+1+odd-s,per),:,256*q:256*q+k].reshape(per*NF,k) for s in range(2)],axis=1)
                emit(m0,odd,q,jnp.dot(lhs,u_ref[odd],preferred_element_type=F32).reshape(per,NF,256))
    loop(rows//per,body)

def turn(src,dst,rows,pad):
    for q in range(4):
        dst[256*q:256*q+256,:]=src[1:rows+1,:,pad+256*q:pad+256*q+256].reshape(rows*NF,256).T

def grad_w(big,yt,rows,out):
    def body(kh,half):
        acc=jnp.zeros((256,512),F32)
        for q in range(4):
            win=big[pl.ds(half,rows),kh-2*half,:,256*q:256*q+512].reshape(rows*NF,512)
            acc=acc+jnp.dot(yt[256*q:256*q+256,:],win,preferred_element_type=F32)
        out[kh]=acc
    for kh in range(4): body(kh,kh//2)

def outer_down(xp,a_ref,emit,per=4):
    def body(g):
        i0=g*per
        lhs=jnp.concatenate([xp[pl.ds(i0+d,per)].reshape(per*NF,384) for d in range(3)],axis=1)
        for q in range(4):
            emit(i0,g*(per//2),q,jnp.dot(lhs,a_ref[:,256*q:256*q+256],preferred_element_type=F32))
    loop(32//per,body)

def outer_up(yp,b_ref,emit,per=4):
    def body(g):
        i0=g*per
        lhs=jnp.concatenate([yp[pl.ds(i0+2-d,per)].reshape(per*NF,1024) for d in range(3)],axis=1)
        emit(i0,jnp.dot(lhs,b_ref[...],preferred_element_type=F32).reshape(per,NF,384))
    loop(32//per,body)

def outer_grad(xp,yt,red):
    lane=lax.broadcasted_iota(jnp.int32,(32,384),1)%64
    for d in range(3):
        x=xp[d:d+32].reshape(32*NF,384)
        tot=jnp.zeros((32,384),F32)
        for jb in range(4):
            g=jnp.dot(yt[256*jb:256*jb+256,:],x,preferred_element_type=F32)
            for jj in range(8):
                j=8*jb+jj
                v=pltpu.roll(g[32*jj:32*jj+32],(385-2*j)%384,1)
                if j==0: v=jnp.where(lane==0,0.0,v)
                if j==31: v=jnp.where(lane==3,0.0,v)
                tot=tot+v
        red[d]=tot

def enc_fwd_kernel(xp,a,t2,t3,t4,z1,z2,z3,z4,feat,m1,m2,m3):
    zero_big(m1,32); zero_big(m2,16); zero_big(m3,8)
    def keep(z,m):
        def emit(i0,half0,q,acc):
            rows=acc.shape[0]//NF
            z[pl.ds(i0,rows),:,256*q:256*q+256]=acc.astype(BF).reshape(rows,NF,256)
            val=(acc*sig(acc)).astype(BF)
            if m is None: feat[pl.ds(i0,rows),:,256*q:256*q+256]=val.reshape(rows,NF,256)
            else: put_big(m,half0,rows,q,val)
        return emit
    outer_down(xp,a,keep(z1,m1))
    down(m1,t2,16,4,keep(z2,m2))
    down(m2,t3,8,4,keep(z3,m3))
    down(m3,t4,4,4,keep(z4,None))

def enc_bwd_kernel(xp,z1,z2,z3,z4,df,u2,u3,u4,b,dx,g2,g3,g4,red,m1,m2,m3,s1,s2,s3,s4,yt1,yt2,yt3,yt4):
    zero_big(m1,32); zero_big(m2,16); zero_big(m3,8)
    zero_small(s1,32,0); zero_small(s2,16,128); zero_small(s3,8,128); zero_small(s4,4,256)
    z=z4[...].astype(F32); s=sig(z)
    s4[1:5,:,256:1280]=(df[...].astype(F32)*(s*(1.0+z*(1.0-s)))).astype(BF)
    def back(z_ref,m,dst,pad):
        def emit(m0,odd,q,acc):
            per=acc.shape[0]
            for t in range(per):
                h=2*(m0+t)+odd
                zz=z_ref[h,:,256*q:256*q+256].astype(F32)
                ss=sig(zz); mm=zz*ss
                dst[h+1,:,pad+256*q:pad+256*q+256]=(acc[t]*(ss+mm*(1.0-ss))).astype(BF)
                m[m0+t+odd,1-odd,:,128+256*q:384+256*q]=mm.astype(BF)
        return emit
    up(s4,u4,4,4,back(z3,m3,s3,128))
    turn(s4,yt4,4,256); grad_w(m3,yt4,4,g4)
    up(s3,u3,8,4,back(z2,m2,s2,128))
    turn(s3,yt3,8,128); grad_w(m2,yt3,8,g3)
    up(s2,u2,16,4,back(z1,m1,s1,0))
    turn(s2,yt2,16,128); grad_w(m1,yt2,16,g2)
    def put(i0,acc): dx[pl.ds(i0,acc.shape[0])]=acc.astype(BF)
    outer_up(s1,b,put)
    turn(s1,yt1,32,0); outer_grad(xp,yt1,red)

def dec_fwd_kernel(dec,u4,u3,u2,b,recon,p3,p2,p1,s4,s3,s2,s1):
    zero_small(s1,32,0); zero_small(s2,16,128); zero_small(s3,8,128); zero_small(s4,4,256)
    z=dec[...].astype(F32)
    s4[1:5,:,256:1280]=(z*sig(z)).astype(BF)
    def fwd(p,dst,pad):
        def emit(m0,odd,q,acc):
            for t in range(acc.shape[0]):
                h=2*(m0+t)+odd
                v=acc[t]
                p[h,:,256*q:256*q+256]=v.astype(BF)
                dst[h+1,:,pad+256*q:pad+256*q+256]=(v*sig(v)).astype(BF)
        return emit
    up(s4,u4,4,4,fwd(p3,s3,128))
    up(s3,u3,8,4,fwd(p2,s2,128))
    up(s2,u2,16,4,fwd(p1,s1,0))
    def put(i0,acc): recon[pl.ds(i0,acc.shape[0])]=acc.astype(BF)
    outer_up(s1,b,put)

def dec_bwd_kernel(c0,c1,c2,c3,dec,p3,p2,p1,a,t2,t3,t4,gdec,g2,g3,g4,red,d1,d2,d3,cp,yt1,yt2,yt3,yt4):
    me=lax.axis_index("strip")
    cp[0]=jnp.zeros((NF,384),BF); cp[33]=jnp.zeros((NF,384),BF)
    for k,part in enumerate((c0,c1,c2,c3)):
        cp[pl.ds(1+8*lax.rem(me+4-k,4),8)]=part[...]
    zero_big(d1,32); zero_big(d2,16); zero_big(d3,8)
    def maps(p,rows,yt):
        for q in range(4):
            zz=p[:,:,256*q:256*q+256].reshape(rows*NF,256).astype(F32)
            yt[256*q:256*q+256,:]=(zz*sig(zz)).astype(BF).T
    def back(p,dst):
        def emit(i0,half0,q,acc):
            rows=acc.shape[0]//NF
            zz=p[pl.ds(i0,rows),:,256*q:256*q+256].astype(F32).reshape(rows*NF,256)
            ss=sig(zz)
            val=(acc*(ss*(1.0+zz*(1.0-ss)))).astype(BF)
            if dst is None: gdec[pl.ds(i0,rows),:,256*q:256*q+256]=val.reshape(rows,NF,256)
            else: put_big(dst,half0,rows,q,val)
        return emit
    maps(p1,32,yt1); outer_grad(cp,yt1,red)
    outer_down(cp,a,back(p1,d1))
    maps(p2,16,yt2); grad_w(d1,yt2,16,g2)
    down(d1,t2,16,4,back(p2,d2))
    maps(p3,8,yt3); grad_w(d2,yt3,8,g3)
    down(d2,t3,8,4,back(p3,d3))
    maps(dec,4,yt4); grad_w(d3,yt4,4,g4)
    down(d3,t4,4,4,back(dec,None))

def S(shape,dt=BF): return jax.ShapeDtypeStruct(shape,dt)
def V(shape,dt=BF): return pltpu.VMEM(shape,dt)
VM=lambda n:[pl.BlockSpec(memory_space=pltpu.VMEM)]*n
def run(kernel,outs,scratch,args,name,lim=60,flops=10**10):
    return pl.pallas_call(kernel,out_shape=outs,in_specs=VM(len(args)),out_specs=tuple(VM(len(outs))),
        scratch_shapes=scratch,compiler_params=pltpu.CompilerParams(vmem_limit_bytes=lim*MIB),
        cost_estimate=pl.CostEstimate(flops=flops,bytes_accessed=20*MIB,transcendentals=0),name=name)(*args)
big=lambda h:V((h//2+1,2,NF,1280))
def enc_fwd(xp,a,t2,t3,t4):
    return run(enc_fwd_kernel,(S((32,NF,1024)),S((16,NF,1024)),S((8,NF,1024)),S((4,NF,1024)),S((4,NF,1024))),
      [big(32),big(16),big(8)],(xp,a,t2,t3,t4),"encode")
GS=tuple([S((4,256,512),F32)]*3+[S((3,32,384),F32)])
small=lambda h,p:V((h+2,NF,1024+2*p))
yts=[V((1024,32*NF)),V((1024,16*NF)),V((1024,8*NF)),V((1024,4*NF))]
def enc_bwd(xp,z1,z2,z3,z4,df,u2,u3,u4,b):
    return run(enc_bwd_kernel,(S((32,NF,384)),)+GS,[big(32),big(16),big(8),small(32,0),small(16,128),small(8,128),small(4,256)]+yts,
      (xp,z1,z2,z3,z4,df,u2,u3,u4,b),"encode_back")
def dec_fwd(dec,u4,u3,u2,b):
    return run(dec_fwd_kernel,(S((32,NF,384)),S((8,NF,1024)),S((16,NF,1024)),S((32,NF,1024))),
      [small(4,256),small(8,128),small(16,128),small(32,0)],(dec,u4,u3,u2,b),"decode")
def dec_bwd(hints,dec,p3,p2,p1,a,t2,t3,t4):
    return run(dec_bwd_kernel,(S((4,NF,1024)),)+GS,[big(32),big(16),big(8),V((34,NF,384))]+yts,
      (*hints,dec,p3,p2,p1,a,t2,t3,t4),"decode_back")


def first_frame(strip):
    return NF * ((strip % 2) * 2 + strip // 2)


def turned_rows(x, i):
    return jnp.concatenate([x[c, 2 * i + p] for p in range(2) for c in range(3)], axis=0).T


def frames_in_kernel(x, out, stage, send_sem, recv_sem):
    me = lax.axis_index("strip")
    row = lax.axis_index("rows")
    out[0] = jnp.zeros((NF, 384), BF)
    out[33] = jnp.zeros((NF, 384), BF)

    def turn_rows(i, carry):
        flat = turned_rows(x, i)
        for k in range(4):
            stage[k, i] = flat[first_frame(k) : first_frame(k) + NF]
        return carry

    lax.fori_loop(0, 8, turn_rows, 0)
    barrier = pltpu.get_barrier_semaphore()
    for k in range(1, 4):
        pl.semaphore_signal(
            barrier, inc=1, device_id=(row, lax.rem(me + k, 4)), device_id_type=MESH
        )
    pl.semaphore_wait(barrier, 3)
    copies = []
    for k in range(1, 4):
        to = lax.rem(me + k, 4)
        copies.append(
            pltpu.make_async_remote_copy(
                src_ref=stage.at[to],
                dst_ref=out.at[pl.ds(1 + 8 * me, 8)],
                send_sem=send_sem.at[k - 1],
                recv_sem=recv_sem.at[k - 1],
                device_id=(row, to),
                device_id_type=MESH,
            )
        )
    for copy in copies:
        copy.start()
    out[pl.ds(1 + 8 * me, 8)] = stage[me]
    for copy in copies:
        copy.wait()


def frames_in(block, ident):
    return pl.pallas_call(
        frames_in_kernel,
        out_shape=jax.ShapeDtypeStruct((34, NF, 384), BF),
        in_specs=VM(1),
        out_specs=VM(1)[0],
        scratch_shapes=[
            pltpu.VMEM((4, 8, NF, 384), BF),
            pltpu.SemaphoreType.DMA((3,)),
            pltpu.SemaphoreType.DMA((3,)),
        ],
        compiler_params=pltpu.CompilerParams(
            collective_id=ident, has_side_effects=True, vmem_limit_bytes=32 * MIB
        ),
        name="frames_in",
    )(jnp.transpose(block, (1, 2, 3, 0)))


def turn_kernel(x, *out):
    me = lax.axis_index("strip")

    def turn_rows(i, carry):
        flat = turned_rows(x, i)
        for k in range(4):
            part = flat[first_frame(k) : first_frame(k) + NF]
            for step in range(4):

                @pl.when(lax.rem(me + step, 4) == k)
                def _():
                    out[step][i] = part

        return carry

    lax.fori_loop(0, 8, turn_rows, 0)


def frames_in_later(block):
    parts = pl.pallas_call(
        turn_kernel,
        out_shape=(jax.ShapeDtypeStruct((8, NF, 384), BF),) * 4,
        in_specs=VM(1),
        out_specs=tuple(VM(4)),
        compiler_params=pltpu.CompilerParams(vmem_limit_bytes=32 * MIB),
        name="turn",
    )(jnp.transpose(block, (1, 2, 3, 0)))
    return [parts[0]] + [
        lax.ppermute(parts[k], "strip", [(s, (s + k) % 4) for s in range(4)]) for k in range(1, 4)
    ]


def finish_kernel(
    count, chunks, v, recon, grad, total, recon_out, grad_out,
    got, from_near, summed, from_far, strip_sems, near_sems, far_sems, back_sems, last_sems,
):
    me = lax.axis_index("strip")
    row = lax.axis_index("rows")
    half = count // 2
    near, far = lax.rem(row, 2), lax.div(row, 2)
    near_device = (row + 1 - 2 * near, me)
    barrier = pltpu.get_barrier_semaphore()
    strip_devices = [(row, lax.rem(me + k, 4)) for k in range(1, 4)]
    far_places = [lax.rem(far + k, half) for k in range(1, half)]
    far_devices = [(2 * place + near, me) for place in far_places]
    for device in strip_devices + [near_device] + far_devices:
        pl.semaphore_signal(barrier, inc=1, device_id=device, device_id_type=MESH)
    pl.semaphore_wait(barrier, 3 + half)

    def copy(src, dst, sems, index, device):
        return pltpu.make_async_remote_copy(
            src_ref=src,
            dst_ref=dst,
            send_sem=sems.at[(0,) + index],
            recv_sem=sems.at[(1,) + index],
            device_id=device,
            device_id_type=MESH,
        )

    near_copies = [
        copy(v.at[c, 1 - near], from_near.at[c], near_sems, (c,), near_device)
        for c in range(chunks)
    ]
    for one in near_copies:
        one.start()
    strip_copies = []
    for slot, pairs in enumerate((recon, grad)):
        for k in range(1, 4):
            to = lax.rem(me + k, 4)
            strip_copies.append(
                copy(
                    pairs.at[pl.ds(8 * to, 8)],
                    got.at[slot, me],
                    strip_sems,
                    (slot, k - 1),
                    (row, to),
                )
            )
    for one in strip_copies:
        one.start()
    for slot, pairs in enumerate((recon, grad)):
        got[slot, me] = pairs[pl.ds(8 * me, 8)]

    def turn(slot, out):
        for one in strip_copies[3 * slot : 3 * slot + 3]:
            one.wait()

        def turn_rows(i, carry):
            block = jnp.concatenate([got[slot, (b % 2) * 2 + b // 2, i] for b in range(4)], axis=0)
            flat = block.T.astype(out.dtype)
            for p in range(2):
                for c in range(3):
                    first = 64 * (3 * p + c)
                    out[c, 2 * i + p] = flat[first : first + 64]
            return carry

        lax.fori_loop(0, 8, turn_rows, 0)

    far_copies, back_copies, last_copies = {}, {}, {}

    def stage_far(c):
        near_copies[c].wait()
        summed[c] = (v[c, near].astype(F32) + from_near[c].astype(F32)).astype(BF)
        far_copies[c] = [
            copy(summed.at[c, place], from_far.at[c, k], far_sems, (c, k), device)
            for k, (place, device) in enumerate(zip(far_places, far_devices))
        ]
        for one in far_copies[c]:
            one.start()

    def stage_back(c):
        for one in far_copies[c]:
            one.wait()
        whole = summed[c, far].astype(F32)
        for k in range(half - 1):
            whole = whole + from_far[c, k].astype(F32)
        total[c, near, far] = whole.astype(BF)
        back_copies[c] = [
            copy(total.at[c, near, far], total.at[c, near, far], back_sems, (c, k), device)
            for k, device in enumerate(far_devices)
        ]
        for one in back_copies[c]:
            one.start()

    def stage_last(c):
        for one in back_copies[c]:
            one.wait()
        last_copies[c] = copy(
            total.at[c, near], total.at[c, near], last_sems, (c,), near_device
        )
        last_copies[c].start()

    for t in range(chunks + 2):
        if t < chunks:
            stage_far(t)
        if t == 1:
            turn(0, recon_out)
        if t == 3:
            turn(1, grad_out)
        if 0 <= t - 1 < chunks:
            stage_back(t - 1)
        if 0 <= t - 2 < chunks:
            stage_last(t - 2)
    for c in range(chunks):
        last_copies[c].wait()


def finish(flat, recon, grad, chunks, ident):
    count = lax.axis_size("rows")
    half = count // 2
    rows = flat.shape[0]
    flat = jnp.pad(flat, ((0, -rows % (16 * count * chunks)), (0, 0)))
    each = flat.shape[0] // (count * chunks)
    shape = (chunks, 2, half, each, 256)
    dma = pltpu.SemaphoreType.DMA
    total, recon_out, grad_out = pl.pallas_call(
        functools.partial(finish_kernel, count, chunks),
        out_shape=(
            jax.ShapeDtypeStruct(shape, BF),
            jax.ShapeDtypeStruct((3, 16, 64, 256), BF),
            jax.ShapeDtypeStruct((3, 16, 64, 256), F32),
        ),
        in_specs=VM(3),
        out_specs=tuple(VM(3)),
        scratch_shapes=[
            pltpu.VMEM((2, 4, 8, NF, 384), BF),
            pltpu.VMEM((chunks, half, each, 256), BF),
            pltpu.VMEM((chunks, half, each, 256), BF),
            pltpu.VMEM((chunks, half - 1, each, 256), BF),
            dma((2, 2, 3)),
            dma((2, chunks)),
            dma((2, chunks, half - 1)),
            dma((2, chunks, half - 1)),
            dma((2, chunks)),
        ],
        compiler_params=pltpu.CompilerParams(
            collective_id=ident, has_side_effects=True, vmem_limit_bytes=56 * MIB
        ),
        name="finish",
    )(flat.reshape(shape), recon, grad)
    return (
        total.reshape(-1, 256)[:rows],
        jnp.transpose(recon_out, (3, 0, 1, 2)),
        jnp.transpose(grad_out, (3, 0, 1, 2)),
    )


def dot(a, b):
    return jnp.dot(a, b, preferred_element_type=F32)


def dot_nt(a, b):
    return lax.dot_general(a, b, (((1,), (1,)), ((), ())), preferred_element_type=F32)


def over_groups(values, join):
    lanes = values.shape[1]
    lane = lax.broadcasted_iota(jnp.int32, values.shape, 1)
    for step in (1, 2, 4, 8, 16):
        upper = lax.rem(lax.div(lane, step), 2) == 1
        other = jnp.where(
            upper, pltpu.roll(values, step, 1), pltpu.roll(values, lanes - step, 1)
        )
        values = join(values, other)
    return values


def unit_of(hidden):
    centred = hidden - jnp.mean(hidden, -1, keepdims=True)
    scale_inv = lax.rsqrt(jnp.mean(centred * centred, -1, keepdims=True) + EPS)
    return centred * scale_inv, scale_inv


def unit_back(grad_normed, unit_rows, scale_inv, gain):
    grad_unit = grad_normed * gain
    grad_gain = jnp.sum(grad_normed * unit_rows, 0, keepdims=True)
    grad_rows = scale_inv * (
        grad_unit
        - jnp.mean(grad_unit, -1, keepdims=True)
        - unit_rows * jnp.mean(grad_unit * unit_rows, -1, keepdims=True)
    )
    return grad_gain, grad_rows


LAYER_ROWS = 1536


def token_rows(layers):
    return layers * LAYER_ROWS + 256 + NF + 16


def middle_kernel(
    layers,
    feat, lh0, lh1, dh0, dh1, emb0, emb1, pos, gains, allow, cot,
    qkv0, qkv1, proj0, proj1, up0, up1, down0, down1,
    tokens, latent_out, chances_out, decoded, flat, grad_latent,
    feat_got, feat_sems, keep, send, sent, spread_sems, parts, gots, pair_sems,
    other, other_got, fold_sems, unit_a, unit_f, normed_a, normed_f, mixed, weights,
    attended, before, inner, gain_rows,
):
    strip = lax.axis_index("strip")
    row = lax.axis_index("rows")
    partner = (row, lax.rem(strip + 2, 4))
    sibling = (row, strip + 1 - 2 * lax.rem(strip, 2))
    barrier = pltpu.get_barrier_semaphore()
    for device in (partner, sibling):
        pl.semaphore_signal(barrier, inc=1, device_id=device, device_id_type=MESH)
    pl.semaphore_wait(barrier, 2)

    def copy(src, dst, sems, index, device):
        return pltpu.make_async_remote_copy(
            src_ref=src,
            dst_ref=dst,
            send_sem=sems.at[0, index],
            recv_sem=sems.at[1, index],
            device_id=device,
            device_id_type=MESH,
        )

    feat_copy = copy(feat, feat_got, feat_sems, 0, partner)
    feat_copy.start()

    def total_start(index, value):
        parts[index] = value.astype(BF)
        one = copy(parts.at[index], gots.at[index], pair_sems, index, partner)
        one.start()
        return one

    def total_wait(index, one):
        one.wait()
        got = jnp.concatenate([gots[index, NF:], gots[index, :NF]], axis=0)
        return parts[index].astype(F32) + got.astype(F32)

    def logits_of(maps):
        halves = []
        for weight in (lh0, lh1):
            total = jnp.zeros((NF, 256), F32)
            for h in range(4):
                total = total + dot(maps[h], weight[1024 * h : 1024 * h + 1024])
            halves.append(total)
        return jnp.concatenate(halves, axis=1)

    mine = logits_of(feat)
    feat_copy.wait()
    logits = jnp.concatenate([mine, logits_of(feat_got)], axis=0)
    raised = jnp.exp(logits - over_groups(logits, jnp.maximum))
    chances = raised / over_groups(raised, jnp.add)
    latent = chances.astype(BF)
    chances_out[...] = chances
    latent_out[...] = latent

    waiting = total_start(0, dot(latent[:, :256], emb0[...]) + dot(latent[:, 256:], emb1[...]))
    for hw in range(16):
        lanes = slice(256 * (hw % 4), 256 * (hw % 4) + 256)
        rows = slice(256 * hw, 256 * hw + 256)
        value = dot_nt(latent[:, :256], dh0[rows]) + dot_nt(latent[:, 256:], dh1[rows])
        value = value.astype(BF)
        keep[hw // 4, :, lanes] = value[:NF]
        send[hw // 4, :, lanes] = value[NF:]
    spread_copy = copy(send, sent, spread_sems, 0, partner)
    spread_copy.start()
    embedded = total_wait(0, waiting)
    place = pos[...].astype(F32)
    hidden = embedded + jnp.concatenate([place, place], axis=0)
    head_lane = lax.div(lax.broadcasted_iota(jnp.int32, (2 * NF, 128), 1), HEAD_DIM)
    allowed = allow[...] > 0.5

    def of_head(value, h):
        return jnp.where(head_lane == h % 2, value, jnp.zeros_like(value))

    def pair_lanes(h):
        return slice(128 * (h // 2), 128 * (h // 2) + 128)

    for k in range(layers):
        unit, inv = unit_of(hidden)
        unit_a[k] = jnp.concatenate([unit, jnp.broadcast_to(inv, (2 * NF, 128))], axis=1)
        normed = (unit * gains[2 * k : 2 * k + 1]).astype(BF)
        normed_a[k] = normed
        for part in range(3):
            mixed[k, part] = jnp.concatenate(
                [dot(normed, qkv0[k, part]), dot(normed, qkv1[k, part])], axis=1
            ).astype(BF)
        for p in range(2):
            both = jnp.zeros((2 * NF, 128), F32)
            for h in (2 * p, 2 * p + 1):
                lanes = pair_lanes(h)
                scores = SCALE * dot_nt(of_head(mixed[k, 0, :, lanes], h), mixed[k, 1, :, lanes])
                scores = jnp.where(allowed, scores, NEG)
                lifted = jnp.exp(scores - jnp.max(scores, -1, keepdims=True))
                weight = lifted / jnp.sum(lifted, -1, keepdims=True)
                weights[k, h] = weight
                both = both + of_head(dot(weight.astype(BF), mixed[k, 2, :, lanes]), h)
            attended[k, :, 128 * p : 128 * p + 128] = both.astype(BF)
        partial = dot(attended[k, :, :128], proj0[k]) + dot(attended[k, :, 128:], proj1[k])
        middle = hidden + total_wait(2 * k + 1, total_start(2 * k + 1, partial))
        unit, inv = unit_of(middle)
        unit_f[k] = jnp.concatenate([unit, jnp.broadcast_to(inv, (2 * NF, 128))], axis=1)
        normed = (unit * gains[2 * k + 1 : 2 * k + 2]).astype(BF)
        normed_f[k] = normed
        partial = jnp.zeros((2 * NF, 512), F32)
        for side, (up, down) in enumerate(((up0, down0), (up1, down1))):
            value = dot(normed, up[k])
            before[k, :, 512 * side : 512 * side + 512] = value
            act = (value * sig(value)).astype(BF)
            inner[k, :, 512 * side : 512 * side + 512] = act
            partial = partial + dot(act, down[k])
        hidden = middle + total_wait(2 * k + 2, total_start(2 * k + 2, partial))
    tokens[...] = hidden.astype(BF)

    spread_copy.wait()
    decoded[...] = (keep[...].astype(F32) + sent[...].astype(F32)).astype(BF)

    fold_copies = []

    def fold_start(first, count):
        rows = pl.ds(first, count)
        one = copy(other.at[rows], other_got.at[rows], fold_sems, len(fold_copies), sibling)
        one.start()
        fold_copies.append((first, count, one))

    grad = cot[...].astype(F32)
    for k in reversed(range(layers)):
        base = LAYER_ROWS * k
        index = 2 * layers + 1 + 2 * (layers - 1 - k)
        low = grad.astype(BF)
        partial = jnp.zeros((2 * NF, 512), F32)
        grads = []
        for side, (up, down) in enumerate(((up0, down0), (up1, down1))):
            value = before[k, :, 512 * side : 512 * side + 512]
            squash = sig(value)
            slope = squash * (1.0 + value * (1.0 - squash))
            grad_before = (dot_nt(low, down[k]) * slope).astype(BF)
            grads.append(grad_before)
            partial = partial + dot_nt(grad_before, up[k])
        waiting = total_start(index, partial)
        turned = normed_f[k].T
        for side, dst in enumerate((flat, other)):
            act = inner[k, :, 512 * side : 512 * side + 512]
            dst[base : base + 512] = dot(act.T, low).astype(BF)
            dst[base + 512 : base + 1024] = dot(turned, grads[side]).astype(BF)
        grad_normed = total_wait(index, waiting)
        gain_f, grad_rows = unit_back(
            grad_normed, unit_f[k, :, :512], unit_f[k, :, 512:513], gains[2 * k + 1 : 2 * k + 2]
        )
        grad = grad + grad_rows
        low = grad.astype(BF)
        grad_mixed = [[], [], []]
        for p, proj in enumerate((proj0, proj1)):
            lanes = pair_lanes(2 * p)
            grad_pair = dot_nt(low, proj[k]).astype(BF)
            queries, keys, vals = mixed[k, 0, :, lanes], mixed[k, 1, :, lanes], mixed[k, 2, :, lanes]
            g_queries = jnp.zeros((2 * NF, 128), F32)
            g_keys, g_vals = g_queries, g_queries
            for h in (2 * p, 2 * p + 1):
                weight = weights[k, h]
                grad_head = of_head(grad_pair, h)
                g_vals = g_vals + dot(weight.astype(BF).T, grad_head)
                grad_weight = dot_nt(grad_head, vals)
                along = jnp.sum(weight * grad_weight, -1, keepdims=True)
                grad_scores = (weight * (grad_weight - along)).astype(BF)
                g_queries = g_queries + of_head(dot(grad_scores, keys), h)
                g_keys = g_keys + dot(grad_scores.T, of_head(queries, h))
            grad_mixed[0].append((SCALE * g_queries).astype(BF))
            grad_mixed[1].append((SCALE * g_keys).astype(BF))
            grad_mixed[2].append(g_vals.astype(BF))
        partial = jnp.zeros((2 * NF, 512), F32)
        for part in range(3):
            for side, qkv in enumerate((qkv0, qkv1)):
                partial = partial + dot_nt(grad_mixed[part][side], qkv[k, part])
        waiting = total_start(index + 1, partial)
        turned = normed_a[k].T
        for side, dst in enumerate((flat, other)):
            act = attended[k, :, 128 * side : 128 * side + 128]
            dst[base + 1024 : base + 1152] = dot(act.T, low).astype(BF)
            for part in range(3):
                value = dot(turned, grad_mixed[part][side]).astype(BF)
                first = base + 1152 + 128 * part
                for b in range(4):
                    dst[first : first + 128, 128 * b : 128 * b + 128] = value[
                        128 * b : 128 * b + 128
                    ]
        fold_start(base, LAYER_ROWS)
        grad_normed = total_wait(index + 1, waiting)
        gain_a, grad_rows = unit_back(
            grad_normed, unit_a[k, :, :512], unit_a[k, :, 512:513], gains[2 * k : 2 * k + 1]
        )
        grad = grad + grad_rows
        gain_rows[2 * k : 2 * k + 1] = gain_a
        gain_rows[2 * k + 1 : 2 * k + 2] = gain_f

    base = LAYER_ROWS * layers
    low = grad.astype(BF)
    own_latent, other_latent = latent_out[:, :256], latent_out[:, 256:]
    flat[base : base + 256] = dot(own_latent.T, low).astype(BF)
    other[base : base + 256] = dot(other_latent.T, low).astype(BF)
    small = jnp.concatenate(
        [
            grad[:NF] + grad[NF:],
            gain_rows[...],
            jnp.zeros((16 - 2 * layers, 512), F32),
        ],
        axis=0,
    ).astype(BF)
    flat[base + 256 : base + 256 + NF + 16] = small
    other[base + 256 : base + 256 + NF + 16] = small
    fold_start(base, 256 + NF + 16)
    grad_latent[:, :256] = dot_nt(low, emb0[...])
    grad_latent[:, 256:] = dot_nt(low, emb1[...])
    for first, count, one in fold_copies:
        one.wait()
        for start in range(first, first + count, 16 * 7 if count % 112 == 0 else 16 * 8):
            size = min(128 if count % 112 else 112, first + count - start)
            rows = slice(start, start + size)
            flat[rows] = (flat[rows].astype(F32) + other_got[rows].astype(F32)).astype(BF)
    spare = flat.shape[0] - token_rows(layers)
    if spare:
        flat[token_rows(layers) :] = jnp.zeros((spare, 512), BF)


def middle(layers, multiple, *args):
    rows = token_rows(layers)
    rows = rows + -rows % multiple
    dma = pltpu.SemaphoreType.DMA
    sums = 4 * layers + 1
    t = 2 * NF
    return pl.pallas_call(
        functools.partial(middle_kernel, layers),
        out_shape=(
            S((t, 512)),
            S((t, 512)),
            S((t, 512), F32),
            S((4, NF, 1024)),
            S((rows, 512)),
            S((t, 512), F32),
        ),
        in_specs=VM(len(args)),
        out_specs=tuple(VM(6)),
        scratch_shapes=[
            V((4, NF, 1024)),
            dma((2, 1)),
            V((4, NF, 1024)),
            V((4, NF, 1024)),
            V((4, NF, 1024)),
            dma((2, 1)),
            V((sums, t, 512)),
            V((sums, t, 512)),
            dma((2, sums)),
            V((rows, 512)),
            V((rows, 512)),
            dma((2, layers + 1)),
            V((layers, t, 640), F32),
            V((layers, t, 640), F32),
            V((layers, t, 512)),
            V((layers, t, 512)),
            V((layers, 3, t, 256)),
            V((layers, 4, t, t), F32),
            V((layers, t, 256)),
            V((layers, t, 1024), F32),
            V((layers, t, 1024)),
            V((2 * layers, 512), F32),
        ],
        compiler_params=pltpu.CompilerParams(
            collective_id=3, has_side_effects=True, vmem_limit_bytes=56 * MIB
        ),
        name="middle",
    )(*args)


def across(value):
    return lax.ppermute(value, "strip", [(0, 2), (2, 0), (1, 3), (3, 1)])


def beside(value):
    return lax.ppermute(value, "strip", [(0, 1), (1, 0), (2, 3), (3, 2)])


def fold(full, axis):
    half = full.shape[axis] // 2
    own = lax.slice_in_dim(full, 0, half, axis=axis)
    other = lax.slice_in_dim(full, half, 2 * half, axis=axis)
    return own + beside(other.astype(BF)).astype(F32)


def make_mask(segment_ids):
    places = jnp.arange(segment_ids.shape[1])
    causal = places[:, None] >= places[None, :]
    return causal[None] & (segment_ids[:, :, None] == segment_ids[:, None, :])


def mm(a, b):
    return jnp.dot(a, b, preferred_element_type=F32)


def mm_t(a, b):
    return lax.dot_general(a, b, (((1,), (1,)), ((), ())), preferred_element_type=F32)


def t_mm(a, b):
    return lax.dot_general(a, b, (((0,), (0,)), ((), ())), preferred_element_type=F32)


def pieces_of(whole, parts):
    pieces = []
    offset = 0
    for part in parts:
        pieces.append(whole[offset : offset + part.shape[0]])
        offset = offset + part.shape[0]
    return pieces


def stacked_rows(parts, multiple):
    flat = jnp.concatenate([part.astype(BF) for part in parts], axis=0)
    return jnp.pad(flat, ((0, -flat.shape[0] % multiple), (0, 0)))


def rows_share(flat):
    return lax.psum_scatter(flat, "rows", scatter_dimension=0, tiled=True)


def rows_whole(share):
    return lax.all_gather(share, "rows", axis=0, tiled=True)


def pack_kernels(outer, first, second, third):
    parts = [
        jnp.concatenate([third[:, :, :256], third[:, :, 256:]], axis=1).reshape(2048, 256),
        second.reshape(512, 256),
        jnp.concatenate([first[:2], first[2:]], axis=2).reshape(128, 256),
        jnp.pad(outer.reshape(6, 256), ((0, 122), (0, 0))),
    ]
    return jnp.concatenate(parts, axis=0)


def unpack_kernels(flat):
    third = flat[:2048].reshape(4, 512, 256)
    third = jnp.concatenate([third[:, :256], third[:, 256:]], axis=2)
    second = flat[2048:2560].reshape(4, 128, 256)
    first = flat[2560:2688].reshape(2, 64, 256)
    first = jnp.concatenate([first[:, :, :128], first[:, :, 128:]], axis=0)
    outer = flat[2688:2694].reshape(4, 3, 4, 32)
    return (outer, first, second, third)


def strip_share(flat, x, core):
    half = flat.shape[0] // 2
    low = flat.astype(BF)
    mine = lax.dynamic_slice_in_dim(low, core * half, half)
    theirs = lax.dynamic_slice_in_dim(low, (1 - core) * half, half)
    summed = mine.astype(F32) + beside(theirs).astype(F32)
    low = summed.astype(BF)
    half = half // 2
    mine = lax.dynamic_slice_in_dim(low, x * half, half)
    theirs = lax.dynamic_slice_in_dim(low, (1 - x) * half, half)
    return mine.astype(F32) + across(theirs).astype(F32)


def strip_whole(share, x, core):
    got = across(share)
    half = jnp.where(
        x == 0, jnp.concatenate([share, got]), jnp.concatenate([got, share])
    )
    got = beside(half)
    return jnp.where(
        core == 0, jnp.concatenate([half, got]), jnp.concatenate([got, half])
    )


def features_first(weight):
    return weight.reshape(256, 16, -1).transpose(1, 0, 2).reshape(weight.shape)


def channels_first(weight):
    return weight.reshape(16, 256, -1).transpose(1, 0, 2).reshape(weight.shape)


def shards(
    frames,
    segment_ids,
    encode_one,
    encode_two,
    encode_three,
    encode_four,
    latent_head,
    token_embed,
    positions,
    norm_gains,
    qkv_weight,
    out_weight,
    up_weight,
    down_weight,
    decode_head,
    decode_one,
    decode_two,
    decode_three,
    decode_four,
    token_cotangent,
    frame_cotangent,
):
    strip = lax.axis_index("strip")
    x, core = strip // 2, strip % 2
    layers = qkv_weight.shape[0]

    enc = [w.transpose(2, 3, 1, 0) for w in (encode_one, encode_two, encode_three, encode_four)]
    dec = [
        jnp.flip(w, (2, 3)).transpose(2, 3, 0, 1)
        for w in (decode_four, decode_three, decode_two, decode_one)
    ]
    folds = (4, 2, 1)
    enc_a = outer_A(enc[0])
    dec_a = outer_A(dec[0])
    enc_b, dec_b = outer_B(enc_a), outer_B(dec_a)
    enc_a, dec_a = enc_a.reshape(1152, 1024), dec_a.reshape(1152, 1024)
    enc_t = [canon_T(w, a) for w, a in zip(enc[1:], folds)]
    dec_t = [canon_T(w, a) for w, a in zip(dec[1:], folds)]
    enc_u = [canon_U(t, a) for t, a in zip(enc_t, folds)]
    dec_u = [canon_U(t, a) for t, a in zip(dec_t, folds)]
    enc_t = [t.reshape(2048, 256) for t in enc_t]
    dec_t = [t.reshape(2048, 256) for t in dec_t]

    head_in = features_first(latent_head)
    head_in = (head_in, beside(head_in))
    head_out = features_first(decode_head.T)
    head_out = (head_out, beside(head_out))
    qkv = jnp.transpose(qkv_weight, (0, 2, 1, 3))
    halves = []
    for shard in (token_embed, qkv, out_weight, up_weight, down_weight):
        halves.append((shard, beside(shard)))
    embed, qkv, project, widen, narrow = halves

    pixels = frames_in(frames, 1)
    hints = frames_in_later(frame_cotangent)
    z1, z2, z3, z4, feat = enc_fwd(pixels, enc_a, *enc_t)
    first = 2 * core

    def mine(array, size):
        own = lax.dynamic_slice_in_dim(array, (first + x) * size, size)
        other = lax.dynamic_slice_in_dim(array, (first + 1 - x) * size, size)
        return jnp.concatenate([own, other], axis=0)

    allowed = make_mask(mine(segment_ids, 1)).astype(F32)
    blank = jnp.zeros((NF, NF), F32)
    allowed = jnp.concatenate(
        [
            jnp.concatenate([allowed[0], blank], axis=1),
            jnp.concatenate([blank, allowed[1]], axis=1),
        ],
        axis=0,
    )
    line = 16 * lax.axis_size("rows")
    tokens, latent, chances, decoded, t_flat, grad_latent = middle(
        layers,
        line,
        feat,
        *head_in,
        *head_out,
        *embed,
        positions,
        norm_gains.reshape(2 * layers, -1),
        allowed,
        mine(token_cotangent, NF),
        *qkv,
        *project,
        *widen,
        *narrow,
    )
    t_share = rows_share(t_flat)
    tokens = jnp.where(
        x == 0, tokens, jnp.concatenate([tokens[NF:], tokens[:NF]], axis=0)
    )
    other_tokens = beside(tokens)
    tokens_out = jnp.where(
        core == 0,
        jnp.concatenate([tokens, other_tokens]),
        jnp.concatenate([other_tokens, tokens]),
    )

    recon_pairs, p3, p2, p1 = dec_fwd(decoded, dec_u[2], dec_u[1], dec_u[0], dec_b)
    g_decoded, h2, h3, h4, h_outer = dec_bwd(hints, decoded, p3, p2, p1, dec_a, *dec_t)
    g_spread = jnp.concatenate([g_decoded, across(g_decoded)], axis=1)
    g_head_out = fold(jnp.concatenate([t_mm(g_spread[h], latent) for h in range(4)]), 1)
    head_out4 = jnp.concatenate(head_out, axis=1).reshape(4, 1024, 512)
    head_in4 = jnp.concatenate(head_in, axis=1).reshape(4, 1024, 512)
    feat = jnp.concatenate([feat, across(feat)], axis=1)
    grad_latent = grad_latent + sum(mm(g_spread[h], head_out4[h]) for h in range(4))
    dec_flat = pack_kernels(
        red_to_we(h_outer),
        gt_to_we(h2, 4, 32, 64),
        gt_to_we(h3, 2, 64, 128),
        gt_to_we(h4, 1, 128, 256),
    )
    dec_share = strip_share(dec_flat, x, core)

    d_parts = [g_head_out, dec_share]
    d_flat = stacked_rows(d_parts, line)

    grouped = chances.reshape(2 * NF, -1, LCLASS)
    grad_grouped = grad_latent.reshape(grouped.shape)
    grad_logits = grouped * (grad_grouped - jnp.sum(grouped * grad_grouped, -1, keepdims=True))
    grad_logits = grad_logits.reshape(2 * NF, -1).astype(BF)
    g_head_in = fold(jnp.concatenate([t_mm(feat[h], grad_logits) for h in range(4)]), 1)
    g_feat = jnp.stack([mm_t(grad_logits, head_in4[h]) for h in range(4)]).astype(BF)
    g_feat = (g_feat[:, :NF].astype(F32) + across(g_feat[:, NF:]).astype(F32)).astype(BF)
    g_feat, t_share, d_flat = lax.optimization_barrier((g_feat, t_share, d_flat))
    d_share = rows_share(d_flat)
    t_total = rows_whole(t_share)
    d_pairs, e2, e3, e4, e_outer = enc_bwd(pixels, z1, z2, z3, z4, g_feat, *enc_u, enc_b)
    enc_flat = pack_kernels(
        red_to_we(e_outer),
        gt_to_we(e2, 4, 32, 64),
        gt_to_we(e3, 2, 64, 128),
        gt_to_we(e4, 1, 128, 256),
    )
    enc_share = strip_share(enc_flat, x, core)
    late_parts = [g_head_in, enc_share]
    late_flat = stacked_rows(late_parts, 16)
    late_flat, d_share = lax.optimization_barrier((late_flat, d_share))
    d_total = pieces_of(rows_whole(d_share), d_parts)
    late, recon, frames_grad = finish(late_flat, recon_pairs, d_pairs, 4, 2)
    late = pieces_of(late, late_parts)

    def of_encoder(part, c, o):
        return part.astype(F32).reshape(4, o, 4, c).transpose(1, 3, 0, 2)

    def of_decoder(part, c, o):
        return jnp.flip(part.astype(F32).reshape(4, o, 4, c), (0, 2)).transpose(3, 1, 0, 2)

    k1, k2, k3, k4 = unpack_kernels(strip_whole(late[1], x, core))
    j1, j2, j3, j4 = unpack_kernels(strip_whole(d_total[1], x, core))
    t_total = t_total.astype(F32)
    t_layers = t_total[: layers * LAYER_ROWS].reshape(layers, LAYER_ROWS, 512)
    t_rest = t_total[layers * LAYER_ROWS :]
    r_qkv = t_layers[:, 1152:].reshape(layers, 3, 128, 4, 128).transpose(0, 3, 2, 1, 4)
    r_qkv = r_qkv.reshape(qkv_weight.shape)
    return (
        tokens_out,
        recon,
        frames_grad,
        k1.astype(F32).transpose(3, 1, 0, 2),
        of_encoder(k2, 32, 64),
        of_encoder(k3, 64, 128),
        of_encoder(k4, 128, 256),
        channels_first(late[0].astype(F32)),
        t_rest[:256],
        t_rest[256 : 256 + NF],
        t_rest[256 + NF : 256 + NF + 2 * layers].reshape(norm_gains.shape),
        r_qkv,
        t_layers[:, 1024:1152],
        t_layers[:, 512:1024],
        t_layers[:, :512],
        channels_first(d_total[0].astype(F32)).T,
        of_decoder(j4, 128, 256),
        of_decoder(j3, 64, 128),
        of_decoder(j2, 32, 64),
        jnp.flip(j1.astype(F32), (0, 2)).transpose(1, 3, 0, 2),
    )


def solution(mesh):
    placed = (
        P("rows", None, "strip", None),
        P("rows", None),
        P(),
        P(),
        P(),
        P(),
        P(None, "strip"),
        P("strip", None),
        P(),
        P(),
        P(None, None, None, "strip"),
        P(None, "strip", None),
        P(None, None, "strip"),
        P(None, "strip", None),
        P("strip", None),
        P(),
        P(),
        P(),
        P(),
        P("rows", None),
        P("rows", None, "strip", None),
    )
    return jax.shard_map(
        shards,
        mesh=mesh,
        in_specs=placed,
        out_specs=(
            P("rows", None),
            P("rows", None, "strip", None),
            P("rows", None, "strip", None),
            P(),
            P(),
            P(),
            P(),
            P(None, "strip"),
            P("strip", None),
            P(),
            P(),
            P(None, None, None, "strip"),
            P(None, "strip", None),
            P(None, None, "strip"),
            P(None, "strip", None),
            P("strip", None),
            P(),
            P(),
            P(),
            P(),
        ),
        check_vma=False,
    )
```

```python
import functools

import jax
import jax.numpy as jnp
from jax import lax
from jax.experimental import pallas as pl
from jax.experimental.pallas import tpu as pltpu
from jax.sharding import PartitionSpec as P

HEAD_DIM = 64
LCLASS = 32
EPS = 1e-05
SCALE = 0.125
NEG = -1e30
F32 = jnp.float32
BF = jnp.bfloat16
NF = 64
MIB = 1 << 20
MESH = pl.DeviceIdType.MESH


def sig(z): return 1.0/(1.0+jnp.exp(-z))

def zero_big(ref,rows):
    z=jnp.zeros((NF,1280),BF)
    ref[0,0]=z; ref[rows//2,1]=z
    e=jnp.zeros((rows//2+1,2,NF,128),BF)
    ref[:,:,:,0:128]=e; ref[:,:,:,1152:1280]=e

def zero_small(ref,rows,pad):
    z=jnp.zeros((NF,1024+2*pad),BF)
    ref[0]=z; ref[rows+1]=z
    if pad:
        e=jnp.zeros((rows+2,NF,pad),BF)
        ref[:,:,0:pad]=e; ref[:,:,1024+pad:]=e

def put_big(ref,half0,rows,q,val):
    v=val.reshape(rows,NF,256)
    for t in range(rows):
        ref[half0+(t+1)//2,(t+1)%2,:,128+256*q:384+256*q]=v[t]

def loop(n,body):
    if n==1: body(0)
    else:
        def step(g,c):
            body(g); return c
        lax.fori_loop(0,n,step,0)

def down(src,t_ref,rows,per,emit):
    def body(g):
        i0=g*per
        for q in range(4):
            lhs=jnp.concatenate([src[pl.ds(i0+kh//2,per),kh%2,:,256*q:256*q+512].reshape(per*NF,512) for kh in range(4)],axis=1)
            emit(i0,g*(per//2),q,jnp.dot(lhs,t_ref[...],preferred_element_type=F32))
    loop(rows//per,body)

def up(src,u_ref,rows,per,emit):
    k=u_ref.shape[1]//2
    def body(g):
        m0=g*per
        for q in range(4):
            for odd in range(2):
                lhs=jnp.concatenate([src[pl.ds(m0+1+odd-s,per),:,256*q:256*q+k].reshape(per*NF,k) for s in range(2)],axis=1)
                emit(m0,odd,q,jnp.dot(lhs,u_ref[odd],preferred_element_type=F32).reshape(per,NF,256))
    loop(rows//per,body)

def turn(src,dst,rows,pad):
    for q in range(4):
        dst[256*q:256*q+256,:]=src[1:rows+1,:,pad+256*q:pad+256*q+256].reshape(rows*NF,256).T

def grad_w(big,yt,rows):
    out=[]
    for kh in range(4):
        acc=jnp.zeros((256,512),F32)
        for q in range(4):
            win=big[pl.ds(kh//2,rows),kh%2,:,256*q:256*q+512].reshape(rows*NF,512)
            acc=acc+jnp.dot(yt[256*q:256*q+256,:],win,preferred_element_type=F32)
        out.append(acc)
    return out

def pack(pk,base,a,c,o,sums,flipped,swap,turned=False):
    taps=[]
    for acc in sums:
        total=None
        for j in range(a):
            first=(a+2*j-1)*c
            part=acc[j*o:j*o+o]
            if first: part=pltpu.roll(part,512-first,1)
            part=part[:,:4*c]
            total=part if total is None else total+part
        taps.append(total.astype(BF) if turned else total.T.astype(BF))
    width,count=(c,o//16) if turned else (o,c//16)
    held=[]
    for b in range(count):
        rows=[]
        for k in range(16):
            kh,kw=divmod(15-k if flipped else k,4)
            if turned: rows.append(taps[kh][16*b:16*b+16,c*kw:c*kw+c])
            else: rows.append(taps[kh][c*kw+16*b:c*kw+16*b+16])
        block=jnp.dot(swap,jnp.concatenate(rows,axis=0),preferred_element_type=F32).astype(BF)
        if width==256: pk[base+256*b:base+256*b+256]=block
        elif width==128:
            side,at=divmod(b,count//2)
            pk[base+256*at:base+256*at+256,128*side:128*side+128]=block
        else: held.extend([block[:128],block[128:]])
    if held: pk[base:base+128]=jnp.concatenate(held,axis=1)

def pack_outer(pk,base,red,flipped):
    r=lax.broadcasted_iota(jnp.int32,(48,1152),0); lane=lax.broadcasted_iota(jnp.int32,(48,1152),1)
    k=lax.rem(r,16)
    if flipped: k=15-k
    kh,kw=lax.div(k,4),lax.rem(k,4)
    at=384*lax.div(kh+1,2)+192*lax.rem(kh+1,2)+64*lax.div(r,16)+kw
    pick=(lane==at).astype(BF)
    value=jnp.concatenate([part.astype(BF) for part in red],axis=1)
    pk[base:base+128]=jnp.zeros((128,256),BF)
    pk[base:base+48,0:32]=lax.dot_general(pick,value,(((1,),(1,)),((),())),preferred_element_type=F32).astype(BF)

def outer_down(xp,a_ref,emit,per=4):
    def body(g):
        i0=g*per
        lhs=jnp.concatenate([xp[pl.ds(i0+d,per)].reshape(per*NF,384) for d in range(3)],axis=1)
        for q in range(4):
            emit(i0,g*(per//2),q,jnp.dot(lhs,a_ref[:,256*q:256*q+256],preferred_element_type=F32))
    loop(32//per,body)

def outer_up(yp,b_ref,emit,per=4):
    def body(g):
        i0=g*per
        lhs=jnp.concatenate([yp[pl.ds(i0+2-d,per)].reshape(per*NF,1024) for d in range(3)],axis=1)
        emit(i0,jnp.dot(lhs,b_ref[...],preferred_element_type=F32).reshape(per,NF,384))
    loop(32//per,body)

def outer_grad(xp,yt):
    red=[]
    lane=lax.broadcasted_iota(jnp.int32,(32,384),1)%64
    for d in range(3):
        x=xp[d:d+32].reshape(32*NF,384)
        tot=jnp.zeros((32,384),F32)
        for jb in range(4):
            g=jnp.dot(yt[256*jb:256*jb+256,:],x,preferred_element_type=F32)
            for jj in range(8):
                j=8*jb+jj
                v=pltpu.roll(g[32*jj:32*jj+32],(385-2*j)%384,1)
                if j==0: v=jnp.where(lane==0,0.0,v)
                if j==31: v=jnp.where(lane==3,0.0,v)
                tot=tot+v
        red.append(tot)
    return red

def enc_fwd_kernel(xp,a,t2,t3,t4,z1,z2,z3,z4,feat,m1,m2,m3):
    zero_big(m1,32); zero_big(m2,16); zero_big(m3,8)
    def keep(z,m):
        def emit(i0,half0,q,acc):
            rows=acc.shape[0]//NF
            z[pl.ds(i0,rows),:,256*q:256*q+256]=acc.astype(BF).reshape(rows,NF,256)
            val=(acc*sig(acc)).astype(BF)
            if m is None: feat[pl.ds(i0,rows),:,256*q:256*q+256]=val.reshape(rows,NF,256)
            else: put_big(m,half0,rows,q,val)
        return emit
    outer_down(xp,a,keep(z1,m1))
    down(m1,t2,16,4,keep(z2,m2))
    down(m2,t3,8,4,keep(z3,m3))
    down(m3,t4,4,4,keep(z4,None))

def enc_bwd_kernel(xp,z1,z2,z3,z4,df,u2,u3,u4,b,dx,pk,m1,m2,m3,s1,s2,s3,s4,yt1,yt2,yt3,yt4):
    zero_big(m1,32); zero_big(m2,16); zero_big(m3,8)
    zero_small(s1,32,0); zero_small(s2,16,128); zero_small(s3,8,128); zero_small(s4,4,256)
    swap=exchange_16()
    z=z4[...].astype(F32); s=sig(z)
    s4[1:5,:,256:1280]=(df[...].astype(F32)*(s*(1.0+z*(1.0-s)))).astype(BF)
    def back(z_ref,m,dst,pad):
        def emit(m0,odd,q,acc):
            per=acc.shape[0]
            for t in range(per):
                h=2*(m0+t)+odd
                zz=z_ref[h,:,256*q:256*q+256].astype(F32)
                ss=sig(zz); mm=zz*ss
                dst[h+1,:,pad+256*q:pad+256*q+256]=(acc[t]*(ss+mm*(1.0-ss))).astype(BF)
                m[m0+t+odd,1-odd,:,128+256*q:384+256*q]=mm.astype(BF)
        return emit
    up(s4,u4,4,4,back(z3,m3,s3,128))
    turn(s4,yt4,4,256); pack(pk,0,1,128,256,grad_w(m3,yt4,4),False,swap,True)
    up(s3,u3,8,4,back(z2,m2,s2,128))
    turn(s3,yt3,8,128); pack(pk,2048,2,64,128,grad_w(m2,yt3,8),False,swap)
    up(s2,u2,16,4,back(z1,m1,s1,0))
    turn(s2,yt2,16,128); pack(pk,2560,4,32,64,grad_w(m1,yt2,16),False,swap)
    def put(i0,acc): dx[pl.ds(i0,acc.shape[0])]=acc.astype(BF)
    outer_up(s1,b,put)
    turn(s1,yt1,32,0); pack_outer(pk,2688,outer_grad(xp,yt1),False)

def dec_fwd_kernel(dec,u4,u3,u2,b,recon,p3,p2,p1,s4,s3,s2,s1):
    zero_small(s1,32,0); zero_small(s2,16,128); zero_small(s3,8,128); zero_small(s4,4,256)
    z=dec[...].astype(F32)
    s4[1:5,:,256:1280]=(z*sig(z)).astype(BF)
    def fwd(p,dst,pad):
        def emit(m0,odd,q,acc):
            for t in range(acc.shape[0]):
                h=2*(m0+t)+odd
                v=acc[t]
                p[h,:,256*q:256*q+256]=v.astype(BF)
                dst[h+1,:,pad+256*q:pad+256*q+256]=(v*sig(v)).astype(BF)
        return emit
    up(s4,u4,4,4,fwd(p3,s3,128))
    up(s3,u3,8,4,fwd(p2,s2,128))
    up(s2,u2,16,4,fwd(p1,s1,0))
    def put(i0,acc): recon[pl.ds(i0,acc.shape[0])]=acc.astype(BF)
    outer_up(s1,b,put)

def dec_bwd_kernel(c0,c1,c2,c3,dec,p3,p2,p1,a,t2,t3,t4,gdec,pk,d1,d2,d3,cp,yt1,yt2,yt3,yt4):
    me=lax.axis_index("strip")
    cp[0]=jnp.zeros((NF,384),BF); cp[33]=jnp.zeros((NF,384),BF)
    for k,part in enumerate((c0,c1,c2,c3)):
        cp[pl.ds(1+8*lax.rem(me+4-k,4),8)]=part[...]
    zero_big(d1,32); zero_big(d2,16); zero_big(d3,8)
    def maps(p,rows,yt):
        for q in range(4):
            zz=p[:,:,256*q:256*q+256].reshape(rows*NF,256).astype(F32)
            yt[256*q:256*q+256,:]=(zz*sig(zz)).astype(BF).T
    def back(p,dst):
        def emit(i0,half0,q,acc):
            rows=acc.shape[0]//NF
            zz=p[pl.ds(i0,rows),:,256*q:256*q+256].astype(F32).reshape(rows*NF,256)
            ss=sig(zz)
            val=(acc*(ss*(1.0+zz*(1.0-ss)))).astype(BF)
            if dst is None: gdec[pl.ds(i0,rows),:,256*q:256*q+256]=val.reshape(rows,NF,256)
            else: put_big(dst,half0,rows,q,val)
        return emit
    swap=exchange_16()
    maps(p1,32,yt1); pack_outer(pk,2688,outer_grad(cp,yt1),True)
    outer_down(cp,a,back(p1,d1))
    maps(p2,16,yt2); pack(pk,2560,4,32,64,grad_w(d1,yt2,16),True,swap)
    down(d1,t2,16,4,back(p2,d2))
    maps(p3,8,yt3); pack(pk,2048,2,64,128,grad_w(d2,yt3,8),True,swap)
    down(d2,t3,8,4,back(p3,d3))
    maps(dec,4,yt4); pack(pk,0,1,128,256,grad_w(d3,yt4,4),True,swap)
    down(d3,t4,4,4,back(dec,None))

def S(shape,dt=BF): return jax.ShapeDtypeStruct(shape,dt)
def V(shape,dt=BF): return pltpu.VMEM(shape,dt)
VM=lambda n:[pl.BlockSpec(memory_space=pltpu.VMEM)]*n
def run(kernel,outs,scratch,args,name,lim=60,flops=10**10):
    return pl.pallas_call(kernel,out_shape=outs,in_specs=VM(len(args)),out_specs=tuple(VM(len(outs))),
        scratch_shapes=scratch,compiler_params=pltpu.CompilerParams(vmem_limit_bytes=lim*MIB),
        cost_estimate=pl.CostEstimate(flops=flops,bytes_accessed=20*MIB,transcendentals=0),name=name)(*args)
big=lambda h:V((h//2+1,2,NF,1280))
def enc_fwd(xp,a,t2,t3,t4):
    return run(enc_fwd_kernel,(S((32,NF,1024)),S((16,NF,1024)),S((8,NF,1024)),S((4,NF,1024)),S((4,NF,1024))),
      [big(32),big(16),big(8)],(xp,a,t2,t3,t4),"encode")
GS=(S((2816,256)),)
small=lambda h,p:V((h+2,NF,1024+2*p))
yts=[V((1024,32*NF)),V((1024,16*NF)),V((1024,8*NF)),V((1024,4*NF))]
def enc_bwd(xp,z1,z2,z3,z4,df,u2,u3,u4,b):
    return run(enc_bwd_kernel,(S((32,NF,384)),)+GS,[big(32),big(16),big(8),small(32,0),small(16,128),small(8,128),small(4,256)]+yts,
      (xp,z1,z2,z3,z4,df,u2,u3,u4,b),"encode_back")
def dec_fwd(dec,u4,u3,u2,b):
    return run(dec_fwd_kernel,(S((32,NF,384)),S((8,NF,1024)),S((16,NF,1024)),S((32,NF,1024))),
      [small(4,256),small(8,128),small(16,128),small(32,0)],(dec,u4,u3,u2,b),"decode")
def dec_bwd(hints,dec,p3,p2,p1,a,t2,t3,t4):
    return run(dec_bwd_kernel,(S((4,NF,1024)),)+GS,[big(32),big(16),big(8),V((34,NF,384))]+yts,
      (*hints,dec,p3,p2,p1,a,t2,t3,t4),"decode_back")


def exchange_16():
    r = lax.broadcasted_iota(jnp.int32, (256, 256), 0)
    s = lax.broadcasted_iota(jnp.int32, (256, 256), 1)
    return (s == lax.rem(r, 16) * 16 + lax.div(r, 16)).astype(BF)


def first_frame(strip):
    return NF * ((strip % 2) * 2 + strip // 2)


def turned_rows(x, i):
    return jnp.concatenate([x[c, 2 * i + p] for p in range(2) for c in range(3)], axis=0).T


def canonical(w, swap, c, o, flipped):
    parts = {}
    for b in range(c // 16):
        block = jnp.dot(swap, w[256 * b : 256 * b + 256, :], preferred_element_type=F32).astype(BF)
        for k in range(16):
            parts[(15 - k if flipped else k, b)] = block[16 * k : 16 * k + 16]
    return [
        jnp.concatenate(
            [parts[(4 * kh + kw, b)] for kw in range(4) for b in range(c // 16)], axis=0
        )
        for kh in range(4)
    ]


def canonical_turned(w, swap):
    parts = {}
    for b in range(16):
        block = jnp.dot(swap, w[256 * b : 256 * b + 256, :], preferred_element_type=F32).astype(BF)
        for k in range(16):
            parts[(k, b)] = block[16 * k : 16 * k + 16]
    return [
        jnp.concatenate(
            [
                jnp.concatenate([parts[(4 * kh + kw, b)] for b in range(16)], axis=0)
                for kw in range(4)
            ],
            axis=1,
        )
        for kh in range(4)
    ]


def band(flat, a, c, o):
    def shifted(value, first):
        above = jnp.zeros((first, value.shape[1]), BF)
        below = jnp.zeros((512 - first - value.shape[0], value.shape[1]), BF)
        return jnp.concatenate([above, value, below], axis=0)

    if a == 1:
        return flat
    if a == 2:
        return jnp.concatenate([shifted(flat, 64), shifted(flat, 192)], axis=1)
    twice = jnp.concatenate([flat, flat], axis=1)
    left = lax.broadcasted_iota(jnp.int32, (512, 128), 1) < 64
    return jnp.concatenate(
        [
            jnp.where(left, shifted(twice, 96), shifted(twice, 160)),
            jnp.where(left, shifted(twice, 224), shifted(twice, 288)),
        ],
        axis=1,
    )


def put_bands(t_ref, u_ref, bands, turned, a):
    for kh in range(4):
        t = bands[kh]
        t_ref[512 * kh : 512 * kh + 512] = t
        tt = t.T if turned is None else turned[kh]
        z = jnp.zeros((256, 128), BF)
        left = jnp.concatenate([tt[:, 384:512], z], axis=1)
        right = jnp.concatenate([z, tt[:, :128]], axis=1)
        if a > 1:
            left, right = left[128:], right[:128]
        k = 512 if a > 1 else 768
        u_ref[1 - kh % 2, k * (kh // 2) : k * (kh // 2) + k] = jnp.concatenate(
            [left, tt[:, 128:384], right], axis=0
        )


def put_outer(a_ref, b_ref, w, flipped):
    row = lax.broadcasted_iota(jnp.int32, (64, 1024), 0)
    col = lax.div(lax.broadcasted_iota(jnp.int32, (64, 1024), 1), 32)
    tap = row - 2 * col + 1
    for kh in range(4):
        d, p = (kh + 1) // 2, (kh + 1) % 2
        for c in range(3):
            total = jnp.zeros((64, 1024), F32)
            for kw in range(4):
                k = 4 * kh + kw
                r = 16 * c + (15 - k if flipped else k)
                total = jnp.where(tap == kw, w[r : r + 1, :], total)
            first = 384 * d + 192 * p + 64 * c
            a_ref[first : first + 64] = total.astype(BF)
    a_ref[0:192] = jnp.zeros((192, 1024), BF)
    a_ref[960:1152] = jnp.zeros((192, 1024), BF)
    for d in range(3):
        b_ref[1024 * d : 1024 * d + 1024] = a_ref[384 * d : 384 * d + 384].T


def start_kernel(
    x, e1, e2, e3, e4, d1, d2, d3, d4, lh, dh, emb, qkv, proj, up, down,
    pixels, ea, eb, et2, et3, et4, eu2, eu3, eu4, da, db, dt2, dt3, dt4, du2, du3, du4,
    lh0, lh1, dh0, dh1, emb1, qkv1, proj1, up1, down1,
    stage, send_sem, recv_sem, side_sems,
    va, vb, vt2, vt3, vt4, vu2, vu3, vu4, wa, wb, wt2, wt3, wt4, wu2, wu3, wu4,
    vl, vd, out_sems,
):
    me = lax.axis_index("strip")
    row = lax.axis_index("rows")
    sibling = (row, me + 1 - 2 * lax.rem(me, 2))
    pixels[0] = jnp.zeros((NF, 384), BF)
    pixels[33] = jnp.zeros((NF, 384), BF)

    def turn_rows(i, carry):
        flat = turned_rows(x, i)
        for k in range(4):
            stage[k, i] = flat[first_frame(k) : first_frame(k) + NF]
        return carry

    lax.fori_loop(0, 8, turn_rows, 0)
    barrier = pltpu.get_barrier_semaphore()
    for k in range(1, 4):
        pl.semaphore_signal(
            barrier, inc=1, device_id=(row, lax.rem(me + k, 4)), device_id_type=MESH
        )
    pl.semaphore_wait(barrier, 3)
    copies = []
    for k in range(1, 4):
        to = lax.rem(me + k, 4)
        copies.append(
            pltpu.make_async_remote_copy(
                src_ref=stage.at[to],
                dst_ref=pixels.at[pl.ds(1 + 8 * me, 8)],
                send_sem=send_sem.at[k - 1],
                recv_sem=recv_sem.at[k - 1],
                device_id=(row, to),
                device_id_type=MESH,
            )
        )
    for copy in copies:
        copy.start()

    def to_sibling(src, dst, index):
        copy = pltpu.make_async_remote_copy(
            src_ref=src,
            dst_ref=dst,
            send_sem=side_sems.at[0, index],
            recv_sem=side_sems.at[1, index],
            device_id=sibling,
            device_id_type=MESH,
        )
        copy.start()
        copies.append(copy)

    for index, (src, dst) in enumerate(
        ((emb, emb1), (qkv, qkv1), (proj, proj1), (up, up1), (down, down1))
    ):
        to_sibling(src, dst, index)
    pixels[pl.ds(1 + 8 * me, 8)] = stage[me]

    stores = []

    def store(src, dst):
        copy = pltpu.make_async_copy(src, dst, out_sems.at[len(stores)])
        copy.start()
        stores.append(copy)

    swap = exchange_16()
    put_outer(va, vb, e1, False)
    store(va, ea)
    store(vb, eb)
    put_bands(vt2, vu2, [band(f, 4, 32, 64) for f in canonical(e2, swap, 32, 64, False)], None, 4)
    store(vt2, et2)
    store(vu2, eu2)
    put_bands(vt3, vu3, [band(f, 2, 64, 128) for f in canonical(e3, swap, 64, 128, False)], None, 2)
    store(vt3, et3)
    store(vu3, eu3)
    turned = canonical_turned(e4, swap)
    put_bands(vt4, vu4, [f.T for f in turned], turned, 1)
    store(vt4, et4)
    store(vu4, eu4)
    for b in range(16):
        rows = slice(256 * b, 256 * b + 256)
        for src, dst in ((lh[rows, :], vl), (dh[:, rows].T, vd)):
            block = jnp.dot(swap, src, preferred_element_type=F32).astype(BF)
            for k in range(16):
                dst[256 * k + 16 * b : 256 * k + 16 * b + 16] = block[16 * k : 16 * k + 16]
    store(vl, lh0)
    store(vd, dh0)
    to_sibling(vl, lh1, 5)
    to_sibling(vd, dh1, 6)
    put_outer(wa, wb, d4, True)
    store(wa, da)
    store(wb, db)
    put_bands(wt2, wu2, [band(f, 4, 32, 64) for f in canonical(d3, swap, 32, 64, True)], None, 4)
    store(wt2, dt2)
    store(wu2, du2)
    put_bands(wt3, wu3, [band(f, 2, 64, 128) for f in canonical(d2, swap, 64, 128, True)], None, 2)
    store(wt3, dt3)
    store(wu3, du3)
    put_bands(wt4, wu4, canonical(d1, swap, 128, 256, True), None, 1)
    store(wt4, dt4)
    store(wu4, du4)
    for copy in copies:
        copy.wait()
    for copy in stores:
        copy.wait()


def start(frames, kernels, latent_head, decode_head, others):
    e1, e2, e3, e4, d1, d2, d3, d4 = kernels
    rows_in = [
        jnp.tile(jnp.transpose(e1, (1, 2, 3, 0)).reshape(48, 32), (1, 32)).astype(F32),
        jnp.transpose(e2, (1, 2, 3, 0)).reshape(512, 64),
        jnp.transpose(e3, (1, 2, 3, 0)).reshape(1024, 128),
        jnp.transpose(e4, (0, 2, 3, 1)).reshape(4096, 128),
        jnp.transpose(d1, (0, 2, 3, 1)).reshape(2048, 256),
        jnp.transpose(d2, (0, 2, 3, 1)).reshape(1024, 128),
        jnp.transpose(d3, (0, 2, 3, 1)).reshape(512, 64),
        jnp.tile(jnp.transpose(d4, (0, 2, 3, 1)).reshape(48, 32), (1, 32)).astype(F32),
    ]
    dma = pltpu.SemaphoreType.DMA
    any_spec = pl.BlockSpec(memory_space=pl.ANY)
    built = [(1152, 1024), (3072, 384)] + [(2048, 256)] * 3
    built = built + [(2, 1024, 256), (2, 1024, 256), (2, 1536, 256)]
    heads = [(4096, 256)] * 4
    shapes = [(34, NF, 384)] + built * 2 + heads + [w.shape for w in others]
    out = pl.pallas_call(
        start_kernel,
        out_shape=tuple(S(shape) for shape in shapes),
        in_specs=VM(11) + [any_spec] * len(others),
        out_specs=tuple(VM(1) + [any_spec] * (len(shapes) - 1)),
        scratch_shapes=[
            V((4, 8, NF, 384)),
            dma((3,)),
            dma((3,)),
            dma((2, 7)),
            *[V(shape) for shape in built * 2],
            V((4096, 256)),
            V((4096, 256)),
            dma((18,)),
        ],
        compiler_params=pltpu.CompilerParams(
            collective_id=1, has_side_effects=True, vmem_limit_bytes=56 * MIB
        ),
        name="start",
    )(jnp.transpose(frames, (1, 2, 3, 0)), *rows_in, latent_head, decode_head, *others)
    encode_forms, decode_forms = out[1:9], out[9:17]
    return out[0], encode_forms, decode_forms, out[17:19], out[19:21], out[21:]


def turn_kernel(x, *out):
    me = lax.axis_index("strip")

    def turn_rows(i, carry):
        flat = turned_rows(x, i)
        for k in range(4):
            part = flat[first_frame(k) : first_frame(k) + NF]
            for step in range(4):

                @pl.when(lax.rem(me + step, 4) == k)
                def _():
                    out[step][i] = part

        return carry

    lax.fori_loop(0, 8, turn_rows, 0)


def around(parts):
    return [parts[0]] + [
        lax.ppermute(parts[k], "strip", [(s, (s + k) % 4) for s in range(4)]) for k in range(1, 4)
    ]


def frames_in_later(block):
    parts = pl.pallas_call(
        turn_kernel,
        out_shape=(S((8, NF, 384)),) * 4,
        in_specs=VM(1),
        out_specs=tuple(VM(4)),
        compiler_params=pltpu.CompilerParams(vmem_limit_bytes=32 * MIB),
        name="turn",
    )(jnp.transpose(block, (1, 2, 3, 0)))
    return around(parts)


def turned_back(got, out):
    def turn_rows(i, carry):
        block = jnp.concatenate([got[(b % 2) * 2 + b // 2, i] for b in range(4)], axis=0)
        flat = block.T.astype(out.dtype)
        for p in range(2):
            for c in range(3):
                first = 64 * (3 * p + c)
                out[c, 2 * i + p] = flat[first : first + 64]
        return carry

    lax.fori_loop(0, 8, turn_rows, 0)


def turn_back_kernel(c0, c1, c2, c3, out, got):
    me = lax.axis_index("strip")
    for k, part in enumerate((c0, c1, c2, c3)):
        got[lax.rem(me + 4 - k, 4)] = part[...]
    turned_back(got, out)


def frames_out_later(pairs, strip):
    parts = around(
        [lax.dynamic_slice_in_dim(pairs, 8 * ((strip + k) % 4), 8) for k in range(4)]
    )
    flat = pl.pallas_call(
        turn_back_kernel,
        out_shape=S((3, 16, 64, 256)),
        in_specs=VM(4),
        out_specs=VM(1)[0],
        scratch_shapes=[V((4, 8, NF, 384))],
        compiler_params=pltpu.CompilerParams(vmem_limit_bytes=32 * MIB),
        name="turn_back",
    )(*parts)
    return jnp.transpose(flat, (3, 0, 1, 2))


def dot(a, b):
    return jnp.dot(a, b, preferred_element_type=F32)


def dot_nt(a, b):
    return lax.dot_general(a, b, (((1,), (1,)), ((), ())), preferred_element_type=F32)


def over_groups(values, join):
    lanes = values.shape[1]
    lane = lax.broadcasted_iota(jnp.int32, values.shape, 1)
    for step in (1, 2, 4, 8, 16):
        upper = lax.rem(lax.div(lane, step), 2) == 1
        other = jnp.where(
            upper, pltpu.roll(values, step, 1), pltpu.roll(values, lanes - step, 1)
        )
        values = join(values, other)
    return values


def unit_of(hidden):
    centred = hidden - jnp.mean(hidden, -1, keepdims=True)
    scale_inv = lax.rsqrt(jnp.mean(centred * centred, -1, keepdims=True) + EPS)
    return centred * scale_inv, scale_inv


def unit_back(grad_normed, unit_rows, scale_inv, gain):
    grad_unit = grad_normed * gain
    grad_gain = jnp.sum(grad_normed * unit_rows, 0, keepdims=True)
    grad_rows = scale_inv * (
        grad_unit
        - jnp.mean(grad_unit, -1, keepdims=True)
        - unit_rows * jnp.mean(grad_unit * unit_rows, -1, keepdims=True)
    )
    return grad_gain, grad_rows


LAYER_ROWS = 1536


def token_rows(layers):
    return layers * LAYER_ROWS + 256 + NF + 16


def middle_kernel(
    layers,
    feat, lh0, lh1, dh0, dh1, emb0, emb1, pos, gains, allow, cot,
    qkv0, qkv1, proj0, proj1, up0, up1, down0, down1,
    tokens, latent_out, chances_out, decoded, flat, grad_latent, feat_got,
    feat_sems, keep, send, sent, spread_sems, parts, gots, pair_sems,
    other, other_got, fold_sems, unit_a, unit_f, normed_a, normed_f, mixed, weights,
    attended, before, inner, gain_rows,
):
    strip = lax.axis_index("strip")
    row = lax.axis_index("rows")
    partner = (row, lax.rem(strip + 2, 4))
    sibling = (row, strip + 1 - 2 * lax.rem(strip, 2))
    barrier = pltpu.get_barrier_semaphore()
    for device in (partner, sibling):
        pl.semaphore_signal(barrier, inc=1, device_id=device, device_id_type=MESH)
    pl.semaphore_wait(barrier, 2)

    def copy(src, dst, sems, index, device):
        return pltpu.make_async_remote_copy(
            src_ref=src,
            dst_ref=dst,
            send_sem=sems.at[0, index],
            recv_sem=sems.at[1, index],
            device_id=device,
            device_id_type=MESH,
        )

    feat_copy = copy(feat, feat_got, feat_sems, 0, partner)
    feat_copy.start()

    def total_start(index, value):
        parts[index] = value.astype(BF)
        one = copy(parts.at[index], gots.at[index], pair_sems, index, partner)
        one.start()
        return one

    def total_wait(index, one):
        one.wait()
        got = jnp.concatenate([gots[index, NF:], gots[index, :NF]], axis=0)
        return parts[index].astype(F32) + got.astype(F32)

    def logits_of(maps):
        halves = []
        for weight in (lh0, lh1):
            total = jnp.zeros((NF, 256), F32)
            for h in range(4):
                total = total + dot(maps[h], weight[1024 * h : 1024 * h + 1024])
            halves.append(total)
        return jnp.concatenate(halves, axis=1)

    mine = logits_of(feat)
    feat_copy.wait()
    logits = jnp.concatenate([mine, logits_of(feat_got)], axis=0)
    raised = jnp.exp(logits - over_groups(logits, jnp.maximum))
    chances = raised / over_groups(raised, jnp.add)
    latent = chances.astype(BF)
    chances_out[...] = chances
    latent_out[...] = latent

    waiting = total_start(0, dot(latent[:, :256], emb0[...]) + dot(latent[:, 256:], emb1[...]))
    for hw in range(16):
        lanes = slice(256 * (hw % 4), 256 * (hw % 4) + 256)
        rows = slice(256 * hw, 256 * hw + 256)
        value = dot_nt(latent[:, :256], dh0[rows]) + dot_nt(latent[:, 256:], dh1[rows])
        value = value.astype(BF)
        keep[hw // 4, :, lanes] = value[:NF]
        send[hw // 4, :, lanes] = value[NF:]
    spread_copy = copy(send, sent, spread_sems, 0, partner)
    spread_copy.start()
    embedded = total_wait(0, waiting)
    place = pos[...].astype(F32)
    hidden = embedded + jnp.concatenate([place, place], axis=0)
    head_lane = lax.div(lax.broadcasted_iota(jnp.int32, (2 * NF, 128), 1), HEAD_DIM)
    allowed = allow[...] > 0.5

    def of_head(value, h):
        return jnp.where(head_lane == h % 2, value, jnp.zeros_like(value))

    def pair_lanes(h):
        return slice(128 * (h // 2), 128 * (h // 2) + 128)

    for k in range(layers):
        unit, inv = unit_of(hidden)
        unit_a[k] = jnp.concatenate([unit, jnp.broadcast_to(inv, (2 * NF, 128))], axis=1)
        normed = (unit * gains[2 * k : 2 * k + 1]).astype(BF)
        normed_a[k] = normed
        for part in range(3):
            mixed[k, part] = jnp.concatenate(
                [dot(normed, qkv0[k, part]), dot(normed, qkv1[k, part])], axis=1
            ).astype(BF)
        for p in range(2):
            both = jnp.zeros((2 * NF, 128), F32)
            for h in (2 * p, 2 * p + 1):
                lanes = pair_lanes(h)
                scores = SCALE * dot_nt(of_head(mixed[k, 0, :, lanes], h), mixed[k, 1, :, lanes])
                scores = jnp.where(allowed, scores, NEG)
                lifted = jnp.exp(scores - jnp.max(scores, -1, keepdims=True))
                weight = lifted / jnp.sum(lifted, -1, keepdims=True)
                weights[k, h] = weight
                both = both + of_head(dot(weight.astype(BF), mixed[k, 2, :, lanes]), h)
            attended[k, :, 128 * p : 128 * p + 128] = both.astype(BF)
        partial = dot(attended[k, :, :128], proj0[k]) + dot(attended[k, :, 128:], proj1[k])
        middle = hidden + total_wait(2 * k + 1, total_start(2 * k + 1, partial))
        unit, inv = unit_of(middle)
        unit_f[k] = jnp.concatenate([unit, jnp.broadcast_to(inv, (2 * NF, 128))], axis=1)
        normed = (unit * gains[2 * k + 1 : 2 * k + 2]).astype(BF)
        normed_f[k] = normed
        partial = jnp.zeros((2 * NF, 512), F32)
        for side, (up, down) in enumerate(((up0, down0), (up1, down1))):
            value = dot(normed, up[k])
            before[k, :, 512 * side : 512 * side + 512] = value
            act = (value * sig(value)).astype(BF)
            inner[k, :, 512 * side : 512 * side + 512] = act
            partial = partial + dot(act, down[k])
        hidden = middle + total_wait(2 * k + 2, total_start(2 * k + 2, partial))
    tokens[...] = hidden.astype(BF)

    spread_copy.wait()
    decoded[...] = (keep[...].astype(F32) + sent[...].astype(F32)).astype(BF)

    fold_copies = []

    def fold_start(first, count):
        rows = pl.ds(first, count)
        one = copy(other.at[rows], other_got.at[rows], fold_sems, len(fold_copies), sibling)
        one.start()
        fold_copies.append((first, count, one))

    grad = cot[...].astype(F32)
    for k in reversed(range(layers)):
        base = LAYER_ROWS * k
        index = 2 * layers + 1 + 2 * (layers - 1 - k)
        low = grad.astype(BF)
        partial = jnp.zeros((2 * NF, 512), F32)
        grads = []
        for side, (up, down) in enumerate(((up0, down0), (up1, down1))):
            value = before[k, :, 512 * side : 512 * side + 512]
            squash = sig(value)
            slope = squash * (1.0 + value * (1.0 - squash))
            grad_before = (dot_nt(low, down[k]) * slope).astype(BF)
            grads.append(grad_before)
            partial = partial + dot_nt(grad_before, up[k])
        waiting = total_start(index, partial)
        turned = normed_f[k].T
        for side, dst in enumerate((flat, other)):
            act = inner[k, :, 512 * side : 512 * side + 512]
            dst[base : base + 512] = dot(act.T, low).astype(BF)
            dst[base + 512 : base + 1024] = dot(turned, grads[side]).astype(BF)
        grad_normed = total_wait(index, waiting)
        gain_f, grad_rows = unit_back(
            grad_normed, unit_f[k, :, :512], unit_f[k, :, 512:513], gains[2 * k + 1 : 2 * k + 2]
        )
        grad = grad + grad_rows
        low = grad.astype(BF)
        grad_mixed = [[], [], []]
        for p, proj in enumerate((proj0, proj1)):
            lanes = pair_lanes(2 * p)
            grad_pair = dot_nt(low, proj[k]).astype(BF)
            queries, keys, vals = mixed[k, 0, :, lanes], mixed[k, 1, :, lanes], mixed[k, 2, :, lanes]
            g_queries = jnp.zeros((2 * NF, 128), F32)
            g_keys, g_vals = g_queries, g_queries
            for h in (2 * p, 2 * p + 1):
                weight = weights[k, h]
                grad_head = of_head(grad_pair, h)
                g_vals = g_vals + dot(weight.astype(BF).T, grad_head)
                grad_weight = dot_nt(grad_head, vals)
                along = jnp.sum(weight * grad_weight, -1, keepdims=True)
                grad_scores = (weight * (grad_weight - along)).astype(BF)
                g_queries = g_queries + of_head(dot(grad_scores, keys), h)
                g_keys = g_keys + dot(grad_scores.T, of_head(queries, h))
            grad_mixed[0].append((SCALE * g_queries).astype(BF))
            grad_mixed[1].append((SCALE * g_keys).astype(BF))
            grad_mixed[2].append(g_vals.astype(BF))
        partial = jnp.zeros((2 * NF, 512), F32)
        for part in range(3):
            for side, qkv in enumerate((qkv0, qkv1)):
                partial = partial + dot_nt(grad_mixed[part][side], qkv[k, part])
        waiting = total_start(index + 1, partial)
        turned = normed_a[k].T
        for side, dst in enumerate((flat, other)):
            act = attended[k, :, 128 * side : 128 * side + 128]
            dst[base + 1024 : base + 1152] = dot(act.T, low).astype(BF)
            for part in range(3):
                value = dot(turned, grad_mixed[part][side]).astype(BF)
                first = base + 1152 + 128 * part
                for b in range(4):
                    dst[first : first + 128, 128 * b : 128 * b + 128] = value[
                        128 * b : 128 * b + 128
                    ]
        fold_start(base, LAYER_ROWS)
        grad_normed = total_wait(index + 1, waiting)
        gain_a, grad_rows = unit_back(
            grad_normed, unit_a[k, :, :512], unit_a[k, :, 512:513], gains[2 * k : 2 * k + 1]
        )
        grad = grad + grad_rows
        gain_rows[2 * k : 2 * k + 1] = gain_a
        gain_rows[2 * k + 1 : 2 * k + 2] = gain_f

    base = LAYER_ROWS * layers
    low = grad.astype(BF)
    own_latent, other_latent = latent_out[:, :256], latent_out[:, 256:]
    flat[base : base + 256] = dot(own_latent.T, low).astype(BF)
    other[base : base + 256] = dot(other_latent.T, low).astype(BF)
    small = jnp.concatenate(
        [
            grad[:NF] + grad[NF:],
            gain_rows[...],
            jnp.zeros((16 - 2 * layers, 512), F32),
        ],
        axis=0,
    ).astype(BF)
    flat[base + 256 : base + 256 + NF + 16] = small
    other[base + 256 : base + 256 + NF + 16] = small
    fold_start(base, 256 + NF + 16)
    grad_latent[:, :256] = dot_nt(low, emb0[...])
    grad_latent[:, 256:] = dot_nt(low, emb1[...])
    for first, count, one in fold_copies:
        one.wait()
        for start in range(first, first + count, 16 * 7 if count % 112 == 0 else 16 * 8):
            size = min(128 if count % 112 else 112, first + count - start)
            rows = slice(start, start + size)
            flat[rows] = (flat[rows].astype(F32) + other_got[rows].astype(F32)).astype(BF)
    spare = flat.shape[0] - token_rows(layers)
    if spare:
        flat[token_rows(layers) :] = jnp.zeros((spare, 512), BF)


def middle(layers, multiple, *args):
    rows = token_rows(layers)
    rows = rows + -rows % multiple
    dma = pltpu.SemaphoreType.DMA
    sums = 4 * layers + 1
    t = 2 * NF
    return pl.pallas_call(
        functools.partial(middle_kernel, layers),
        out_shape=(
            S((t, 512)),
            S((t, 512)),
            S((t, 512), F32),
            S((4, NF, 1024)),
            S((rows, 512)),
            S((t, 512), F32),
            S((4, NF, 1024)),
        ),
        in_specs=VM(len(args)),
        out_specs=tuple(VM(7)),
        scratch_shapes=[
            dma((2, 1)),
            V((4, NF, 1024)),
            V((4, NF, 1024)),
            V((4, NF, 1024)),
            dma((2, 1)),
            V((sums, t, 512)),
            V((sums, t, 512)),
            dma((2, sums)),
            V((rows, 512)),
            V((rows, 512)),
            dma((2, layers + 1)),
            V((layers, t, 640), F32),
            V((layers, t, 640), F32),
            V((layers, t, 512)),
            V((layers, t, 512)),
            V((layers, 3, t, 256)),
            V((layers, 4, t, t), F32),
            V((layers, t, 256)),
            V((layers, t, 1024), F32),
            V((layers, t, 1024)),
            V((2 * layers, 512), F32),
        ],
        compiler_params=pltpu.CompilerParams(
            collective_id=3, has_side_effects=True, vmem_limit_bytes=56 * MIB
        ),
        name="middle",
    )(*args)


def back_kernel(
    grad, latent, chances, grad_embed, feat0, feat1, lh0, lh1, dh0, dh1,
    grad_feat, out_rows, in_rows,
    got, got_sems, keep, send, sent, sent_sems, own, other, other_got, fold_sems,
):
    strip = lax.axis_index("strip")
    row = lax.axis_index("rows")
    partner = (row, lax.rem(strip + 2, 4))
    sibling = (row, strip + 1 - 2 * lax.rem(strip, 2))
    barrier = pltpu.get_barrier_semaphore()
    for device in (partner, sibling):
        pl.semaphore_signal(barrier, inc=1, device_id=device, device_id_type=MESH)
    pl.semaphore_wait(barrier, 2)

    def copy(src, dst, sems, index, device):
        return pltpu.make_async_remote_copy(
            src_ref=src,
            dst_ref=dst,
            send_sem=sems.at[0, index],
            recv_sem=sems.at[1, index],
            device_id=device,
            device_id_type=MESH,
        )

    grad_copy = copy(grad, got, got_sems, 0, partner)
    grad_copy.start()

    def through(maps):
        halves = []
        for weight in (dh0, dh1):
            total = jnp.zeros((NF, 256), F32)
            for h in range(4):
                total = total + dot(maps[h], weight[1024 * h : 1024 * h + 1024])
            halves.append(total)
        return jnp.concatenate(halves, axis=1)

    mine = through(grad)
    grad_copy.wait()
    grad_latent = grad_embed[...] + jnp.concatenate([mine, through(got)], axis=0)
    probs = chances[...]
    along = over_groups(probs * grad_latent, jnp.add)
    grad_logits = (probs * (grad_latent - along)).astype(BF)
    sends = []
    for h in range(4):
        for w in range(4):
            lanes = slice(256 * w, 256 * w + 256)
            rows = slice(1024 * h + 256 * w, 1024 * h + 256 * w + 256)
            value = dot_nt(grad_logits[:, :256], lh0[rows]) + dot_nt(grad_logits[:, 256:], lh1[rows])
            value = value.astype(BF)
            keep[h, :, lanes] = value[:NF]
            send[h, :, lanes] = value[NF:]
        one = copy(send.at[h], sent.at[h], sent_sems, h, partner)
        one.start()
        sends.append(one)
    folds = []
    for slot, (first, second, rhs) in enumerate(
        ((grad, got, latent[...]), (feat0, feat1, grad_logits))
    ):
        for h in range(4):
            for w in range(4):
                lanes = slice(256 * w, 256 * w + 256)
                rows = slice(1024 * h + 256 * w, 1024 * h + 256 * w + 256)
                maps = jnp.concatenate([first[h, :, lanes], second[h, :, lanes]], axis=0)
                value = dot(maps.T, rhs).astype(BF)
                own[slot, rows] = value[:, :256]
                other[slot, rows] = value[:, 256:]
        one = copy(other.at[slot], other_got.at[slot], fold_sems, slot, sibling)
        one.start()
        folds.append(one)
    for one in sends:
        one.wait()
    grad_feat[...] = (keep[...].astype(F32) + sent[...].astype(F32)).astype(BF)
    swap = exchange_16()
    for slot, (out, one) in enumerate(zip((out_rows, in_rows), folds)):
        one.wait()
        for b in range(16):
            parts = []
            for k in range(16):
                rows = slice(256 * k + 16 * b, 256 * k + 16 * b + 16)
                value = own[slot, rows].astype(F32) + other_got[slot, rows].astype(F32)
                parts.append(value.astype(BF))
            block = dot(swap, jnp.concatenate(parts, axis=0)).astype(BF)
            out[256 * b : 256 * b + 256] = block.T if slot == 0 else block


def latents_back(*args):
    dma = pltpu.SemaphoreType.DMA
    maps = (4, NF, 1024)
    rows = (4096, 256)
    return pl.pallas_call(
        back_kernel,
        out_shape=(S(maps), S(rows), S(rows)),
        in_specs=VM(len(args)),
        out_specs=tuple(VM(3)),
        scratch_shapes=[
            V(maps),
            dma((2, 1)),
            V(maps),
            V(maps),
            V(maps),
            dma((2, 4)),
            V((2,) + rows),
            V((2,) + rows),
            V((2,) + rows),
            dma((2, 2)),
        ],
        compiler_params=pltpu.CompilerParams(
            collective_id=4, has_side_effects=True, vmem_limit_bytes=56 * MIB
        ),
        name="latents_back",
    )(*args)


def finish_kernel(
    count, v, dec, enc, grad, total, conv, grad_out,
    got, strip_sems, from_near, summed, from_far, conv_v, conv_near, conv_summed, conv_far,
    side_got, side_sum, cross_got, sems, far_sems, back_sems,
):
    me = lax.axis_index("strip")
    row = lax.axis_index("rows")
    half = count // 2
    chunks = v.shape[0]
    near, far = lax.rem(row, 2), lax.div(row, 2)
    core, x = lax.rem(me, 2), lax.div(me, 2)
    near_device = (row + 1 - 2 * near, me)
    sibling, partner = (row, me + 1 - 2 * core), (row, lax.rem(me + 2, 4))
    barrier = pltpu.get_barrier_semaphore()
    strip_devices = [(row, lax.rem(me + k, 4)) for k in range(1, 4)]
    far_places = [lax.rem(far + k, half) for k in range(1, half)]
    far_devices = [(2 * place + near, me) for place in far_places]
    for device in strip_devices + [near_device] + far_devices:
        pl.semaphore_signal(barrier, inc=1, device_id=device, device_id_type=MESH)
    pl.semaphore_wait(barrier, 3 + half)

    def copy(src, dst, pair, index, device):
        one = pltpu.make_async_remote_copy(
            src_ref=src,
            dst_ref=dst,
            send_sem=pair.at[(0,) + index],
            recv_sem=pair.at[(1,) + index],
            device_id=device,
            device_id_type=MESH,
        )
        one.start()
        return one

    places = [
        (v.at[c], from_near.at[c], summed.at[c], from_far.at[c], total.at[c])
        for c in range(chunks)
    ]
    places.append((conv_v, conv_near, conv_summed, conv_far, conv.at[core, x]))
    near_copies, far_copies, back_copies, last_copies = {}, {}, {}, {}

    def stage_near(c):
        near_copies[c] = copy(places[c][0].at[1 - near], places[c][1], sems, (c,), near_device)

    def stage_far(c):
        values, arrived, both, slots, _ = places[c]
        near_copies[c].wait()
        both[...] = (values[near].astype(F32) + arrived[...].astype(F32)).astype(BF)
        far_copies[c] = [
            copy(both.at[place], slots.at[k], far_sems, (c, k), device)
            for k, (place, device) in enumerate(zip(far_places, far_devices))
        ]

    def stage_back(c):
        _, _, both, slots, out = places[c]
        for one in far_copies[c]:
            one.wait()
        whole = both[far].astype(F32)
        for k in range(half - 1):
            whole = whole + slots[k].astype(F32)
        out[near, far] = whole.astype(BF)
        back_copies[c] = [
            copy(out.at[near, far], out.at[near, far], back_sems, (c, k), device)
            for k, device in enumerate(far_devices)
        ]

    def stage_last(c):
        out = places[c][4]
        for one in back_copies[c]:
            one.wait()
        last_copies[c] = copy(
            out.at[near], out.at[near], sems, (chunks + 1 + c,), near_device
        )

    side = 2 * (chunks + 1)
    side_copies = [
        copy(part.at[1 - core], side_got.at[k], sems, (side + k,), sibling)
        for k, part in enumerate((dec, enc))
    ]
    for c in range(chunks):
        stage_near(c)
    cross_copies = []
    for k, part in enumerate((dec, enc)):
        side_copies[k].wait()
        side_sum[k] = (part[core].astype(F32) + side_got[k].astype(F32)).astype(BF)
        cross_copies.append(
            copy(side_sum.at[k, 1 - x], cross_got.at[k], sems, (side + 2 + k,), partner)
        )
    strip_copies = []
    for k in range(1, 4):
        to = lax.rem(me + k, 4)
        strip_copies.append(
            copy(grad.at[pl.ds(8 * to, 8)], got.at[me], strip_sems, (k - 1,), (row, to))
        )
    got[me] = grad[pl.ds(8 * me, 8)]

    stage_far(0)
    stage_far(1)
    shares = []
    for k in range(2):
        cross_copies[k].wait()
        shares.append(
            (side_sum[k, x].astype(F32) + cross_got[k].astype(F32)).astype(BF)
        )
    share = jnp.concatenate(shares, axis=0)
    each = conv_v.shape[2]
    spare = 2 * half * each - share.shape[0]
    if spare:
        share = jnp.concatenate([share, jnp.zeros((spare, 256), BF)], axis=0)
    for piece in range(2 * half):
        conv_v[piece // half, piece % half] = share[piece * each : piece * each + each]
    last = chunks
    stage_near(last)
    stage_back(0)
    stage_far(2)
    stage_back(1)
    stage_last(0)
    stage_far(last)
    stage_far(3)
    stage_back(2)
    stage_last(1)
    for one in strip_copies:
        one.wait()
    turned_back(got, grad_out)
    stage_back(last)
    stage_last(2)
    stage_back(3)
    stage_last(last)
    stage_last(3)
    last_copies[last].wait()
    cross = copy(conv.at[core, x], conv.at[core, x], sems, (side + 4,), partner)
    cross.wait()
    beside_copy = copy(conv.at[core], conv.at[core], sems, (side + 5,), sibling)
    for c in range(chunks):
        last_copies[c].wait()
    beside_copy.wait()


def finish(flat, dec, enc, grad):
    count = lax.axis_size("rows")
    half = count // 2
    chunks = 4
    each = flat.shape[0] // (count * chunks)
    share = dec.shape[0] // 2
    conv_each = -(-share // (16 * count)) * 16
    shape = (chunks, 2, half, each, 256)
    dma = pltpu.SemaphoreType.DMA
    quarter = dec.shape[0] // 4
    total, conv, grad_out = pl.pallas_call(
        functools.partial(finish_kernel, count),
        out_shape=(
            S(shape),
            S((2, 2, 2, half, conv_each, 256)),
            S((3, 16, 64, 256), F32),
        ),
        in_specs=VM(4),
        out_specs=tuple(VM(3)),
        scratch_shapes=[
            V((4, 8, NF, 384)),
            dma((2, 3)),
            V((chunks, half, each, 256)),
            V((chunks, half, each, 256)),
            V((chunks, half - 1, each, 256)),
            V((2, half, conv_each, 256)),
            V((half, conv_each, 256)),
            V((half, conv_each, 256)),
            V((half - 1, conv_each, 256)),
            V((2, 2, quarter, 256)),
            V((2, 2, quarter, 256)),
            V((2, quarter, 256)),
            dma((2, 2 * (chunks + 1) + 6)),
            dma((2, chunks + 1, half - 1)),
            dma((2, chunks + 1, half - 1)),
        ],
        compiler_params=pltpu.CompilerParams(
            collective_id=2, has_side_effects=True, vmem_limit_bytes=56 * MIB
        ),
        name="finish",
    )(
        flat.reshape(shape),
        dec.reshape(2, 2, quarter, 256),
        enc.reshape(2, 2, quarter, 256),
        grad,
    )
    conv = conv.reshape(2, 2, -1, 256)
    return (
        total.reshape(-1, 256),
        conv[:, :, :quarter].reshape(-1, 256),
        conv[:, :, quarter : 2 * quarter].reshape(-1, 256),
        jnp.transpose(grad_out, (3, 0, 1, 2)),
    )


def beside(value):
    return lax.ppermute(value, "strip", [(0, 1), (1, 0), (2, 3), (3, 2)])


def make_mask(segment_ids):
    places = jnp.arange(segment_ids.shape[1])
    causal = places[:, None] >= places[None, :]
    return causal[None] & (segment_ids[:, :, None] == segment_ids[:, None, :])


def rows_share(flat):
    return lax.psum_scatter(flat, "rows", scatter_dimension=0, tiled=True)


def rows_whole(share):
    return lax.all_gather(share, "rows", axis=0, tiled=True)


def unpack_kernels(flat):
    flat = flat.astype(F32)
    second = jnp.concatenate([flat[2048:2560, :128], flat[2048:2560, 128:]], axis=0)
    first = jnp.concatenate([flat[2560:2688, 64 * k : 64 * k + 64] for k in range(4)], axis=0)
    return (
        flat[2688:2736, :32].reshape(3, 4, 4, 32),
        first.reshape(32, 4, 4, 64),
        second.reshape(64, 4, 4, 128),
        flat[:2048],
    )


def shards(
    frames,
    segment_ids,
    encode_one,
    encode_two,
    encode_three,
    encode_four,
    latent_head,
    token_embed,
    positions,
    norm_gains,
    qkv_weight,
    out_weight,
    up_weight,
    down_weight,
    decode_head,
    decode_one,
    decode_two,
    decode_three,
    decode_four,
    token_cotangent,
    frame_cotangent,
):
    strip = lax.axis_index("strip")
    x, core = strip // 2, strip % 2
    layers = qkv_weight.shape[0]

    kernels = (
        encode_one,
        encode_two,
        encode_three,
        encode_four,
        decode_one,
        decode_two,
        decode_three,
        decode_four,
    )
    qkv = jnp.transpose(qkv_weight, (0, 2, 1, 3))
    shards_here = (token_embed, qkv, out_weight, up_weight, down_weight)
    pixels, enc_f, dec_f, head_in, head_out, theirs = start(
        frames, kernels, latent_head, decode_head, shards_here
    )
    enc_a, enc_b, enc_t, enc_u = enc_f[0], enc_f[1], enc_f[2:5], enc_f[5:8]
    dec_a, dec_b, dec_t, dec_u = dec_f[0], dec_f[1], dec_f[2:5], dec_f[5:8]
    embed, qkv, project, widen, narrow = zip(shards_here, theirs)
    hints = frames_in_later(frame_cotangent)
    z1, z2, z3, z4, feat = enc_fwd(pixels, enc_a, *enc_t)

    first = 2 * core

    def mine(array, size):
        own = lax.dynamic_slice_in_dim(array, (first + x) * size, size)
        other = lax.dynamic_slice_in_dim(array, (first + 1 - x) * size, size)
        return jnp.concatenate([own, other], axis=0)

    allowed = make_mask(mine(segment_ids, 1)).astype(F32)
    blank = jnp.zeros((NF, NF), F32)
    allowed = jnp.concatenate(
        [
            jnp.concatenate([allowed[0], blank], axis=1),
            jnp.concatenate([blank, allowed[1]], axis=1),
        ],
        axis=0,
    )
    line = 16 * lax.axis_size("rows")
    tokens, latent, chances, decoded, t_flat, grad_latent, feat_got = middle(
        layers,
        line,
        feat,
        *head_in,
        *head_out,
        *embed,
        positions,
        norm_gains.reshape(2 * layers, -1),
        allowed,
        mine(token_cotangent, NF),
        *qkv,
        *project,
        *widen,
        *narrow,
    )
    t_share = rows_share(t_flat)
    tokens = jnp.where(
        x == 0, tokens, jnp.concatenate([tokens[NF:], tokens[:NF]], axis=0)
    )
    other_tokens = beside(tokens)
    tokens_out = jnp.where(
        core == 0,
        jnp.concatenate([tokens, other_tokens]),
        jnp.concatenate([other_tokens, tokens]),
    )

    recon_pairs, p3, p2, p1 = dec_fwd(decoded, dec_u[2], dec_u[1], dec_u[0], dec_b)
    recon = frames_out_later(recon_pairs, strip)
    g_decoded, dec_flat = dec_bwd(hints, decoded, p3, p2, p1, dec_a, *dec_t)
    g_decoded, t_share = lax.optimization_barrier((g_decoded, t_share))
    t_total = rows_whole(t_share)
    g_feat, d_rows, l_rows = latents_back(
        g_decoded, latent, chances, grad_latent, feat, feat_got, *head_in, *head_out
    )
    d_share = rows_share(d_rows)

    d_pairs, enc_flat = enc_bwd(pixels, z1, z2, z3, z4, g_feat, *enc_u, enc_b)
    d_pairs, t_total, d_share = lax.optimization_barrier((d_pairs, t_total, d_share))
    d_total = rows_whole(d_share)
    l_total, dec_total, enc_total, frames_grad = finish(l_rows, dec_flat, enc_flat, d_pairs)

    t_total = t_total.astype(F32)
    t_layers = t_total[: layers * LAYER_ROWS].reshape(layers, LAYER_ROWS, 512)
    t_rest = t_total[layers * LAYER_ROWS :]
    r_qkv = t_layers[:, 1152:].reshape(layers, 3, 128, 4, 128).transpose(0, 3, 2, 1, 4)
    r_qkv = r_qkv.reshape(qkv_weight.shape)
    e_one, e_two, e_three, e_four = unpack_kernels(enc_total)
    d_four, d_three, d_two, d_one = unpack_kernels(dec_total)
    e_four = jnp.concatenate([e_four[:, :128], e_four[:, 128:]], axis=0)
    return (
        tokens_out,
        recon,
        frames_grad,
        e_one.transpose(3, 0, 1, 2),
        e_two.transpose(3, 0, 1, 2),
        e_three.transpose(3, 0, 1, 2),
        e_four.reshape(256, 4, 4, 128).transpose(0, 3, 1, 2),
        l_total.astype(F32),
        t_rest[:256],
        t_rest[256 : 256 + NF],
        t_rest[256 + NF : 256 + NF + 2 * layers].reshape(norm_gains.shape),
        r_qkv,
        t_layers[:, 1024:1152],
        t_layers[:, 512:1024],
        t_layers[:, :512],
        d_total.astype(F32).reshape(16, 256, 256).transpose(1, 0, 2).reshape(256, 4096),
        d_one.reshape(128, 4, 4, 256).transpose(0, 3, 1, 2),
        d_two.transpose(0, 3, 1, 2),
        d_three.transpose(0, 3, 1, 2),
        d_four.transpose(0, 3, 1, 2),
    )


def solution(mesh):
    placed = (
        P("rows", None, "strip", None),
        P("rows", None),
        P(),
        P(),
        P(),
        P(),
        P(None, "strip"),
        P("strip", None),
        P(),
        P(),
        P(None, None, None, "strip"),
        P(None, "strip", None),
        P(None, None, "strip"),
        P(None, "strip", None),
        P("strip", None),
        P(),
        P(),
        P(),
        P(),
        P("rows", None),
        P("rows", None, "strip", None),
    )
    return jax.shard_map(
        shards,
        mesh=mesh,
        in_specs=placed,
        out_specs=(
            P("rows", None),
            P("rows", None, "strip", None),
            P("rows", None, "strip", None),
            P(),
            P(),
            P(),
            P(),
            P(None, "strip"),
            P("strip", None),
            P(),
            P(),
            P(None, None, None, "strip"),
            P(None, "strip", None),
            P(None, None, "strip"),
            P(None, "strip", None),
            P("strip", None),
            P(),
            P(),
            P(),
            P(),
        ),
        check_vma=False,
    )
```

```python
import functools

import jax
import jax.numpy as jnp
from jax import lax
from jax.experimental import pallas as pl
from jax.experimental.pallas import tpu as pltpu
from jax.sharding import PartitionSpec as P

HEAD_DIM = 64
LCLASS = 32
EPS = 1e-05
SCALE = 0.125
NEG = -1e30
F32 = jnp.float32
BF = jnp.bfloat16
NF = 64
MIB = 1 << 20
MESH = pl.DeviceIdType.MESH


def sig(z): return 1.0/(1.0+jnp.exp(-z))

def zero_big(ref,rows):
    z=jnp.zeros((NF,1280),BF)
    ref[0,0]=z; ref[rows//2,1]=z
    e=jnp.zeros((rows//2+1,2,NF,128),BF)
    ref[:,:,:,0:128]=e; ref[:,:,:,1152:1280]=e

def zero_small(ref,rows,pad):
    z=jnp.zeros((NF,1024+2*pad),BF)
    ref[0]=z; ref[rows+1]=z
    if pad:
        e=jnp.zeros((rows+2,NF,pad),BF)
        ref[:,:,0:pad]=e; ref[:,:,1024+pad:]=e

def put_big(ref,half0,rows,q,val):
    v=val.reshape(rows,NF,256)
    for t in range(rows):
        ref[half0+(t+1)//2,(t+1)%2,:,128+256*q:384+256*q]=v[t]

def loop(n,body):
    if n==1: body(0)
    else:
        def step(g,c):
            body(g); return c
        lax.fori_loop(0,n,step,0)

def down(src,t_ref,rows,per,emit):
    def body(g):
        i0=g*per
        for q in range(4):
            lhs=jnp.concatenate([src[pl.ds(i0+kh//2,per),kh%2,:,256*q:256*q+512].reshape(per*NF,512) for kh in range(4)],axis=1)
            emit(i0,g*(per//2),q,jnp.dot(lhs,t_ref[...],preferred_element_type=F32))
    loop(rows//per,body)

def up(src,u_ref,rows,per,emit):
    k=u_ref.shape[1]//2
    def body(g):
        m0=g*per
        for q in range(4):
            for odd in range(2):
                lhs=jnp.concatenate([src[pl.ds(m0+1+odd-s,per),:,256*q:256*q+k].reshape(per*NF,k) for s in range(2)],axis=1)
                emit(m0,odd,q,jnp.dot(lhs,u_ref[odd],preferred_element_type=F32).reshape(per,NF,256))
    loop(rows//per,body)

def turn(src,dst,rows,pad):
    for q in range(4):
        dst[256*q:256*q+256,:rows*NF]=src[1:rows+1,:,pad+256*q:pad+256*q+256].reshape(rows*NF,256).T

def grad_w(big,yt,rows):
    out=[]
    for kh in range(4):
        acc=jnp.zeros((256,512),F32)
        for q in range(4):
            win=big[pl.ds(kh//2,rows),kh%2,:,256*q:256*q+512].reshape(rows*NF,512)
            acc=acc+jnp.dot(yt[256*q:256*q+256,:rows*NF],win,preferred_element_type=F32)
        out.append(acc)
    return out

def pack(pk,base,a,c,o,sums,flipped,swap,turned=False):
    taps=[]
    for acc in sums:
        total=None
        for j in range(a):
            first=(a+2*j-1)*c
            part=acc[j*o:j*o+o]
            if first: part=pltpu.roll(part,512-first,1)
            part=part[:,:4*c]
            total=part if total is None else total+part
        taps.append(total.astype(BF) if turned else total.T.astype(BF))
    width,count=(c,o//16) if turned else (o,c//16)
    held=[]
    for b in range(count):
        rows=[]
        for k in range(16):
            kh,kw=divmod(15-k if flipped else k,4)
            if turned: rows.append(taps[kh][16*b:16*b+16,c*kw:c*kw+c])
            else: rows.append(taps[kh][c*kw+16*b:c*kw+16*b+16])
        block=jnp.dot(swap,jnp.concatenate(rows,axis=0),preferred_element_type=F32).astype(BF)
        if width==256: pk[base+256*b:base+256*b+256]=block
        elif width==128:
            side,at=divmod(b,count//2)
            pk[base+256*at:base+256*at+256,128*side:128*side+128]=block
        else: held.extend([block[:128],block[128:]])
    if held: pk[base:base+128]=jnp.concatenate(held,axis=1)

def pack_outer(pk,base,red,flipped):
    r=lax.broadcasted_iota(jnp.int32,(48,1152),0); lane=lax.broadcasted_iota(jnp.int32,(48,1152),1)
    k=lax.rem(r,16)
    if flipped: k=15-k
    kh,kw=lax.div(k,4),lax.rem(k,4)
    at=384*lax.div(kh+1,2)+192*lax.rem(kh+1,2)+64*lax.div(r,16)+kw
    pick=(lane==at).astype(BF)
    value=jnp.concatenate([part.astype(BF) for part in red],axis=1)
    pk[base:base+128]=jnp.zeros((128,256),BF)
    pk[base:base+48,0:32]=lax.dot_general(pick,value,(((1,),(1,)),((),())),preferred_element_type=F32).astype(BF)

def outer_down(xp,a_ref,emit,per=4):
    def body(g):
        i0=g*per
        lhs=jnp.concatenate([xp[pl.ds(i0+d,per)].reshape(per*NF,384) for d in range(3)],axis=1)
        for q in range(4):
            emit(i0,g*(per//2),q,jnp.dot(lhs,a_ref[:,256*q:256*q+256],preferred_element_type=F32))
    loop(32//per,body)

def outer_up(yp,b_ref,emit,per=4):
    def body(g):
        i0=g*per
        lhs=jnp.concatenate([yp[pl.ds(i0+2-d,per)].reshape(per*NF,1024) for d in range(3)],axis=1)
        emit(i0,jnp.dot(lhs,b_ref[...],preferred_element_type=F32).reshape(per,NF,384))
    loop(32//per,body)

def outer_grad(xp,yt):
    red=[]
    lane=lax.broadcasted_iota(jnp.int32,(32,384),1)%64
    for d in range(3):
        x=xp[d:d+32].reshape(32*NF,384)
        tot=jnp.zeros((32,384),F32)
        for jb in range(4):
            g=jnp.dot(yt[256*jb:256*jb+256,:],x,preferred_element_type=F32)
            for jj in range(8):
                j=8*jb+jj
                v=pltpu.roll(g[32*jj:32*jj+32],(385-2*j)%384,1)
                if j==0: v=jnp.where(lane==0,0.0,v)
                if j==31: v=jnp.where(lane==3,0.0,v)
                tot=tot+v
        red.append(tot)
    return red

def enc_fwd_kernel(xp,a,t2,t3,t4,z1,z2,z3,z4,feat,m1,m2,m3):
    zero_big(m1,32); zero_big(m2,16); zero_big(m3,8)
    def keep(z,m):
        def emit(i0,half0,q,acc):
            rows=acc.shape[0]//NF
            z[pl.ds(i0,rows),:,256*q:256*q+256]=acc.astype(BF).reshape(rows,NF,256)
            val=(acc*sig(acc)).astype(BF)
            if m is None: feat[pl.ds(i0,rows),:,256*q:256*q+256]=val.reshape(rows,NF,256)
            else: put_big(m,half0,rows,q,val)
        return emit
    outer_down(xp,a,keep(z1,m1))
    down(m1,t2,16,4,keep(z2,m2))
    down(m2,t3,8,4,keep(z3,m3))
    down(m3,t4,4,4,keep(z4,None))

def dec_fwd_kernel(count,dec,u4,u3,u2,b,upper_both,lower,recon,p3,p2,p1,upper_piece,lower_both,
                   s4,s3,s2,s1,upper_slots,lower_near,remote):
    place=Place(count); sems=Sems(remote,None)
    place.greet([place.near_device]+place.far_devices)
    upper_far=far_start(place,sems,upper_both,upper_slots)
    lower_copy=near_start(place,sems,lower,lower_near)
    zero_small(s1,32,0); zero_small(s2,16,128); zero_small(s3,8,128); zero_small(s4,4,256)
    z=dec[...].astype(F32)
    s4[1:5,:,256:1280]=(z*sig(z)).astype(BF)
    def fwd(p,dst,pad):
        def emit(m0,odd,q,acc):
            for t in range(acc.shape[0]):
                h=2*(m0+t)+odd
                v=acc[t]
                p[h,:,256*q:256*q+256]=v.astype(BF)
                dst[h+1,:,pad+256*q:pad+256*q+256]=(v*sig(v)).astype(BF)
        return emit
    up(s4,u4,4,4,fwd(p3,s3,128))
    up(s3,u3,8,4,fwd(p2,s2,128))
    up(s2,u2,16,4,fwd(p1,s1,0))
    def put(i0,acc): recon[pl.ds(i0,acc.shape[0])]=acc.astype(BF)
    outer_up(s1,b,put)
    far_end(place,upper_far,upper_both,upper_slots,upper_piece)
    near_end(place,lower_copy,lower,lower_near,lower_both)

def dec_bwd_kernel(count,c0,c1,c2,c3,dec,p3,p2,p1,a,t2,t3,t4,upper_piece,lower_both,
                   gdec,pk,upper_half,lower_piece,d1,d2,d3,cp,yt,lower_slots,remote,here):
    place=Place(count); sems=Sems(remote,here); me=place.me
    place.greet(place.far_devices)
    upper_back=back_start(place,sems,upper_piece,upper_half)
    lower_far=far_start(place,sems,lower_both,lower_slots)
    cp[0]=jnp.zeros((NF,384),BF); cp[33]=jnp.zeros((NF,384),BF)
    for k,part in enumerate((c0,c1,c2,c3)):
        cp[pl.ds(1+8*lax.rem(me+4-k,4),8)]=part[...]
    zero_big(d1,32); zero_big(d2,16); zero_big(d3,8)
    def maps(p,rows,yt):
        for q in range(4):
            zz=p[:,:,256*q:256*q+256].reshape(rows*NF,256).astype(F32)
            yt[256*q:256*q+256,:rows*NF]=(zz*sig(zz)).astype(BF).T
    def back(p,dst):
        def emit(i0,half0,q,acc):
            rows=acc.shape[0]//NF
            zz=p[pl.ds(i0,rows),:,256*q:256*q+256].astype(F32).reshape(rows*NF,256)
            ss=sig(zz)
            val=(acc*(ss*(1.0+zz*(1.0-ss)))).astype(BF)
            if dst is None: gdec[pl.ds(i0,rows),:,256*q:256*q+256]=val.reshape(rows,NF,256)
            else: put_big(dst,half0,rows,q,val)
        return emit
    swap=exchange_16()
    maps(p1,32,yt); pack_outer(pk,2688,outer_grad(cp,yt),True)
    outer_down(cp,a,back(p1,d1))
    maps(p2,16,yt); pack(pk,2560,4,32,64,grad_w(d1,yt,16),True,swap)
    down(d1,t2,16,4,back(p2,d2))
    maps(p3,8,yt); pack(pk,2048,2,64,128,grad_w(d2,yt,8),True,swap)
    down(d2,t3,8,4,back(p3,d3))
    maps(dec,4,yt); pack(pk,0,1,128,256,grad_w(d3,yt,4),True,swap)
    down(d3,t4,4,4,back(dec,None))
    pk[2816-80:2816]=jnp.zeros((80,256),BF)
    far_end(place,lower_far,lower_both,lower_slots,lower_piece)
    for one in upper_back: one.wait()

def estimate(us):
    return pl.CostEstimate(flops=us*1150*10**6,bytes_accessed=MIB,transcendentals=0)

def S(shape,dt=BF): return jax.ShapeDtypeStruct(shape,dt)
def V(shape,dt=BF): return pltpu.VMEM(shape,dt)
VM=lambda n:[pl.BlockSpec(memory_space=pltpu.VMEM)]*n
def run(kernel,outs,scratch,args,name,us,lim=60,ident=None):
    extra={} if ident is None else dict(collective_id=ident,has_side_effects=True)
    return pl.pallas_call(kernel,out_shape=outs,in_specs=VM(len(args)),out_specs=tuple(VM(len(outs))),
        scratch_shapes=scratch,compiler_params=pltpu.CompilerParams(vmem_limit_bytes=lim*MIB,**extra),
        cost_estimate=estimate(us),name=name)(*args)
big=lambda h:V((h//2+1,2,NF,1280))
def enc_fwd(xp,a,t2,t3,t4):
    return run(enc_fwd_kernel,(S((32,NF,1024)),S((16,NF,1024)),S((8,NF,1024)),S((4,NF,1024)),S((4,NF,1024))),
      [big(32),big(16),big(8)],(xp,a,t2,t3,t4),"encode",22)
small=lambda h,p:V((h+2,NF,1024+2*p))
def enc_fwd(xp,a,t2,t3,t4):
    return run(enc_fwd_kernel,(S((32,NF,1024)),S((16,NF,1024)),S((8,NF,1024)),S((4,NF,1024)),S((4,NF,1024))),
      [big(32),big(16),big(8)],(xp,a,t2,t3,t4),"encode",22)
small=lambda h,p:V((h+2,NF,1024+2*p))
yts=[V((1024,32*NF)),V((1024,16*NF)),V((1024,8*NF)),V((1024,4*NF))]
def dec_fwd(dec,u4,u3,u2,b,upper_both,lower):
    count=lax.axis_size("rows"); half=count//2
    upper,rows=2*upper_both.shape[0],lower.shape[0]
    dma=pltpu.SemaphoreType.DMA
    return run(functools.partial(dec_fwd_kernel,count),
      (S((32,NF,384)),S((8,NF,1024)),S((16,NF,1024)),S((32,NF,1024)),S((upper//count,512)),S((rows//2,512))),
      [small(4,256),small(8,128),small(16,128),small(32,0),V((half-1,upper//count,512)),V((rows//2,512)),dma((2,half))],
      (dec,u4,u3,u2,b,upper_both,lower),"decode",24,ident=5)
def dec_bwd(hints,dec,p3,p2,p1,a,t2,t3,t4,upper_piece,lower_both):
    count=lax.axis_size("rows"); half=count//2
    upper,rows=count*upper_piece.shape[0],2*lower_both.shape[0]
    dma=pltpu.SemaphoreType.DMA
    return run(functools.partial(dec_bwd_kernel,count),
      (S((4,NF,1024)),S((2816,256)),S((upper//2,512)),S((rows//count,512))),
      [big(32),big(16),big(8),V((34,NF,384)),V((1024,32*NF)),V((half-1,rows//count,512)),dma((2,2*(half-1))),dma((1,))],
      (*hints,dec,p3,p2,p1,a,t2,t3,t4,upper_piece,lower_both),"decode_back",42,ident=6)


def rows_of(ref, index, size):
    return ref.at[pl.ds(pl.multiple_of(index * size, 16), size)]


class Place:
    def __init__(self, count):
        self.me, self.row = lax.axis_index("strip"), lax.axis_index("rows")
        self.half = count // 2
        self.near, self.far = lax.rem(self.row, 2), lax.div(self.row, 2)
        self.core, self.x = lax.rem(self.me, 2), lax.div(self.me, 2)
        self.near_device = (self.row + 1 - 2 * self.near, self.me)
        self.sibling = (self.row, self.me + 1 - 2 * self.core)
        self.partner = (self.row, lax.rem(self.me + 2, 4))
        self.others = [(self.row, lax.rem(self.me + k, 4)) for k in range(1, 4)]
        self.far_places = [lax.rem(self.far + k, self.half) for k in range(1, self.half)]
        self.far_devices = [(2 * place + self.near, self.me) for place in self.far_places]

    def greet(self, devices):
        barrier = pltpu.get_barrier_semaphore()
        for device in devices:
            pl.semaphore_signal(barrier, inc=1, device_id=device, device_id_type=MESH)
        pl.semaphore_wait(barrier, len(devices))


class Sems:
    def __init__(self, remote, local):
        self.remote, self.local, self.used, self.used_here = remote, local, 0, 0

    def copy(self, src, dst, device):
        one = pltpu.make_async_remote_copy(
            src_ref=src,
            dst_ref=dst,
            send_sem=self.remote.at[0, self.used],
            recv_sem=self.remote.at[1, self.used],
            device_id=device,
            device_id_type=MESH,
        )
        self.used = self.used + 1
        one.start()
        return one

    def here(self, src, dst):
        one = pltpu.make_async_copy(src, dst, self.local.at[self.used_here])
        self.used_here = self.used_here + 1
        one.start()
        return one


def near_start(place, sems, values, arrived):
    half = values.shape[0] // 2
    return sems.copy(rows_of(values, 1 - place.near, half), arrived, place.near_device)


def near_end(place, copy, values, arrived, both):
    copy.wait()
    half = values.shape[0] // 2
    total = rows_of(values, place.near, half)[...].astype(F32) + arrived[...].astype(F32)
    both[...] = total.astype(BF)


def far_start(place, sems, both, slots):
    each = slots.shape[1]
    return [
        sems.copy(rows_of(both, at, each), slots.at[k], device)
        for k, (at, device) in enumerate(zip(place.far_places, place.far_devices))
    ]


def far_end(place, copies, both, slots, piece):
    for one in copies:
        one.wait()
    total = rows_of(both, place.far, slots.shape[1])[...].astype(F32)
    for k in range(slots.shape[0]):
        total = total + slots[k].astype(F32)
    piece[...] = total.astype(BF)


def back_start(place, sems, piece, home):
    out = rows_of(home, place.far, piece.shape[0])
    return [sems.here(piece, out)] + [sems.copy(piece, out, d) for d in place.far_devices]


def last_start(place, sems, home, out):
    half = out.shape[0] // 2
    return sems.copy(home, rows_of(out, place.near, half), place.near_device)


def exchange_16():
    r = lax.broadcasted_iota(jnp.int32, (256, 256), 0)
    s = lax.broadcasted_iota(jnp.int32, (256, 256), 1)
    return (s == lax.rem(r, 16) * 16 + lax.div(r, 16)).astype(BF)


def first_frame(strip):
    return NF * ((strip % 2) * 2 + strip // 2)


def turned_rows(x, i):
    return jnp.concatenate([x[c, 2 * i + p] for p in range(2) for c in range(3)], axis=0).T


def canonical(w, swap, c, o, flipped):
    parts = {}
    for b in range(c // 16):
        block = jnp.dot(swap, w[256 * b : 256 * b + 256, :], preferred_element_type=F32).astype(BF)
        for k in range(16):
            parts[(15 - k if flipped else k, b)] = block[16 * k : 16 * k + 16]
    return [
        jnp.concatenate(
            [parts[(4 * kh + kw, b)] for kw in range(4) for b in range(c // 16)], axis=0
        )
        for kh in range(4)
    ]


def canonical_turned(w, swap):
    parts = {}
    for b in range(16):
        block = jnp.dot(swap, w[256 * b : 256 * b + 256, :], preferred_element_type=F32).astype(BF)
        for k in range(16):
            parts[(k, b)] = block[16 * k : 16 * k + 16]
    return [
        jnp.concatenate(
            [
                jnp.concatenate([parts[(4 * kh + kw, b)] for b in range(16)], axis=0)
                for kw in range(4)
            ],
            axis=1,
        )
        for kh in range(4)
    ]


def band(flat, a, c, o):
    def shifted(value, first):
        above = jnp.zeros((first, value.shape[1]), BF)
        below = jnp.zeros((512 - first - value.shape[0], value.shape[1]), BF)
        return jnp.concatenate([above, value, below], axis=0)

    if a == 1:
        return flat
    if a == 2:
        return jnp.concatenate([shifted(flat, 64), shifted(flat, 192)], axis=1)
    twice = jnp.concatenate([flat, flat], axis=1)
    left = lax.broadcasted_iota(jnp.int32, (512, 128), 1) < 64
    return jnp.concatenate(
        [
            jnp.where(left, shifted(twice, 96), shifted(twice, 160)),
            jnp.where(left, shifted(twice, 224), shifted(twice, 288)),
        ],
        axis=1,
    )


def put_bands(t_ref, u_ref, bands, turned, a):
    for kh in range(4):
        t = bands[kh]
        t_ref[512 * kh : 512 * kh + 512] = t
        tt = t.T if turned is None else turned[kh]
        z = jnp.zeros((256, 128), BF)
        left = jnp.concatenate([tt[:, 384:512], z], axis=1)
        right = jnp.concatenate([z, tt[:, :128]], axis=1)
        if a > 1:
            left, right = left[128:], right[:128]
        k = 512 if a > 1 else 768
        u_ref[1 - kh % 2, k * (kh // 2) : k * (kh // 2) + k] = jnp.concatenate(
            [left, tt[:, 128:384], right], axis=0
        )


def put_outer(a_ref, b_ref, w, flipped):
    row = lax.broadcasted_iota(jnp.int32, (64, 1024), 0)
    col = lax.div(lax.broadcasted_iota(jnp.int32, (64, 1024), 1), 32)
    tap = row - 2 * col + 1
    for kh in range(4):
        d, p = (kh + 1) // 2, (kh + 1) % 2
        for c in range(3):
            total = jnp.zeros((64, 1024), F32)
            for kw in range(4):
                k = 4 * kh + kw
                r = 16 * c + (15 - k if flipped else k)
                total = jnp.where(tap == kw, w[r : r + 1, :], total)
            first = 384 * d + 192 * p + 64 * c
            a_ref[first : first + 64] = total.astype(BF)
    a_ref[0:192] = jnp.zeros((192, 1024), BF)
    a_ref[960:1152] = jnp.zeros((192, 1024), BF)
    for d in range(3):
        b_ref[1024 * d : 1024 * d + 1024] = a_ref[384 * d : 384 * d + 384].T


def start_kernel(
    x, later, e1, e2, e3, e4, d1, d2, d3, d4, lh, dh, emb, qkv, proj, up, down,
    pixels, ea, eb, et2, et3, et4, eu2, eu3, eu4, da, db, dt2, dt3, dt4, du2, du3, du4,
    lh0, lh1, dh0, dh1, emb1, qkv1, proj1, up1, down1, t0, t1, t2, t3,
    stage, send_sem, recv_sem, side_sems,
    va, vb, vt2, vt3, vt4, vu2, vu3, vu4, wa, wb, wt2, wt3, wt4, wu2, wu3, wu4,
    vl, vd, out_sems,
):
    me = lax.axis_index("strip")
    row = lax.axis_index("rows")
    sibling = (row, me + 1 - 2 * lax.rem(me, 2))
    pixels[0] = jnp.zeros((NF, 384), BF)
    pixels[33] = jnp.zeros((NF, 384), BF)

    def turn_rows(i, carry):
        flat = turned_rows(x, i)
        for k in range(4):
            stage[k, i] = flat[first_frame(k) : first_frame(k) + NF]
        return carry

    lax.fori_loop(0, 8, turn_rows, 0)
    barrier = pltpu.get_barrier_semaphore()
    for k in range(1, 4):
        pl.semaphore_signal(
            barrier, inc=1, device_id=(row, lax.rem(me + k, 4)), device_id_type=MESH
        )
    pl.semaphore_wait(barrier, 3)
    copies = []
    for k in range(1, 4):
        to = lax.rem(me + k, 4)
        copies.append(
            pltpu.make_async_remote_copy(
                src_ref=stage.at[to],
                dst_ref=pixels.at[pl.ds(1 + 8 * me, 8)],
                send_sem=send_sem.at[k - 1],
                recv_sem=recv_sem.at[k - 1],
                device_id=(row, to),
                device_id_type=MESH,
            )
        )
    for copy in copies:
        copy.start()

    def to_sibling(src, dst, index):
        copy = pltpu.make_async_remote_copy(
            src_ref=src,
            dst_ref=dst,
            send_sem=side_sems.at[0, index],
            recv_sem=side_sems.at[1, index],
            device_id=sibling,
            device_id_type=MESH,
        )
        copy.start()
        copies.append(copy)

    for index, (src, dst) in enumerate(
        ((emb, emb1), (qkv, qkv1), (proj, proj1), (up, up1), (down, down1))
    ):
        to_sibling(src, dst, index)
    pixels[pl.ds(1 + 8 * me, 8)] = stage[me]

    turn_kernel(later, t0, t1, t2, t3)
    stores = []

    def store(src, dst):
        copy = pltpu.make_async_copy(src, dst, out_sems.at[len(stores)])
        copy.start()
        stores.append(copy)

    swap = exchange_16()
    put_outer(va, vb, e1, False)
    store(va, ea)
    store(vb, eb)
    put_bands(vt2, vu2, [band(f, 4, 32, 64) for f in canonical(e2, swap, 32, 64, False)], None, 4)
    store(vt2, et2)
    store(vu2, eu2)
    put_bands(vt3, vu3, [band(f, 2, 64, 128) for f in canonical(e3, swap, 64, 128, False)], None, 2)
    store(vt3, et3)
    store(vu3, eu3)
    turned = canonical_turned(e4, swap)
    put_bands(vt4, vu4, [f.T for f in turned], turned, 1)
    store(vt4, et4)
    store(vu4, eu4)
    for b in range(16):
        rows = slice(256 * b, 256 * b + 256)
        for src, dst in ((lh[rows, :], vl), (dh[:, rows].T, vd)):
            block = jnp.dot(swap, src, preferred_element_type=F32).astype(BF)
            for k in range(16):
                dst[256 * k + 16 * b : 256 * k + 16 * b + 16] = block[16 * k : 16 * k + 16]
    store(vl, lh0)
    store(vd, dh0)
    to_sibling(vl, lh1, 5)
    to_sibling(vd, dh1, 6)
    put_outer(wa, wb, d4, True)
    store(wa, da)
    store(wb, db)
    put_bands(wt2, wu2, [band(f, 4, 32, 64) for f in canonical(d3, swap, 32, 64, True)], None, 4)
    store(wt2, dt2)
    store(wu2, du2)
    put_bands(wt3, wu3, [band(f, 2, 64, 128) for f in canonical(d2, swap, 64, 128, True)], None, 2)
    store(wt3, dt3)
    store(wu3, du3)
    put_bands(wt4, wu4, canonical(d1, swap, 128, 256, True), None, 1)
    store(wt4, dt4)
    store(wu4, du4)
    for copy in copies:
        copy.wait()
    for copy in stores:
        copy.wait()


def start(frames, later, kernels, latent_head, decode_head, others):
    e1, e2, e3, e4, d1, d2, d3, d4 = kernels
    rows_in = [
        jnp.tile(jnp.transpose(e1, (1, 2, 3, 0)).reshape(48, 32), (1, 32)).astype(F32),
        jnp.transpose(e2, (1, 2, 3, 0)).reshape(512, 64),
        jnp.transpose(e3, (1, 2, 3, 0)).reshape(1024, 128),
        jnp.transpose(e4, (0, 2, 3, 1)).reshape(4096, 128),
        jnp.transpose(d1, (0, 2, 3, 1)).reshape(2048, 256),
        jnp.transpose(d2, (0, 2, 3, 1)).reshape(1024, 128),
        jnp.transpose(d3, (0, 2, 3, 1)).reshape(512, 64),
        jnp.tile(jnp.transpose(d4, (0, 2, 3, 1)).reshape(48, 32), (1, 32)).astype(F32),
    ]
    dma = pltpu.SemaphoreType.DMA
    any_spec = pl.BlockSpec(memory_space=pl.ANY)
    built = [(1152, 1024), (3072, 384)] + [(2048, 256)] * 3
    built = built + [(2, 1024, 256), (2, 1024, 256), (2, 1536, 256)]
    heads = [(4096, 256)] * 4
    shapes = [(34, NF, 384)] + built * 2 + heads + [w.shape for w in others]
    shapes = shapes + [(8, NF, 384)] * 4
    out = pl.pallas_call(
        start_kernel,
        out_shape=tuple(S(shape) for shape in shapes),
        in_specs=VM(12) + [any_spec] * len(others),
        out_specs=tuple(VM(1) + [any_spec] * (len(shapes) - 5) + VM(4)),
        scratch_shapes=[
            V((4, 8, NF, 384)),
            dma((3,)),
            dma((3,)),
            dma((2, 7)),
            *[V(shape) for shape in built * 2],
            V((4096, 256)),
            V((4096, 256)),
            dma((18,)),
        ],
        compiler_params=pltpu.CompilerParams(
            collective_id=1, has_side_effects=True, vmem_limit_bytes=56 * MIB
        ),
        cost_estimate=estimate(26),
        name="start",
    )(
        jnp.transpose(frames, (1, 2, 3, 0)),
        jnp.transpose(later, (1, 2, 3, 0)),
        *rows_in,
        latent_head,
        decode_head,
        *others,
    )
    hints = around(out[-4:])
    return out[0], out[1:9], out[9:17], out[17:19], out[19:21], out[21:-4], hints


def turn_kernel(x, *out):
    me = lax.axis_index("strip")

    def turn_rows(i, carry):
        flat = turned_rows(x, i)
        for k in range(4):
            part = flat[first_frame(k) : first_frame(k) + NF]
            for step in range(4):

                @pl.when(lax.rem(me + step, 4) == k)
                def _():
                    out[step][i] = part

        return carry

    lax.fori_loop(0, 8, turn_rows, 0)


def around(parts):
    return [parts[0]] + [
        lax.ppermute(parts[k], "strip", [(s, (s + k) % 4) for s in range(4)]) for k in range(1, 4)
    ]


def turned_back(got, out):
    def turn_rows(i, carry):
        block = jnp.concatenate([got[(b % 2) * 2 + b // 2, i] for b in range(4)], axis=0)
        flat = block.T.astype(out.dtype)
        for p in range(2):
            for c in range(3):
                first = 64 * (3 * p + c)
                out[c, 2 * i + p] = flat[first : first + 64]
        return carry

    lax.fori_loop(0, 8, turn_rows, 0)


def turn_back_kernel(c0, c1, c2, c3, out, got):
    me = lax.axis_index("strip")
    for k, part in enumerate((c0, c1, c2, c3)):
        got[lax.rem(me + 4 - k, 4)] = part[...]
    turned_back(got, out)


def blocks_around(pairs, strip):
    return around([lax.dynamic_slice_in_dim(pairs, 8 * ((strip + k) % 4), 8) for k in range(4)])


def frames_out_later(parts):
    flat = pl.pallas_call(
        turn_back_kernel,
        out_shape=S((3, 16, 64, 256)),
        in_specs=VM(4),
        out_specs=VM(1)[0],
        scratch_shapes=[V((4, 8, NF, 384))],
        compiler_params=pltpu.CompilerParams(vmem_limit_bytes=32 * MIB),
        cost_estimate=estimate(2),
        name="turn_back",
    )(*parts)
    return jnp.transpose(flat, (3, 0, 1, 2))


def dot(a, b):
    return jnp.dot(a, b, preferred_element_type=F32)


def dot_nt(a, b):
    return lax.dot_general(a, b, (((1,), (1,)), ((), ())), preferred_element_type=F32)


def over_groups(values, join):
    lanes = values.shape[1]
    lane = lax.broadcasted_iota(jnp.int32, values.shape, 1)
    for step in (1, 2, 4, 8, 16):
        upper = lax.rem(lax.div(lane, step), 2) == 1
        other = jnp.where(
            upper, pltpu.roll(values, step, 1), pltpu.roll(values, lanes - step, 1)
        )
        values = join(values, other)
    return values


def unit_of(hidden):
    centred = hidden - jnp.mean(hidden, -1, keepdims=True)
    scale_inv = lax.rsqrt(jnp.mean(centred * centred, -1, keepdims=True) + EPS)
    return centred * scale_inv, scale_inv


def unit_back(grad_normed, unit_rows, scale_inv, gain):
    grad_unit = grad_normed * gain
    grad_gain = jnp.sum(grad_normed * unit_rows, 0, keepdims=True)
    grad_rows = scale_inv * (
        grad_unit
        - jnp.mean(grad_unit, -1, keepdims=True)
        - unit_rows * jnp.mean(grad_unit * unit_rows, -1, keepdims=True)
    )
    return grad_gain, grad_rows


LAYER_ROWS = 1536


def token_rows(layers, count):
    upper = max(layers - 1, 1) * LAYER_ROWS
    lower = LAYER_ROWS + 256 + NF + 16
    return share_rows(upper, count), share_rows(lower, count)


def middle_kernel(
    layers, count,
    feat, lh0, lh1, dh0, dh1, emb0, emb1, pos, gains, allow, cot,
    qkv0, qkv1, proj0, proj1, up0, up1, down0, down1,
    tokens, latent_out, chances_out, decoded, upper_both, lower, grad_latent, feat_got,
    feat_sems, keep, send, sent, spread_sems, parts, gots, pair_sems,
    upper, upper_other, upper_got, lower_other, lower_got, upper_near, fold_sems, near_sems, unit_a, unit_f, normed_a, normed_f, mixed, weights,
    attended, before, inner, gain_rows,
):
    strip = lax.axis_index("strip")
    row = lax.axis_index("rows")
    place_here = Place(count)
    partner, sibling = place_here.partner, place_here.sibling
    place_here.greet([partner, sibling, place_here.near_device])

    def copy(src, dst, sems, index, device):
        return pltpu.make_async_remote_copy(
            src_ref=src,
            dst_ref=dst,
            send_sem=sems.at[0, index],
            recv_sem=sems.at[1, index],
            device_id=device,
            device_id_type=MESH,
        )

    feat_copy = copy(feat, feat_got, feat_sems, 0, partner)
    feat_copy.start()

    def total_start(index, value):
        parts[index] = value.astype(BF)
        one = copy(parts.at[index], gots.at[index], pair_sems, index, partner)
        one.start()
        return one

    def total_wait(index, one):
        one.wait()
        got = jnp.concatenate([gots[index, NF:], gots[index, :NF]], axis=0)
        return parts[index].astype(F32) + got.astype(F32)

    def logits_of(maps):
        halves = []
        for weight in (lh0, lh1):
            total = jnp.zeros((NF, 256), F32)
            for h in range(4):
                total = total + dot(maps[h], weight[1024 * h : 1024 * h + 1024])
            halves.append(total)
        return jnp.concatenate(halves, axis=1)

    mine = logits_of(feat)
    feat_copy.wait()
    logits = jnp.concatenate([mine, logits_of(feat_got)], axis=0)
    raised = jnp.exp(logits - over_groups(logits, jnp.maximum))
    chances = raised / over_groups(raised, jnp.add)
    latent = chances.astype(BF)
    chances_out[...] = chances
    latent_out[...] = latent

    waiting = total_start(0, dot(latent[:, :256], emb0[...]) + dot(latent[:, 256:], emb1[...]))
    for hw in range(16):
        lanes = slice(256 * (hw % 4), 256 * (hw % 4) + 256)
        rows = slice(256 * hw, 256 * hw + 256)
        value = dot_nt(latent[:, :256], dh0[rows]) + dot_nt(latent[:, 256:], dh1[rows])
        value = value.astype(BF)
        keep[hw // 4, :, lanes] = value[:NF]
        send[hw // 4, :, lanes] = value[NF:]
    spread_copy = copy(send, sent, spread_sems, 0, partner)
    spread_copy.start()
    embedded = total_wait(0, waiting)
    place = pos[...].astype(F32)
    hidden = embedded + jnp.concatenate([place, place], axis=0)
    head_lane = lax.div(lax.broadcasted_iota(jnp.int32, (2 * NF, 128), 1), HEAD_DIM)
    allowed = allow[...] > 0.5

    def of_head(value, h):
        return jnp.where(head_lane == h % 2, value, jnp.zeros_like(value))

    def pair_lanes(h):
        return slice(128 * (h // 2), 128 * (h // 2) + 128)

    for k in range(layers):
        unit, inv = unit_of(hidden)
        unit_a[k] = jnp.concatenate([unit, jnp.broadcast_to(inv, (2 * NF, 128))], axis=1)
        normed = (unit * gains[2 * k : 2 * k + 1]).astype(BF)
        normed_a[k] = normed
        for part in range(3):
            mixed[k, part] = jnp.concatenate(
                [dot(normed, qkv0[k, part]), dot(normed, qkv1[k, part])], axis=1
            ).astype(BF)
        for p in range(2):
            both = jnp.zeros((2 * NF, 128), F32)
            for h in (2 * p, 2 * p + 1):
                lanes = pair_lanes(h)
                scores = SCALE * dot_nt(of_head(mixed[k, 0, :, lanes], h), mixed[k, 1, :, lanes])
                scores = jnp.where(allowed, scores, NEG)
                lifted = jnp.exp(scores - jnp.max(scores, -1, keepdims=True))
                weight = lifted / jnp.sum(lifted, -1, keepdims=True)
                weights[k, h] = weight
                both = both + of_head(dot(weight.astype(BF), mixed[k, 2, :, lanes]), h)
            attended[k, :, 128 * p : 128 * p + 128] = both.astype(BF)
        partial = dot(attended[k, :, :128], proj0[k]) + dot(attended[k, :, 128:], proj1[k])
        middle = hidden + total_wait(2 * k + 1, total_start(2 * k + 1, partial))
        unit, inv = unit_of(middle)
        unit_f[k] = jnp.concatenate([unit, jnp.broadcast_to(inv, (2 * NF, 128))], axis=1)
        normed = (unit * gains[2 * k + 1 : 2 * k + 2]).astype(BF)
        normed_f[k] = normed
        partial = jnp.zeros((2 * NF, 512), F32)
        for side, (up, down) in enumerate(((up0, down0), (up1, down1))):
            value = dot(normed, up[k])
            before[k, :, 512 * side : 512 * side + 512] = value
            act = (value * sig(value)).astype(BF)
            inner[k, :, 512 * side : 512 * side + 512] = act
            partial = partial + dot(act, down[k])
        hidden = middle + total_wait(2 * k + 2, total_start(2 * k + 2, partial))
    tokens[...] = hidden.astype(BF)

    spread_copy.wait()
    decoded[...] = (keep[...].astype(F32) + sent[...].astype(F32)).astype(BF)

    def fold_start(index, part, got):
        one = copy(part, got, fold_sems, index, sibling)
        one.start()
        return one

    def fold_end(one, own, got, count):
        one.wait()
        for first in range(0, count, 128):
            rows = slice(first, min(first + 128, count))
            own[rows] = (own[rows].astype(F32) + got[rows].astype(F32)).astype(BF)
        if own.shape[0] > count:
            own[count:] = jnp.zeros((own.shape[0] - count, 512), BF)

    lower_rows = LAYER_ROWS + 256 + NF + 16

    grad = cot[...].astype(F32)
    for k in reversed(range(layers)):
        flat, other = (upper, upper_other) if k else (lower, lower_other)
        base = LAYER_ROWS * (k - 1) if k else 0
        index = 2 * layers + 1 + 2 * (layers - 1 - k)
        low = grad.astype(BF)
        partial = jnp.zeros((2 * NF, 512), F32)
        grads = []
        for side, (up, down) in enumerate(((up0, down0), (up1, down1))):
            value = before[k, :, 512 * side : 512 * side + 512]
            squash = sig(value)
            slope = squash * (1.0 + value * (1.0 - squash))
            grad_before = (dot_nt(low, down[k]) * slope).astype(BF)
            grads.append(grad_before)
            partial = partial + dot_nt(grad_before, up[k])
        waiting = total_start(index, partial)
        turned = normed_f[k].T
        for side, dst in enumerate((flat, other)):
            act = inner[k, :, 512 * side : 512 * side + 512]
            dst[base : base + 512] = dot(act.T, low).astype(BF)
            dst[base + 512 : base + 1024] = dot(turned, grads[side]).astype(BF)
        if k == 0:
            fold_end(upper_fold, upper, upper_got, LAYER_ROWS * (layers - 1))
            near_copy = near_start(place_here, Sems(near_sems, None), upper, upper_near)
        grad_normed = total_wait(index, waiting)
        gain_f, grad_rows = unit_back(
            grad_normed, unit_f[k, :, :512], unit_f[k, :, 512:513], gains[2 * k + 1 : 2 * k + 2]
        )
        grad = grad + grad_rows
        low = grad.astype(BF)
        grad_mixed = [[], [], []]
        for p, proj in enumerate((proj0, proj1)):
            lanes = pair_lanes(2 * p)
            grad_pair = dot_nt(low, proj[k]).astype(BF)
            queries, keys, vals = mixed[k, 0, :, lanes], mixed[k, 1, :, lanes], mixed[k, 2, :, lanes]
            g_queries = jnp.zeros((2 * NF, 128), F32)
            g_keys, g_vals = g_queries, g_queries
            for h in (2 * p, 2 * p + 1):
                weight = weights[k, h]
                grad_head = of_head(grad_pair, h)
                g_vals = g_vals + dot(weight.astype(BF).T, grad_head)
                grad_weight = dot_nt(grad_head, vals)
                along = jnp.sum(weight * grad_weight, -1, keepdims=True)
                grad_scores = (weight * (grad_weight - along)).astype(BF)
                g_queries = g_queries + of_head(dot(grad_scores, keys), h)
                g_keys = g_keys + dot(grad_scores.T, of_head(queries, h))
            grad_mixed[0].append((SCALE * g_queries).astype(BF))
            grad_mixed[1].append((SCALE * g_keys).astype(BF))
            grad_mixed[2].append(g_vals.astype(BF))
        partial = jnp.zeros((2 * NF, 512), F32)
        for part in range(3):
            for side, qkv in enumerate((qkv0, qkv1)):
                partial = partial + dot_nt(grad_mixed[part][side], qkv[k, part])
        waiting = total_start(index + 1, partial)
        turned = normed_a[k].T
        for side, dst in enumerate((flat, other)):
            act = attended[k, :, 128 * side : 128 * side + 128]
            dst[base + 1024 : base + 1152] = dot(act.T, low).astype(BF)
            for part in range(3):
                value = dot(turned, grad_mixed[part][side]).astype(BF)
                first = base + 1152 + 128 * part
                for b in range(4):
                    dst[first : first + 128, 128 * b : 128 * b + 128] = value[
                        128 * b : 128 * b + 128
                    ]
        if k == 1:
            upper_fold = fold_start(0, upper_other, upper_got)
        grad_normed = total_wait(index + 1, waiting)
        gain_a, grad_rows = unit_back(
            grad_normed, unit_a[k, :, :512], unit_a[k, :, 512:513], gains[2 * k : 2 * k + 1]
        )
        grad = grad + grad_rows
        gain_rows[2 * k : 2 * k + 1] = gain_a
        gain_rows[2 * k + 1 : 2 * k + 2] = gain_f

    low = grad.astype(BF)
    own_latent, other_latent = latent_out[:, :256], latent_out[:, 256:]
    lower[LAYER_ROWS : LAYER_ROWS + 256] = dot(own_latent.T, low).astype(BF)
    lower_other[LAYER_ROWS : LAYER_ROWS + 256] = dot(other_latent.T, low).astype(BF)
    rest = jnp.concatenate(
        [
            grad[:NF] + grad[NF:],
            gain_rows[...],
            jnp.zeros((16 - 2 * layers, 512), F32),
        ],
        axis=0,
    ).astype(BF)
    lower[LAYER_ROWS + 256 : lower_rows] = rest
    lower_other[LAYER_ROWS + 256 : lower_rows] = rest
    lower_fold = fold_start(1, lower_other, lower_got)
    grad_latent[:, :256] = dot_nt(low, emb0[...])
    grad_latent[:, 256:] = dot_nt(low, emb1[...])
    near_end(place_here, near_copy, upper, upper_near, upper_both)
    fold_end(lower_fold, lower, lower_got, lower_rows)


def middle(layers, *args):
    count = lax.axis_size("rows")
    upper, lower = token_rows(layers, count)
    dma = pltpu.SemaphoreType.DMA
    sums = 4 * layers + 1
    t = 2 * NF
    return pl.pallas_call(
        functools.partial(middle_kernel, layers, count),
        out_shape=(
            S((t, 512)),
            S((t, 512)),
            S((t, 512), F32),
            S((4, NF, 1024)),
            S((upper // 2, 512)),
            S((lower, 512)),
            S((t, 512), F32),
            S((4, NF, 1024)),
        ),
        in_specs=VM(len(args)),
        out_specs=tuple(VM(8)),
        scratch_shapes=[
            dma((2, 1)),
            V((4, NF, 1024)),
            V((4, NF, 1024)),
            V((4, NF, 1024)),
            dma((2, 1)),
            V((sums, t, 512)),
            V((sums, t, 512)),
            dma((2, sums)),
            V((upper, 512)),
            V((upper, 512)),
            V((upper, 512)),
            V((lower, 512)),
            V((lower, 512)),
            V((upper // 2, 512)),
            dma((2, 2)),
            dma((2, 1)),
            V((layers, t, 640), F32),
            V((layers, t, 640), F32),
            V((layers, t, 512)),
            V((layers, t, 512)),
            V((layers, 3, t, 256)),
            V((layers, 4, t, t), F32),
            V((layers, t, 256)),
            V((layers, t, 1024), F32),
            V((layers, t, 1024)),
            V((2 * layers, 512), F32),
        ],
        compiler_params=pltpu.CompilerParams(
            collective_id=3, has_side_effects=True, vmem_limit_bytes=56 * MIB
        ),
        cost_estimate=estimate(84),
        name="middle",
    )(*args)


def back_kernel(
    count, grad, latent, chances, grad_embed, feat0, feat1, lh0, lh1, dh0, dh1, flat, upper_half, lower_piece,
    grad_feat, in_rows, share, d_both, upper_total, lower_half,
    side_got, side_sum, cross_got, side_sems, got, got_sems, keep, send, sent, sent_sems,
    own, other, other_got, fold_sems, values, from_near, remote, here,
):
    place = Place(count)
    near, core, x = place.near, place.core, place.x
    partner, sibling = place.partner, place.sibling
    place.greet([partner, sibling, place.near_device] + place.far_devices)
    sems = Sems(remote, here)

    def copy(src, dst, pair, index, device):
        one = pltpu.make_async_remote_copy(
            src_ref=src,
            dst_ref=dst,
            send_sem=pair.at[(0,) + index],
            recv_sem=pair.at[(1,) + index],
            device_id=device,
            device_id_type=MESH,
        )
        one.start()
        return one

    grad_copy = copy(grad, got, got_sems, (0,), partner)
    upper_own = sems.here(upper_half, rows_of(upper_total, near, upper_half.shape[0]))
    upper_last = last_start(place, sems, upper_half, upper_total)
    lower_back = back_start(place, sems, lower_piece, lower_half)
    side_copy = copy(flat.at[1 - core], side_got, side_sems, (0,), sibling)

    def through(maps):
        halves = []
        for weight in (dh0, dh1):
            total = jnp.zeros((NF, 256), F32)
            for h in range(4):
                total = total + dot(maps[h], weight[1024 * h : 1024 * h + 1024])
            halves.append(total)
        return jnp.concatenate(halves, axis=1)

    def head_grad(slot, first, second, rhs):
        for h in range(4):
            for w in range(4):
                lanes = slice(256 * w, 256 * w + 256)
                rows = slice(1024 * h + 256 * w, 1024 * h + 256 * w + 256)
                maps = jnp.concatenate([first[h, :, lanes], second[h, :, lanes]], axis=0)
                value = dot(maps.T, rhs).astype(BF)
                own[slot, rows] = value[:, :256]
                other[slot, rows] = value[:, 256:]
        return copy(other.at[slot], other_got.at[slot], fold_sems, (slot,), sibling)

    swap = exchange_16()

    def folded(slot, b):
        parts = []
        for k in range(16):
            rows = slice(256 * k + 16 * b, 256 * k + 16 * b + 16)
            value = own[slot, rows].astype(F32) + other_got[slot, rows].astype(F32)
            parts.append(value.astype(BF))
        return dot(swap, jnp.concatenate(parts, axis=0)).astype(BF)

    mine = through(grad)
    side_copy.wait()
    side_sum[...] = (flat[core].astype(F32) + side_got[...].astype(F32)).astype(BF)
    cross_copy = copy(side_sum.at[1 - x], cross_got, side_sems, (1,), partner)
    grad_copy.wait()
    out_fold = head_grad(0, grad, got, latent[...])
    grad_latent = grad_embed[...] + jnp.concatenate([mine, through(got)], axis=0)
    probs = chances[...]
    along = over_groups(probs * grad_latent, jnp.add)
    grad_logits = (probs * (grad_latent - along)).astype(BF)
    sends = []
    for h in range(4):
        for w in range(4):
            lanes = slice(256 * w, 256 * w + 256)
            rows = slice(1024 * h + 256 * w, 1024 * h + 256 * w + 256)
            value = dot_nt(grad_logits[:, :256], lh0[rows]) + dot_nt(grad_logits[:, 256:], lh1[rows])
            value = value.astype(BF)
            keep[h, :, lanes] = value[:NF]
            send[h, :, lanes] = value[NF:]
        sends.append(copy(send.at[h], sent.at[h], sent_sems, (h,), partner))
    out_fold.wait()
    for b in range(16):
        values[256 * b : 256 * b + 256] = folded(0, b).T
    near_copy = near_start(place, sems, values, from_near)
    in_fold = head_grad(1, feat0, feat1, grad_logits)
    cross_copy.wait()
    share[...] = (side_sum[x].astype(F32) + cross_got[...].astype(F32)).astype(BF)
    for one in sends:
        one.wait()
    grad_feat[...] = (keep[...].astype(F32) + sent[...].astype(F32)).astype(BF)
    in_fold.wait()
    for b in range(16):
        in_rows[256 * b : 256 * b + 256] = folded(1, b)
    near_end(place, near_copy, values, from_near, d_both)
    upper_own.wait()
    upper_last.wait()
    for one in lower_back:
        one.wait()


def latents_back(*args):
    dma = pltpu.SemaphoreType.DMA
    count = lax.axis_size("rows")
    half = count // 2
    flat, upper_half, lower_piece = args[-3:]
    quarter = flat.shape[0] // 4
    args = args[:-3] + (flat.reshape(2, 2, quarter, 256), upper_half, lower_piece)
    maps = (4, NF, 1024)
    rows = (4096, 256)
    return pl.pallas_call(
        functools.partial(back_kernel, count),
        out_shape=(
            S(maps),
            S(rows),
            S((quarter, 256)),
            S((2048, 256)),
            S((2 * upper_half.shape[0], 512)),
            S((half * lower_piece.shape[0], 512)),
        ),
        in_specs=VM(len(args)),
        out_specs=tuple(VM(4) + [pl.BlockSpec(memory_space=pl.ANY)] + VM(1)),
        scratch_shapes=[
            V((2, quarter, 256)),
            V((2, quarter, 256)),
            V((quarter, 256)),
            dma((2, 2)),
            V(maps),
            dma((2, 1)),
            V(maps),
            V(maps),
            V(maps),
            dma((2, 4)),
            V((2,) + rows),
            V((2,) + rows),
            V((2,) + rows),
            dma((2, 2)),
            V(rows),
            V((2048, 256)),
            dma((2, half + 1)),
            dma((2,)),
        ],
        compiler_params=pltpu.CompilerParams(
            collective_id=4, has_side_effects=True, vmem_limit_bytes=58 * MIB
        ),
        cost_estimate=estimate(50),
        name="latents_back",
    )(*args)


def strip_fold_start(place, sems, flat, first, size, got):
    half = size // 2
    return sems.copy(
        flat.at[pl.ds(pl.multiple_of(first + (1 - place.core) * half, 16), half)], got, place.sibling
    )


def strip_cross_start(place, sems, copy, flat, first, size, got, both, cross):
    copy.wait()
    half = size // 2
    own = flat[pl.ds(pl.multiple_of(first + place.core * half, 16), half)]
    both[...] = (own.astype(F32) + got[...].astype(F32)).astype(BF)
    return sems.copy(rows_of(both, 1 - place.x, half // 2), cross, place.partner)


def strip_share(place, copy, both, cross):
    copy.wait()
    own = rows_of(both, place.x, cross.shape[0])[...]
    return (own.astype(F32) + cross[...].astype(F32)).astype(BF)


def padded_share(ref, parts):
    share = jnp.concatenate(parts, axis=0)
    spare = ref.shape[0] - share.shape[0]
    if spare:
        share = jnp.concatenate([share, jnp.zeros((spare, 256), BF)], axis=0)
    ref[...] = share


def enc_bwd_kernel(
    count, xp, z1, z2, z3, z4, df, u2, u3, u4, b, dec, d_both, t_half, l_rows,
    d_total, l_total, t_total, early, late, grad_out,
    m1, m2, m3, s1, s2, s3, s4, yt, pk, dx, got, rows_out,
    d_slots, d_piece, l_near, l_both, l_slots, l_piece,
    e_fold, e_sum, e_cross, e_values, e_near, e_both, e_slots, e_piece,
    f_fold, f_sum, f_cross, f_values, f_near, f_both, f_slots, f_piece,
    remote, here,
):
    place = Place(count)
    near, core, x = place.near, place.core, place.x
    sems = Sems(remote, here)
    place.greet(place.others + [place.near_device] + place.far_devices)

    def home(ref):
        return rows_of(ref, near, ref.shape[0] // 2)

    def waits(copies):
        for one in copies:
            one.wait()

    d_far = far_start(place, sems, d_both, d_slots)
    l_copy = near_start(place, sems, l_rows, l_near)
    l_own = sems.here(rows_of(l_rows, near, l_rows.shape[0] // 2), l_both)
    t_own = sems.here(t_half, home(t_total))
    t_last = last_start(place, sems, t_half, t_total)

    zero_big(m1, 32)
    zero_big(m2, 16)
    zero_big(m3, 8)
    zero_small(s1, 32, 0)
    zero_small(s2, 16, 128)
    zero_small(s3, 8, 128)
    zero_small(s4, 4, 256)
    swap = exchange_16()
    z = z4[...].astype(F32)
    s = sig(z)
    s4[1:5, :, 256:1280] = (df[...].astype(F32) * (s * (1.0 + z * (1.0 - s)))).astype(BF)

    def back(z_ref, m, dst, pad):
        def emit(m0, odd, q, acc):
            for t in range(acc.shape[0]):
                h = 2 * (m0 + t) + odd
                zz = z_ref[h, :, 256 * q : 256 * q + 256].astype(F32)
                ss = sig(zz)
                mm = zz * ss
                dst[h + 1, :, pad + 256 * q : pad + 256 * q + 256] = (
                    acc[t] * (ss + mm * (1.0 - ss))
                ).astype(BF)
                m[m0 + t + odd, 1 - odd, :, 128 + 256 * q : 384 + 256 * q] = mm.astype(BF)

        return emit

    up(s4, u4, 4, 4, back(z3, m3, s3, 128))
    turn(s4, yt, 4, 256)
    pack(pk, 0, 1, 128, 256, grad_w(m3, yt, 4), False, swap, True)
    up(s3, u3, 8, 4, back(z2, m2, s2, 128))
    turn(s3, yt, 8, 128)
    pack(pk, 2048, 2, 64, 128, grad_w(m2, yt, 8), False, swap)
    e_copy = strip_fold_start(place, sems, pk, 0, 2560, e_fold)
    far_end(place, d_far, d_both, d_slots, d_piece)
    d_back = back_start(place, sems, d_piece, home(d_total))
    up(s2, u2, 16, 4, back(z1, m1, s1, 0))
    e_copy = strip_cross_start(place, sems, e_copy, pk, 0, 2560, e_fold, e_sum, e_cross)
    l_own.wait()
    l_copy.wait()
    l_both[...] = (l_both[...].astype(F32) + l_near[...].astype(F32)).astype(BF)
    l_far = far_start(place, sems, l_both, l_slots)

    def put(i0, acc):
        dx[pl.ds(i0, acc.shape[0])] = acc.astype(BF)

    outer_up(s1, b, put)
    padded_share(e_values, [dec[...], strip_share(place, e_copy, e_sum, e_cross)])
    e_copy = near_start(place, sems, e_values, e_near)
    strips = [
        sems.copy(dx.at[pl.ds(8 * device[1], 8)], got.at[place.me], device)
        for device in place.others
    ]
    got[place.me] = dx[pl.ds(8 * place.me, 8)]
    turn(s2, yt, 16, 128)
    pack(pk, 2560, 4, 32, 64, grad_w(m1, yt, 16), False, swap)
    waits(d_back)
    d_last = last_start(place, sems, home(d_total), d_total)
    near_end(place, e_copy, e_values, e_near, e_both)
    e_far = far_start(place, sems, e_both, e_slots)
    turn(s1, yt, 32, 0)
    pack_outer(pk, 2688, outer_grad(xp, yt), False)
    f_copy = strip_fold_start(place, sems, pk, 2560, 256, f_fold)
    f_copy = strip_cross_start(place, sems, f_copy, pk, 2560, 256, f_fold, f_sum, f_cross)
    padded_share(f_values, [strip_share(place, f_copy, f_sum, f_cross)])
    f_copy = near_start(place, sems, f_values, f_near)
    far_end(place, l_far, l_both, l_slots, l_piece)
    l_back = back_start(place, sems, l_piece, home(l_total))
    far_end(place, e_far, e_both, e_slots, e_piece)
    e_out = early.at[core, x]
    e_back = back_start(place, sems, e_piece, home(e_out))
    near_end(place, f_copy, f_values, f_near, f_both)
    f_far = far_start(place, sems, f_both, f_slots)
    far_end(place, f_far, f_both, f_slots, f_piece)
    f_out = late.at[core, x]
    f_back = back_start(place, sems, f_piece, home(f_out))
    waits(strips)
    stores = []
    for i in range(8):
        slot = i % 2
        if i > 1:
            stores[i - 2].wait()
        block = jnp.concatenate([got[(k % 2) * 2 + k // 2, i] for k in range(4)], axis=0)
        flat = block.T.astype(F32)
        for p in range(2):
            for c in range(3):
                rows_out[slot, c, p] = flat[64 * (3 * p + c) : 64 * (3 * p + c) + 64]
        stores.append(sems.here(rows_out.at[slot], grad_out.at[:, 2 * i : 2 * i + 2]))
    waits(stores[-2:])
    waits(e_back)
    e_last = last_start(place, sems, home(e_out), e_out)
    waits(f_back)
    f_last = last_start(place, sems, home(f_out), f_out)
    e_last.wait()
    e_cross_out = sems.copy(e_out, e_out, place.partner)
    f_last.wait()
    f_cross_out = sems.copy(f_out, f_out, place.partner)
    waits(l_back)
    l_last = last_start(place, sems, home(l_total), l_total)
    e_cross_out.wait()
    e_side = sems.copy(early.at[core], early.at[core], place.sibling)
    f_cross_out.wait()
    f_side = sems.copy(late.at[core], late.at[core], place.sibling)
    t_own.wait()
    waits([t_last, d_last, e_side, f_side, l_last])


def share_rows(rows, count):
    return rows + -rows % (16 * count)


def enc_bwd(maps, dec, d_both, t_half, l_rows):
    count = lax.axis_size("rows")
    half = count // 2
    dma = pltpu.SemaphoreType.DMA
    any_spec = pl.BlockSpec(memory_space=pl.ANY)
    head = l_rows.shape[0]
    quarter = dec.shape[0]
    early = share_rows(quarter + 640, count)
    late = share_rows(64, count)

    def steps(rows):
        return [
            V((rows, 256)),
            V((rows // 2, 256)),
            V((rows // 2, 256)),
            V((half - 1, rows // count, 256)),
            V((rows // count, 256)),
        ]

    d_total, l_total, t_total, e_out, f_out, grad_out = pl.pallas_call(
        functools.partial(enc_bwd_kernel, count),
        out_shape=(
            S((head, 256)),
            S((head, 256)),
            S((2 * t_half.shape[0], 512)),
            S((2, 2, early, 256)),
            S((2, 2, late, 256)),
            S((3, 16, 64, 256), F32),
        ),
        in_specs=VM(len(maps) + 2) + [any_spec] * 2,
        out_specs=tuple([any_spec] * 6),
        scratch_shapes=[
            big(32),
            big(16),
            big(8),
            small(32, 0),
            small(16, 128),
            small(8, 128),
            small(4, 256),
            V((1024, 32 * NF)),
            V((2816, 256)),
            V((32, NF, 384)),
            V((4, 8, NF, 384)),
            V((2, 3, 2, 64, 256), F32),
            *steps(head)[3:],
            *steps(head)[1:],
            V((1280, 256)),
            V((1280, 256)),
            V((640, 256)),
            *steps(early),
            V((128, 256)),
            V((128, 256)),
            V((64, 256)),
            *steps(late),
            dma((2, 8 * (half - 1) + 20)),
            dma((16,)),
        ],
        compiler_params=pltpu.CompilerParams(
            collective_id=2, has_side_effects=True, vmem_limit_bytes=60 * MIB
        ),
        cost_estimate=estimate(110),
        name="encode_back",
    )(*maps, dec, d_both, t_half, l_rows)
    enc = [e_out[:, :, quarter : quarter + 640], f_out[:, :, :64]]
    return (
        d_total,
        l_total,
        t_total,
        e_out[:, :, :quarter].reshape(-1, 256),
        jnp.concatenate([part.reshape(-1, 256) for part in enc], axis=0),
        jnp.transpose(grad_out, (3, 0, 1, 2)),
    )


def beside(value):
    return lax.ppermute(value, "strip", [(0, 1), (1, 0), (2, 3), (3, 2)])


def make_mask(segment_ids):
    places = jnp.arange(segment_ids.shape[1])
    causal = places[:, None] >= places[None, :]
    return causal[None] & (segment_ids[:, :, None] == segment_ids[:, None, :])


def unpack_kernels(flat):
    flat = flat.astype(F32)
    second = jnp.concatenate([flat[2048:2560, :128], flat[2048:2560, 128:]], axis=0)
    first = jnp.concatenate([flat[2560:2688, 64 * k : 64 * k + 64] for k in range(4)], axis=0)
    return (
        flat[2688:2736, :32].reshape(3, 4, 4, 32),
        first.reshape(32, 4, 4, 64),
        second.reshape(64, 4, 4, 128),
        flat[:2048],
    )


def shards(
    frames,
    segment_ids,
    encode_one,
    encode_two,
    encode_three,
    encode_four,
    latent_head,
    token_embed,
    positions,
    norm_gains,
    qkv_weight,
    out_weight,
    up_weight,
    down_weight,
    decode_head,
    decode_one,
    decode_two,
    decode_three,
    decode_four,
    token_cotangent,
    frame_cotangent,
):
    strip = lax.axis_index("strip")
    x, core = strip // 2, strip % 2
    layers = qkv_weight.shape[0]

    kernels = (
        encode_one,
        encode_two,
        encode_three,
        encode_four,
        decode_one,
        decode_two,
        decode_three,
        decode_four,
    )
    qkv = jnp.transpose(qkv_weight, (0, 2, 1, 3))
    shards_here = (token_embed, qkv, out_weight, up_weight, down_weight)
    pixels, enc_f, dec_f, head_in, head_out, theirs, hints = start(
        frames, frame_cotangent, kernels, latent_head, decode_head, shards_here
    )
    enc_a, enc_b, enc_t, enc_u = enc_f[0], enc_f[1], enc_f[2:5], enc_f[5:8]
    dec_a, dec_b, dec_t, dec_u = dec_f[0], dec_f[1], dec_f[2:5], dec_f[5:8]
    embed, qkv, project, widen, narrow = zip(shards_here, theirs)
    z1, z2, z3, z4, feat = enc_fwd(pixels, enc_a, *enc_t)

    first = 2 * core

    def mine(array, size):
        own = lax.dynamic_slice_in_dim(array, (first + x) * size, size)
        other = lax.dynamic_slice_in_dim(array, (first + 1 - x) * size, size)
        return jnp.concatenate([own, other], axis=0)

    allowed = make_mask(mine(segment_ids, 1)).astype(F32)
    blank = jnp.zeros((NF, NF), F32)
    allowed = jnp.concatenate(
        [
            jnp.concatenate([allowed[0], blank], axis=1),
            jnp.concatenate([blank, allowed[1]], axis=1),
        ],
        axis=0,
    )
    tokens, latent, chances, decoded, upper, lower, grad_latent, feat_got = middle(
        layers,
        feat,
        *head_in,
        *head_out,
        *embed,
        positions,
        norm_gains.reshape(2 * layers, -1),
        allowed,
        mine(token_cotangent, NF),
        *qkv,
        *project,
        *widen,
        *narrow,
    )
    tokens = jnp.where(
        x == 0, tokens, jnp.concatenate([tokens[NF:], tokens[:NF]], axis=0)
    )
    other_tokens = beside(tokens)
    tokens_out = jnp.where(
        core == 0,
        jnp.concatenate([tokens, other_tokens]),
        jnp.concatenate([other_tokens, tokens]),
    )

    recon_pairs, p3, p2, p1, upper, lower = dec_fwd(
        decoded, dec_u[2], dec_u[1], dec_u[0], dec_b, upper, lower
    )
    recon_parts = blocks_around(recon_pairs, strip)
    g_decoded, dec_flat, upper, lower = dec_bwd(
        hints, decoded, p3, p2, p1, dec_a, *dec_t, upper, lower
    )
    recon_parts, g_decoded = lax.optimization_barrier((recon_parts, g_decoded))
    recon = frames_out_later(recon_parts)
    g_feat, l_rows, dec_share, d_both, upper, lower = latents_back(
        g_decoded, latent, chances, grad_latent, feat, feat_got, *head_in, *head_out, dec_flat,
        upper, lower,
    )

    d_total, l_total, lower, dec_total, enc_total, frames_grad = enc_bwd(
        (pixels, z1, z2, z3, z4, g_feat, *enc_u, enc_b), dec_share, d_both, lower, l_rows
    )

    t_layers = jnp.concatenate([lower[:LAYER_ROWS], upper[: LAYER_ROWS * (layers - 1)]], axis=0)
    t_layers = t_layers.astype(F32).reshape(layers, LAYER_ROWS, 512)
    t_rest = lower[LAYER_ROWS:].astype(F32)
    r_qkv = t_layers[:, 1152:].reshape(layers, 3, 128, 4, 128).transpose(0, 3, 2, 1, 4)
    r_qkv = r_qkv.reshape(qkv_weight.shape)
    e_one, e_two, e_three, e_four = unpack_kernels(enc_total)
    d_four, d_three, d_two, d_one = unpack_kernels(dec_total)
    e_four = jnp.concatenate([e_four[:, :128], e_four[:, 128:]], axis=0)
    return (
        tokens_out,
        recon,
        frames_grad,
        e_one.transpose(3, 0, 1, 2),
        e_two.transpose(3, 0, 1, 2),
        e_three.transpose(3, 0, 1, 2),
        e_four.reshape(256, 4, 4, 128).transpose(0, 3, 1, 2),
        l_total.astype(F32),
        t_rest[:256],
        t_rest[256 : 256 + NF],
        t_rest[256 + NF : 256 + NF + 2 * layers].reshape(norm_gains.shape),
        r_qkv,
        t_layers[:, 1024:1152],
        t_layers[:, 512:1024],
        t_layers[:, :512],
        d_total.astype(F32).reshape(16, 256, 256).transpose(1, 0, 2).reshape(256, 4096),
        d_one.reshape(128, 4, 4, 256).transpose(0, 3, 1, 2),
        d_two.transpose(0, 3, 1, 2),
        d_three.transpose(0, 3, 1, 2),
        d_four.transpose(0, 3, 1, 2),
    )


def solution(mesh):
    placed = (
        P("rows", None, "strip", None),
        P("rows", None),
        P(),
        P(),
        P(),
        P(),
        P(None, "strip"),
        P("strip", None),
        P(),
        P(),
        P(None, None, None, "strip"),
        P(None, "strip", None),
        P(None, None, "strip"),
        P(None, "strip", None),
        P("strip", None),
        P(),
        P(),
        P(),
        P(),
        P("rows", None),
        P("rows", None, "strip", None),
    )
    return jax.shard_map(
        shards,
        mesh=mesh,
        in_specs=placed,
        out_specs=(
            P("rows", None),
            P("rows", None, "strip", None),
            P("rows", None, "strip", None),
            P(),
            P(),
            P(),
            P(),
            P(None, "strip"),
            P("strip", None),
            P(),
            P(),
            P(None, None, None, "strip"),
            P(None, "strip", None),
            P(None, None, "strip"),
            P(None, "strip", None),
            P("strip", None),
            P(),
            P(),
            P(),
            P(),
        ),
        check_vma=False,
    )
```

```python
import functools

import jax
import jax.numpy as jnp
from jax import lax
from jax.experimental import pallas as pl
from jax.experimental.pallas import tpu as pltpu
from jax.sharding import PartitionSpec as P

HEAD_DIM = 64
LCLASS = 32
EPS = 1e-05
SCALE = 0.125
NEG = -1e30
F32 = jnp.float32
BF = jnp.bfloat16
NF = 64
MIB = 1 << 20
MESH = pl.DeviceIdType.MESH


def sig(z): return 1.0/(1.0+jnp.exp(-z))

def zero_big(ref,rows):
    z=jnp.zeros((NF,1280),BF)
    ref[0,0]=z; ref[rows//2,1]=z
    e=jnp.zeros((rows//2+1,2,NF,128),BF)
    ref[:,:,:,0:128]=e; ref[:,:,:,1152:1280]=e

def zero_small(ref,rows,pad):
    z=jnp.zeros((NF,1024+2*pad),BF)
    ref[0]=z; ref[rows+1]=z
    if pad:
        e=jnp.zeros((rows+2,NF,pad),BF)
        ref[:,:,0:pad]=e; ref[:,:,1024+pad:]=e

def put_big(ref,half0,rows,q,val):
    v=val.reshape(rows,NF,256)
    for t in range(rows):
        ref[half0+(t+1)//2,(t+1)%2,:,128+256*q:384+256*q]=v[t]

def loop(n,body):
    if n==1: body(0)
    else:
        def step(g,c):
            body(g); return c
        lax.fori_loop(0,n,step,0)

def down(src,t_ref,rows,per,emit):
    def body(g):
        i0=g*per
        for q in range(4):
            lhs=jnp.concatenate([src[pl.ds(i0+kh//2,per),kh%2,:,256*q:256*q+512].reshape(per*NF,512) for kh in range(4)],axis=1)
            emit(i0,g*(per//2),q,jnp.dot(lhs,t_ref[...],preferred_element_type=F32))
    loop(rows//per,body)

def up(src,u_ref,rows,per,emit):
    k=u_ref.shape[1]//2
    def body(g):
        m0=g*per
        for q in range(4):
            for odd in range(2):
                lhs=jnp.concatenate([src[pl.ds(m0+1+odd-s,per),:,256*q:256*q+k].reshape(per*NF,k) for s in range(2)],axis=1)
                emit(m0,odd,q,jnp.dot(lhs,u_ref[odd],preferred_element_type=F32).reshape(per,NF,256))
    loop(rows//per,body)

def turn(src,dst,rows,pad):
    for q in range(4):
        dst[256*q:256*q+256,:rows*NF]=src[1:rows+1,:,pad+256*q:pad+256*q+256].reshape(rows*NF,256).T

def grad_w(big,yt,rows):
    out=[]
    for kh in range(4):
        acc=jnp.zeros((256,512),F32)
        for q in range(4):
            win=big[pl.ds(kh//2,rows),kh%2,:,256*q:256*q+512].reshape(rows*NF,512)
            acc=acc+jnp.dot(yt[256*q:256*q+256,:rows*NF],win,preferred_element_type=F32)
        out.append(acc)
    return out

def pack(pk,base,a,c,o,sums,flipped,swap,turned=False):
    taps=[]
    for acc in sums:
        total=None
        for j in range(a):
            first=(a+2*j-1)*c
            part=acc[j*o:j*o+o]
            if first: part=pltpu.roll(part,512-first,1)
            part=part[:,:4*c]
            total=part if total is None else total+part
        taps.append(total.astype(BF) if turned else total.T.astype(BF))
    width,count=(c,o//16) if turned else (o,c//16)
    held=[]
    for b in range(count):
        rows=[]
        for k in range(16):
            kh,kw=divmod(15-k if flipped else k,4)
            if turned: rows.append(taps[kh][16*b:16*b+16,c*kw:c*kw+c])
            else: rows.append(taps[kh][c*kw+16*b:c*kw+16*b+16])
        block=jnp.dot(swap,jnp.concatenate(rows,axis=0),preferred_element_type=F32).astype(BF)
        if width==256: pk[base+256*b:base+256*b+256]=block
        elif width==128:
            side,at=divmod(b,count//2)
            pk[base+256*at:base+256*at+256,128*side:128*side+128]=block
        else: held.extend([block[:128],block[128:]])
    if held: pk[base:base+128]=jnp.concatenate(held,axis=1)

def pack_outer(pk,base,red,flipped):
    r=lax.broadcasted_iota(jnp.int32,(48,1152),0); lane=lax.broadcasted_iota(jnp.int32,(48,1152),1)
    k=lax.rem(r,16)
    if flipped: k=15-k
    kh,kw=lax.div(k,4),lax.rem(k,4)
    at=384*lax.div(kh+1,2)+192*lax.rem(kh+1,2)+64*lax.div(r,16)+kw
    pick=(lane==at).astype(BF)
    value=jnp.concatenate([part.astype(BF) for part in red],axis=1)
    pk[base:base+128]=jnp.zeros((128,256),BF)
    pk[base:base+48,0:32]=lax.dot_general(pick,value,(((1,),(1,)),((),())),preferred_element_type=F32).astype(BF)

def outer_down(xp,a_ref,emit,per=4):
    def body(g):
        i0=g*per
        lhs=jnp.concatenate([xp[pl.ds(i0+d,per)].reshape(per*NF,384) for d in range(3)],axis=1)
        for q in range(4):
            emit(i0,g*(per//2),q,jnp.dot(lhs,a_ref[:,256*q:256*q+256],preferred_element_type=F32))
    loop(32//per,body)

def outer_up(yp,b_ref,emit,per=4):
    def body(g):
        i0=g*per
        lhs=jnp.concatenate([yp[pl.ds(i0+2-d,per)].reshape(per*NF,1024) for d in range(3)],axis=1)
        emit(i0,jnp.dot(lhs,b_ref[...],preferred_element_type=F32).reshape(per,NF,384))
    loop(32//per,body)

def outer_grad(xp,yt):
    red=[]
    lane=lax.broadcasted_iota(jnp.int32,(32,384),1)%64
    for d in range(3):
        x=xp[d:d+32].reshape(32*NF,384)
        tot=jnp.zeros((32,384),F32)
        for jb in range(4):
            g=jnp.dot(yt[256*jb:256*jb+256,:],x,preferred_element_type=F32)
            for jj in range(8):
                j=8*jb+jj
                v=pltpu.roll(g[32*jj:32*jj+32],(385-2*j)%384,1)
                if j==0: v=jnp.where(lane==0,0.0,v)
                if j==31: v=jnp.where(lane==3,0.0,v)
                tot=tot+v
        red.append(tot)
    return red

def enc_fwd_kernel(xp,a,t2,t3,t4,z1,z2,z3,z4,feat,m1,m2,m3):
    zero_big(m1,32); zero_big(m2,16); zero_big(m3,8)
    def keep(z,m):
        def emit(i0,half0,q,acc):
            rows=acc.shape[0]//NF
            z[pl.ds(i0,rows),:,256*q:256*q+256]=acc.astype(BF).reshape(rows,NF,256)
            val=(acc*sig(acc)).astype(BF)
            if m is None: feat[pl.ds(i0,rows),:,256*q:256*q+256]=val.reshape(rows,NF,256)
            else: put_big(m,half0,rows,q,val)
        return emit
    outer_down(xp,a,keep(z1,m1))
    down(m1,t2,16,4,keep(z2,m2))
    down(m2,t3,8,4,keep(z3,m3))
    down(m3,t4,4,4,keep(z4,None))

def dec_fwd_kernel(count,dec,u4,u3,u2,b,upper_both,lower,recon,p3,p2,p1,upper_piece,lower_both,
                   s4,s3,s2,s1,upper_slots,lower_near,remote):
    place=Place(count); sems=Sems(remote,None)
    place.greet([place.near_device]+place.far_devices)
    upper_far=far_start(place,sems,upper_both,upper_slots)
    lower_copy=near_start(place,sems,lower,lower_near)
    zero_small(s1,32,0); zero_small(s2,16,128); zero_small(s3,8,128); zero_small(s4,4,256)
    z=dec[...].astype(F32)
    s4[1:5,:,256:1280]=(z*sig(z)).astype(BF)
    def fwd(p,dst,pad):
        def emit(m0,odd,q,acc):
            for t in range(acc.shape[0]):
                h=2*(m0+t)+odd
                v=acc[t]
                p[h,:,256*q:256*q+256]=v.astype(BF)
                dst[h+1,:,pad+256*q:pad+256*q+256]=(v*sig(v)).astype(BF)
        return emit
    up(s4,u4,4,4,fwd(p3,s3,128))
    up(s3,u3,8,4,fwd(p2,s2,128))
    up(s2,u2,16,4,fwd(p1,s1,0))
    def put(i0,acc): recon[pl.ds(i0,acc.shape[0])]=acc.astype(BF)
    outer_up(s1,b,put)
    far_end(place,upper_far,upper_both,upper_slots,upper_piece)
    near_end(place,lower_copy,lower,lower_near,lower_both)

def dec_bwd_kernel(count,c0,c1,c2,c3,dec,p3,p2,p1,a,t2,t3,t4,upper_piece,lower_both,
                   gdec,pk,upper_half,lower_piece,d1,d2,d3,cp,yt,lower_slots,remote,here):
    place=Place(count); sems=Sems(remote,here); me=place.me
    place.greet(place.far_devices)
    upper_back=back_start(place,sems,upper_piece,upper_half)
    lower_far=far_start(place,sems,lower_both,lower_slots)
    cp[0]=jnp.zeros((NF,384),BF); cp[33]=jnp.zeros((NF,384),BF)
    for k,part in enumerate((c0,c1,c2,c3)):
        cp[pl.ds(1+8*lax.rem(me+4-k,4),8)]=part[...]
    zero_big(d1,32); zero_big(d2,16); zero_big(d3,8)
    def maps(p,rows,yt):
        for q in range(4):
            zz=p[:,:,256*q:256*q+256].reshape(rows*NF,256).astype(F32)
            yt[256*q:256*q+256,:rows*NF]=(zz*sig(zz)).astype(BF).T
    def back(p,dst):
        def emit(i0,half0,q,acc):
            rows=acc.shape[0]//NF
            zz=p[pl.ds(i0,rows),:,256*q:256*q+256].astype(F32).reshape(rows*NF,256)
            ss=sig(zz)
            val=(acc*(ss*(1.0+zz*(1.0-ss)))).astype(BF)
            if dst is None: gdec[pl.ds(i0,rows),:,256*q:256*q+256]=val.reshape(rows,NF,256)
            else: put_big(dst,half0,rows,q,val)
        return emit
    swap=exchange_16()
    maps(p1,32,yt); pack_outer(pk,2688,outer_grad(cp,yt),True)
    outer_down(cp,a,back(p1,d1))
    maps(p2,16,yt); pack(pk,2560,4,32,64,grad_w(d1,yt,16),True,swap)
    down(d1,t2,16,4,back(p2,d2))
    maps(p3,8,yt); pack(pk,2048,2,64,128,grad_w(d2,yt,8),True,swap)
    down(d2,t3,8,4,back(p3,d3))
    maps(dec,4,yt); pack(pk,0,1,128,256,grad_w(d3,yt,4),True,swap)
    down(d3,t4,4,4,back(dec,None))
    pk[2816-80:2816]=jnp.zeros((80,256),BF)
    far_end(place,lower_far,lower_both,lower_slots,lower_piece)
    for one in upper_back: one.wait()

def estimate(us):
    return pl.CostEstimate(flops=us*1150*10**6,bytes_accessed=MIB,transcendentals=0)

def S(shape,dt=BF): return jax.ShapeDtypeStruct(shape,dt)
def V(shape,dt=BF): return pltpu.VMEM(shape,dt)
VM=lambda n:[pl.BlockSpec(memory_space=pltpu.VMEM)]*n
def run(kernel,outs,scratch,args,name,us,lim=60,ident=None):
    extra={} if ident is None else dict(collective_id=ident,has_side_effects=True)
    return pl.pallas_call(kernel,out_shape=outs,in_specs=VM(len(args)),out_specs=tuple(VM(len(outs))),
        scratch_shapes=scratch,compiler_params=pltpu.CompilerParams(vmem_limit_bytes=lim*MIB,**extra),
        cost_estimate=estimate(us),name=name)(*args)
big=lambda h:V((h//2+1,2,NF,1280))
def enc_fwd(xp,a,t2,t3,t4):
    return run(enc_fwd_kernel,(S((32,NF,1024)),S((16,NF,1024)),S((8,NF,1024)),S((4,NF,1024)),S((4,NF,1024))),
      [big(32),big(16),big(8)],(xp,a,t2,t3,t4),"encode",22)
small=lambda h,p:V((h+2,NF,1024+2*p))
def enc_fwd(xp,a,t2,t3,t4):
    return run(enc_fwd_kernel,(S((32,NF,1024)),S((16,NF,1024)),S((8,NF,1024)),S((4,NF,1024)),S((4,NF,1024))),
      [big(32),big(16),big(8)],(xp,a,t2,t3,t4),"encode",22)
small=lambda h,p:V((h+2,NF,1024+2*p))
yts=[V((1024,32*NF)),V((1024,16*NF)),V((1024,8*NF)),V((1024,4*NF))]
def dec_fwd(dec,u4,u3,u2,b,upper_both,lower):
    count=lax.axis_size("rows"); half=count//2
    upper,rows=2*upper_both.shape[0],lower.shape[0]
    dma=pltpu.SemaphoreType.DMA
    return run(functools.partial(dec_fwd_kernel,count),
      (S((32,NF,384)),S((8,NF,1024)),S((16,NF,1024)),S((32,NF,1024)),S((upper//count,512)),S((rows//2,512))),
      [small(4,256),small(8,128),small(16,128),small(32,0),V((half-1,upper//count,512)),V((rows//2,512)),dma((2,half))],
      (dec,u4,u3,u2,b,upper_both,lower),"decode",24,ident=5)
def dec_bwd(hints,dec,p3,p2,p1,a,t2,t3,t4,upper_piece,lower_both):
    count=lax.axis_size("rows"); half=count//2
    upper,rows=count*upper_piece.shape[0],2*lower_both.shape[0]
    dma=pltpu.SemaphoreType.DMA
    return run(functools.partial(dec_bwd_kernel,count),
      (S((4,NF,1024)),S((2816,256)),S((upper//2,512)),S((rows//count,512))),
      [big(32),big(16),big(8),V((34,NF,384)),V((1024,32*NF)),V((half-1,rows//count,512)),dma((2,2*(half-1))),dma((1,))],
      (*hints,dec,p3,p2,p1,a,t2,t3,t4,upper_piece,lower_both),"decode_back",42,ident=6)


def rows_of(ref, index, size):
    return ref.at[pl.ds(pl.multiple_of(index * size, 16), size)]


class Place:
    def __init__(self, count):
        self.me, self.row = lax.axis_index("strip"), lax.axis_index("rows")
        self.half = count // 2
        self.near, self.far = lax.rem(self.row, 2), lax.div(self.row, 2)
        self.core, self.x = lax.rem(self.me, 2), lax.div(self.me, 2)
        self.near_device = (self.row + 1 - 2 * self.near, self.me)
        self.sibling = (self.row, self.me + 1 - 2 * self.core)
        self.partner = (self.row, lax.rem(self.me + 2, 4))
        self.others = [(self.row, lax.rem(self.me + k, 4)) for k in range(1, 4)]
        self.far_places = [lax.rem(self.far + k, self.half) for k in range(1, self.half)]
        self.far_devices = [(2 * place + self.near, self.me) for place in self.far_places]

    def greet(self, devices):
        barrier = pltpu.get_barrier_semaphore()
        for device in devices:
            pl.semaphore_signal(barrier, inc=1, device_id=device, device_id_type=MESH)
        pl.semaphore_wait(barrier, len(devices))


class Sems:
    def __init__(self, remote, local):
        self.remote, self.local, self.used, self.used_here = remote, local, 0, 0

    def copy(self, src, dst, device):
        assert self.used < self.remote.shape[1]
        one = pltpu.make_async_remote_copy(
            src_ref=src,
            dst_ref=dst,
            send_sem=self.remote.at[0, self.used],
            recv_sem=self.remote.at[1, self.used],
            device_id=device,
            device_id_type=MESH,
        )
        self.used = self.used + 1
        one.start()
        return one

    def here(self, src, dst):
        assert self.used_here < self.local.shape[0]
        one = pltpu.make_async_copy(src, dst, self.local.at[self.used_here])
        self.used_here = self.used_here + 1
        one.start()
        return one


def near_start(place, sems, values, arrived):
    half = values.shape[0] // 2
    return sems.copy(rows_of(values, 1 - place.near, half), arrived, place.near_device)


def near_end(place, copy, values, arrived, both):
    copy.wait()
    half = values.shape[0] // 2
    total = rows_of(values, place.near, half)[...].astype(F32) + arrived[...].astype(F32)
    both[...] = total.astype(BF)


def far_start(place, sems, both, slots):
    each = slots.shape[1]
    return [
        sems.copy(rows_of(both, at, each), slots.at[k], device)
        for k, (at, device) in enumerate(zip(place.far_places, place.far_devices))
    ]


def far_end(place, copies, both, slots, piece):
    for one in copies:
        one.wait()
    total = rows_of(both, place.far, slots.shape[1])[...].astype(F32)
    for k in range(slots.shape[0]):
        total = total + slots[k].astype(F32)
    piece[...] = total.astype(BF)


def back_start(place, sems, piece, home):
    out = rows_of(home, place.far, piece.shape[0])
    return [sems.here(piece, out)] + [sems.copy(piece, out, d) for d in place.far_devices]


def back_part(place, sems, piece, home, part):
    size = piece.shape[0] // 2
    src = piece.at[pl.ds(part * size, size)]
    first = place.far * piece.shape[0] + part * size
    out = home.at[pl.ds(pl.multiple_of(first, 16), size)]
    return [sems.here(src, out)] + [sems.copy(src, out, d) for d in place.far_devices]


def last_part(place, sems, home, each, part):
    size = each // 2
    refs = [home.at[pl.ds(each * k + part * size, size)] for k in range(place.half)]
    return [sems.copy(ref, ref, place.near_device) for ref in refs]


def half_lanes(place, w):
    return pl.ds(pl.multiple_of(256 * w + 128 * (1 - place.near), 128), 128)


def last_start(place, sems, home, out):
    half = out.shape[0] // 2
    return sems.copy(home, rows_of(out, place.near, half), place.near_device)


def exchange_16():
    r = lax.broadcasted_iota(jnp.int32, (256, 256), 0)
    s = lax.broadcasted_iota(jnp.int32, (256, 256), 1)
    return (s == lax.rem(r, 16) * 16 + lax.div(r, 16)).astype(BF)


def first_frame(strip):
    return NF * ((strip % 2) * 2 + strip // 2)


def turned_rows(x, i):
    return jnp.concatenate([x[c, 2 * i + p] for p in range(2) for c in range(3)], axis=0).T


def canonical(w, swap, c, o, flipped):
    parts = {}
    for b in range(c // 16):
        block = jnp.dot(swap, w[256 * b : 256 * b + 256, :], preferred_element_type=F32).astype(BF)
        for k in range(16):
            parts[(15 - k if flipped else k, b)] = block[16 * k : 16 * k + 16]
    return [
        jnp.concatenate(
            [parts[(4 * kh + kw, b)] for kw in range(4) for b in range(c // 16)], axis=0
        )
        for kh in range(4)
    ]


def canonical_turned(w, swap):
    parts = {}
    for b in range(16):
        block = jnp.dot(swap, w[256 * b : 256 * b + 256, :], preferred_element_type=F32).astype(BF)
        for k in range(16):
            parts[(k, b)] = block[16 * k : 16 * k + 16]
    return [
        jnp.concatenate(
            [
                jnp.concatenate([parts[(4 * kh + kw, b)] for b in range(16)], axis=0)
                for kw in range(4)
            ],
            axis=1,
        )
        for kh in range(4)
    ]


def band(flat, a, c, o):
    def shifted(value, first):
        above = jnp.zeros((first, value.shape[1]), BF)
        below = jnp.zeros((512 - first - value.shape[0], value.shape[1]), BF)
        return jnp.concatenate([above, value, below], axis=0)

    if a == 1:
        return flat
    if a == 2:
        return jnp.concatenate([shifted(flat, 64), shifted(flat, 192)], axis=1)
    twice = jnp.concatenate([flat, flat], axis=1)
    left = lax.broadcasted_iota(jnp.int32, (512, 128), 1) < 64
    return jnp.concatenate(
        [
            jnp.where(left, shifted(twice, 96), shifted(twice, 160)),
            jnp.where(left, shifted(twice, 224), shifted(twice, 288)),
        ],
        axis=1,
    )


def put_bands(t_ref, u_ref, bands, turned, a):
    for kh in range(4):
        t = bands[kh]
        t_ref[512 * kh : 512 * kh + 512] = t
        tt = t.T if turned is None else turned[kh]
        z = jnp.zeros((256, 128), BF)
        left = jnp.concatenate([tt[:, 384:512], z], axis=1)
        right = jnp.concatenate([z, tt[:, :128]], axis=1)
        if a > 1:
            left, right = left[128:], right[:128]
        k = 512 if a > 1 else 768
        u_ref[1 - kh % 2, k * (kh // 2) : k * (kh // 2) + k] = jnp.concatenate(
            [left, tt[:, 128:384], right], axis=0
        )


def put_outer(a_ref, b_ref, w, flipped):
    row = lax.broadcasted_iota(jnp.int32, (64, 1024), 0)
    col = lax.div(lax.broadcasted_iota(jnp.int32, (64, 1024), 1), 32)
    tap = row - 2 * col + 1
    for kh in range(4):
        d, p = (kh + 1) // 2, (kh + 1) % 2
        for c in range(3):
            total = jnp.zeros((64, 1024), F32)
            for kw in range(4):
                k = 4 * kh + kw
                r = 16 * c + (15 - k if flipped else k)
                total = jnp.where(tap == kw, w[r : r + 1, :], total)
            first = 384 * d + 192 * p + 64 * c
            a_ref[first : first + 64] = total.astype(BF)
    a_ref[0:192] = jnp.zeros((192, 1024), BF)
    a_ref[960:1152] = jnp.zeros((192, 1024), BF)
    for d in range(3):
        b_ref[1024 * d : 1024 * d + 1024] = a_ref[384 * d : 384 * d + 384].T


def start_kernel(
    x, later, e1, e2, e3, e4, d1, d2, d3, d4, lh, dh, emb, qkv, proj, up, down,
    pixels, ea, eb, et2, et3, et4, eu2, eu3, eu4, da, db, dt2, dt3, dt4, du2, du3, du4,
    lh0, lh1, dh0, dh1, emb1, qkv1, proj1, up1, down1, t0, t1, t2, t3,
    stage, send_sem, recv_sem, side_sems,
    va, vb, vt2, vt3, vt4, vu2, vu3, vu4, wa, wb, wt2, wt3, wt4, wu2, wu3, wu4,
    vl, vd, out_sems,
):
    me = lax.axis_index("strip")
    row = lax.axis_index("rows")
    sibling = (row, me + 1 - 2 * lax.rem(me, 2))
    pixels[0] = jnp.zeros((NF, 384), BF)
    pixels[33] = jnp.zeros((NF, 384), BF)

    def turn_rows(i, carry):
        flat = turned_rows(x, i)
        for k in range(4):
            stage[k, i] = flat[first_frame(k) : first_frame(k) + NF]
        return carry

    lax.fori_loop(0, 8, turn_rows, 0)
    barrier = pltpu.get_barrier_semaphore()
    for k in range(1, 4):
        pl.semaphore_signal(
            barrier, inc=1, device_id=(row, lax.rem(me + k, 4)), device_id_type=MESH
        )
    pl.semaphore_wait(barrier, 3)
    copies = []
    for k in range(1, 4):
        to = lax.rem(me + k, 4)
        copies.append(
            pltpu.make_async_remote_copy(
                src_ref=stage.at[to],
                dst_ref=pixels.at[pl.ds(1 + 8 * me, 8)],
                send_sem=send_sem.at[k - 1],
                recv_sem=recv_sem.at[k - 1],
                device_id=(row, to),
                device_id_type=MESH,
            )
        )
    for copy in copies:
        copy.start()

    def to_sibling(src, dst, index):
        copy = pltpu.make_async_remote_copy(
            src_ref=src,
            dst_ref=dst,
            send_sem=side_sems.at[0, index],
            recv_sem=side_sems.at[1, index],
            device_id=sibling,
            device_id_type=MESH,
        )
        copy.start()
        copies.append(copy)

    for index, (src, dst) in enumerate(
        ((emb, emb1), (qkv, qkv1), (proj, proj1), (up, up1), (down, down1))
    ):
        to_sibling(src, dst, index)
    pixels[pl.ds(1 + 8 * me, 8)] = stage[me]

    turn_kernel(later, t0, t1, t2, t3)
    stores = []

    def store(src, dst):
        copy = pltpu.make_async_copy(src, dst, out_sems.at[len(stores)])
        copy.start()
        stores.append(copy)

    swap = exchange_16()
    put_outer(va, vb, e1, False)
    store(va, ea)
    store(vb, eb)
    put_bands(vt2, vu2, [band(f, 4, 32, 64) for f in canonical(e2, swap, 32, 64, False)], None, 4)
    store(vt2, et2)
    store(vu2, eu2)
    put_bands(vt3, vu3, [band(f, 2, 64, 128) for f in canonical(e3, swap, 64, 128, False)], None, 2)
    store(vt3, et3)
    store(vu3, eu3)
    turned = canonical_turned(e4, swap)
    put_bands(vt4, vu4, [f.T for f in turned], turned, 1)
    store(vt4, et4)
    store(vu4, eu4)
    for b in range(16):
        rows = slice(256 * b, 256 * b + 256)
        for src, dst in ((lh[rows, :], vl), (dh[:, rows].T, vd)):
            block = jnp.dot(swap, src, preferred_element_type=F32).astype(BF)
            for k in range(16):
                dst[256 * k + 16 * b : 256 * k + 16 * b + 16] = block[16 * k : 16 * k + 16]
    store(vl, lh0)
    store(vd, dh0)
    to_sibling(vl, lh1, 5)
    to_sibling(vd, dh1, 6)
    put_outer(wa, wb, d4, True)
    store(wa, da)
    store(wb, db)
    put_bands(wt2, wu2, [band(f, 4, 32, 64) for f in canonical(d3, swap, 32, 64, True)], None, 4)
    store(wt2, dt2)
    store(wu2, du2)
    put_bands(wt3, wu3, [band(f, 2, 64, 128) for f in canonical(d2, swap, 64, 128, True)], None, 2)
    store(wt3, dt3)
    store(wu3, du3)
    put_bands(wt4, wu4, canonical(d1, swap, 128, 256, True), None, 1)
    store(wt4, dt4)
    store(wu4, du4)
    for copy in copies:
        copy.wait()
    for copy in stores:
        copy.wait()


def start(frames, later, kernels, latent_head, decode_head, others):
    e1, e2, e3, e4, d1, d2, d3, d4 = kernels
    rows_in = [
        jnp.tile(jnp.transpose(e1, (1, 2, 3, 0)).reshape(48, 32), (1, 32)).astype(F32),
        jnp.transpose(e2, (1, 2, 3, 0)).reshape(512, 64),
        jnp.transpose(e3, (1, 2, 3, 0)).reshape(1024, 128),
        jnp.transpose(e4, (0, 2, 3, 1)).reshape(4096, 128),
        jnp.transpose(d1, (0, 2, 3, 1)).reshape(2048, 256),
        jnp.transpose(d2, (0, 2, 3, 1)).reshape(1024, 128),
        jnp.transpose(d3, (0, 2, 3, 1)).reshape(512, 64),
        jnp.tile(jnp.transpose(d4, (0, 2, 3, 1)).reshape(48, 32), (1, 32)).astype(F32),
    ]
    dma = pltpu.SemaphoreType.DMA
    any_spec = pl.BlockSpec(memory_space=pl.ANY)
    built = [(1152, 1024), (3072, 384)] + [(2048, 256)] * 3
    built = built + [(2, 1024, 256), (2, 1024, 256), (2, 1536, 256)]
    heads = [(4096, 256)] * 4
    shapes = [(34, NF, 384)] + built * 2 + heads + [w.shape for w in others]
    shapes = shapes + [(8, NF, 384)] * 4
    out = pl.pallas_call(
        start_kernel,
        out_shape=tuple(S(shape) for shape in shapes),
        in_specs=VM(12) + [any_spec] * len(others),
        out_specs=tuple(VM(1) + [any_spec] * (len(shapes) - 5) + VM(4)),
        scratch_shapes=[
            V((4, 8, NF, 384)),
            dma((3,)),
            dma((3,)),
            dma((2, 7)),
            *[V(shape) for shape in built * 2],
            V((4096, 256)),
            V((4096, 256)),
            dma((18,)),
        ],
        compiler_params=pltpu.CompilerParams(
            collective_id=1, has_side_effects=True, vmem_limit_bytes=56 * MIB
        ),
        cost_estimate=estimate(26),
        name="start",
    )(
        jnp.transpose(frames, (1, 2, 3, 0)),
        jnp.transpose(later, (1, 2, 3, 0)),
        *rows_in,
        latent_head,
        decode_head,
        *others,
    )
    hints = around(out[-4:])
    return out[0], out[1:9], out[9:17], out[17:19], out[19:21], out[21:-4], hints


def turn_kernel(x, *out):
    me = lax.axis_index("strip")

    def turn_rows(i, carry):
        flat = turned_rows(x, i)
        for k in range(4):
            part = flat[first_frame(k) : first_frame(k) + NF]
            for step in range(4):

                @pl.when(lax.rem(me + step, 4) == k)
                def _():
                    out[step][i] = part

        return carry

    lax.fori_loop(0, 8, turn_rows, 0)


def around(parts):
    return [parts[0]] + [
        lax.ppermute(parts[k], "strip", [(s, (s + k) % 4) for s in range(4)]) for k in range(1, 4)
    ]


def turned_back(got, out):
    def turn_rows(i, carry):
        block = jnp.concatenate([got[(b % 2) * 2 + b // 2, i] for b in range(4)], axis=0)
        flat = block.T.astype(out.dtype)
        for p in range(2):
            for c in range(3):
                first = 64 * (3 * p + c)
                out[c, 2 * i + p] = flat[first : first + 64]
        return carry

    lax.fori_loop(0, 8, turn_rows, 0)


def turn_back_kernel(c0, c1, c2, c3, out, got):
    me = lax.axis_index("strip")
    for k, part in enumerate((c0, c1, c2, c3)):
        got[lax.rem(me + 4 - k, 4)] = part[...]
    turned_back(got, out)


def blocks_around(pairs, strip):
    return around([lax.dynamic_slice_in_dim(pairs, 8 * ((strip + k) % 4), 8) for k in range(4)])


def frames_out_later(parts):
    flat = pl.pallas_call(
        turn_back_kernel,
        out_shape=S((3, 16, 64, 256)),
        in_specs=VM(4),
        out_specs=VM(1)[0],
        scratch_shapes=[V((4, 8, NF, 384))],
        compiler_params=pltpu.CompilerParams(vmem_limit_bytes=32 * MIB),
        cost_estimate=estimate(2),
        name="turn_back",
    )(*parts)
    return jnp.transpose(flat, (3, 0, 1, 2))


def dot(a, b):
    return jnp.dot(a, b, preferred_element_type=F32)


def dot_nt(a, b):
    return lax.dot_general(a, b, (((1,), (1,)), ((), ())), preferred_element_type=F32)


def over_groups(values, join):
    lanes = values.shape[1]
    lane = lax.broadcasted_iota(jnp.int32, values.shape, 1)
    for step in (1, 2, 4, 8, 16):
        upper = lax.rem(lax.div(lane, step), 2) == 1
        other = jnp.where(
            upper, pltpu.roll(values, step, 1), pltpu.roll(values, lanes - step, 1)
        )
        values = join(values, other)
    return values


def unit_of(hidden):
    centred = hidden - jnp.mean(hidden, -1, keepdims=True)
    scale_inv = lax.rsqrt(jnp.mean(centred * centred, -1, keepdims=True) + EPS)
    return centred * scale_inv, scale_inv


def unit_back(grad_normed, unit_rows, scale_inv, gain):
    grad_unit = grad_normed * gain
    grad_gain = jnp.sum(grad_normed * unit_rows, 0, keepdims=True)
    grad_rows = scale_inv * (
        grad_unit
        - jnp.mean(grad_unit, -1, keepdims=True)
        - unit_rows * jnp.mean(grad_unit * unit_rows, -1, keepdims=True)
    )
    return grad_gain, grad_rows


LAYER_ROWS = 1536


def token_rows(layers, count):
    upper = max(layers - 1, 1) * LAYER_ROWS
    lower = LAYER_ROWS + 256 + NF + 16
    return share_rows(upper, count), share_rows(lower, count)


def middle_kernel(
    layers, count,
    feat, lh0, lh1, dh0, dh1, emb0, emb1, pos, gains, allow, cot,
    qkv0, qkv1, proj0, proj1, up0, up1, down0, down1,
    tokens, latent_out, chances_out, decoded, upper_both, lower, grad_latent, feat_got,
    latent_near, feat_near, got_near,
    feat_sems, keep, send, sent, spread_sems, parts, gots, pair_sems,
    upper, upper_other, upper_got, lower_other, lower_got, upper_near, fold_sems, near_sems, unit_a, unit_f, normed_a, normed_f, mixed, weights,
    attended, before, inner, gain_rows,
):
    strip = lax.axis_index("strip")
    row = lax.axis_index("rows")
    place_here = Place(count)
    partner, sibling = place_here.partner, place_here.sibling
    place_here.greet([partner, sibling, place_here.near_device])

    def copy(src, dst, sems, index, device):
        return pltpu.make_async_remote_copy(
            src_ref=src,
            dst_ref=dst,
            send_sem=sems.at[0, index],
            recv_sem=sems.at[1, index],
            device_id=device,
            device_id_type=MESH,
        )

    feat_copy = copy(feat, feat_got, feat_sems, 0, partner)
    feat_copy.start()

    def total_start(index, value):
        parts[index] = value.astype(BF)
        one = copy(parts.at[index], gots.at[index], pair_sems, index, partner)
        one.start()
        return one

    def total_wait(index, one):
        one.wait()
        got = jnp.concatenate([gots[index, NF:], gots[index, :NF]], axis=0)
        return parts[index].astype(F32) + got.astype(F32)

    def logits_of(maps):
        halves = []
        for weight in (lh0, lh1):
            total = jnp.zeros((NF, 256), F32)
            for h in range(4):
                total = total + dot(maps[h], weight[1024 * h : 1024 * h + 1024])
            halves.append(total)
        return jnp.concatenate(halves, axis=1)

    mine = logits_of(feat)
    feat_copy.wait()
    near_sends = Sems(near_sems, None)
    near_copies = [
        near_sends.copy(
            src.at[:, :, half_lanes(place_here, w)],
            dst.at[:, :, 128 * w : 128 * w + 128],
            place_here.near_device,
        )
        for src, dst in ((feat, feat_near), (feat_got, got_near))
        for w in range(4)
    ]
    logits = jnp.concatenate([mine, logits_of(feat_got)], axis=0)
    raised = jnp.exp(logits - over_groups(logits, jnp.maximum))
    chances = raised / over_groups(raised, jnp.add)
    latent = chances.astype(BF)
    chances_out[...] = chances
    latent_out[...] = latent
    near_copies.append(near_sends.copy(latent_out, latent_near, place_here.near_device))

    waiting = total_start(0, dot(latent[:, :256], emb0[...]) + dot(latent[:, 256:], emb1[...]))
    for hw in range(16):
        lanes = slice(256 * (hw % 4), 256 * (hw % 4) + 256)
        rows = slice(256 * hw, 256 * hw + 256)
        value = dot_nt(latent[:, :256], dh0[rows]) + dot_nt(latent[:, 256:], dh1[rows])
        value = value.astype(BF)
        keep[hw // 4, :, lanes] = value[:NF]
        send[hw // 4, :, lanes] = value[NF:]
    spread_copy = copy(send, sent, spread_sems, 0, partner)
    spread_copy.start()
    embedded = total_wait(0, waiting)
    place = pos[...].astype(F32)
    hidden = embedded + jnp.concatenate([place, place], axis=0)
    head_lane = lax.div(lax.broadcasted_iota(jnp.int32, (2 * NF, 128), 1), HEAD_DIM)
    allowed = allow[...] > 0.5

    def of_head(value, h):
        return jnp.where(head_lane == h % 2, value, jnp.zeros_like(value))

    def pair_lanes(h):
        return slice(128 * (h // 2), 128 * (h // 2) + 128)

    for k in range(layers):
        unit, inv = unit_of(hidden)
        unit_a[k] = jnp.concatenate([unit, jnp.broadcast_to(inv, (2 * NF, 128))], axis=1)
        normed = (unit * gains[2 * k : 2 * k + 1]).astype(BF)
        normed_a[k] = normed
        for part in range(3):
            mixed[k, part] = jnp.concatenate(
                [dot(normed, qkv0[k, part]), dot(normed, qkv1[k, part])], axis=1
            ).astype(BF)
        for p in range(2):
            both = jnp.zeros((2 * NF, 128), F32)
            for h in (2 * p, 2 * p + 1):
                lanes = pair_lanes(h)
                scores = SCALE * dot_nt(of_head(mixed[k, 0, :, lanes], h), mixed[k, 1, :, lanes])
                scores = jnp.where(allowed, scores, NEG)
                lifted = jnp.exp(scores - jnp.max(scores, -1, keepdims=True))
                weight = lifted / jnp.sum(lifted, -1, keepdims=True)
                weights[k, h] = weight
                both = both + of_head(dot(weight.astype(BF), mixed[k, 2, :, lanes]), h)
            attended[k, :, 128 * p : 128 * p + 128] = both.astype(BF)
        partial = dot(attended[k, :, :128], proj0[k]) + dot(attended[k, :, 128:], proj1[k])
        middle = hidden + total_wait(2 * k + 1, total_start(2 * k + 1, partial))
        unit, inv = unit_of(middle)
        unit_f[k] = jnp.concatenate([unit, jnp.broadcast_to(inv, (2 * NF, 128))], axis=1)
        normed = (unit * gains[2 * k + 1 : 2 * k + 2]).astype(BF)
        normed_f[k] = normed
        partial = jnp.zeros((2 * NF, 512), F32)
        for side, (up, down) in enumerate(((up0, down0), (up1, down1))):
            value = dot(normed, up[k])
            before[k, :, 512 * side : 512 * side + 512] = value
            act = (value * sig(value)).astype(BF)
            inner[k, :, 512 * side : 512 * side + 512] = act
            partial = partial + dot(act, down[k])
        hidden = middle + total_wait(2 * k + 2, total_start(2 * k + 2, partial))
    tokens[...] = hidden.astype(BF)

    spread_copy.wait()
    decoded[...] = (keep[...].astype(F32) + sent[...].astype(F32)).astype(BF)

    def fold_start(index, part, got):
        one = copy(part, got, fold_sems, index, sibling)
        one.start()
        return one

    def fold_end(one, own, got, count):
        one.wait()
        for first in range(0, count, 128):
            rows = slice(first, min(first + 128, count))
            own[rows] = (own[rows].astype(F32) + got[rows].astype(F32)).astype(BF)
        if own.shape[0] > count:
            own[count:] = jnp.zeros((own.shape[0] - count, 512), BF)

    lower_rows = LAYER_ROWS + 256 + NF + 16

    grad = cot[...].astype(F32)
    for k in reversed(range(layers)):
        flat, other = (upper, upper_other) if k else (lower, lower_other)
        base = LAYER_ROWS * (k - 1) if k else 0
        index = 2 * layers + 1 + 2 * (layers - 1 - k)
        low = grad.astype(BF)
        partial = jnp.zeros((2 * NF, 512), F32)
        grads = []
        for side, (up, down) in enumerate(((up0, down0), (up1, down1))):
            value = before[k, :, 512 * side : 512 * side + 512]
            squash = sig(value)
            slope = squash * (1.0 + value * (1.0 - squash))
            grad_before = (dot_nt(low, down[k]) * slope).astype(BF)
            grads.append(grad_before)
            partial = partial + dot_nt(grad_before, up[k])
        waiting = total_start(index, partial)
        turned = normed_f[k].T
        for side, dst in enumerate((flat, other)):
            act = inner[k, :, 512 * side : 512 * side + 512]
            dst[base : base + 512] = dot(act.T, low).astype(BF)
            dst[base + 512 : base + 1024] = dot(turned, grads[side]).astype(BF)
        if k == 0:
            fold_end(upper_fold, upper, upper_got, LAYER_ROWS * (layers - 1))
            near_copy = near_start(place_here, near_sends, upper, upper_near)
        grad_normed = total_wait(index, waiting)
        gain_f, grad_rows = unit_back(
            grad_normed, unit_f[k, :, :512], unit_f[k, :, 512:513], gains[2 * k + 1 : 2 * k + 2]
        )
        grad = grad + grad_rows
        low = grad.astype(BF)
        grad_mixed = [[], [], []]
        for p, proj in enumerate((proj0, proj1)):
            lanes = pair_lanes(2 * p)
            grad_pair = dot_nt(low, proj[k]).astype(BF)
            queries, keys, vals = mixed[k, 0, :, lanes], mixed[k, 1, :, lanes], mixed[k, 2, :, lanes]
            g_queries = jnp.zeros((2 * NF, 128), F32)
            g_keys, g_vals = g_queries, g_queries
            for h in (2 * p, 2 * p + 1):
                weight = weights[k, h]
                grad_head = of_head(grad_pair, h)
                g_vals = g_vals + dot(weight.astype(BF).T, grad_head)
                grad_weight = dot_nt(grad_head, vals)
                along = jnp.sum(weight * grad_weight, -1, keepdims=True)
                grad_scores = (weight * (grad_weight - along)).astype(BF)
                g_queries = g_queries + of_head(dot(grad_scores, keys), h)
                g_keys = g_keys + dot(grad_scores.T, of_head(queries, h))
            grad_mixed[0].append((SCALE * g_queries).astype(BF))
            grad_mixed[1].append((SCALE * g_keys).astype(BF))
            grad_mixed[2].append(g_vals.astype(BF))
        partial = jnp.zeros((2 * NF, 512), F32)
        for part in range(3):
            for side, qkv in enumerate((qkv0, qkv1)):
                partial = partial + dot_nt(grad_mixed[part][side], qkv[k, part])
        waiting = total_start(index + 1, partial)
        turned = normed_a[k].T
        for side, dst in enumerate((flat, other)):
            act = attended[k, :, 128 * side : 128 * side + 128]
            dst[base + 1024 : base + 1152] = dot(act.T, low).astype(BF)
            for part in range(3):
                value = dot(turned, grad_mixed[part][side]).astype(BF)
                first = base + 1152 + 128 * part
                for b in range(4):
                    dst[first : first + 128, 128 * b : 128 * b + 128] = value[
                        128 * b : 128 * b + 128
                    ]
        if k == 1:
            upper_fold = fold_start(0, upper_other, upper_got)
        grad_normed = total_wait(index + 1, waiting)
        gain_a, grad_rows = unit_back(
            grad_normed, unit_a[k, :, :512], unit_a[k, :, 512:513], gains[2 * k : 2 * k + 1]
        )
        grad = grad + grad_rows
        gain_rows[2 * k : 2 * k + 1] = gain_a
        gain_rows[2 * k + 1 : 2 * k + 2] = gain_f

    low = grad.astype(BF)
    own_latent, other_latent = latent_out[:, :256], latent_out[:, 256:]
    lower[LAYER_ROWS : LAYER_ROWS + 256] = dot(own_latent.T, low).astype(BF)
    lower_other[LAYER_ROWS : LAYER_ROWS + 256] = dot(other_latent.T, low).astype(BF)
    rest = jnp.concatenate(
        [
            grad[:NF] + grad[NF:],
            gain_rows[...],
            jnp.zeros((16 - 2 * layers, 512), F32),
        ],
        axis=0,
    ).astype(BF)
    lower[LAYER_ROWS + 256 : lower_rows] = rest
    lower_other[LAYER_ROWS + 256 : lower_rows] = rest
    lower_fold = fold_start(1, lower_other, lower_got)
    grad_latent[:, :256] = dot_nt(low, emb0[...])
    grad_latent[:, 256:] = dot_nt(low, emb1[...])
    near_end(place_here, near_copy, upper, upper_near, upper_both)
    fold_end(lower_fold, lower, lower_got, lower_rows)
    for one in near_copies:
        one.wait()


def middle(layers, *args):
    count = lax.axis_size("rows")
    upper, lower = token_rows(layers, count)
    dma = pltpu.SemaphoreType.DMA
    sums = 4 * layers + 1
    t = 2 * NF
    return pl.pallas_call(
        functools.partial(middle_kernel, layers, count),
        out_shape=(
            S((t, 512)),
            S((t, 512)),
            S((t, 512), F32),
            S((4, NF, 1024)),
            S((upper // 2, 512)),
            S((lower, 512)),
            S((t, 512), F32),
            S((4, NF, 1024)),
            S((t, 512)),
            S((4, NF, 512)),
            S((4, NF, 512)),
        ),
        in_specs=VM(len(args)),
        out_specs=tuple(VM(11)),
        scratch_shapes=[
            dma((2, 1)),
            V((4, NF, 1024)),
            V((4, NF, 1024)),
            V((4, NF, 1024)),
            dma((2, 1)),
            V((sums, t, 512)),
            V((sums, t, 512)),
            dma((2, sums)),
            V((upper, 512)),
            V((upper, 512)),
            V((upper, 512)),
            V((lower, 512)),
            V((lower, 512)),
            V((upper // 2, 512)),
            dma((2, 2)),
            dma((2, 10)),
            V((layers, t, 640), F32),
            V((layers, t, 640), F32),
            V((layers, t, 512)),
            V((layers, t, 512)),
            V((layers, 3, t, 256)),
            V((layers, 4, t, t), F32),
            V((layers, t, 256)),
            V((layers, t, 1024), F32),
            V((layers, t, 1024)),
            V((2 * layers, 512), F32),
        ],
        compiler_params=pltpu.CompilerParams(
            collective_id=3, has_side_effects=True, vmem_limit_bytes=56 * MIB
        ),
        cost_estimate=estimate(84),
        name="middle",
    )(*args)


def back_kernel(
    count, grad, latent, latent_near, chances, grad_embed, feat0, feat1, feat2, feat3,
    lh0, lh1, dh0, dh1, flat, upper_half, lower_piece,
    grad_feat, share, d_piece, l_both, upper_total, lower_half,
    got, got_near, got_cross, keep, send, sent, logits_here, logits_near, own, other, other_got,
    d_both, d_slots, side_got, side_sum, cross_got, remote, here,
):
    place = Place(count)
    near, core, x = place.near, place.core, place.x
    cross_device = (place.near_device[0], place.partner[1])
    place.greet(
        [place.partner, place.sibling, place.near_device, cross_device] + place.far_devices
    )
    sems = Sems(remote, here)
    grad_copies = [sems.copy(grad, got, place.partner)]
    for device, dst in ((place.near_device, got_near), (cross_device, got_cross)):
        for w in range(4):
            grad_copies.append(
                sems.copy(
                    grad.at[:, :, half_lanes(place, w)], dst.at[:, :, 128 * w : 128 * w + 128], device
                )
            )
    upper_own = sems.here(upper_half, rows_of(upper_total, near, upper_half.shape[0]))
    upper_last = last_start(place, sems, upper_half, upper_total)
    lower_back = back_start(place, sems, lower_piece, lower_half)
    side_copy = sems.copy(flat.at[1 - core], side_got, place.sibling)

    def through(maps):
        halves = []
        for weight in (dh0, dh1):
            total = jnp.zeros((NF, 256), F32)
            for h in range(4):
                total = total + dot(maps[h], weight[1024 * h : 1024 * h + 1024])
            halves.append(total)
        return jnp.concatenate(halves, axis=1)

    def head_grad(slot, wide, narrow, rhs):
        for h in range(4):
            for w in range(4):
                lanes = pl.ds(pl.multiple_of(256 * w + 128 * near, 128), 128)
                maps = [ref[h, :, lanes] for ref in wide]
                maps = maps + [ref[h, :, 128 * w : 128 * w + 128] for ref in narrow]
                rows = slice(512 * h + 128 * w, 512 * h + 128 * w + 128)
                value = dot(jnp.concatenate(maps, axis=0).T, rhs).astype(BF)
                own[slot, rows] = value[:, :256]
                other[slot, rows] = value[:, 256:]
        return sems.copy(other.at[slot], other_got.at[slot], place.sibling)

    swap = exchange_16()

    def folded(slot, b):
        parts = []
        for k in range(16):
            rows = slice(128 * k + 16 * b, 128 * k + 16 * b + 16)
            value = own[slot, rows].astype(F32) + other_got[slot, rows].astype(F32)
            parts.append(value.astype(BF))
        return dot(swap, jnp.concatenate(parts, axis=0)).astype(BF)

    mine = through(grad)
    side_copy.wait()
    side_sum[...] = (flat[core].astype(F32) + side_got[...].astype(F32)).astype(BF)
    for one in grad_copies:
        one.wait()
    cross_copy = sems.copy(side_sum.at[1 - x], cross_got, place.partner)
    both_latents = jnp.concatenate([latent[...], latent_near[...]], axis=0)
    out_fold = head_grad(0, (grad, got), (got_near, got_cross), both_latents)
    grad_latent = grad_embed[...] + jnp.concatenate([mine, through(got)], axis=0)
    probs = chances[...]
    along = over_groups(probs * grad_latent, jnp.add)
    grad_logits = (probs * (grad_latent - along)).astype(BF)
    logits_here[...] = grad_logits
    logits_copy = sems.copy(logits_here, logits_near, place.near_device)
    out_fold.wait()
    for b in range(8):
        d_both[256 * b : 256 * b + 256] = folded(0, b).T
    d_far = far_start(place, sems, d_both, d_slots)
    logits_copy.wait()
    both_logits = jnp.concatenate([grad_logits, logits_near[...]], axis=0)
    in_fold = head_grad(1, (feat0, feat1), (feat2, feat3), both_logits)
    sends = []
    for h in range(4):
        for w in range(4):
            lanes = slice(256 * w, 256 * w + 256)
            rows = slice(1024 * h + 256 * w, 1024 * h + 256 * w + 256)
            value = dot_nt(grad_logits[:, :256], lh0[rows]) + dot_nt(grad_logits[:, 256:], lh1[rows])
            value = value.astype(BF)
            keep[h, :, lanes] = value[:NF]
            send[h, :, lanes] = value[NF:]
        sends.append(sems.copy(send.at[h], sent.at[h], place.partner))
    in_fold.wait()
    for b in range(8):
        l_both[256 * b : 256 * b + 256] = folded(1, b)
    cross_copy.wait()
    share[...] = (side_sum[x].astype(F32) + cross_got[...].astype(F32)).astype(BF)
    upper_own.wait()
    upper_last.wait()
    for one in lower_back + sends:
        one.wait()
    grad_feat[...] = (keep[...].astype(F32) + sent[...].astype(F32)).astype(BF)
    far_end(place, d_far, d_both, d_slots, d_piece)


def latents_back(*args):
    dma = pltpu.SemaphoreType.DMA
    count = lax.axis_size("rows")
    half = count // 2
    flat, upper_half, lower_piece = args[-3:]
    quarter = flat.shape[0] // 4
    args = args[:-3] + (flat.reshape(2, 2, quarter, 256), upper_half, lower_piece)
    maps = (4, NF, 1024)
    narrow = (4, NF, 512)
    rows = (2048, 256)
    return pl.pallas_call(
        functools.partial(back_kernel, count),
        out_shape=(
            S(maps),
            S((quarter, 256)),
            S((4096 // count, 256)),
            S(rows),
            S((2 * upper_half.shape[0], 512)),
            S((half * lower_piece.shape[0], 512)),
        ),
        in_specs=VM(len(args)),
        out_specs=tuple(VM(4) + [pl.BlockSpec(memory_space=pl.ANY)] + VM(1)),
        scratch_shapes=[
            V(maps),
            V(narrow),
            V(narrow),
            V(maps),
            V(maps),
            V(maps),
            V((2 * NF, 512)),
            V((2 * NF, 512)),
            V((2,) + rows),
            V((2,) + rows),
            V((2,) + rows),
            V(rows),
            V((half - 1, 4096 // count, 256)),
            V((2, quarter, 256)),
            V((2, quarter, 256)),
            V((quarter, 256)),
            dma((2, 2 * half + 20)),
            dma((2,)),
        ],
        compiler_params=pltpu.CompilerParams(
            collective_id=4, has_side_effects=True, vmem_limit_bytes=58 * MIB
        ),
        cost_estimate=estimate(55),
        name="latents_back",
    )(*args)


def strip_fold_start(place, sems, flat, first, size, got):
    half = size // 2
    return sems.copy(
        flat.at[pl.ds(pl.multiple_of(first + (1 - place.core) * half, 16), half)], got, place.sibling
    )


def strip_cross_start(place, sems, copy, flat, first, size, got, both, cross):
    copy.wait()
    half = size // 2
    own = flat[pl.ds(pl.multiple_of(first + place.core * half, 16), half)]
    both[...] = (own.astype(F32) + got[...].astype(F32)).astype(BF)
    return sems.copy(rows_of(both, 1 - place.x, half // 2), cross, place.partner)


def strip_share(place, copy, both, cross):
    copy.wait()
    own = rows_of(both, place.x, cross.shape[0])[...]
    return (own.astype(F32) + cross[...].astype(F32)).astype(BF)


def padded_share(ref, parts):
    share = jnp.concatenate(parts, axis=0)
    spare = ref.shape[0] - share.shape[0]
    if spare:
        share = jnp.concatenate([share, jnp.zeros((spare, 256), BF)], axis=0)
    ref[...] = share


def enc_bwd_kernel(
    count, xp, z1, z2, z3, z4, df, u2, u3, u4, b, dec, d_piece, l_both, t_half,
    d_total, l_total, t_total, early, late, grad_out,
    m1, m2, m3, s1, s2, s3, s4, yt, pk, dx, got, rows_out,
    l_slots, l_piece,
    e_fold, e_sum, e_cross, e_values, e_near, e_both, e_slots, e_piece,
    f_fold, f_sum, f_cross, f_values, f_slots, f_piece,
    remote, here,
):
    place = Place(count)
    near, core, x = place.near, place.core, place.x
    sems = Sems(remote, here)
    row_places = [lax.rem(place.row + k, count) for k in range(1, count)]
    row_devices = [(at, place.me) for at in row_places]
    cross_device = (place.near_device[0], place.partner[1])
    place.greet(place.others + row_devices + [cross_device])

    def home(ref):
        return rows_of(ref, near, ref.shape[0] // 2)

    def waits(copies):
        for one in copies:
            one.wait()

    l_far = far_start(place, sems, l_both, l_slots)
    t_own = sems.here(t_half, home(t_total))
    t_last = last_start(place, sems, t_half, t_total)

    zero_big(m1, 32)
    zero_big(m2, 16)
    zero_big(m3, 8)
    zero_small(s1, 32, 0)
    zero_small(s2, 16, 128)
    zero_small(s3, 8, 128)
    zero_small(s4, 4, 256)
    swap = exchange_16()
    z = z4[...].astype(F32)
    s = sig(z)
    s4[1:5, :, 256:1280] = (df[...].astype(F32) * (s * (1.0 + z * (1.0 - s)))).astype(BF)

    def back(z_ref, m, dst, pad):
        def emit(m0, odd, q, acc):
            for t in range(acc.shape[0]):
                h = 2 * (m0 + t) + odd
                zz = z_ref[h, :, 256 * q : 256 * q + 256].astype(F32)
                ss = sig(zz)
                mm = zz * ss
                dst[h + 1, :, pad + 256 * q : pad + 256 * q + 256] = (
                    acc[t] * (ss + mm * (1.0 - ss))
                ).astype(BF)
                m[m0 + t + odd, 1 - odd, :, 128 + 256 * q : 384 + 256 * q] = mm.astype(BF)

        return emit

    up(s4, u4, 4, 4, back(z3, m3, s3, 128))
    turn(s4, yt, 4, 256)
    pack(pk, 0, 1, 128, 256, grad_w(m3, yt, 4), False, swap, True)
    up(s3, u3, 8, 4, back(z2, m2, s2, 128))
    turn(s3, yt, 8, 128)
    pack(pk, 2048, 2, 64, 128, grad_w(m2, yt, 8), False, swap)
    e_copy = strip_fold_start(place, sems, pk, 0, 2560, e_fold)
    far_end(place, l_far, l_both, l_slots, l_piece)
    l_back = [back_part(place, sems, l_piece, home(l_total), part) for part in range(2)]
    e_copy = strip_cross_start(place, sems, e_copy, pk, 0, 2560, e_fold, e_sum, e_cross)
    up(s2, u2, 16, 4, back(z1, m1, s1, 0))
    padded_share(e_values, [dec[...], strip_share(place, e_copy, e_sum, e_cross)])
    e_copy = near_start(place, sems, e_values, e_near)

    def put(i0, acc):
        dx[pl.ds(i0, acc.shape[0])] = acc.astype(BF)

    outer_up(s1, b, put)
    strips = [
        sems.copy(dx.at[pl.ds(8 * device[1], 8)], got.at[place.me], device)
        for device in place.others
    ]
    got[place.me] = dx[pl.ds(8 * place.me, 8)]
    near_end(place, e_copy, e_values, e_near, e_both)
    e_far = far_start(place, sems, e_both, e_slots)
    waits(l_back[0])
    l_last = last_part(place, sems, home(l_total), l_piece.shape[0], 0)
    turn(s2, yt, 16, 128)
    pack(pk, 2560, 4, 32, 64, grad_w(m1, yt, 16), False, swap)
    far_end(place, e_far, e_both, e_slots, e_piece)
    e_out = early.at[core, x]
    e_back = back_start(place, sems, e_piece, home(e_out))
    waits(l_back[1])
    l_last = l_last + last_part(place, sems, home(l_total), l_piece.shape[0], 1)
    d_back = [back_part(place, sems, d_piece, home(d_total), part) for part in range(2)]
    turn(s1, yt, 32, 0)
    pack_outer(pk, 2688, outer_grad(xp, yt), False)
    f_copy = strip_fold_start(place, sems, pk, 2560, 256, f_fold)
    waits(e_back)
    e_last = [
        sems.copy(home(e_out), home(e_out), device)
        for device in (place.near_device, place.partner, cross_device)
    ]
    f_copy = strip_cross_start(place, sems, f_copy, pk, 2560, 256, f_fold, f_sum, f_cross)
    waits(strips)
    stores = []

    def turn_out(first, count_here):
        for i in range(first, first + count_here):
            slot = i % 2
            if i > 1:
                stores[i - 2].wait()
            block = jnp.concatenate([got[(k % 2) * 2 + k // 2, i] for k in range(4)], axis=0)
            flat = block.T.astype(F32)
            for p in range(2):
                for c in range(3):
                    rows_out[slot, c, p] = flat[64 * (3 * p + c) : 64 * (3 * p + c) + 64]
            stores.append(sems.here(rows_out.at[slot], grad_out.at[:, 2 * i : 2 * i + 2]))

    turn_out(0, 4)
    waits(d_back[0])
    d_last = last_part(place, sems, home(d_total), d_piece.shape[0], 0)
    padded_share(f_values, [strip_share(place, f_copy, f_sum, f_cross)])
    each = f_piece.shape[0]
    f_rows = [
        sems.copy(rows_of(f_values, at, each), f_slots.at[k], device)
        for k, (at, device) in enumerate(zip(row_places, row_devices))
    ]
    turn_out(4, 4)
    waits(f_rows)
    whole = rows_of(f_values, place.row, each)[...].astype(F32)
    for k in range(count - 1):
        whole = whole + f_slots[k].astype(F32)
    f_piece[...] = whole.astype(BF)
    f_out = rows_of(late.at[core, x], place.row, each)
    f_back = [sems.here(f_piece, f_out)]
    f_back = f_back + [sems.copy(f_piece, f_out, device) for device in row_devices]
    waits(d_back[1])
    d_last = d_last + last_part(place, sems, home(d_total), d_piece.shape[0], 1)
    waits(e_last)
    e_side = sems.copy(early.at[core], early.at[core], place.sibling)
    waits(f_back)
    f_cross_out = sems.copy(late.at[core, x], late.at[core, x], place.partner)
    f_cross_out.wait()
    f_side = sems.copy(late.at[core], late.at[core], place.sibling)
    waits(stores[-2:])
    t_own.wait()
    waits([t_last, e_side, f_side] + d_last + l_last)


def share_rows(rows, count):
    return rows + -rows % (16 * count)


def enc_bwd(maps, dec, d_piece, l_both, t_half):
    count = lax.axis_size("rows")
    half = count // 2
    dma = pltpu.SemaphoreType.DMA
    any_spec = pl.BlockSpec(memory_space=pl.ANY)
    head = 2 * l_both.shape[0]
    quarter = dec.shape[0]
    early = share_rows(quarter + 640, count)
    late = share_rows(64, count)

    def steps(rows):
        return [
            V((rows, 256)),
            V((rows // 2, 256)),
            V((rows // 2, 256)),
            V((half - 1, rows // count, 256)),
            V((rows // count, 256)),
        ]

    d_total, l_total, t_total, e_out, f_out, grad_out = pl.pallas_call(
        functools.partial(enc_bwd_kernel, count),
        out_shape=(
            S((head, 256)),
            S((head, 256)),
            S((2 * t_half.shape[0], 512)),
            S((2, 2, early, 256)),
            S((2, 2, late, 256)),
            S((3, 16, 64, 256), F32),
        ),
        in_specs=VM(len(maps) + 4),
        out_specs=tuple([any_spec] * 6),
        scratch_shapes=[
            big(32),
            big(16),
            big(8),
            small(32, 0),
            small(16, 128),
            small(8, 128),
            small(4, 256),
            V((1024, 32 * NF)),
            V((2816, 256)),
            V((32, NF, 384)),
            V((4, 8, NF, 384)),
            V((2, 3, 2, 64, 256), F32),
            *steps(head)[3:],
            V((1280, 256)),
            V((1280, 256)),
            V((640, 256)),
            *steps(early),
            V((128, 256)),
            V((128, 256)),
            V((64, 256)),
            V((late, 256)),
            V((count - 1, late // count, 256)),
            V((late // count, 256)),
            dma((2, 7 * (half - 1) + 4 * half + 2 * (count - 1) + 15)),
            dma((18,)),
        ],
        compiler_params=pltpu.CompilerParams(
            collective_id=2, has_side_effects=True, vmem_limit_bytes=60 * MIB
        ),
        cost_estimate=estimate(110),
        name="encode_back",
    )(*maps, dec, d_piece, l_both, t_half)
    return d_total, l_total, t_total, e_out, f_out, jnp.transpose(grad_out, (3, 0, 1, 2))


def unpack_kernel(
    layers, quarter, d_total, l_total, upper, lower, early, late,
    latent_out, head_out, down_out, up_out, project_out, qkv_out, embed_out, rest_out, *outs,
):
    kernels, scratch, sems = outs[:8], outs[8:-1], outs[-1]
    (
        latent_v, head_v, down_v, up_v, project_v, qkv_v, embed_v, rest_v, *kernel_v
    ) = scratch
    stores = []

    def store(src, dst):
        one = pltpu.make_async_copy(src, dst, sems.at[len(stores)])
        one.start()
        stores.append(one)

    for k in range(layers):
        src, base = (upper, LAYER_ROWS * (k - 1)) if k else (lower, 0)
        down_v[k] = src[base : base + 512].astype(F32)
        up_v[k] = src[base + 512 : base + 1024].astype(F32)
        project_v[k] = src[base + 1024 : base + 1152].astype(F32)
        for part in range(3):
            first = base + 1152 + 128 * part
            for b in range(4):
                qkv_v[k, part, 128 * b : 128 * b + 128] = src[
                    first : first + 128, 128 * b : 128 * b + 128
                ].astype(F32)
    embed_v[...] = lower[LAYER_ROWS : LAYER_ROWS + 256].astype(F32)
    rest_v[...] = lower[LAYER_ROWS + 256 : LAYER_ROWS + 256 + NF + 16].astype(F32)
    for src, dst in (
        (down_v, down_out), (up_v, up_out), (project_v, project_out), (qkv_v, qkv_out),
        (embed_v, embed_out), (rest_v, rest_out),
    ):
        store(src, dst)
    for b in range(16):
        rows = slice(256 * b, 256 * b + 256)
        head_v[:, rows] = d_total[rows].astype(F32)
        latent_v[rows] = l_total[rows].astype(F32)
    store(head_v, head_out)
    store(latent_v, latent_out)

    def piece(first, is_enc):
        if not is_enc:
            at, place = divmod(first, quarter)
            return early[at // 2, at % 2, place : place + 64].astype(F32)
        if first < 2560:
            at, place = divmod(first, 640)
            return early[at // 2, at % 2, quarter + place : quarter + place + 64].astype(F32)
        at = (first - 2560) // 64
        return late[at // 2, at % 2, 0:64].astype(F32)

    for is_enc in (False, True):
        outer, first, second, third = kernel_v[4:] if is_enc else kernel_v[:4]
        for r in range(0, 2048, 64):
            value = piece(r, is_enc)
            if is_enc:
                third[r : r + 64] = value[:, :128]
                third[2048 + r : 2048 + r + 64] = value[:, 128:]
            else:
                third[r : r + 64] = value
        for r in range(0, 512, 64):
            value = piece(2048 + r, is_enc)
            second[r : r + 64] = value[:, :128]
            second[512 + r : 512 + r + 64] = value[:, 128:]
        for r in range(0, 128, 64):
            value = piece(2560 + r, is_enc)
            for k in range(4):
                first[128 * k + r : 128 * k + r + 64] = value[:, 64 * k : 64 * k + 64]
        outer[...] = piece(2688, is_enc)[:48, :32]
        for src, dst in zip(kernel_v[4:] if is_enc else kernel_v[:4], kernels[4:] if is_enc else kernels[:4]):
            store(src, dst)
    for one in stores:
        one.wait()


def unpack(layers, quarter, *args):
    dma = pltpu.SemaphoreType.DMA
    any_spec = pl.BlockSpec(memory_space=pl.ANY)
    shapes = [
        (4096, 256),
        (256, 4096),
        (layers, 512, 512),
        (layers, 512, 512),
        (layers, 128, 512),
        (layers, 3, 512, 128),
        (256, 512),
        (NF + 16, 512),
        (48, 32),
        (512, 64),
        (1024, 128),
        (2048, 256),
        (48, 32),
        (512, 64),
        (1024, 128),
        (4096, 128),
    ]
    return pl.pallas_call(
        functools.partial(unpack_kernel, layers, quarter),
        out_shape=tuple(S(shape, F32) for shape in shapes),
        in_specs=VM(len(args)),
        out_specs=tuple([any_spec] * len(shapes)),
        scratch_shapes=[V(shape, F32) for shape in shapes] + [dma((len(shapes),))],
        compiler_params=pltpu.CompilerParams(vmem_limit_bytes=56 * MIB),
        cost_estimate=estimate(12),
        name="unpack",
    )(*args)


def beside(value):
    return lax.ppermute(value, "strip", [(0, 1), (1, 0), (2, 3), (3, 2)])


def make_mask(segment_ids):
    places = jnp.arange(segment_ids.shape[1])
    causal = places[:, None] >= places[None, :]
    return causal[None] & (segment_ids[:, :, None] == segment_ids[:, None, :])


def shards(
    frames,
    segment_ids,
    encode_one,
    encode_two,
    encode_three,
    encode_four,
    latent_head,
    token_embed,
    positions,
    norm_gains,
    qkv_weight,
    out_weight,
    up_weight,
    down_weight,
    decode_head,
    decode_one,
    decode_two,
    decode_three,
    decode_four,
    token_cotangent,
    frame_cotangent,
):
    strip = lax.axis_index("strip")
    x, core = strip // 2, strip % 2
    layers = qkv_weight.shape[0]

    kernels = (
        encode_one,
        encode_two,
        encode_three,
        encode_four,
        decode_one,
        decode_two,
        decode_three,
        decode_four,
    )
    qkv = jnp.transpose(qkv_weight, (0, 2, 1, 3))
    shards_here = (token_embed, qkv, out_weight, up_weight, down_weight)
    pixels, enc_f, dec_f, head_in, head_out, theirs, hints = start(
        frames, frame_cotangent, kernels, latent_head, decode_head, shards_here
    )
    enc_a, enc_b, enc_t, enc_u = enc_f[0], enc_f[1], enc_f[2:5], enc_f[5:8]
    dec_a, dec_b, dec_t, dec_u = dec_f[0], dec_f[1], dec_f[2:5], dec_f[5:8]
    embed, qkv, project, widen, narrow = zip(shards_here, theirs)
    z1, z2, z3, z4, feat = enc_fwd(pixels, enc_a, *enc_t)

    first = 2 * core

    def mine(array, size):
        own = lax.dynamic_slice_in_dim(array, (first + x) * size, size)
        other = lax.dynamic_slice_in_dim(array, (first + 1 - x) * size, size)
        return jnp.concatenate([own, other], axis=0)

    allowed = make_mask(mine(segment_ids, 1)).astype(F32)
    blank = jnp.zeros((NF, NF), F32)
    allowed = jnp.concatenate(
        [
            jnp.concatenate([allowed[0], blank], axis=1),
            jnp.concatenate([blank, allowed[1]], axis=1),
        ],
        axis=0,
    )
    (
        tokens, latent, chances, decoded, upper, lower, grad_latent, feat_got,
        latent_near, feat_near, got_near,
    ) = middle(
        layers,
        feat,
        *head_in,
        *head_out,
        *embed,
        positions,
        norm_gains.reshape(2 * layers, -1),
        allowed,
        mine(token_cotangent, NF),
        *qkv,
        *project,
        *widen,
        *narrow,
    )
    tokens = jnp.where(
        x == 0, tokens, jnp.concatenate([tokens[NF:], tokens[:NF]], axis=0)
    )
    other_tokens = beside(tokens)
    tokens_out = jnp.where(
        core == 0,
        jnp.concatenate([tokens, other_tokens]),
        jnp.concatenate([other_tokens, tokens]),
    )

    recon_pairs, p3, p2, p1, upper, lower = dec_fwd(
        decoded, dec_u[2], dec_u[1], dec_u[0], dec_b, upper, lower
    )
    recon_parts = blocks_around(recon_pairs, strip)
    g_decoded, dec_flat, upper, lower = dec_bwd(
        hints, decoded, p3, p2, p1, dec_a, *dec_t, upper, lower
    )
    recon_parts, g_decoded = lax.optimization_barrier((recon_parts, g_decoded))
    recon = frames_out_later(recon_parts)
    g_feat, dec_share, d_piece, l_both, upper, lower = latents_back(
        g_decoded, latent, latent_near, chances, grad_latent, feat, feat_got, feat_near, got_near,
        *head_in, *head_out, dec_flat, upper, lower,
    )

    d_total, l_total, lower, early, late, frames_grad = enc_bwd(
        (pixels, z1, z2, z3, z4, g_feat, *enc_u, enc_b), dec_share, d_piece, l_both, lower
    )
    (
        g_latent_head, g_decode_head, g_down, g_up, g_out, g_qkv, g_embed, g_rest,
        d_four, d_three, d_two, d_one, e_one, e_two, e_three, e_four,
    ) = unpack(layers, dec_share.shape[0], d_total, l_total, upper, lower, early, late)

    def of_input(rows, count):
        return rows.reshape(count, 4, 4, -1).transpose(3, 0, 1, 2)

    def of_output(rows, count):
        return rows.reshape(count, 4, 4, -1).transpose(0, 3, 1, 2)

    return (
        tokens_out,
        recon,
        frames_grad,
        of_input(e_one, 3),
        of_input(e_two, 32),
        of_input(e_three, 64),
        of_output(e_four, 256),
        g_latent_head,
        g_embed,
        g_rest[:NF],
        g_rest[NF : NF + 2 * layers].reshape(norm_gains.shape),
        g_qkv.transpose(0, 2, 1, 3),
        g_out,
        g_up,
        g_down,
        g_decode_head,
        of_output(d_one, 128),
        of_output(d_two, 64),
        of_output(d_three, 32),
        of_output(d_four, 3),
    )


def solution(mesh):
    placed = (
        P("rows", None, "strip", None),
        P("rows", None),
        P(),
        P(),
        P(),
        P(),
        P(None, "strip"),
        P("strip", None),
        P(),
        P(),
        P(None, None, None, "strip"),
        P(None, "strip", None),
        P(None, None, "strip"),
        P(None, "strip", None),
        P("strip", None),
        P(),
        P(),
        P(),
        P(),
        P("rows", None),
        P("rows", None, "strip", None),
    )
    return jax.shard_map(
        shards,
        mesh=mesh,
        in_specs=placed,
        out_specs=(
            P("rows", None),
            P("rows", None, "strip", None),
            P("rows", None, "strip", None),
            P(),
            P(),
            P(),
            P(),
            P(None, "strip"),
            P("strip", None),
            P(),
            P(),
            P(None, None, None, "strip"),
            P(None, "strip", None),
            P(None, None, "strip"),
            P(None, "strip", None),
            P("strip", None),
            P(),
            P(),
            P(),
            P(),
        ),
        check_vma=False,
    )
```

```python
import functools

import jax
import jax.numpy as jnp
from jax import lax
from jax.experimental import pallas as pl
from jax.experimental.pallas import tpu as pltpu
from jax.sharding import PartitionSpec as P

HEAD_DIM = 64
LCLASS = 32
EPS = 1e-05
SCALE = 0.125
NEG = -1e30
F32 = jnp.float32
BF = jnp.bfloat16
NF = 64
MIB = 1 << 20
MESH = pl.DeviceIdType.MESH


def sig(z): return 0.5*jnp.tanh(0.5*z)+0.5

def zero_big(ref,rows):
    z=jnp.zeros((NF,1280),BF)
    ref[0,0]=z; ref[rows//2,1]=z
    e=jnp.zeros((rows//2+1,2,NF,128),BF)
    ref[:,:,:,0:128]=e; ref[:,:,:,1152:1280]=e

def zero_small(ref,rows,pad):
    z=jnp.zeros((NF,1024+2*pad),BF)
    ref[0]=z; ref[rows+1]=z
    if pad:
        e=jnp.zeros((rows+2,NF,pad),BF)
        ref[:,:,0:pad]=e; ref[:,:,1024+pad:]=e

def put_big(ref,half0,rows,q,val):
    v=val.reshape(rows,NF,256)
    for t in range(rows):
        ref[half0+(t+1)//2,(t+1)%2,:,128+256*q:384+256*q]=v[t]

def loop(n,body):
    if n==1: body(0)
    else:
        def step(g,c):
            body(g); return c
        lax.fori_loop(0,n,step,0)

def down(src,t_ref,rows,per,emit):
    def body(g):
        i0=g*per
        for q in range(4):
            lhs=jnp.concatenate([src[pl.ds(i0+kh//2,per),kh%2,:,256*q:256*q+512].reshape(per*NF,512) for kh in range(4)],axis=1)
            emit(i0,g*(per//2),q,jnp.dot(lhs,t_ref[...],preferred_element_type=F32))
    loop(rows//per,body)

def up(src,u_ref,rows,per,emit):
    k=u_ref.shape[1]//2
    def body(g):
        m0=g*per
        for q in range(4):
            for odd in range(2):
                lhs=jnp.concatenate([src[pl.ds(m0+1+odd-s,per),:,256*q:256*q+k].reshape(per*NF,k) for s in range(2)],axis=1)
                emit(m0,odd,q,jnp.dot(lhs,u_ref[odd],preferred_element_type=F32).reshape(per,NF,256))
    loop(rows//per,body)

def turn(src,dst,rows,pad):
    for q in range(4):
        dst[256*q:256*q+256,:rows*NF]=src[1:rows+1,:,pad+256*q:pad+256*q+256].reshape(rows*NF,256).T

def grad_w(big,yt,rows):
    out=[]
    for kh in range(4):
        acc=jnp.zeros((256,512),F32)
        for q in range(4):
            win=big[pl.ds(kh//2,rows),kh%2,:,256*q:256*q+512].reshape(rows*NF,512)
            acc=acc+jnp.dot(yt[256*q:256*q+256,:rows*NF],win,preferred_element_type=F32)
        out.append(acc)
    return out

def pack(pk,base,a,c,o,sums,flipped,swap,turned=False):
    taps=[]
    for acc in sums:
        total=None
        for j in range(a):
            first=(a+2*j-1)*c
            part=acc[j*o:j*o+o]
            if first: part=pltpu.roll(part,512-first,1)
            part=part[:,:4*c]
            total=part if total is None else total+part
        taps.append(total.astype(BF) if turned else total.T.astype(BF))
    width,count=(c,o//16) if turned else (o,c//16)
    held=[]
    for b in range(count):
        rows=[]
        for k in range(16):
            kh,kw=divmod(15-k if flipped else k,4)
            if turned: rows.append(taps[kh][16*b:16*b+16,c*kw:c*kw+c])
            else: rows.append(taps[kh][c*kw+16*b:c*kw+16*b+16])
        block=jnp.dot(swap,jnp.concatenate(rows,axis=0),preferred_element_type=F32).astype(BF)
        if width==256: pk[base+256*b:base+256*b+256]=block
        elif width==128:
            side,at=divmod(b,count//2)
            pk[base+256*at:base+256*at+256,128*side:128*side+128]=block
        else: held.extend([block[:128],block[128:]])
    if held: pk[base:base+128]=jnp.concatenate(held,axis=1)

def pack_outer(pk,base,red,flipped):
    r=lax.broadcasted_iota(jnp.int32,(48,1152),0); lane=lax.broadcasted_iota(jnp.int32,(48,1152),1)
    k=lax.rem(r,16)
    if flipped: k=15-k
    kh,kw=lax.div(k,4),lax.rem(k,4)
    at=384*lax.div(kh+1,2)+192*lax.rem(kh+1,2)+64*lax.div(r,16)+kw
    pick=(lane==at).astype(BF)
    value=jnp.concatenate([part.astype(BF) for part in red],axis=1)
    pk[base:base+128]=jnp.zeros((128,256),BF)
    pk[base:base+48,0:32]=lax.dot_general(pick,value,(((1,),(1,)),((),())),preferred_element_type=F32).astype(BF)

def outer_down(xp,a_ref,emit,per=4):
    def body(g):
        i0=g*per
        lhs=jnp.concatenate([xp[pl.ds(i0+d,per)].reshape(per*NF,384) for d in range(3)],axis=1)
        for q in range(4):
            emit(i0,g*(per//2),q,jnp.dot(lhs,a_ref[:,256*q:256*q+256],preferred_element_type=F32))
    loop(32//per,body)

def outer_up(yp,b_ref,emit,per=4):
    def body(g):
        i0=g*per
        lhs=jnp.concatenate([yp[pl.ds(i0+2-d,per)].reshape(per*NF,1024) for d in range(3)],axis=1)
        emit(i0,jnp.dot(lhs,b_ref[...],preferred_element_type=F32).reshape(per,NF,384))
    loop(32//per,body)

def outer_grad(xp,yt):
    red=[]
    lane=lax.broadcasted_iota(jnp.int32,(32,384),1)%64
    for d in range(3):
        x=xp[d:d+32].reshape(32*NF,384)
        tot=jnp.zeros((32,384),F32)
        for jb in range(4):
            g=jnp.dot(yt[256*jb:256*jb+256,:],x,preferred_element_type=F32)
            for jj in range(8):
                j=8*jb+jj
                v=pltpu.roll(g[32*jj:32*jj+32],(385-2*j)%384,1)
                if j==0: v=jnp.where(lane==0,0.0,v)
                if j==31: v=jnp.where(lane==3,0.0,v)
                tot=tot+v
        red.append(tot)
    return red

def enc_fwd_kernel(xp,a,t2,t3,t4,z1,z2,z3,z4,feat,m1,m2,m3):
    zero_big(m1,32); zero_big(m2,16); zero_big(m3,8)
    def keep(z,m):
        def emit(i0,half0,q,acc):
            rows=acc.shape[0]//NF
            z[pl.ds(i0,rows),:,256*q:256*q+256]=acc.astype(BF).reshape(rows,NF,256)
            val=(acc*sig(acc)).astype(BF)
            if m is None: feat[pl.ds(i0,rows),:,256*q:256*q+256]=val.reshape(rows,NF,256)
            else: put_big(m,half0,rows,q,val)
        return emit
    outer_down(xp,a,keep(z1,m1))
    down(m1,t2,16,4,keep(z2,m2))
    down(m2,t3,8,4,keep(z3,m3))
    down(m3,t4,4,4,keep(z4,None))

def dec_kernel(count,c0,c1,c2,c3,dec,u4,u3,u2,b,a,t2,t3,t4,upper_both,lower,
               gdec,pk,recon_out,upper_total,got,lower_piece,
               p3,p2,p1,s4,s3,s2,s1,d1,d2,d3,cp,yt,recon,
               upper_slots,upper_piece,rows_out,lower_near,lower_both,lower_slots,remote,here):
    place=Place(count); sems=Sems(remote,here); me=place.me
    place.greet(place.others+[place.near_device]+place.far_devices)
    upper_far=far_start(place,sems,upper_both,upper_slots)
    lower_copy=near_start(place,sems,lower,lower_near)
    lower_own=sems.here(rows_of(lower,place.near,lower.shape[0]//2),lower_both)
    zero_small(s1,32,0); zero_small(s2,16,128); zero_small(s3,8,128); zero_small(s4,4,256)
    zero_big(d1,32); zero_big(d2,16); zero_big(d3,8)
    z=dec[...].astype(F32)
    s4[1:5,:,256:1280]=(z*sig(z)).astype(BF)
    def fwd(p,dst,pad):
        def emit(m0,odd,q,acc):
            for t in range(acc.shape[0]):
                h=2*(m0+t)+odd
                v=acc[t]
                p[h,:,256*q:256*q+256]=v.astype(BF)
                dst[h+1,:,pad+256*q:pad+256*q+256]=(v*sig(v)).astype(BF)
        return emit
    up(s4,u4,4,4,fwd(p3,s3,128))
    up(s3,u3,8,4,fwd(p2,s2,128))
    up(s2,u2,16,4,fwd(p1,s1,0))
    far_end(place,upper_far,upper_both,upper_slots,upper_piece)
    upper_home=rows_of(upper_total,place.near,upper_total.shape[0]//2)
    upper_back=back_start(place,sems,upper_piece,upper_home)
    def put(i0,acc): recon[pl.ds(i0,acc.shape[0])]=acc.astype(BF)
    outer_up(s1,b,put)
    strips=[sems.copy(recon.at[pl.ds(8*device[1],8)],got.at[pl.ds(8*me,8)],device) for device in place.others]
    cp[0]=jnp.zeros((NF,384),BF); cp[33]=jnp.zeros((NF,384),BF)
    for k,part in enumerate((c0,c1,c2,c3)): cp[pl.ds(1+8*lax.rem(me+4-k,4),8)]=part[...]
    swap=exchange_16()
    def back(p,dst):
        def emit(i0,half0,q,acc):
            rows=acc.shape[0]//NF
            zz=p[pl.ds(i0,rows),:,256*q:256*q+256].astype(F32).reshape(rows*NF,256)
            ss=sig(zz)
            val=(acc*(ss*(1.0+zz*(1.0-ss)))).astype(BF)
            if dst is None: gdec[pl.ds(i0,rows),:,256*q:256*q+256]=val.reshape(rows,NF,256)
            else: put_big(dst,half0,rows,q,val)
        return emit
    lower_own.wait(); lower_copy.wait()
    lower_both[...]=(lower_both[...].astype(F32)+lower_near[...].astype(F32)).astype(BF)
    turn(s1,yt,32,0); pack_outer(pk,2688,outer_grad(cp,yt),True)
    for one in upper_back: one.wait()
    upper_last=last_start(place,sems,upper_home,upper_total)
    lower_far=far_start(place,sems,lower_both,lower_slots)
    outer_down(cp,a,back(p1,d1))
    turn(s2,yt,16,128); pack(pk,2560,4,32,64,grad_w(d1,yt,16),True,swap)
    down(d1,t2,16,4,back(p2,d2))
    for one in strips: one.wait()
    arrived=[sems.here(got.at[pl.ds(8*device[1],8)],recon.at[pl.ds(8*device[1],8)]) for device in place.others]
    for one in arrived: one.wait()
    stores=[]
    for i in range(8):
        if i: stores[i-1].wait()
        block=jnp.concatenate([recon[8*((k%2)*2+k//2)+i] for k in range(4)],axis=0).T
        for p in range(2):
            for c in range(3): rows_out[c,p]=block[64*(3*p+c):64*(3*p+c)+64]
        stores.append(sems.here(rows_out,recon_out.at[:,2*i:2*i+2]))
    turn(s3,yt,8,128); pack(pk,2048,2,64,128,grad_w(d2,yt,8),True,swap)
    down(d2,t3,8,4,back(p3,d3))
    turn(s4,yt,4,256); pack(pk,0,1,128,256,grad_w(d3,yt,4),True,swap)
    down(d3,t4,4,4,back(dec,None))
    pk[2816-80:2816]=jnp.zeros((80,256),BF)
    far_end(place,lower_far,lower_both,lower_slots,lower_piece)
    for one in stores[-1:]+[upper_last]: one.wait()

def estimate(us):
    return pl.CostEstimate(flops=us*1150*10**6,bytes_accessed=MIB,transcendentals=0)

def S(shape,dt=BF): return jax.ShapeDtypeStruct(shape,dt)
def V(shape,dt=BF): return pltpu.VMEM(shape,dt)
VM=lambda n:[pl.BlockSpec(memory_space=pltpu.VMEM)]*n
def run(kernel,outs,scratch,args,name,us,lim=60,ident=None):
    extra={} if ident is None else dict(collective_id=ident,has_side_effects=True)
    return pl.pallas_call(kernel,out_shape=outs,in_specs=VM(len(args)),out_specs=tuple(VM(len(outs))),
        scratch_shapes=scratch,compiler_params=pltpu.CompilerParams(vmem_limit_bytes=lim*MIB,**extra),
        cost_estimate=estimate(us),name=name)(*args)
big=lambda h:V((h//2+1,2,NF,1280))
def enc_fwd(xp,a,t2,t3,t4):
    return run(enc_fwd_kernel,(S((32,NF,1024)),S((16,NF,1024)),S((8,NF,1024)),S((4,NF,1024)),S((4,NF,1024))),
      [big(32),big(16),big(8)],(xp,a,t2,t3,t4),"encode",22)
small=lambda h,p:V((h+2,NF,1024+2*p))
def enc_fwd(xp,a,t2,t3,t4):
    return run(enc_fwd_kernel,(S((32,NF,1024)),S((16,NF,1024)),S((8,NF,1024)),S((4,NF,1024)),S((4,NF,1024))),
      [big(32),big(16),big(8)],(xp,a,t2,t3,t4),"encode",22)
small=lambda h,p:V((h+2,NF,1024+2*p))
yts=[V((1024,32*NF)),V((1024,16*NF)),V((1024,8*NF)),V((1024,4*NF))]
def decode(hints,dec,u4,u3,u2,b,a,t2,t3,t4,upper_both,lower):
    count=lax.axis_size("rows"); half=count//2
    upper,rows=2*upper_both.shape[0],lower.shape[0]
    dma=pltpu.SemaphoreType.DMA
    args=(*hints,dec,u4,u3,u2,b,a,t2,t3,t4,upper_both,lower)
    return pl.pallas_call(
        functools.partial(dec_kernel,count),
        out_shape=(S((4,NF,1024)),S((2816,256)),S((3,16,64,256)),S((upper,512)),S((32,NF,384)),S((rows//count,512))),
        in_specs=VM(len(args)-1)+[pl.BlockSpec(memory_space=pl.ANY)],
        out_specs=tuple(VM(2)+[pl.BlockSpec(memory_space=pl.ANY)]*3+VM(1)),
        scratch_shapes=[V((8,NF,1024)),V((16,NF,1024)),V((32,NF,1024)),small(4,256),small(8,128),small(16,128),small(32,0),
            big(32),big(16),big(8),V((34,NF,384)),V((1024,32*NF)),V((32,NF,384)),
            V((half-1,upper//count,512)),V((upper//count,512)),V((3,2,64,256)),
            V((rows//2,512)),V((rows//2,512)),V((half-1,rows//count,512)),
            dma((2,3*(half-1)+5)),dma((13,))],
        compiler_params=pltpu.CompilerParams(collective_id=5,has_side_effects=True,vmem_limit_bytes=60*MIB),
        cost_estimate=estimate(65),
        name="decode",
    )(*args)


def rows_of(ref, index, size):
    return ref.at[pl.ds(pl.multiple_of(index * size, 16), size)]


class Place:
    def __init__(self, count):
        self.me, self.row = lax.axis_index("strip"), lax.axis_index("rows")
        self.half = count // 2
        self.near, self.far = lax.rem(self.row, 2), lax.div(self.row, 2)
        self.core, self.x = lax.rem(self.me, 2), lax.div(self.me, 2)
        self.near_device = (self.row + 1 - 2 * self.near, self.me)
        self.sibling = (self.row, self.me + 1 - 2 * self.core)
        self.partner = (self.row, lax.rem(self.me + 2, 4))
        self.others = [(self.row, lax.rem(self.me + k, 4)) for k in range(1, 4)]
        self.far_places = [lax.rem(self.far + k, self.half) for k in range(1, self.half)]
        self.far_devices = [(2 * place + self.near, self.me) for place in self.far_places]

    def greet(self, devices):
        barrier = pltpu.get_barrier_semaphore()
        for device in devices:
            pl.semaphore_signal(barrier, inc=1, device_id=device, device_id_type=MESH)
        pl.semaphore_wait(barrier, len(devices))


class Sems:
    def __init__(self, remote, local):
        self.remote, self.local, self.used, self.used_here = remote, local, 0, 0

    def copy(self, src, dst, device):
        assert self.used < self.remote.shape[1]
        one = pltpu.make_async_remote_copy(
            src_ref=src,
            dst_ref=dst,
            send_sem=self.remote.at[0, self.used],
            recv_sem=self.remote.at[1, self.used],
            device_id=device,
            device_id_type=MESH,
        )
        self.used = self.used + 1
        one.start()
        return one

    def here(self, src, dst):
        assert self.used_here < self.local.shape[0]
        one = pltpu.make_async_copy(src, dst, self.local.at[self.used_here])
        self.used_here = self.used_here + 1
        one.start()
        return one


def near_start(place, sems, values, arrived):
    half = values.shape[0] // 2
    return sems.copy(rows_of(values, 1 - place.near, half), arrived, place.near_device)


def near_end(place, copy, values, arrived, both):
    copy.wait()
    half = values.shape[0] // 2
    total = rows_of(values, place.near, half)[...].astype(F32) + arrived[...].astype(F32)
    both[...] = total.astype(BF)


def far_start(place, sems, both, slots):
    each = slots.shape[1]
    return [
        sems.copy(rows_of(both, at, each), slots.at[k], device)
        for k, (at, device) in enumerate(zip(place.far_places, place.far_devices))
    ]


def far_end(place, copies, both, slots, piece):
    for one in copies:
        one.wait()
    total = rows_of(both, place.far, slots.shape[1])[...].astype(F32)
    for k in range(slots.shape[0]):
        total = total + slots[k].astype(F32)
    piece[...] = total.astype(BF)


def back_start(place, sems, piece, home):
    out = rows_of(home, place.far, piece.shape[0])
    return [sems.here(piece, out)] + [sems.copy(piece, out, d) for d in place.far_devices]


def back_part(place, sems, piece, home, part):
    size = piece.shape[0] // 2
    src = piece.at[pl.ds(part * size, size)]
    first = place.far * piece.shape[0] + part * size
    out = home.at[pl.ds(pl.multiple_of(first, 16), size)]
    return [sems.here(src, out)] + [sems.copy(src, out, d) for d in place.far_devices]


def last_part(place, sems, home, each, part):
    size = each // 2
    refs = [home.at[pl.ds(each * k + part * size, size)] for k in range(place.half)]
    return [sems.copy(ref, ref, place.near_device) for ref in refs]


def half_lanes(place, w):
    return pl.ds(pl.multiple_of(256 * w + 128 * (1 - place.near), 128), 128)


def last_start(place, sems, home, out):
    half = out.shape[0] // 2
    return sems.copy(home, rows_of(out, place.near, half), place.near_device)


def exchange_16():
    r = lax.broadcasted_iota(jnp.int32, (256, 256), 0)
    s = lax.broadcasted_iota(jnp.int32, (256, 256), 1)
    return (s == lax.rem(r, 16) * 16 + lax.div(r, 16)).astype(BF)


def first_frame(strip):
    return NF * ((strip % 2) * 2 + strip // 2)


def turned_rows(x, i):
    return jnp.concatenate([x[c, 2 * i + p] for p in range(2) for c in range(3)], axis=0).T


def canonical(w, swap, c, o, flipped):
    parts = {}
    for b in range(c // 16):
        block = jnp.dot(swap, w[256 * b : 256 * b + 256, :], preferred_element_type=F32).astype(BF)
        for k in range(16):
            parts[(15 - k if flipped else k, b)] = block[16 * k : 16 * k + 16]
    return [
        jnp.concatenate(
            [parts[(4 * kh + kw, b)] for kw in range(4) for b in range(c // 16)], axis=0
        )
        for kh in range(4)
    ]


def canonical_turned(w, swap):
    parts = {}
    for b in range(16):
        block = jnp.dot(swap, w[256 * b : 256 * b + 256, :], preferred_element_type=F32).astype(BF)
        for k in range(16):
            parts[(k, b)] = block[16 * k : 16 * k + 16]
    return [
        jnp.concatenate(
            [
                jnp.concatenate([parts[(4 * kh + kw, b)] for b in range(16)], axis=0)
                for kw in range(4)
            ],
            axis=1,
        )
        for kh in range(4)
    ]


def band(flat, a, c, o):
    def shifted(value, first):
        above = jnp.zeros((first, value.shape[1]), BF)
        below = jnp.zeros((512 - first - value.shape[0], value.shape[1]), BF)
        return jnp.concatenate([above, value, below], axis=0)

    if a == 1:
        return flat
    if a == 2:
        return jnp.concatenate([shifted(flat, 64), shifted(flat, 192)], axis=1)
    twice = jnp.concatenate([flat, flat], axis=1)
    left = lax.broadcasted_iota(jnp.int32, (512, 128), 1) < 64
    return jnp.concatenate(
        [
            jnp.where(left, shifted(twice, 96), shifted(twice, 160)),
            jnp.where(left, shifted(twice, 224), shifted(twice, 288)),
        ],
        axis=1,
    )


def put_bands(t_ref, u_ref, bands, turned, a):
    for kh in range(4):
        t = bands[kh]
        t_ref[512 * kh : 512 * kh + 512] = t
        tt = t.T if turned is None else turned[kh]
        z = jnp.zeros((256, 128), BF)
        left = jnp.concatenate([tt[:, 384:512], z], axis=1)
        right = jnp.concatenate([z, tt[:, :128]], axis=1)
        if a > 1:
            left, right = left[128:], right[:128]
        k = 512 if a > 1 else 768
        u_ref[1 - kh % 2, k * (kh // 2) : k * (kh // 2) + k] = jnp.concatenate(
            [left, tt[:, 128:384], right], axis=0
        )


def put_outer(a_ref, b_ref, w, flipped):
    row = lax.broadcasted_iota(jnp.int32, (64, 1024), 0)
    col = lax.div(lax.broadcasted_iota(jnp.int32, (64, 1024), 1), 32)
    tap = row - 2 * col + 1
    for kh in range(4):
        d, p = (kh + 1) // 2, (kh + 1) % 2
        for c in range(3):
            total = jnp.zeros((64, 1024), F32)
            for kw in range(4):
                k = 4 * kh + kw
                r = 16 * c + (15 - k if flipped else k)
                total = jnp.where(tap == kw, w[r : r + 1, :], total)
            first = 384 * d + 192 * p + 64 * c
            a_ref[first : first + 64] = total.astype(BF)
    a_ref[0:192] = jnp.zeros((192, 1024), BF)
    a_ref[960:1152] = jnp.zeros((192, 1024), BF)
    for d in range(3):
        b_ref[1024 * d : 1024 * d + 1024] = a_ref[384 * d : 384 * d + 384].T


def start_kernel(
    x, later, e1, e2, e3, e4, lh, dh, emb, qkv, proj, up, down,
    pixels, ea, eb, et2, et3, et4, eu2, eu3, eu4,
    lh0, lh1, dh0, dh1, emb1, qkv1, proj1, up1, down1, t0, t1, t2, t3,
    stage, send_sem, recv_sem, side_sems,
    va, vb, vt2, vt3, vt4, vu2, vu3, vu4,
    vl, vd, out_sems,
):
    me = lax.axis_index("strip")
    row = lax.axis_index("rows")
    sibling = (row, me + 1 - 2 * lax.rem(me, 2))
    pixels[0] = jnp.zeros((NF, 384), BF)
    pixels[33] = jnp.zeros((NF, 384), BF)

    def turn_rows(i, carry):
        flat = turned_rows(x, i)
        for k in range(4):
            stage[k, i] = flat[first_frame(k) : first_frame(k) + NF]
        return carry

    barrier = pltpu.get_barrier_semaphore()
    for k in range(1, 4):
        pl.semaphore_signal(
            barrier, inc=1, device_id=(row, lax.rem(me + k, 4)), device_id_type=MESH
        )
    lax.fori_loop(0, 4, turn_rows, 0)
    pl.semaphore_wait(barrier, 3)
    copies = []

    def send(part):
        for k in range(1, 4):
            to = lax.rem(me + k, 4)
            copy = pltpu.make_async_remote_copy(
                src_ref=stage.at[to, pl.ds(4 * part, 4)],
                dst_ref=pixels.at[pl.ds(1 + 8 * me + 4 * part, 4)],
                send_sem=send_sem.at[3 * part + k - 1],
                recv_sem=recv_sem.at[3 * part + k - 1],
                device_id=(row, to),
                device_id_type=MESH,
            )
            copy.start()
            copies.append(copy)

    send(0)
    lax.fori_loop(4, 8, turn_rows, 0)
    send(1)

    def to_sibling(src, dst, index):
        copy = pltpu.make_async_remote_copy(
            src_ref=src,
            dst_ref=dst,
            send_sem=side_sems.at[0, index],
            recv_sem=side_sems.at[1, index],
            device_id=sibling,
            device_id_type=MESH,
        )
        copy.start()
        copies.append(copy)

    for index, (src, dst) in enumerate(
        ((emb, emb1), (qkv, qkv1), (proj, proj1), (up, up1), (down, down1))
    ):
        to_sibling(src, dst, index)
    pixels[pl.ds(1 + 8 * me, 8)] = stage[me]

    turn_kernel(later, t0, t1, t2, t3)
    stores = []

    def store(src, dst):
        copy = pltpu.make_async_copy(src, dst, out_sems.at[len(stores)])
        copy.start()
        stores.append(copy)

    swap = exchange_16()
    put_outer(va, vb, e1, False)
    store(va, ea)
    store(vb, eb)
    put_bands(vt2, vu2, [band(f, 4, 32, 64) for f in canonical(e2, swap, 32, 64, False)], None, 4)
    store(vt2, et2)
    store(vu2, eu2)
    put_bands(vt3, vu3, [band(f, 2, 64, 128) for f in canonical(e3, swap, 64, 128, False)], None, 2)
    store(vt3, et3)
    store(vu3, eu3)
    turned = canonical_turned(e4, swap)
    put_bands(vt4, vu4, [f.T for f in turned], turned, 1)
    store(vt4, et4)
    store(vu4, eu4)
    for b in range(16):
        rows = slice(256 * b, 256 * b + 256)
        for src, dst in ((lh[rows, :], vl), (dh[:, rows].T, vd)):
            block = jnp.dot(swap, src, preferred_element_type=F32).astype(BF)
            for k in range(16):
                dst[256 * k + 16 * b : 256 * k + 16 * b + 16] = block[16 * k : 16 * k + 16]
    store(vl, lh0)
    store(vd, dh0)
    to_sibling(vl, lh1, 5)
    to_sibling(vd, dh1, 6)
    for copy in copies:
        copy.wait()
    for copy in stores:
        copy.wait()


BUILT = [(1152, 1024), (3072, 384)] + [(2048, 256)] * 3
BUILT = BUILT + [(2, 1024, 256), (2, 1024, 256), (2, 1536, 256)]


def start(frames, later, kernels, latent_head, decode_head, others):
    e1, e2, e3, e4 = kernels
    rows_in = [
        jnp.tile(jnp.transpose(e1, (1, 2, 3, 0)).reshape(48, 32), (1, 32)).astype(F32),
        jnp.transpose(e2, (1, 2, 3, 0)).reshape(512, 64),
        jnp.transpose(e3, (1, 2, 3, 0)).reshape(1024, 128),
        jnp.transpose(e4, (0, 2, 3, 1)).reshape(4096, 128),
    ]
    dma = pltpu.SemaphoreType.DMA
    any_spec = pl.BlockSpec(memory_space=pl.ANY)
    heads = [(4096, 256)] * 4
    shapes = [(34, NF, 384)] + BUILT + heads + [w.shape for w in others]
    shapes = shapes + [(8, NF, 384)] * 4
    out = pl.pallas_call(
        start_kernel,
        out_shape=tuple(S(shape) for shape in shapes),
        in_specs=VM(8) + [any_spec] * len(others),
        out_specs=tuple(VM(1) + [any_spec] * (len(shapes) - 5) + VM(4)),
        scratch_shapes=[
            V((4, 8, NF, 384)),
            dma((6,)),
            dma((6,)),
            dma((2, 7)),
            *[V(shape) for shape in BUILT],
            V((4096, 256)),
            V((4096, 256)),
            dma((10,)),
        ],
        compiler_params=pltpu.CompilerParams(
            collective_id=1, has_side_effects=True, vmem_limit_bytes=56 * MIB
        ),
        cost_estimate=estimate(22),
        name="start",
    )(
        jnp.transpose(frames, (1, 2, 3, 0)),
        jnp.transpose(later, (1, 2, 3, 0)),
        *rows_in,
        latent_head,
        decode_head,
        *others,
    )
    hints = around(out[-4:])
    return out[0], out[1:9], out[9:11], out[11:13], out[13:-4], hints


def decoder_rows(kernels):
    d1, d2, d3, d4 = kernels
    return (
        jnp.transpose(d1, (0, 2, 3, 1)).reshape(2048, 256),
        jnp.transpose(d2, (0, 2, 3, 1)).reshape(1024, 128),
        jnp.transpose(d3, (0, 2, 3, 1)).reshape(512, 64),
        jnp.tile(jnp.transpose(d4, (0, 2, 3, 1)).reshape(48, 32), (1, 32)).astype(F32),
    )


def turn_kernel(x, *out):
    me = lax.axis_index("strip")

    def turn_rows(i, carry):
        flat = turned_rows(x, i)
        for k in range(4):
            part = flat[first_frame(k) : first_frame(k) + NF]
            for step in range(4):

                @pl.when(lax.rem(me + step, 4) == k)
                def _():
                    out[step][i] = part

        return carry

    lax.fori_loop(0, 8, turn_rows, 0)


def around(parts):
    return [parts[0]] + [
        lax.ppermute(parts[k], "strip", [(s, (s + k) % 4) for s in range(4)]) for k in range(1, 4)
    ]


def dot(a, b):
    return jnp.dot(a, b, preferred_element_type=F32)


def dot_nt(a, b):
    return lax.dot_general(a, b, (((1,), (1,)), ((), ())), preferred_element_type=F32)


def over_groups(values, join):
    lanes = values.shape[1]
    lane = lax.broadcasted_iota(jnp.int32, values.shape, 1)
    for step in (1, 2, 4, 8, 16):
        upper = lax.rem(lax.div(lane, step), 2) == 1
        other = jnp.where(
            upper, pltpu.roll(values, step, 1), pltpu.roll(values, lanes - step, 1)
        )
        values = join(values, other)
    return values


def unit_of(hidden):
    centred = hidden - jnp.mean(hidden, -1, keepdims=True)
    scale_inv = lax.rsqrt(jnp.mean(centred * centred, -1, keepdims=True) + EPS)
    return centred * scale_inv, scale_inv


def unit_back(grad_normed, unit_rows, scale_inv, gain):
    grad_unit = grad_normed * gain
    grad_gain = jnp.sum(grad_normed * unit_rows, 0, keepdims=True)
    grad_rows = scale_inv * (
        grad_unit
        - jnp.mean(grad_unit, -1, keepdims=True)
        - unit_rows * jnp.mean(grad_unit * unit_rows, -1, keepdims=True)
    )
    return grad_gain, grad_rows


LAYER_ROWS = 1536


def token_rows(layers, count):
    upper = max(layers - 1, 1) * LAYER_ROWS
    lower = LAYER_ROWS + 256 + NF + 16
    return share_rows(upper, count), share_rows(lower, count)


def middle_kernel(
    layers, count,
    feat, lh0, lh1, dh0, dh1, emb0, emb1, pos, gains, allow, cot,
    qkv0, qkv1, proj0, proj1, up0, up1, down0, down1, d1, d2, d3, d4,
    tokens, latent_out, chances_out, decoded, upper_both, lower, grad_latent, feat_got,
    latent_near, feat_near, got_near, da, db, dt2, dt3, dt4, du2, du3, du4,
    feat_sems, keep, send, sent, spread_sems, parts, gots, pair_sems,
    upper, upper_other, upper_got, lower_other, lower_got, upper_near, fold_sems, near_sems, unit_a, unit_f, normed_a, normed_f, mixed, weights,
    attended, before, inner, gain_rows, wa, wb, wt2, wt3, wt4, wu2, wu3, wu4, form_sems,
):
    strip = lax.axis_index("strip")
    row = lax.axis_index("rows")
    place_here = Place(count)
    partner, sibling = place_here.partner, place_here.sibling
    place_here.greet([partner, sibling, place_here.near_device])

    def copy(src, dst, sems, index, device):
        return pltpu.make_async_remote_copy(
            src_ref=src,
            dst_ref=dst,
            send_sem=sems.at[0, index],
            recv_sem=sems.at[1, index],
            device_id=device,
            device_id_type=MESH,
        )

    feat_copy = copy(feat, feat_got, feat_sems, 0, partner)
    feat_copy.start()

    def total_start(index, value):
        parts[index] = value.astype(BF)
        one = copy(parts.at[index], gots.at[index], pair_sems, index, partner)
        one.start()
        return one

    def total_wait(index, one):
        one.wait()
        got = jnp.concatenate([gots[index, NF:], gots[index, :NF]], axis=0)
        return parts[index].astype(F32) + got.astype(F32)

    def logits_of(maps):
        halves = []
        for weight in (lh0, lh1):
            total = jnp.zeros((NF, 256), F32)
            for h in range(4):
                total = total + dot(maps[h], weight[1024 * h : 1024 * h + 1024])
            halves.append(total)
        return jnp.concatenate(halves, axis=1)

    mine = logits_of(feat)
    feat_copy.wait()
    near_sends = Sems(near_sems, None)
    near_copies = [
        near_sends.copy(
            src.at[:, :, half_lanes(place_here, w)],
            dst.at[:, :, 128 * w : 128 * w + 128],
            place_here.near_device,
        )
        for src, dst in ((feat, feat_near), (feat_got, got_near))
        for w in range(4)
    ]
    logits = jnp.concatenate([mine, logits_of(feat_got)], axis=0)
    raised = jnp.exp(logits - over_groups(logits, jnp.maximum))
    chances = raised / over_groups(raised, jnp.add)
    latent = chances.astype(BF)
    chances_out[...] = chances
    latent_out[...] = latent
    near_copies.append(near_sends.copy(latent_out, latent_near, place_here.near_device))

    waiting = total_start(0, dot(latent[:, :256], emb0[...]) + dot(latent[:, 256:], emb1[...]))
    for hw in range(16):
        lanes = slice(256 * (hw % 4), 256 * (hw % 4) + 256)
        rows = slice(256 * hw, 256 * hw + 256)
        value = dot_nt(latent[:, :256], dh0[rows]) + dot_nt(latent[:, 256:], dh1[rows])
        value = value.astype(BF)
        keep[hw // 4, :, lanes] = value[:NF]
        send[hw // 4, :, lanes] = value[NF:]
    spread_copy = copy(send, sent, spread_sems, 0, partner)
    spread_copy.start()
    embedded = total_wait(0, waiting)
    place = pos[...].astype(F32)
    hidden = embedded + jnp.concatenate([place, place], axis=0)
    swap = exchange_16()
    forms = []

    def store(src, dst):
        one = pltpu.make_async_copy(src, dst, form_sems.at[len(forms)])
        one.start()
        forms.append(one)

    def build(step):
        if step == 0:
            put_outer(wa, wb, d4, True)
            store(wa, da)
            store(wb, db)
        if step == 1:
            bands = [band(f, 4, 32, 64) for f in canonical(d3, swap, 32, 64, True)]
            put_bands(wt2, wu2, bands, None, 4)
            store(wt2, dt2)
            store(wu2, du2)
        if step == 2:
            bands = [band(f, 2, 64, 128) for f in canonical(d2, swap, 64, 128, True)]
            put_bands(wt3, wu3, bands, None, 2)
            store(wt3, dt3)
            store(wu3, du3)
        if step == 3:
            put_bands(wt4, wu4, canonical(d1, swap, 128, 256, True), None, 1)
            store(wt4, dt4)
            store(wu4, du4)

    head_lane = lax.div(lax.broadcasted_iota(jnp.int32, (2 * NF, 128), 1), HEAD_DIM)
    allowed = allow[...] > 0.5

    def of_head(value, h):
        return jnp.where(head_lane == h % 2, value, jnp.zeros_like(value))

    def pair_lanes(h):
        return slice(128 * (h // 2), 128 * (h // 2) + 128)

    for k in range(layers):
        unit, inv = unit_of(hidden)
        unit_a[k] = jnp.concatenate([unit, jnp.broadcast_to(inv, (2 * NF, 128))], axis=1)
        normed = (unit * gains[2 * k : 2 * k + 1]).astype(BF)
        normed_a[k] = normed
        for part in range(3):
            mixed[k, part] = jnp.concatenate(
                [dot(normed, qkv0[k, part]), dot(normed, qkv1[k, part])], axis=1
            ).astype(BF)
        for p in range(2):
            both = jnp.zeros((2 * NF, 128), F32)
            for h in (2 * p, 2 * p + 1):
                lanes = pair_lanes(h)
                scores = SCALE * dot_nt(of_head(mixed[k, 0, :, lanes], h), mixed[k, 1, :, lanes])
                scores = jnp.where(allowed, scores, NEG)
                lifted = jnp.exp(scores - jnp.max(scores, -1, keepdims=True))
                weight = lifted / jnp.sum(lifted, -1, keepdims=True)
                weights[k, h] = weight
                both = both + of_head(dot(weight.astype(BF), mixed[k, 2, :, lanes]), h)
            attended[k, :, 128 * p : 128 * p + 128] = both.astype(BF)
        partial = dot(attended[k, :, :128], proj0[k]) + dot(attended[k, :, 128:], proj1[k])
        waiting = total_start(2 * k + 1, partial)
        build(2 * k)
        middle = hidden + total_wait(2 * k + 1, waiting)
        unit, inv = unit_of(middle)
        unit_f[k] = jnp.concatenate([unit, jnp.broadcast_to(inv, (2 * NF, 128))], axis=1)
        normed = (unit * gains[2 * k + 1 : 2 * k + 2]).astype(BF)
        normed_f[k] = normed
        partial = jnp.zeros((2 * NF, 512), F32)
        for side, (up, down) in enumerate(((up0, down0), (up1, down1))):
            value = dot(normed, up[k])
            before[k, :, 512 * side : 512 * side + 512] = value
            act = (value * sig(value)).astype(BF)
            inner[k, :, 512 * side : 512 * side + 512] = act
            partial = partial + dot(act, down[k])
        waiting = total_start(2 * k + 2, partial)
        build(2 * k + 1)
        hidden = middle + total_wait(2 * k + 2, waiting)
    tokens[...] = hidden.astype(BF)

    spread_copy.wait()
    decoded[...] = (keep[...].astype(F32) + sent[...].astype(F32)).astype(BF)

    def fold_start(index, part, got):
        one = copy(part, got, fold_sems, index, sibling)
        one.start()
        return one

    def fold_end(one, own, got, count):
        one.wait()
        for first in range(0, count, 128):
            rows = slice(first, min(first + 128, count))
            own[rows] = (own[rows].astype(F32) + got[rows].astype(F32)).astype(BF)
        if own.shape[0] > count:
            own[count:] = jnp.zeros((own.shape[0] - count, 512), BF)

    lower_rows = LAYER_ROWS + 256 + NF + 16

    grad = cot[...].astype(F32)
    for k in reversed(range(layers)):
        flat, other = (upper, upper_other) if k else (lower, lower_other)
        base = LAYER_ROWS * (k - 1) if k else 0
        index = 2 * layers + 1 + 2 * (layers - 1 - k)
        low = grad.astype(BF)
        partial = jnp.zeros((2 * NF, 512), F32)
        grads = []
        for side, (up, down) in enumerate(((up0, down0), (up1, down1))):
            value = before[k, :, 512 * side : 512 * side + 512]
            squash = sig(value)
            slope = squash * (1.0 + value * (1.0 - squash))
            grad_before = (dot_nt(low, down[k]) * slope).astype(BF)
            grads.append(grad_before)
            partial = partial + dot_nt(grad_before, up[k])
        waiting = total_start(index, partial)
        turned = normed_f[k].T
        for side, dst in enumerate((flat, other)):
            act = inner[k, :, 512 * side : 512 * side + 512]
            dst[base : base + 512] = dot(act.T, low).astype(BF)
            dst[base + 512 : base + 1024] = dot(turned, grads[side]).astype(BF)
        if k == 0:
            fold_end(upper_fold, upper, upper_got, LAYER_ROWS * (layers - 1))
            near_copy = near_start(place_here, near_sends, upper, upper_near)
        grad_normed = total_wait(index, waiting)
        gain_f, grad_rows = unit_back(
            grad_normed, unit_f[k, :, :512], unit_f[k, :, 512:513], gains[2 * k + 1 : 2 * k + 2]
        )
        grad = grad + grad_rows
        low = grad.astype(BF)
        grad_mixed = [[], [], []]
        for p, proj in enumerate((proj0, proj1)):
            lanes = pair_lanes(2 * p)
            grad_pair = dot_nt(low, proj[k]).astype(BF)
            queries, keys, vals = mixed[k, 0, :, lanes], mixed[k, 1, :, lanes], mixed[k, 2, :, lanes]
            g_queries = jnp.zeros((2 * NF, 128), F32)
            g_keys, g_vals = g_queries, g_queries
            for h in (2 * p, 2 * p + 1):
                weight = weights[k, h]
                grad_head = of_head(grad_pair, h)
                g_vals = g_vals + dot(weight.astype(BF).T, grad_head)
                grad_weight = dot_nt(grad_head, vals)
                along = jnp.sum(weight * grad_weight, -1, keepdims=True)
                grad_scores = (weight * (grad_weight - along)).astype(BF)
                g_queries = g_queries + of_head(dot(grad_scores, keys), h)
                g_keys = g_keys + dot(grad_scores.T, of_head(queries, h))
            grad_mixed[0].append((SCALE * g_queries).astype(BF))
            grad_mixed[1].append((SCALE * g_keys).astype(BF))
            grad_mixed[2].append(g_vals.astype(BF))
        partial = jnp.zeros((2 * NF, 512), F32)
        for part in range(3):
            for side, qkv in enumerate((qkv0, qkv1)):
                partial = partial + dot_nt(grad_mixed[part][side], qkv[k, part])
        waiting = total_start(index + 1, partial)
        turned = normed_a[k].T
        for side, dst in enumerate((flat, other)):
            act = attended[k, :, 128 * side : 128 * side + 128]
            dst[base + 1024 : base + 1152] = dot(act.T, low).astype(BF)
            for part in range(3):
                value = dot(turned, grad_mixed[part][side]).astype(BF)
                first = base + 1152 + 128 * part
                for b in range(4):
                    dst[first : first + 128, 128 * b : 128 * b + 128] = value[
                        128 * b : 128 * b + 128
                    ]
        if k == 1:
            upper_fold = fold_start(0, upper_other, upper_got)
        grad_normed = total_wait(index + 1, waiting)
        gain_a, grad_rows = unit_back(
            grad_normed, unit_a[k, :, :512], unit_a[k, :, 512:513], gains[2 * k : 2 * k + 1]
        )
        grad = grad + grad_rows
        gain_rows[2 * k : 2 * k + 1] = gain_a
        gain_rows[2 * k + 1 : 2 * k + 2] = gain_f

    low = grad.astype(BF)
    own_latent, other_latent = latent_out[:, :256], latent_out[:, 256:]
    lower[LAYER_ROWS : LAYER_ROWS + 256] = dot(own_latent.T, low).astype(BF)
    lower_other[LAYER_ROWS : LAYER_ROWS + 256] = dot(other_latent.T, low).astype(BF)
    rest = jnp.concatenate(
        [
            grad[:NF] + grad[NF:],
            gain_rows[...],
            jnp.zeros((16 - 2 * layers, 512), F32),
        ],
        axis=0,
    ).astype(BF)
    lower[LAYER_ROWS + 256 : lower_rows] = rest
    lower_other[LAYER_ROWS + 256 : lower_rows] = rest
    lower_fold = fold_start(1, lower_other, lower_got)
    grad_latent[:, :256] = dot_nt(low, emb0[...])
    grad_latent[:, 256:] = dot_nt(low, emb1[...])
    near_end(place_here, near_copy, upper, upper_near, upper_both)
    fold_end(lower_fold, lower, lower_got, lower_rows)
    for step in range(2 * layers, 4):
        build(step)
    for one in near_copies + forms:
        one.wait()


def middle(layers, *args):
    count = lax.axis_size("rows")
    upper, lower = token_rows(layers, count)
    dma = pltpu.SemaphoreType.DMA
    sums = 4 * layers + 1
    t = 2 * NF
    return pl.pallas_call(
        functools.partial(middle_kernel, layers, count),
        out_shape=(
            S((t, 512)),
            S((t, 512)),
            S((t, 512), F32),
            S((4, NF, 1024)),
            S((upper // 2, 512)),
            S((lower, 512)),
            S((t, 512), F32),
            S((4, NF, 1024)),
            S((t, 512)),
            S((4, NF, 512)),
            S((4, NF, 512)),
            *[S(shape) for shape in BUILT],
        ),
        in_specs=VM(len(args)),
        out_specs=tuple(VM(11) + [pl.BlockSpec(memory_space=pl.ANY)] * 8),
        scratch_shapes=[
            dma((2, 1)),
            V((4, NF, 1024)),
            V((4, NF, 1024)),
            V((4, NF, 1024)),
            dma((2, 1)),
            V((sums, t, 512)),
            V((sums, t, 512)),
            dma((2, sums)),
            V((upper, 512)),
            V((upper, 512)),
            V((upper, 512)),
            V((lower, 512)),
            V((lower, 512)),
            V((upper // 2, 512)),
            dma((2, 2)),
            dma((2, 10)),
            V((layers, t, 640), F32),
            V((layers, t, 640), F32),
            V((layers, t, 512)),
            V((layers, t, 512)),
            V((layers, 3, t, 256)),
            V((layers, 4, t, t), F32),
            V((layers, t, 256)),
            V((layers, t, 1024), F32),
            V((layers, t, 1024)),
            V((2 * layers, 512), F32),
            *[V(shape) for shape in BUILT],
            dma((8,)),
        ],
        compiler_params=pltpu.CompilerParams(
            collective_id=3, has_side_effects=True, vmem_limit_bytes=56 * MIB
        ),
        cost_estimate=estimate(84),
        name="middle",
    )(*args)


def back_kernel(
    count, grad, latent, latent_near, chances, grad_embed, feat0, feat1, feat2, feat3,
    lh0, lh1, dh0, dh1, flat, lower_piece,
    grad_feat, share, d_piece, l_both, lower_total,
    lower_half, got, got_near, got_cross, keep, send, sent, logits_here, logits_near, own, other, other_got,
    d_both, d_slots, side_got, side_sum, cross_got, remote, here,
):
    place = Place(count)
    near, core, x = place.near, place.core, place.x
    cross_device = (place.near_device[0], place.partner[1])
    place.greet(
        [place.partner, place.sibling, place.near_device, cross_device] + place.far_devices
    )
    sems = Sems(remote, here)
    grad_copies = [sems.copy(grad, got, place.partner)]
    for device, dst in ((place.near_device, got_near), (cross_device, got_cross)):
        for w in range(4):
            grad_copies.append(
                sems.copy(
                    grad.at[:, :, half_lanes(place, w)], dst.at[:, :, 128 * w : 128 * w + 128], device
                )
            )
    lower_back = back_start(place, sems, lower_piece, lower_half)
    side_copy = sems.copy(flat.at[1 - core], side_got, place.sibling)

    def through(maps):
        halves = []
        for weight in (dh0, dh1):
            total = jnp.zeros((NF, 256), F32)
            for h in range(4):
                total = total + dot(maps[h], weight[1024 * h : 1024 * h + 1024])
            halves.append(total)
        return jnp.concatenate(halves, axis=1)

    def head_grad(slot, wide, narrow, rhs):
        for h in range(4):
            for w in range(4):
                lanes = pl.ds(pl.multiple_of(256 * w + 128 * near, 128), 128)
                maps = [ref[h, :, lanes] for ref in wide]
                maps = maps + [ref[h, :, 128 * w : 128 * w + 128] for ref in narrow]
                rows = slice(512 * h + 128 * w, 512 * h + 128 * w + 128)
                value = dot(jnp.concatenate(maps, axis=0).T, rhs).astype(BF)
                own[slot, rows] = value[:, :256]
                other[slot, rows] = value[:, 256:]
        return sems.copy(other.at[slot], other_got.at[slot], place.sibling)

    swap = exchange_16()

    def folded(slot, b):
        parts = []
        for k in range(16):
            rows = slice(128 * k + 16 * b, 128 * k + 16 * b + 16)
            value = own[slot, rows].astype(F32) + other_got[slot, rows].astype(F32)
            parts.append(value.astype(BF))
        return dot(swap, jnp.concatenate(parts, axis=0)).astype(BF)

    mine = through(grad)
    side_copy.wait()
    side_sum[...] = (flat[core].astype(F32) + side_got[...].astype(F32)).astype(BF)
    for one in grad_copies:
        one.wait()
    cross_copy = sems.copy(side_sum.at[1 - x], cross_got, place.partner)
    both_latents = jnp.concatenate([latent[...], latent_near[...]], axis=0)
    out_fold = head_grad(0, (grad, got), (got_near, got_cross), both_latents)
    grad_latent = grad_embed[...] + jnp.concatenate([mine, through(got)], axis=0)
    probs = chances[...]
    along = over_groups(probs * grad_latent, jnp.add)
    grad_logits = (probs * (grad_latent - along)).astype(BF)
    logits_here[...] = grad_logits
    logits_copy = sems.copy(logits_here, logits_near, place.near_device)
    out_fold.wait()
    for b in range(8):
        d_both[256 * b : 256 * b + 256] = folded(0, b).T
    d_far = far_start(place, sems, d_both, d_slots)
    logits_copy.wait()
    for one in lower_back:
        one.wait()
    lower_own = sems.here(lower_half, rows_of(lower_total, near, lower_half.shape[0]))
    lower_last = last_start(place, sems, lower_half, lower_total)
    both_logits = jnp.concatenate([grad_logits, logits_near[...]], axis=0)
    in_fold = head_grad(1, (feat0, feat1), (feat2, feat3), both_logits)
    sends = []
    for h in range(4):
        for w in range(4):
            lanes = slice(256 * w, 256 * w + 256)
            rows = slice(1024 * h + 256 * w, 1024 * h + 256 * w + 256)
            value = dot_nt(grad_logits[:, :256], lh0[rows]) + dot_nt(grad_logits[:, 256:], lh1[rows])
            value = value.astype(BF)
            keep[h, :, lanes] = value[:NF]
            send[h, :, lanes] = value[NF:]
        sends.append(sems.copy(send.at[h], sent.at[h], place.partner))
    in_fold.wait()
    for b in range(8):
        l_both[256 * b : 256 * b + 256] = folded(1, b)
    cross_copy.wait()
    share[...] = (side_sum[x].astype(F32) + cross_got[...].astype(F32)).astype(BF)
    lower_own.wait()
    for one in sends + [lower_last]:
        one.wait()
    grad_feat[...] = (keep[...].astype(F32) + sent[...].astype(F32)).astype(BF)
    far_end(place, d_far, d_both, d_slots, d_piece)


def latents_back(*args):
    dma = pltpu.SemaphoreType.DMA
    count = lax.axis_size("rows")
    half = count // 2
    flat, lower_piece = args[-2:]
    quarter = flat.shape[0] // 4
    args = args[:-2] + (flat.reshape(2, 2, quarter, 256), lower_piece)
    maps = (4, NF, 1024)
    narrow = (4, NF, 512)
    rows = (2048, 256)
    return pl.pallas_call(
        functools.partial(back_kernel, count),
        out_shape=(
            S(maps),
            S((quarter, 256)),
            S((4096 // count, 256)),
            S(rows),
            S((count * lower_piece.shape[0], 512)),
        ),
        in_specs=VM(len(args)),
        out_specs=tuple(VM(4) + [pl.BlockSpec(memory_space=pl.ANY)]),
        scratch_shapes=[
            V((half * lower_piece.shape[0], 512)),
            V(maps),
            V(narrow),
            V(narrow),
            V(maps),
            V(maps),
            V(maps),
            V((2 * NF, 512)),
            V((2 * NF, 512)),
            V((2,) + rows),
            V((2,) + rows),
            V((2,) + rows),
            V(rows),
            V((half - 1, 4096 // count, 256)),
            V((2, quarter, 256)),
            V((2, quarter, 256)),
            V((quarter, 256)),
            dma((2, 2 * half + 20)),
            dma((2,)),
        ],
        compiler_params=pltpu.CompilerParams(
            collective_id=4, has_side_effects=True, vmem_limit_bytes=58 * MIB
        ),
        cost_estimate=estimate(55),
        name="latents_back",
    )(*args)


def strip_fold_start(place, sems, flat, first, size, got):
    half = size // 2
    return sems.copy(
        flat.at[pl.ds(pl.multiple_of(first + (1 - place.core) * half, 16), half)], got, place.sibling
    )


def strip_cross_start(place, sems, copy, flat, first, size, got, both, cross):
    copy.wait()
    half = size // 2
    own = flat[pl.ds(pl.multiple_of(first + place.core * half, 16), half)]
    both[...] = (own.astype(F32) + got[...].astype(F32)).astype(BF)
    return sems.copy(rows_of(both, 1 - place.x, half // 2), cross, place.partner)


def strip_share(place, copy, both, cross):
    copy.wait()
    own = rows_of(both, place.x, cross.shape[0])[...]
    return (own.astype(F32) + cross[...].astype(F32)).astype(BF)


def padded_share(ref, parts):
    share = jnp.concatenate(parts, axis=0)
    spare = ref.shape[0] - share.shape[0]
    if spare:
        share = jnp.concatenate([share, jnp.zeros((spare, 256), BF)], axis=0)
    ref[...] = share


def enc_bwd_kernel(
    count, xp, z1, z2, z3, z4, df, u2, u3, u4, b, dec, d_piece, l_both,
    d_total, l_total, early, late, grad_out,
    m1, m2, m3, s1, s2, s3, s4, yt, pk, dx, got, rows_out,
    l_slots, l_piece,
    e_fold, e_sum, e_cross, e_values, e_near, e_both, e_slots, e_piece,
    f_fold, f_sum, f_cross, f_values, f_slots, f_piece,
    remote, here,
):
    place = Place(count)
    near, core, x = place.near, place.core, place.x
    sems = Sems(remote, here)
    row_places = [lax.rem(place.row + k, count) for k in range(1, count)]
    row_devices = [(at, place.me) for at in row_places]
    cross_device = (place.near_device[0], place.partner[1])
    place.greet(place.others + row_devices + [cross_device])

    def home(ref):
        return rows_of(ref, near, ref.shape[0] // 2)

    def waits(copies):
        for one in copies:
            one.wait()

    l_far = far_start(place, sems, l_both, l_slots)

    zero_big(m1, 32)
    zero_big(m2, 16)
    zero_big(m3, 8)
    zero_small(s1, 32, 0)
    zero_small(s2, 16, 128)
    zero_small(s3, 8, 128)
    zero_small(s4, 4, 256)
    swap = exchange_16()
    z = z4[...].astype(F32)
    s = sig(z)
    s4[1:5, :, 256:1280] = (df[...].astype(F32) * (s * (1.0 + z * (1.0 - s)))).astype(BF)

    def back(z_ref, m, dst, pad):
        def emit(m0, odd, q, acc):
            for t in range(acc.shape[0]):
                h = 2 * (m0 + t) + odd
                zz = z_ref[h, :, 256 * q : 256 * q + 256].astype(F32)
                ss = sig(zz)
                mm = zz * ss
                dst[h + 1, :, pad + 256 * q : pad + 256 * q + 256] = (
                    acc[t] * (ss + mm * (1.0 - ss))
                ).astype(BF)
                m[m0 + t + odd, 1 - odd, :, 128 + 256 * q : 384 + 256 * q] = mm.astype(BF)

        return emit

    up(s4, u4, 4, 4, back(z3, m3, s3, 128))
    turn(s4, yt, 4, 256)
    pack(pk, 0, 1, 128, 256, grad_w(m3, yt, 4), False, swap, True)
    up(s3, u3, 8, 4, back(z2, m2, s2, 128))
    turn(s3, yt, 8, 128)
    pack(pk, 2048, 2, 64, 128, grad_w(m2, yt, 8), False, swap)
    e_copy = strip_fold_start(place, sems, pk, 0, 2560, e_fold)
    far_end(place, l_far, l_both, l_slots, l_piece)
    l_back = [back_part(place, sems, l_piece, home(l_total), part) for part in range(2)]
    e_copy = strip_cross_start(place, sems, e_copy, pk, 0, 2560, e_fold, e_sum, e_cross)
    up(s2, u2, 16, 4, back(z1, m1, s1, 0))
    padded_share(e_values, [dec[...], strip_share(place, e_copy, e_sum, e_cross)])
    e_copy = near_start(place, sems, e_values, e_near)

    def put(i0, acc):
        dx[pl.ds(i0, acc.shape[0])] = acc.astype(BF)

    outer_up(s1, b, put)
    strips = [
        sems.copy(dx.at[pl.ds(8 * device[1], 8)], got.at[place.me], device)
        for device in place.others
    ]
    got[place.me] = dx[pl.ds(8 * place.me, 8)]
    near_end(place, e_copy, e_values, e_near, e_both)
    e_far = far_start(place, sems, e_both, e_slots)
    waits(l_back[0])
    l_last = last_part(place, sems, home(l_total), l_piece.shape[0], 0)
    turn(s2, yt, 16, 128)
    pack(pk, 2560, 4, 32, 64, grad_w(m1, yt, 16), False, swap)
    far_end(place, e_far, e_both, e_slots, e_piece)
    e_out = early.at[core, x]
    e_back = back_start(place, sems, e_piece, home(e_out))
    waits(l_back[1])
    l_last = l_last + last_part(place, sems, home(l_total), l_piece.shape[0], 1)
    d_back = [back_part(place, sems, d_piece, home(d_total), part) for part in range(2)]
    turn(s1, yt, 32, 0)
    pack_outer(pk, 2688, outer_grad(xp, yt), False)
    f_copy = strip_fold_start(place, sems, pk, 2560, 256, f_fold)
    waits(e_back)
    e_last = [
        sems.copy(home(e_out), home(e_out), device)
        for device in (place.near_device, place.partner, cross_device)
    ]
    f_copy = strip_cross_start(place, sems, f_copy, pk, 2560, 256, f_fold, f_sum, f_cross)
    waits(strips)
    stores = []

    def turn_out(first, count_here):
        for i in range(first, first + count_here):
            slot = i % 2
            if i > 1:
                stores[i - 2].wait()
            block = jnp.concatenate([got[(k % 2) * 2 + k // 2, i] for k in range(4)], axis=0)
            flat = block.T.astype(F32)
            for p in range(2):
                for c in range(3):
                    rows_out[slot, c, p] = flat[64 * (3 * p + c) : 64 * (3 * p + c) + 64]
            stores.append(sems.here(rows_out.at[slot], grad_out.at[:, 2 * i : 2 * i + 2]))

    turn_out(0, 4)
    waits(d_back[0])
    d_last = last_part(place, sems, home(d_total), d_piece.shape[0], 0)
    padded_share(f_values, [strip_share(place, f_copy, f_sum, f_cross)])
    each = f_piece.shape[0]
    f_rows = [
        sems.copy(rows_of(f_values, at, each), f_slots.at[k], device)
        for k, (at, device) in enumerate(zip(row_places, row_devices))
    ]
    turn_out(4, 4)
    waits(f_rows)
    whole = rows_of(f_values, place.row, each)[...].astype(F32)
    for k in range(count - 1):
        whole = whole + f_slots[k].astype(F32)
    f_piece[...] = whole.astype(BF)
    f_out = rows_of(late.at[core, x], place.row, each)
    f_back = [sems.here(f_piece, f_out)]
    f_back = f_back + [sems.copy(f_piece, f_out, device) for device in row_devices]
    waits(d_back[1])
    d_last = d_last + last_part(place, sems, home(d_total), d_piece.shape[0], 1)
    waits(e_last)
    e_side = sems.copy(early.at[core], early.at[core], place.sibling)
    waits(f_back)
    f_cross_out = sems.copy(late.at[core, x], late.at[core, x], place.partner)
    f_cross_out.wait()
    f_side = sems.copy(late.at[core], late.at[core], place.sibling)
    waits(stores[-2:])
    waits([e_side, f_side] + d_last + l_last)


def share_rows(rows, count):
    return rows + -rows % (16 * count)


def enc_bwd(maps, dec, d_piece, l_both):
    count = lax.axis_size("rows")
    half = count // 2
    dma = pltpu.SemaphoreType.DMA
    any_spec = pl.BlockSpec(memory_space=pl.ANY)
    head = 2 * l_both.shape[0]
    quarter = dec.shape[0]
    early = share_rows(quarter + 640, count)
    late = share_rows(64, count)

    def steps(rows):
        return [
            V((rows, 256)),
            V((rows // 2, 256)),
            V((rows // 2, 256)),
            V((half - 1, rows // count, 256)),
            V((rows // count, 256)),
        ]

    d_total, l_total, e_out, f_out, grad_out = pl.pallas_call(
        functools.partial(enc_bwd_kernel, count),
        out_shape=(
            S((head, 256)),
            S((head, 256)),
            S((2, 2, early, 256)),
            S((2, 2, late, 256)),
            S((3, 16, 64, 256), F32),
        ),
        in_specs=VM(len(maps) + 3),
        out_specs=tuple([any_spec] * 5),
        scratch_shapes=[
            big(32),
            big(16),
            big(8),
            small(32, 0),
            small(16, 128),
            small(8, 128),
            small(4, 256),
            V((1024, 32 * NF)),
            V((2816, 256)),
            V((32, NF, 384)),
            V((4, 8, NF, 384)),
            V((2, 3, 2, 64, 256), F32),
            *steps(head)[3:],
            V((1280, 256)),
            V((1280, 256)),
            V((640, 256)),
            *steps(early),
            V((128, 256)),
            V((128, 256)),
            V((64, 256)),
            V((late, 256)),
            V((count - 1, late // count, 256)),
            V((late // count, 256)),
            dma((2, 7 * (half - 1) + 4 * half + 2 * (count - 1) + 15)),
            dma((18,)),
        ],
        compiler_params=pltpu.CompilerParams(
            collective_id=2, has_side_effects=True, vmem_limit_bytes=60 * MIB
        ),
        cost_estimate=estimate(110),
        name="encode_back",
    )(*maps, dec, d_piece, l_both)
    return d_total, l_total, e_out, f_out, jnp.transpose(grad_out, (3, 0, 1, 2))


def unpack_kernel(
    layers, quarter, d_total, l_total, upper, lower, early, late,
    latent_out, head_out, down_out, up_out, project_out, qkv_out, embed_out, place_out, gain_out, *outs,
):
    kernels, scratch, sems = outs[:8], outs[8:-1], outs[-1]
    (
        latent_v, head_v, down_v, up_v, project_v, qkv_v, embed_v, place_v, gain_v, *kernel_v
    ) = scratch
    stores = []

    def store(src, dst):
        one = pltpu.make_async_copy(src, dst, sems.at[len(stores)])
        one.start()
        stores.append(one)

    for k in range(layers):
        src, base = (upper, LAYER_ROWS * (k - 1)) if k else (lower, 0)
        down_v[k] = src[base : base + 512].astype(F32)
        up_v[k] = src[base + 512 : base + 1024].astype(F32)
        project_v[k] = src[base + 1024 : base + 1152].astype(F32)
        for part in range(3):
            first = base + 1152 + 128 * part
            for b in range(4):
                qkv_v[k, part, 128 * b : 128 * b + 128] = src[
                    first : first + 128, 128 * b : 128 * b + 128
                ].astype(F32)
    embed_v[...] = lower[LAYER_ROWS : LAYER_ROWS + 256].astype(F32)
    place_v[...] = lower[LAYER_ROWS + 256 : LAYER_ROWS + 256 + NF].astype(F32)
    gain_v[...] = lower[LAYER_ROWS + 256 + NF : LAYER_ROWS + 256 + NF + 16].astype(F32)[: 2 * layers]
    for src, dst in (
        (down_v, down_out), (up_v, up_out), (project_v, project_out), (qkv_v, qkv_out),
        (embed_v, embed_out), (place_v, place_out), (gain_v, gain_out),
    ):
        store(src, dst)
    for b in range(16):
        rows = slice(256 * b, 256 * b + 256)
        head_v[:, rows] = d_total[rows].astype(F32)
        latent_v[rows] = l_total[rows].astype(F32)
    store(head_v, head_out)
    store(latent_v, latent_out)

    def piece(first, is_enc):
        if not is_enc:
            at, place = divmod(first, quarter)
            return early[at // 2, at % 2, place : place + 64].astype(F32)
        if first < 2560:
            at, place = divmod(first, 640)
            return early[at // 2, at % 2, quarter + place : quarter + place + 64].astype(F32)
        at = (first - 2560) // 64
        return late[at // 2, at % 2, 0:64].astype(F32)

    for is_enc in (False, True):
        outer, first, second, third = kernel_v[4:] if is_enc else kernel_v[:4]
        for r in range(0, 2048, 64):
            value = piece(r, is_enc)
            if is_enc:
                third[r : r + 64] = value[:, :128]
                third[2048 + r : 2048 + r + 64] = value[:, 128:]
            else:
                third[r : r + 64] = value
        for r in range(0, 512, 64):
            value = piece(2048 + r, is_enc)
            second[r : r + 64] = value[:, :128]
            second[512 + r : 512 + r + 64] = value[:, 128:]
        for r in range(0, 128, 64):
            value = piece(2560 + r, is_enc)
            for k in range(4):
                first[128 * k + r : 128 * k + r + 64] = value[:, 64 * k : 64 * k + 64]
        outer[...] = piece(2688, is_enc)[:48, :32]
        for src, dst in zip(kernel_v[4:] if is_enc else kernel_v[:4], kernels[4:] if is_enc else kernels[:4]):
            store(src, dst)
    for one in stores:
        one.wait()


def unpack(layers, quarter, *args):
    dma = pltpu.SemaphoreType.DMA
    any_spec = pl.BlockSpec(memory_space=pl.ANY)
    shapes = [
        (4096, 256),
        (256, 4096),
        (layers, 512, 512),
        (layers, 512, 512),
        (layers, 128, 512),
        (layers, 3, 512, 128),
        (256, 512),
        (NF, 512),
        (2 * layers, 512),
        (48, 32),
        (512, 64),
        (1024, 128),
        (2048, 256),
        (48, 32),
        (512, 64),
        (1024, 128),
        (4096, 128),
    ]
    return pl.pallas_call(
        functools.partial(unpack_kernel, layers, quarter),
        out_shape=tuple(S(shape, F32) for shape in shapes),
        in_specs=VM(len(args)),
        out_specs=tuple([any_spec] * len(shapes)),
        scratch_shapes=[V(shape, F32) for shape in shapes] + [dma((len(shapes),))],
        compiler_params=pltpu.CompilerParams(vmem_limit_bytes=56 * MIB),
        cost_estimate=estimate(12),
        name="unpack",
    )(*args)


def beside(value):
    return lax.ppermute(value, "strip", [(0, 1), (1, 0), (2, 3), (3, 2)])


def make_mask(segment_ids):
    places = jnp.arange(segment_ids.shape[1])
    causal = places[:, None] >= places[None, :]
    return causal[None] & (segment_ids[:, :, None] == segment_ids[:, None, :])


def shards(
    frames,
    segment_ids,
    encode_one,
    encode_two,
    encode_three,
    encode_four,
    latent_head,
    token_embed,
    positions,
    norm_gains,
    qkv_weight,
    out_weight,
    up_weight,
    down_weight,
    decode_head,
    decode_one,
    decode_two,
    decode_three,
    decode_four,
    token_cotangent,
    frame_cotangent,
):
    strip = lax.axis_index("strip")
    x, core = strip // 2, strip % 2
    layers = qkv_weight.shape[0]

    kernels = (encode_one, encode_two, encode_three, encode_four)
    dec_rows = decoder_rows((decode_one, decode_two, decode_three, decode_four))
    qkv = jnp.transpose(qkv_weight, (0, 2, 1, 3))
    shards_here = (token_embed, qkv, out_weight, up_weight, down_weight)
    pixels, enc_f, head_in, head_out, theirs, hints = start(
        frames, frame_cotangent, kernels, latent_head, decode_head, shards_here
    )
    enc_a, enc_b, enc_t, enc_u = enc_f[0], enc_f[1], enc_f[2:5], enc_f[5:8]
    embed, qkv, project, widen, narrow = zip(shards_here, theirs)
    z1, z2, z3, z4, feat = enc_fwd(pixels, enc_a, *enc_t)

    first = 2 * core

    def mine(array, size):
        own = lax.dynamic_slice_in_dim(array, (first + x) * size, size)
        other = lax.dynamic_slice_in_dim(array, (first + 1 - x) * size, size)
        return jnp.concatenate([own, other], axis=0)

    allowed = make_mask(mine(segment_ids, 1)).astype(F32)
    blank = jnp.zeros((NF, NF), F32)
    allowed = jnp.concatenate(
        [
            jnp.concatenate([allowed[0], blank], axis=1),
            jnp.concatenate([blank, allowed[1]], axis=1),
        ],
        axis=0,
    )
    (
        tokens, latent, chances, decoded, upper, lower, grad_latent, feat_got,
        latent_near, feat_near, got_near, *dec_f,
    ) = middle(
        layers,
        feat,
        *head_in,
        *head_out,
        *embed,
        positions,
        norm_gains.reshape(2 * layers, -1),
        allowed,
        mine(token_cotangent, NF),
        *qkv,
        *project,
        *widen,
        *narrow,
        *dec_rows,
    )
    dec_a, dec_b, dec_t, dec_u = dec_f[0], dec_f[1], dec_f[2:5], dec_f[5:8]
    tokens = jnp.where(
        x == 0, tokens, jnp.concatenate([tokens[NF:], tokens[:NF]], axis=0)
    )
    other_tokens = beside(tokens)
    tokens_out = jnp.where(
        core == 0,
        jnp.concatenate([tokens, other_tokens]),
        jnp.concatenate([other_tokens, tokens]),
    )

    g_decoded, dec_flat, recon, upper, _, lower = decode(
        hints, decoded, dec_u[2], dec_u[1], dec_u[0], dec_b, dec_a, *dec_t, upper, lower
    )
    recon = jnp.transpose(recon, (3, 0, 1, 2))
    g_feat, dec_share, d_piece, l_both, lower = latents_back(
        g_decoded, latent, latent_near, chances, grad_latent, feat, feat_got, feat_near, got_near,
        *head_in, *head_out, dec_flat, lower,
    )

    d_total, l_total, early, late, frames_grad = enc_bwd(
        (pixels, z1, z2, z3, z4, g_feat, *enc_u, enc_b), dec_share, d_piece, l_both
    )
    (
        g_latent_head, g_decode_head, g_down, g_up, g_out, g_qkv, g_embed, g_place, g_gain,
        d_four, d_three, d_two, d_one, e_one, e_two, e_three, e_four,
    ) = unpack(layers, dec_share.shape[0], d_total, l_total, upper, lower, early, late)

    def of_input(rows, count):
        return rows.reshape(count, 4, 4, -1).transpose(3, 0, 1, 2)

    def of_output(rows, count):
        return rows.reshape(count, 4, 4, -1).transpose(0, 3, 1, 2)

    return (
        tokens_out,
        recon,
        frames_grad,
        of_input(e_one, 3),
        of_input(e_two, 32),
        of_input(e_three, 64),
        of_output(e_four, 256),
        g_latent_head,
        g_embed,
        g_place,
        g_gain.reshape(norm_gains.shape),
        g_qkv.transpose(0, 2, 1, 3),
        g_out,
        g_up,
        g_down,
        g_decode_head,
        of_output(d_one, 128),
        of_output(d_two, 64),
        of_output(d_three, 32),
        of_output(d_four, 3),
    )


def solution(mesh):
    placed = (
        P("rows", None, "strip", None),
        P("rows", None),
        P(),
        P(),
        P(),
        P(),
        P(None, "strip"),
        P("strip", None),
        P(),
        P(),
        P(None, None, None, "strip"),
        P(None, "strip", None),
        P(None, None, "strip"),
        P(None, "strip", None),
        P("strip", None),
        P(),
        P(),
        P(),
        P(),
        P("rows", None),
        P("rows", None, "strip", None),
    )
    return jax.shard_map(
        shards,
        mesh=mesh,
        in_specs=placed,
        out_specs=(
            P("rows", None),
            P("rows", None, "strip", None),
            P("rows", None, "strip", None),
            P(),
            P(),
            P(),
            P(),
            P(None, "strip"),
            P("strip", None),
            P(),
            P(),
            P(None, None, None, "strip"),
            P(None, "strip", None),
            P(None, None, "strip"),
            P(None, "strip", None),
            P("strip", None),
            P(),
            P(),
            P(),
            P(),
        ),
        check_vma=False,
    )
```

```python
import functools

import jax
import jax.numpy as jnp
from jax import lax
from jax.experimental import pallas as pl
from jax.experimental.pallas import tpu as pltpu
from jax.sharding import PartitionSpec as P

HEAD_DIM = 64
LCLASS = 32
EPS = 1e-05
SCALE = 0.125
NEG = -1e30
F32 = jnp.float32
BF = jnp.bfloat16
NF = 64
MIB = 1 << 20
MESH = pl.DeviceIdType.MESH


def sig(z): return 0.5*jnp.tanh(0.5*z)+0.5

def zero_big(ref,rows):
    z=jnp.zeros((NF,1280),BF)
    ref[0,0]=z; ref[rows//2,1]=z
    e=jnp.zeros((rows//2+1,2,NF,128),BF)
    ref[:,:,:,0:128]=e; ref[:,:,:,1152:1280]=e

def zero_small(ref,rows,pad):
    z=jnp.zeros((NF,1024+2*pad),BF)
    ref[0]=z; ref[rows+1]=z
    if pad:
        e=jnp.zeros((rows+2,NF,pad),BF)
        ref[:,:,0:pad]=e; ref[:,:,1024+pad:]=e

def put_big(ref,half0,rows,q,val):
    v=val.reshape(rows,NF,256)
    for t in range(rows):
        ref[half0+(t+1)//2,(t+1)%2,:,128+256*q:384+256*q]=v[t]

def loop(n,body):
    if n==1: body(0)
    else:
        def step(g,c):
            body(g); return c
        lax.fori_loop(0,n,step,0)

def down(src,t_ref,rows,per,emit):
    def body(g):
        i0=g*per
        for q in range(4):
            lhs=jnp.concatenate([src[pl.ds(i0+kh//2,per),kh%2,:,256*q:256*q+512].reshape(per*NF,512) for kh in range(4)],axis=1)
            emit(i0,g*(per//2),q,jnp.dot(lhs,t_ref[...],preferred_element_type=F32))
    loop(rows//per,body)

def up(src,u_ref,rows,per,emit):
    k=u_ref.shape[1]//2
    def body(g):
        m0=g*per
        for q in range(4):
            for odd in range(2):
                lhs=jnp.concatenate([src[pl.ds(m0+1+odd-s,per),:,256*q:256*q+k].reshape(per*NF,k) for s in range(2)],axis=1)
                emit(m0,odd,q,jnp.dot(lhs,u_ref[odd],preferred_element_type=F32).reshape(per,NF,256))
    loop(rows//per,body)

def turn(src,dst,rows,pad):
    for q in range(4):
        dst[256*q:256*q+256,:rows*NF]=src[1:rows+1,:,pad+256*q:pad+256*q+256].reshape(rows*NF,256).T

def grad_w(big,yt,rows):
    out=[]
    for kh in range(4):
        acc=jnp.zeros((256,512),F32)
        for q in range(4):
            win=big[pl.ds(kh//2,rows),kh%2,:,256*q:256*q+512].reshape(rows*NF,512)
            acc=acc+jnp.dot(yt[256*q:256*q+256,:rows*NF],win,preferred_element_type=F32)
        out.append(acc)
    return out

def pack(pk,base,a,c,o,sums,flipped,swap,turned=False):
    taps=[]
    for acc in sums:
        total=None
        for j in range(a):
            first=(a+2*j-1)*c
            part=acc[j*o:j*o+o]
            if first: part=pltpu.roll(part,512-first,1)
            part=part[:,:4*c]
            total=part if total is None else total+part
        taps.append(total.astype(BF) if turned else total.T.astype(BF))
    width,count=(c,o//16) if turned else (o,c//16)
    held=[]
    for b in range(count):
        rows=[]
        for k in range(16):
            kh,kw=divmod(15-k if flipped else k,4)
            if turned: rows.append(taps[kh][16*b:16*b+16,c*kw:c*kw+c])
            else: rows.append(taps[kh][c*kw+16*b:c*kw+16*b+16])
        block=jnp.dot(swap,jnp.concatenate(rows,axis=0),preferred_element_type=F32).astype(BF)
        if width==256: pk[base+256*b:base+256*b+256]=block
        elif width==128:
            side,at=divmod(b,count//2)
            pk[base+256*at:base+256*at+256,128*side:128*side+128]=block
        else: held.extend([block[:128],block[128:]])
    if held: pk[base:base+128]=jnp.concatenate(held,axis=1)

def pack_outer(pk,base,red,flipped):
    r=lax.broadcasted_iota(jnp.int32,(48,1152),0); lane=lax.broadcasted_iota(jnp.int32,(48,1152),1)
    k=lax.rem(r,16)
    if flipped: k=15-k
    kh,kw=lax.div(k,4),lax.rem(k,4)
    at=384*lax.div(kh+1,2)+192*lax.rem(kh+1,2)+64*lax.div(r,16)+kw
    pick=(lane==at).astype(BF)
    value=jnp.concatenate([part.astype(BF) for part in red],axis=1)
    pk[base:base+128]=jnp.zeros((128,256),BF)
    pk[base:base+48,0:32]=lax.dot_general(pick,value,(((1,),(1,)),((),())),preferred_element_type=F32).astype(BF)

def outer_down(xp,a_ref,emit,per=4):
    def body(g):
        i0=g*per
        lhs=jnp.concatenate([xp[pl.ds(i0+d,per)].reshape(per*NF,384) for d in range(3)],axis=1)
        for q in range(4):
            emit(i0,g*(per//2),q,jnp.dot(lhs,a_ref[:,256*q:256*q+256],preferred_element_type=F32))
    loop(32//per,body)

def outer_up(yp,b_ref,emit,per=4):
    def body(g):
        i0=g*per
        lhs=jnp.concatenate([yp[pl.ds(i0+2-d,per)].reshape(per*NF,1024) for d in range(3)],axis=1)
        emit(i0,jnp.dot(lhs,b_ref[...],preferred_element_type=F32).reshape(per,NF,384))
    loop(32//per,body)

def outer_grad(xp,yt):
    red=[]
    lane=lax.broadcasted_iota(jnp.int32,(32,384),1)%64
    for d in range(3):
        x=xp[d:d+32].reshape(32*NF,384)
        tot=jnp.zeros((32,384),F32)
        for jb in range(4):
            g=jnp.dot(yt[256*jb:256*jb+256,:],x,preferred_element_type=F32)
            for jj in range(8):
                j=8*jb+jj
                v=pltpu.roll(g[32*jj:32*jj+32],(385-2*j)%384,1)
                if j==0: v=jnp.where(lane==0,0.0,v)
                if j==31: v=jnp.where(lane==3,0.0,v)
                tot=tot+v
        red.append(tot)
    return red

def enc_fwd_kernel(xp,a,t2,t3,t4,z1,z2,z3,z4,feat,m1,m2,m3):
    zero_big(m1,32); zero_big(m2,16); zero_big(m3,8)
    def keep(z,m):
        def emit(i0,half0,q,acc):
            rows=acc.shape[0]//NF
            z[pl.ds(i0,rows),:,256*q:256*q+256]=acc.astype(BF).reshape(rows,NF,256)
            val=(acc*sig(acc)).astype(BF)
            if m is None: feat[pl.ds(i0,rows),:,256*q:256*q+256]=val.reshape(rows,NF,256)
            else: put_big(m,half0,rows,q,val)
        return emit
    outer_down(xp,a,keep(z1,m1),8)
    down(m1,t2,16,8,keep(z2,m2))
    down(m2,t3,8,8,keep(z3,m3))
    down(m3,t4,4,4,keep(z4,None))

def dec_kernel(count,c0,c1,c2,c3,dec,u4,u3,u2,b,a,t2,t3,t4,upper_both,lower,
               gdec,pk,recon_out,upper_total,got,lower_piece,
               p3,p2,p1,s4,s3,s2,s1,d1,d2,d3,cp,yt,recon,
               upper_slots,upper_piece,rows_out,lower_near,lower_both,lower_slots,remote,here):
    place=Place(count); sems=Sems(remote,here); me=place.me
    place.greet(place.others+[place.near_device]+place.far_devices)
    upper_far=far_start(place,sems,upper_both,upper_slots)
    lower_copy=near_start(place,sems,lower,lower_near)
    lower_own=sems.here(rows_of(lower,place.near,lower.shape[0]//2),lower_both)
    zero_small(s1,32,0); zero_small(s2,16,128); zero_small(s3,8,128); zero_small(s4,4,256)
    zero_big(d1,32); zero_big(d2,16); zero_big(d3,8)
    z=dec[...].astype(F32)
    s4[1:5,:,256:1280]=(z*sig(z)).astype(BF)
    def fwd(p,dst,pad):
        def emit(m0,odd,q,acc):
            for t in range(acc.shape[0]):
                h=2*(m0+t)+odd
                v=acc[t]
                p[h,:,256*q:256*q+256]=v.astype(BF)
                dst[h+1,:,pad+256*q:pad+256*q+256]=(v*sig(v)).astype(BF)
        return emit
    up(s4,u4,4,4,fwd(p3,s3,128))
    up(s3,u3,8,4,fwd(p2,s2,128))
    up(s2,u2,16,4,fwd(p1,s1,0))
    far_end(place,upper_far,upper_both,upper_slots,upper_piece)
    upper_home=rows_of(upper_total,place.near,upper_total.shape[0]//2)
    upper_back=back_start(place,sems,upper_piece,upper_home)
    def put(i0,acc): recon[pl.ds(i0,acc.shape[0])]=acc.astype(BF)
    outer_up(s1,b,put)
    strips=[sems.copy(recon.at[pl.ds(8*device[1],8)],got.at[pl.ds(8*me,8)],device) for device in place.others]
    cp[0]=jnp.zeros((NF,384),BF); cp[33]=jnp.zeros((NF,384),BF)
    for k,part in enumerate((c0,c1,c2,c3)): cp[pl.ds(1+8*lax.rem(me+4-k,4),8)]=part[...]
    swap=exchange_16()
    def back(p,dst):
        def emit(i0,half0,q,acc):
            rows=acc.shape[0]//NF
            zz=p[pl.ds(i0,rows),:,256*q:256*q+256].astype(F32).reshape(rows*NF,256)
            ss=sig(zz)
            val=(acc*(ss*(1.0+zz*(1.0-ss)))).astype(BF)
            if dst is None: gdec[pl.ds(i0,rows),:,256*q:256*q+256]=val.reshape(rows,NF,256)
            else: put_big(dst,half0,rows,q,val)
        return emit
    lower_own.wait(); lower_copy.wait()
    lower_both[...]=(lower_both[...].astype(F32)+lower_near[...].astype(F32)).astype(BF)
    turn(s1,yt,32,0); pack_outer(pk,2688,outer_grad(cp,yt),True)
    for one in upper_back: one.wait()
    upper_last=last_start(place,sems,upper_home,upper_total)
    lower_far=far_start(place,sems,lower_both,lower_slots)
    outer_down(cp,a,back(p1,d1))
    turn(s2,yt,16,128); pack(pk,2560,4,32,64,grad_w(d1,yt,16),True,swap)
    down(d1,t2,16,4,back(p2,d2))
    for one in strips: one.wait()
    arrived=[sems.here(got.at[pl.ds(8*device[1],8)],recon.at[pl.ds(8*device[1],8)]) for device in place.others]
    for one in arrived: one.wait()
    stores=[]
    for i in range(8):
        if i: stores[i-1].wait()
        block=jnp.concatenate([recon[8*((k%2)*2+k//2)+i] for k in range(4)],axis=0).T
        for p in range(2):
            for c in range(3): rows_out[c,p]=block[64*(3*p+c):64*(3*p+c)+64]
        stores.append(sems.here(rows_out,recon_out.at[:,2*i:2*i+2]))
    turn(s3,yt,8,128); pack(pk,2048,2,64,128,grad_w(d2,yt,8),True,swap)
    down(d2,t3,8,4,back(p3,d3))
    turn(s4,yt,4,256); pack(pk,0,1,128,256,grad_w(d3,yt,4),True,swap)
    down(d3,t4,4,4,back(dec,None))
    pk[2816-80:2816]=jnp.zeros((80,256),BF)
    far_end(place,lower_far,lower_both,lower_slots,lower_piece)
    for one in stores[-1:]+[upper_last]: one.wait()

def estimate(us):
    return pl.CostEstimate(flops=us*1150*10**6,bytes_accessed=MIB,transcendentals=0)

def S(shape,dt=BF): return jax.ShapeDtypeStruct(shape,dt)
def V(shape,dt=BF): return pltpu.VMEM(shape,dt)
VM=lambda n:[pl.BlockSpec(memory_space=pltpu.VMEM)]*n
def run(kernel,outs,scratch,args,name,us,lim=60,ident=None):
    extra={} if ident is None else dict(collective_id=ident,has_side_effects=True)
    return pl.pallas_call(kernel,out_shape=outs,in_specs=VM(len(args)),out_specs=tuple(VM(len(outs))),
        scratch_shapes=scratch,compiler_params=pltpu.CompilerParams(vmem_limit_bytes=lim*MIB,**extra),
        cost_estimate=estimate(us),name=name)(*args)
big=lambda h:V((h//2+1,2,NF,1280))
def enc_fwd(xp,a,t2,t3,t4):
    return run(enc_fwd_kernel,(S((32,NF,1024)),S((16,NF,1024)),S((8,NF,1024)),S((4,NF,1024)),S((4,NF,1024))),
      [big(32),big(16),big(8)],(xp,a,t2,t3,t4),"encode",22)
small=lambda h,p:V((h+2,NF,1024+2*p))
def enc_fwd(xp,a,t2,t3,t4):
    return run(enc_fwd_kernel,(S((32,NF,1024)),S((16,NF,1024)),S((8,NF,1024)),S((4,NF,1024)),S((4,NF,1024))),
      [big(32),big(16),big(8)],(xp,a,t2,t3,t4),"encode",22)
small=lambda h,p:V((h+2,NF,1024+2*p))
yts=[V((1024,32*NF)),V((1024,16*NF)),V((1024,8*NF)),V((1024,4*NF))]
def decode(hints,dec,u4,u3,u2,b,a,t2,t3,t4,upper_both,lower):
    count=lax.axis_size("rows"); half=count//2
    upper,rows=2*upper_both.shape[0],lower.shape[0]
    dma=pltpu.SemaphoreType.DMA
    args=(*hints,dec,u4,u3,u2,b,a,t2,t3,t4,upper_both,lower)
    return pl.pallas_call(
        functools.partial(dec_kernel,count),
        out_shape=(S((4,NF,1024)),S((2816,256)),S((3,16,64,256)),S((upper,512)),S((32,NF,384)),S((rows//count,512))),
        in_specs=VM(len(args)-1)+[pl.BlockSpec(memory_space=pl.ANY)],
        out_specs=tuple(VM(2)+[pl.BlockSpec(memory_space=pl.ANY)]*3+VM(1)),
        scratch_shapes=[V((8,NF,1024)),V((16,NF,1024)),V((32,NF,1024)),small(4,256),small(8,128),small(16,128),small(32,0),
            big(32),big(16),big(8),V((34,NF,384)),V((1024,32*NF)),V((32,NF,384)),
            V((half-1,upper//count,512)),V((upper//count,512)),V((3,2,64,256)),
            V((rows//2,512)),V((rows//2,512)),V((half-1,rows//count,512)),
            dma((2,3*(half-1)+5)),dma((13,))],
        compiler_params=pltpu.CompilerParams(collective_id=5,has_side_effects=True,vmem_limit_bytes=60*MIB),
        cost_estimate=estimate(65),
        name="decode",
    )(*args)


def rows_of(ref, index, size):
    return ref.at[pl.ds(pl.multiple_of(index * size, 16), size)]


class Place:
    def __init__(self, count):
        self.me, self.row = lax.axis_index("strip"), lax.axis_index("rows")
        self.half = count // 2
        self.near, self.far = lax.rem(self.row, 2), lax.div(self.row, 2)
        self.core, self.x = lax.rem(self.me, 2), lax.div(self.me, 2)
        self.near_device = (self.row + 1 - 2 * self.near, self.me)
        self.sibling = (self.row, self.me + 1 - 2 * self.core)
        self.partner = (self.row, lax.rem(self.me + 2, 4))
        self.others = [(self.row, lax.rem(self.me + k, 4)) for k in range(1, 4)]
        self.far_places = [lax.rem(self.far + k, self.half) for k in range(1, self.half)]
        self.far_devices = [(2 * place + self.near, self.me) for place in self.far_places]

    def greet(self, devices):
        barrier = pltpu.get_barrier_semaphore()
        for device in devices:
            pl.semaphore_signal(barrier, inc=1, device_id=device, device_id_type=MESH)
        pl.semaphore_wait(barrier, len(devices))


class Sems:
    def __init__(self, remote, local):
        self.remote, self.local, self.used, self.used_here = remote, local, 0, 0

    def copy(self, src, dst, device):
        assert self.used < self.remote.shape[1]
        one = pltpu.make_async_remote_copy(
            src_ref=src,
            dst_ref=dst,
            send_sem=self.remote.at[0, self.used],
            recv_sem=self.remote.at[1, self.used],
            device_id=device,
            device_id_type=MESH,
        )
        self.used = self.used + 1
        one.start()
        return one

    def here(self, src, dst):
        assert self.used_here < self.local.shape[0]
        one = pltpu.make_async_copy(src, dst, self.local.at[self.used_here])
        self.used_here = self.used_here + 1
        one.start()
        return one


def near_start(place, sems, values, arrived):
    half = values.shape[0] // 2
    return sems.copy(rows_of(values, 1 - place.near, half), arrived, place.near_device)


def near_end(place, copy, values, arrived, both):
    copy.wait()
    half = values.shape[0] // 2
    total = rows_of(values, place.near, half)[...].astype(F32) + arrived[...].astype(F32)
    both[...] = total.astype(BF)


def far_start(place, sems, both, slots):
    each = slots.shape[1]
    return [
        sems.copy(rows_of(both, at, each), slots.at[k], device)
        for k, (at, device) in enumerate(zip(place.far_places, place.far_devices))
    ]


def far_end(place, copies, both, slots, piece):
    for one in copies:
        one.wait()
    total = rows_of(both, place.far, slots.shape[1])[...].astype(F32)
    for k in range(slots.shape[0]):
        total = total + slots[k].astype(F32)
    piece[...] = total.astype(BF)


def back_start(place, sems, piece, home):
    out = rows_of(home, place.far, piece.shape[0])
    return [sems.here(piece, out)] + [sems.copy(piece, out, d) for d in place.far_devices]


def back_part(place, sems, piece, home, part):
    size = piece.shape[0] // 2
    src = piece.at[pl.ds(part * size, size)]
    first = place.far * piece.shape[0] + part * size
    out = home.at[pl.ds(pl.multiple_of(first, 16), size)]
    return [sems.here(src, out)] + [sems.copy(src, out, d) for d in place.far_devices]


def last_part(place, sems, home, each, part):
    size = each // 2
    refs = [home.at[pl.ds(each * k + part * size, size)] for k in range(place.half)]
    return [sems.copy(ref, ref, place.near_device) for ref in refs]


def half_lanes(place, w):
    return pl.ds(pl.multiple_of(256 * w + 128 * (1 - place.near), 128), 128)


def last_start(place, sems, home, out):
    half = out.shape[0] // 2
    return sems.copy(home, rows_of(out, place.near, half), place.near_device)


def exchange_16():
    r = lax.broadcasted_iota(jnp.int32, (256, 256), 0)
    s = lax.broadcasted_iota(jnp.int32, (256, 256), 1)
    return (s == lax.rem(r, 16) * 16 + lax.div(r, 16)).astype(BF)


def first_frame(strip):
    return NF * ((strip % 2) * 2 + strip // 2)


def turned_rows(x, i):
    return jnp.concatenate([x[c, 2 * i + p] for p in range(2) for c in range(3)], axis=0).T


def canonical(w, swap, c, o, flipped):
    parts = {}
    for b in range(c // 16):
        block = jnp.dot(swap, w[256 * b : 256 * b + 256, :], preferred_element_type=F32).astype(BF)
        for k in range(16):
            parts[(15 - k if flipped else k, b)] = block[16 * k : 16 * k + 16]
    return [
        jnp.concatenate(
            [parts[(4 * kh + kw, b)] for kw in range(4) for b in range(c // 16)], axis=0
        )
        for kh in range(4)
    ]


def canonical_turned(w, swap):
    parts = {}
    for b in range(16):
        block = jnp.dot(swap, w[256 * b : 256 * b + 256, :], preferred_element_type=F32).astype(BF)
        for k in range(16):
            parts[(k, b)] = block[16 * k : 16 * k + 16]
    return [
        jnp.concatenate(
            [
                jnp.concatenate([parts[(4 * kh + kw, b)] for b in range(16)], axis=0)
                for kw in range(4)
            ],
            axis=1,
        )
        for kh in range(4)
    ]


def band(flat, a, c, o):
    def shifted(value, first):
        above = jnp.zeros((first, value.shape[1]), BF)
        below = jnp.zeros((512 - first - value.shape[0], value.shape[1]), BF)
        return jnp.concatenate([above, value, below], axis=0)

    if a == 1:
        return flat
    if a == 2:
        return jnp.concatenate([shifted(flat, 64), shifted(flat, 192)], axis=1)
    twice = jnp.concatenate([flat, flat], axis=1)
    left = lax.broadcasted_iota(jnp.int32, (512, 128), 1) < 64
    return jnp.concatenate(
        [
            jnp.where(left, shifted(twice, 96), shifted(twice, 160)),
            jnp.where(left, shifted(twice, 224), shifted(twice, 288)),
        ],
        axis=1,
    )


def put_bands(t_ref, u_ref, bands, turned, a):
    for kh in range(4):
        t = bands[kh]
        t_ref[512 * kh : 512 * kh + 512] = t
        tt = t.T if turned is None else turned[kh]
        z = jnp.zeros((256, 128), BF)
        left = jnp.concatenate([tt[:, 384:512], z], axis=1)
        right = jnp.concatenate([z, tt[:, :128]], axis=1)
        if a > 1:
            left, right = left[128:], right[:128]
        k = 512 if a > 1 else 768
        u_ref[1 - kh % 2, k * (kh // 2) : k * (kh // 2) + k] = jnp.concatenate(
            [left, tt[:, 128:384], right], axis=0
        )


def put_outer(a_ref, b_ref, w, flipped):
    row = lax.broadcasted_iota(jnp.int32, (64, 1024), 0)
    col = lax.div(lax.broadcasted_iota(jnp.int32, (64, 1024), 1), 32)
    tap = row - 2 * col + 1
    for kh in range(4):
        d, p = (kh + 1) // 2, (kh + 1) % 2
        for c in range(3):
            total = jnp.zeros((64, 1024), F32)
            for kw in range(4):
                k = 4 * kh + kw
                r = 16 * c + (15 - k if flipped else k)
                total = jnp.where(tap == kw, w[r : r + 1, :], total)
            first = 384 * d + 192 * p + 64 * c
            a_ref[first : first + 64] = total.astype(BF)
    a_ref[0:192] = jnp.zeros((192, 1024), BF)
    a_ref[960:1152] = jnp.zeros((192, 1024), BF)
    for d in range(3):
        b_ref[1024 * d : 1024 * d + 1024] = a_ref[384 * d : 384 * d + 384].T


def start_kernel(
    x, later, e1, e2, e3, e4, lh, dh, emb, qkv, proj, up, down,
    pixels, ea, eb, et2, et3, et4, eu2, eu3, eu4,
    lh0, lh1, dh0, dh1, emb1, qkv1, proj1, up1, down1, t0, t1, t2, t3,
    stage, send_sem, recv_sem, side_sems,
    va, vb, vt2, vt3, vt4, vu2, vu3, vu4,
    vl, vd, out_sems,
):
    me = lax.axis_index("strip")
    row = lax.axis_index("rows")
    sibling = (row, me + 1 - 2 * lax.rem(me, 2))
    pixels[0] = jnp.zeros((NF, 384), BF)
    pixels[33] = jnp.zeros((NF, 384), BF)

    def turn_rows(i, carry):
        flat = turned_rows(x, i)
        for k in range(4):
            stage[k, i] = flat[first_frame(k) : first_frame(k) + NF]
        return carry

    barrier = pltpu.get_barrier_semaphore()
    for k in range(1, 4):
        pl.semaphore_signal(
            barrier, inc=1, device_id=(row, lax.rem(me + k, 4)), device_id_type=MESH
        )
    lax.fori_loop(0, 4, turn_rows, 0)
    pl.semaphore_wait(barrier, 3)
    copies = []

    def send(part):
        for k in range(1, 4):
            to = lax.rem(me + k, 4)
            copy = pltpu.make_async_remote_copy(
                src_ref=stage.at[to, pl.ds(4 * part, 4)],
                dst_ref=pixels.at[pl.ds(1 + 8 * me + 4 * part, 4)],
                send_sem=send_sem.at[3 * part + k - 1],
                recv_sem=recv_sem.at[3 * part + k - 1],
                device_id=(row, to),
                device_id_type=MESH,
            )
            copy.start()
            copies.append(copy)

    send(0)
    lax.fori_loop(4, 8, turn_rows, 0)
    send(1)

    def to_sibling(src, dst, index):
        copy = pltpu.make_async_remote_copy(
            src_ref=src,
            dst_ref=dst,
            send_sem=side_sems.at[0, index],
            recv_sem=side_sems.at[1, index],
            device_id=sibling,
            device_id_type=MESH,
        )
        copy.start()
        copies.append(copy)

    for index, (src, dst) in enumerate(
        ((emb, emb1), (qkv, qkv1), (proj, proj1), (up, up1), (down, down1))
    ):
        to_sibling(src, dst, index)
    pixels[pl.ds(1 + 8 * me, 8)] = stage[me]

    turn_kernel(later, t0, t1, t2, t3)
    stores = []

    def store(src, dst):
        copy = pltpu.make_async_copy(src, dst, out_sems.at[len(stores)])
        copy.start()
        stores.append(copy)

    swap = exchange_16()
    put_outer(va, vb, e1, False)
    store(va, ea)
    store(vb, eb)
    put_bands(vt2, vu2, [band(f, 4, 32, 64) for f in canonical(e2, swap, 32, 64, False)], None, 4)
    store(vt2, et2)
    store(vu2, eu2)
    put_bands(vt3, vu3, [band(f, 2, 64, 128) for f in canonical(e3, swap, 64, 128, False)], None, 2)
    store(vt3, et3)
    store(vu3, eu3)
    turned = canonical_turned(e4, swap)
    put_bands(vt4, vu4, [f.T for f in turned], turned, 1)
    store(vt4, et4)
    store(vu4, eu4)
    for b in range(16):
        rows = slice(256 * b, 256 * b + 256)
        for src, dst in ((lh[rows, :], vl), (dh[:, rows].T, vd)):
            block = jnp.dot(swap, src, preferred_element_type=F32).astype(BF)
            for k in range(16):
                dst[256 * k + 16 * b : 256 * k + 16 * b + 16] = block[16 * k : 16 * k + 16]
    store(vl, lh0)
    store(vd, dh0)
    to_sibling(vl, lh1, 5)
    to_sibling(vd, dh1, 6)
    for copy in copies:
        copy.wait()
    for copy in stores:
        copy.wait()


BUILT = [(1152, 1024), (3072, 384)] + [(2048, 256)] * 3
BUILT = BUILT + [(2, 1024, 256), (2, 1024, 256), (2, 1536, 256)]


def start(frames, later, kernels, latent_head, decode_head, others):
    e1, e2, e3, e4 = kernels
    rows_in = [
        jnp.tile(jnp.transpose(e1, (1, 2, 3, 0)).reshape(48, 32), (1, 32)).astype(F32),
        jnp.transpose(e2, (1, 2, 3, 0)).reshape(512, 64),
        jnp.transpose(e3, (1, 2, 3, 0)).reshape(1024, 128),
        jnp.transpose(e4, (0, 2, 3, 1)).reshape(4096, 128),
    ]
    dma = pltpu.SemaphoreType.DMA
    any_spec = pl.BlockSpec(memory_space=pl.ANY)
    heads = [(4096, 256)] * 4
    shapes = [(34, NF, 384)] + BUILT + heads + [w.shape for w in others]
    shapes = shapes + [(8, NF, 384)] * 4
    out = pl.pallas_call(
        start_kernel,
        out_shape=tuple(S(shape) for shape in shapes),
        in_specs=VM(8) + [any_spec] * len(others),
        out_specs=tuple(VM(1) + [any_spec] * (len(shapes) - 5) + VM(4)),
        scratch_shapes=[
            V((4, 8, NF, 384)),
            dma((6,)),
            dma((6,)),
            dma((2, 7)),
            *[V(shape) for shape in BUILT],
            V((4096, 256)),
            V((4096, 256)),
            dma((10,)),
        ],
        compiler_params=pltpu.CompilerParams(
            collective_id=1, has_side_effects=True, vmem_limit_bytes=56 * MIB
        ),
        cost_estimate=estimate(22),
        name="start",
    )(
        jnp.transpose(frames, (1, 2, 3, 0)),
        jnp.transpose(later, (1, 2, 3, 0)),
        *rows_in,
        latent_head,
        decode_head,
        *others,
    )
    hints = around(out[-4:])
    return out[0], out[1:9], out[9:11], out[11:13], out[13:-4], hints


def decoder_rows(kernels):
    d1, d2, d3, d4 = kernels
    return (
        jnp.transpose(d1, (0, 2, 3, 1)).reshape(2048, 256),
        jnp.transpose(d2, (0, 2, 3, 1)).reshape(1024, 128),
        jnp.transpose(d3, (0, 2, 3, 1)).reshape(512, 64),
        jnp.tile(jnp.transpose(d4, (0, 2, 3, 1)).reshape(48, 32), (1, 32)).astype(F32),
    )


def turn_kernel(x, *out):
    me = lax.axis_index("strip")

    def turn_rows(i, carry):
        flat = turned_rows(x, i)
        for k in range(4):
            part = flat[first_frame(k) : first_frame(k) + NF]
            for step in range(4):

                @pl.when(lax.rem(me + step, 4) == k)
                def _():
                    out[step][i] = part

        return carry

    lax.fori_loop(0, 8, turn_rows, 0)


def around(parts):
    return [parts[0]] + [
        lax.ppermute(parts[k], "strip", [(s, (s + k) % 4) for s in range(4)]) for k in range(1, 4)
    ]


def dot(a, b):
    return jnp.dot(a, b, preferred_element_type=F32)


def dot_nt(a, b):
    return lax.dot_general(a, b, (((1,), (1,)), ((), ())), preferred_element_type=F32)


def over_groups(values, join):
    lanes = values.shape[1]
    lane = lax.broadcasted_iota(jnp.int32, values.shape, 1)
    for step in (1, 2, 4, 8, 16):
        upper = lax.rem(lax.div(lane, step), 2) == 1
        other = jnp.where(
            upper, pltpu.roll(values, step, 1), pltpu.roll(values, lanes - step, 1)
        )
        values = join(values, other)
    return values


def unit_of(hidden):
    centred = hidden - jnp.mean(hidden, -1, keepdims=True)
    scale_inv = lax.rsqrt(jnp.mean(centred * centred, -1, keepdims=True) + EPS)
    return centred * scale_inv, scale_inv


def unit_back(grad_normed, unit_rows, scale_inv, gain):
    grad_unit = grad_normed * gain
    grad_gain = jnp.sum(grad_normed * unit_rows, 0, keepdims=True)
    grad_rows = scale_inv * (
        grad_unit
        - jnp.mean(grad_unit, -1, keepdims=True)
        - unit_rows * jnp.mean(grad_unit * unit_rows, -1, keepdims=True)
    )
    return grad_gain, grad_rows


LAYER_ROWS = 1536


def token_rows(layers, count):
    upper = max(layers - 1, 1) * LAYER_ROWS
    lower = LAYER_ROWS + 256 + NF + 16
    return share_rows(upper, count), share_rows(lower, count)


def middle_kernel(
    layers, count,
    feat, lh0, lh1, dh0, dh1, emb0, emb1, pos, gains, allow, cot,
    qkv0, qkv1, proj0, proj1, up0, up1, down0, down1, d1, d2, d3, d4,
    tokens, latent_out, chances_out, decoded, upper_both, lower, grad_latent, feat_got,
    latent_near, feat_near, got_near, da, db, dt2, dt3, dt4, du2, du3, du4,
    feat_sems, keep, send, sent, spread_sems, parts, gots, pair_sems,
    upper, upper_other, upper_got, lower_other, lower_got, upper_near, fold_sems, near_sems, unit_a, unit_f, normed_a, normed_f, mixed, weights,
    attended, before, inner, gain_rows, wa, wb, wt2, wt3, wt4, wu2, wu3, wu4, form_sems,
):
    strip = lax.axis_index("strip")
    row = lax.axis_index("rows")
    place_here = Place(count)
    partner, sibling = place_here.partner, place_here.sibling
    place_here.greet([partner, sibling, place_here.near_device])

    def copy(src, dst, sems, index, device):
        return pltpu.make_async_remote_copy(
            src_ref=src,
            dst_ref=dst,
            send_sem=sems.at[0, index],
            recv_sem=sems.at[1, index],
            device_id=device,
            device_id_type=MESH,
        )

    feat_copy = copy(feat, feat_got, feat_sems, 0, partner)
    feat_copy.start()

    def total_start(index, value):
        parts[index] = value.astype(BF)
        one = copy(parts.at[index], gots.at[index], pair_sems, index, partner)
        one.start()
        return one

    def total_wait(index, one):
        one.wait()
        got = jnp.concatenate([gots[index, NF:], gots[index, :NF]], axis=0)
        return parts[index].astype(F32) + got.astype(F32)

    def logits_of(maps):
        halves = []
        for weight in (lh0, lh1):
            total = jnp.zeros((NF, 256), F32)
            for h in range(4):
                total = total + dot(maps[h], weight[1024 * h : 1024 * h + 1024])
            halves.append(total)
        return jnp.concatenate(halves, axis=1)

    mine = logits_of(feat)
    feat_copy.wait()
    near_sends = Sems(near_sems, None)
    near_copies = [
        near_sends.copy(
            src.at[:, :, half_lanes(place_here, w)],
            dst.at[:, :, 128 * w : 128 * w + 128],
            place_here.near_device,
        )
        for src, dst in ((feat, feat_near), (feat_got, got_near))
        for w in range(4)
    ]
    logits = jnp.concatenate([mine, logits_of(feat_got)], axis=0)
    raised = jnp.exp(logits - over_groups(logits, jnp.maximum))
    chances = raised / over_groups(raised, jnp.add)
    latent = chances.astype(BF)
    chances_out[...] = chances
    latent_out[...] = latent
    near_copies.append(near_sends.copy(latent_out, latent_near, place_here.near_device))

    waiting = total_start(0, dot(latent[:, :256], emb0[...]) + dot(latent[:, 256:], emb1[...]))
    for hw in range(16):
        lanes = slice(256 * (hw % 4), 256 * (hw % 4) + 256)
        rows = slice(256 * hw, 256 * hw + 256)
        value = dot_nt(latent[:, :256], dh0[rows]) + dot_nt(latent[:, 256:], dh1[rows])
        value = value.astype(BF)
        keep[hw // 4, :, lanes] = value[:NF]
        send[hw // 4, :, lanes] = value[NF:]
    spread_copy = copy(send, sent, spread_sems, 0, partner)
    spread_copy.start()
    embedded = total_wait(0, waiting)
    place = pos[...].astype(F32)
    hidden = embedded + jnp.concatenate([place, place], axis=0)
    swap = exchange_16()
    forms = []

    def store(src, dst):
        one = pltpu.make_async_copy(src, dst, form_sems.at[len(forms)])
        one.start()
        forms.append(one)

    def build(step):
        if step == 0:
            put_outer(wa, wb, d4, True)
            store(wa, da)
            store(wb, db)
        if step == 1:
            bands = [band(f, 4, 32, 64) for f in canonical(d3, swap, 32, 64, True)]
            put_bands(wt2, wu2, bands, None, 4)
            store(wt2, dt2)
            store(wu2, du2)
        if step == 2:
            bands = [band(f, 2, 64, 128) for f in canonical(d2, swap, 64, 128, True)]
            put_bands(wt3, wu3, bands, None, 2)
            store(wt3, dt3)
            store(wu3, du3)
        if step == 3:
            put_bands(wt4, wu4, canonical(d1, swap, 128, 256, True), None, 1)
            store(wt4, dt4)
            store(wu4, du4)

    head_lane = lax.div(lax.broadcasted_iota(jnp.int32, (2 * NF, 128), 1), HEAD_DIM)
    allowed = allow[...] > 0.5

    def of_head(value, h):
        return jnp.where(head_lane == h % 2, value, jnp.zeros_like(value))

    def pair_lanes(h):
        return slice(128 * (h // 2), 128 * (h // 2) + 128)

    for k in range(layers):
        unit, inv = unit_of(hidden)
        unit_a[k] = jnp.concatenate([unit, jnp.broadcast_to(inv, (2 * NF, 128))], axis=1)
        normed = (unit * gains[2 * k : 2 * k + 1]).astype(BF)
        normed_a[k] = normed
        for part in range(3):
            mixed[k, part] = jnp.concatenate(
                [dot(normed, qkv0[k, part]), dot(normed, qkv1[k, part])], axis=1
            ).astype(BF)
        for p in range(2):
            both = jnp.zeros((2 * NF, 128), F32)
            for h in (2 * p, 2 * p + 1):
                lanes = pair_lanes(h)
                scores = SCALE * dot_nt(of_head(mixed[k, 0, :, lanes], h), mixed[k, 1, :, lanes])
                scores = jnp.where(allowed, scores, NEG)
                lifted = jnp.exp(scores - jnp.max(scores, -1, keepdims=True))
                weight = lifted / jnp.sum(lifted, -1, keepdims=True)
                weights[k, h] = weight
                both = both + of_head(dot(weight.astype(BF), mixed[k, 2, :, lanes]), h)
            attended[k, :, 128 * p : 128 * p + 128] = both.astype(BF)
        partial = dot(attended[k, :, :128], proj0[k]) + dot(attended[k, :, 128:], proj1[k])
        waiting = total_start(2 * k + 1, partial)
        build(2 * k)
        middle = hidden + total_wait(2 * k + 1, waiting)
        unit, inv = unit_of(middle)
        unit_f[k] = jnp.concatenate([unit, jnp.broadcast_to(inv, (2 * NF, 128))], axis=1)
        normed = (unit * gains[2 * k + 1 : 2 * k + 2]).astype(BF)
        normed_f[k] = normed
        partial = jnp.zeros((2 * NF, 512), F32)
        for side, (up, down) in enumerate(((up0, down0), (up1, down1))):
            value = dot(normed, up[k])
            before[k, :, 512 * side : 512 * side + 512] = value
            act = (value * sig(value)).astype(BF)
            inner[k, :, 512 * side : 512 * side + 512] = act
            partial = partial + dot(act, down[k])
        waiting = total_start(2 * k + 2, partial)
        build(2 * k + 1)
        hidden = middle + total_wait(2 * k + 2, waiting)
    tokens[...] = hidden.astype(BF)

    spread_copy.wait()
    decoded[...] = (keep[...].astype(F32) + sent[...].astype(F32)).astype(BF)

    def fold_start(index, part, got):
        one = copy(part, got, fold_sems, index, sibling)
        one.start()
        return one

    def fold_end(one, own, got, count):
        one.wait()
        for first in range(0, count, 128):
            rows = slice(first, min(first + 128, count))
            own[rows] = (own[rows].astype(F32) + got[rows].astype(F32)).astype(BF)
        if own.shape[0] > count:
            own[count:] = jnp.zeros((own.shape[0] - count, 512), BF)

    lower_rows = LAYER_ROWS + 256 + NF + 16

    grad = cot[...].astype(F32)
    for k in reversed(range(layers)):
        flat, other = (upper, upper_other) if k else (lower, lower_other)
        base = LAYER_ROWS * (k - 1) if k else 0
        index = 2 * layers + 1 + 2 * (layers - 1 - k)
        low = grad.astype(BF)
        partial = jnp.zeros((2 * NF, 512), F32)
        grads = []
        for side, (up, down) in enumerate(((up0, down0), (up1, down1))):
            value = before[k, :, 512 * side : 512 * side + 512]
            squash = sig(value)
            slope = squash * (1.0 + value * (1.0 - squash))
            grad_before = (dot_nt(low, down[k]) * slope).astype(BF)
            grads.append(grad_before)
            partial = partial + dot_nt(grad_before, up[k])
        waiting = total_start(index, partial)
        turned = normed_f[k].T
        for side, dst in enumerate((flat, other)):
            act = inner[k, :, 512 * side : 512 * side + 512]
            dst[base : base + 512] = dot(act.T, low).astype(BF)
            dst[base + 512 : base + 1024] = dot(turned, grads[side]).astype(BF)
        if k == 0:
            fold_end(upper_fold, upper, upper_got, LAYER_ROWS * (layers - 1))
            near_copy = near_start(place_here, near_sends, upper, upper_near)
        grad_normed = total_wait(index, waiting)
        gain_f, grad_rows = unit_back(
            grad_normed, unit_f[k, :, :512], unit_f[k, :, 512:513], gains[2 * k + 1 : 2 * k + 2]
        )
        grad = grad + grad_rows
        low = grad.astype(BF)
        grad_mixed = [[], [], []]
        for p, proj in enumerate((proj0, proj1)):
            lanes = pair_lanes(2 * p)
            grad_pair = dot_nt(low, proj[k]).astype(BF)
            queries, keys, vals = mixed[k, 0, :, lanes], mixed[k, 1, :, lanes], mixed[k, 2, :, lanes]
            g_queries = jnp.zeros((2 * NF, 128), F32)
            g_keys, g_vals = g_queries, g_queries
            for h in (2 * p, 2 * p + 1):
                weight = weights[k, h]
                grad_head = of_head(grad_pair, h)
                g_vals = g_vals + dot(weight.astype(BF).T, grad_head)
                grad_weight = dot_nt(grad_head, vals)
                along = jnp.sum(weight * grad_weight, -1, keepdims=True)
                grad_scores = (weight * (grad_weight - along)).astype(BF)
                g_queries = g_queries + of_head(dot(grad_scores, keys), h)
                g_keys = g_keys + dot(grad_scores.T, of_head(queries, h))
            grad_mixed[0].append((SCALE * g_queries).astype(BF))
            grad_mixed[1].append((SCALE * g_keys).astype(BF))
            grad_mixed[2].append(g_vals.astype(BF))
        partial = jnp.zeros((2 * NF, 512), F32)
        for part in range(3):
            for side, qkv in enumerate((qkv0, qkv1)):
                partial = partial + dot_nt(grad_mixed[part][side], qkv[k, part])
        waiting = total_start(index + 1, partial)
        turned = normed_a[k].T
        for side, dst in enumerate((flat, other)):
            act = attended[k, :, 128 * side : 128 * side + 128]
            dst[base + 1024 : base + 1152] = dot(act.T, low).astype(BF)
            for part in range(3):
                value = dot(turned, grad_mixed[part][side]).astype(BF)
                first = base + 1152 + 128 * part
                for b in range(4):
                    dst[first : first + 128, 128 * b : 128 * b + 128] = value[
                        128 * b : 128 * b + 128
                    ]
        if k == 1:
            upper_fold = fold_start(0, upper_other, upper_got)
        grad_normed = total_wait(index + 1, waiting)
        gain_a, grad_rows = unit_back(
            grad_normed, unit_a[k, :, :512], unit_a[k, :, 512:513], gains[2 * k : 2 * k + 1]
        )
        grad = grad + grad_rows
        gain_rows[2 * k : 2 * k + 1] = gain_a
        gain_rows[2 * k + 1 : 2 * k + 2] = gain_f

    low = grad.astype(BF)
    own_latent, other_latent = latent_out[:, :256], latent_out[:, 256:]
    lower[LAYER_ROWS : LAYER_ROWS + 256] = dot(own_latent.T, low).astype(BF)
    lower_other[LAYER_ROWS : LAYER_ROWS + 256] = dot(other_latent.T, low).astype(BF)
    rest = jnp.concatenate(
        [
            grad[:NF] + grad[NF:],
            gain_rows[...],
            jnp.zeros((16 - 2 * layers, 512), F32),
        ],
        axis=0,
    ).astype(BF)
    lower[LAYER_ROWS + 256 : lower_rows] = rest
    lower_other[LAYER_ROWS + 256 : lower_rows] = rest
    lower_fold = fold_start(1, lower_other, lower_got)
    grad_latent[:, :256] = dot_nt(low, emb0[...])
    grad_latent[:, 256:] = dot_nt(low, emb1[...])
    near_end(place_here, near_copy, upper, upper_near, upper_both)
    fold_end(lower_fold, lower, lower_got, lower_rows)
    for step in range(2 * layers, 4):
        build(step)
    for one in near_copies + forms:
        one.wait()


def middle(layers, *args):
    count = lax.axis_size("rows")
    upper, lower = token_rows(layers, count)
    dma = pltpu.SemaphoreType.DMA
    sums = 4 * layers + 1
    t = 2 * NF
    return pl.pallas_call(
        functools.partial(middle_kernel, layers, count),
        out_shape=(
            S((t, 512)),
            S((t, 512)),
            S((t, 512), F32),
            S((4, NF, 1024)),
            S((upper // 2, 512)),
            S((lower, 512)),
            S((t, 512), F32),
            S((4, NF, 1024)),
            S((t, 512)),
            S((4, NF, 512)),
            S((4, NF, 512)),
            *[S(shape) for shape in BUILT],
        ),
        in_specs=VM(len(args)),
        out_specs=tuple(VM(11) + [pl.BlockSpec(memory_space=pl.ANY)] * 8),
        scratch_shapes=[
            dma((2, 1)),
            V((4, NF, 1024)),
            V((4, NF, 1024)),
            V((4, NF, 1024)),
            dma((2, 1)),
            V((sums, t, 512)),
            V((sums, t, 512)),
            dma((2, sums)),
            V((upper, 512)),
            V((upper, 512)),
            V((upper, 512)),
            V((lower, 512)),
            V((lower, 512)),
            V((upper // 2, 512)),
            dma((2, 2)),
            dma((2, 10)),
            V((layers, t, 640), F32),
            V((layers, t, 640), F32),
            V((layers, t, 512)),
            V((layers, t, 512)),
            V((layers, 3, t, 256)),
            V((layers, 4, t, t), F32),
            V((layers, t, 256)),
            V((layers, t, 1024), F32),
            V((layers, t, 1024)),
            V((2 * layers, 512), F32),
            *[V(shape) for shape in BUILT],
            dma((8,)),
        ],
        compiler_params=pltpu.CompilerParams(
            collective_id=3, has_side_effects=True, vmem_limit_bytes=56 * MIB
        ),
        cost_estimate=estimate(84),
        name="middle",
    )(*args)


def back_kernel(
    count, grad, latent, latent_near, chances, grad_embed, feat0, feat1, feat2, feat3,
    lh0, lh1, dh0, dh1, flat, lower_piece,
    grad_feat, share, d_piece, l_both, lower_half,
    got, got_near, got_cross, keep, send, sent, logits_here, logits_near, own, other, other_got,
    d_both, d_slots, side_got, side_sum, cross_got, remote, here,
):
    place = Place(count)
    near, core, x = place.near, place.core, place.x
    cross_device = (place.near_device[0], place.partner[1])
    place.greet(
        [place.partner, place.sibling, place.near_device, cross_device] + place.far_devices
    )
    sems = Sems(remote, here)
    grad_copies = [sems.copy(grad, got, place.partner)]
    for device, dst in ((place.near_device, got_near), (cross_device, got_cross)):
        for w in range(4):
            grad_copies.append(
                sems.copy(
                    grad.at[:, :, half_lanes(place, w)], dst.at[:, :, 128 * w : 128 * w + 128], device
                )
            )
    lower_back = back_start(place, sems, lower_piece, lower_half)
    side_copy = sems.copy(flat.at[1 - core], side_got, place.sibling)

    def through(maps):
        halves = []
        for weight in (dh0, dh1):
            total = jnp.zeros((NF, 256), F32)
            for h in range(4):
                total = total + dot(maps[h], weight[1024 * h : 1024 * h + 1024])
            halves.append(total)
        return jnp.concatenate(halves, axis=1)

    def head_grad(slot, wide, narrow, rhs):
        for h in range(4):
            for w in range(4):
                lanes = pl.ds(pl.multiple_of(256 * w + 128 * near, 128), 128)
                maps = [ref[h, :, lanes] for ref in wide]
                maps = maps + [ref[h, :, 128 * w : 128 * w + 128] for ref in narrow]
                rows = slice(512 * h + 128 * w, 512 * h + 128 * w + 128)
                value = dot(jnp.concatenate(maps, axis=0).T, rhs).astype(BF)
                own[slot, rows] = value[:, :256]
                other[slot, rows] = value[:, 256:]
        return sems.copy(other.at[slot], other_got.at[slot], place.sibling)

    swap = exchange_16()

    def folded(slot, b):
        parts = []
        for k in range(16):
            rows = slice(128 * k + 16 * b, 128 * k + 16 * b + 16)
            value = own[slot, rows].astype(F32) + other_got[slot, rows].astype(F32)
            parts.append(value.astype(BF))
        return dot(swap, jnp.concatenate(parts, axis=0)).astype(BF)

    mine = through(grad)
    side_copy.wait()
    side_sum[...] = (flat[core].astype(F32) + side_got[...].astype(F32)).astype(BF)
    for one in grad_copies:
        one.wait()
    cross_copy = sems.copy(side_sum.at[1 - x], cross_got, place.partner)
    both_latents = jnp.concatenate([latent[...], latent_near[...]], axis=0)
    out_fold = head_grad(0, (grad, got), (got_near, got_cross), both_latents)
    grad_latent = grad_embed[...] + jnp.concatenate([mine, through(got)], axis=0)
    probs = chances[...]
    along = over_groups(probs * grad_latent, jnp.add)
    grad_logits = (probs * (grad_latent - along)).astype(BF)
    logits_here[...] = grad_logits
    logits_copy = sems.copy(logits_here, logits_near, place.near_device)
    out_fold.wait()
    for b in range(8):
        d_both[256 * b : 256 * b + 256] = folded(0, b).T
    d_far = far_start(place, sems, d_both, d_slots)
    logits_copy.wait()
    both_logits = jnp.concatenate([grad_logits, logits_near[...]], axis=0)
    in_fold = head_grad(1, (feat0, feat1), (feat2, feat3), both_logits)
    sends = []
    for h in range(4):
        for w in range(4):
            lanes = slice(256 * w, 256 * w + 256)
            rows = slice(1024 * h + 256 * w, 1024 * h + 256 * w + 256)
            value = dot_nt(grad_logits[:, :256], lh0[rows]) + dot_nt(grad_logits[:, 256:], lh1[rows])
            value = value.astype(BF)
            keep[h, :, lanes] = value[:NF]
            send[h, :, lanes] = value[NF:]
        sends.append(sems.copy(send.at[h], sent.at[h], place.partner))
    in_fold.wait()
    for b in range(8):
        l_both[256 * b : 256 * b + 256] = folded(1, b)
    cross_copy.wait()
    share[...] = (side_sum[x].astype(F32) + cross_got[...].astype(F32)).astype(BF)
    for one in sends + lower_back:
        one.wait()
    grad_feat[...] = (keep[...].astype(F32) + sent[...].astype(F32)).astype(BF)
    far_end(place, d_far, d_both, d_slots, d_piece)


def latents_back(*args):
    dma = pltpu.SemaphoreType.DMA
    count = lax.axis_size("rows")
    half = count // 2
    flat, lower_piece = args[-2:]
    quarter = flat.shape[0] // 4
    args = args[:-2] + (flat.reshape(2, 2, quarter, 256), lower_piece)
    maps = (4, NF, 1024)
    narrow = (4, NF, 512)
    rows = (2048, 256)
    return pl.pallas_call(
        functools.partial(back_kernel, count),
        out_shape=(
            S(maps),
            S((quarter, 256)),
            S((4096 // count, 256)),
            S(rows),
            S((half * lower_piece.shape[0], 512)),
        ),
        in_specs=VM(len(args)),
        out_specs=tuple(VM(5)),
        scratch_shapes=[
            V(maps),
            V(narrow),
            V(narrow),
            V(maps),
            V(maps),
            V(maps),
            V((2 * NF, 512)),
            V((2 * NF, 512)),
            V((2,) + rows),
            V((2,) + rows),
            V((2,) + rows),
            V(rows),
            V((half - 1, 4096 // count, 256)),
            V((2, quarter, 256)),
            V((2, quarter, 256)),
            V((quarter, 256)),
            dma((2, 2 * half + 20)),
            dma((2,)),
        ],
        compiler_params=pltpu.CompilerParams(
            collective_id=4, has_side_effects=True, vmem_limit_bytes=58 * MIB
        ),
        cost_estimate=estimate(55),
        name="latents_back",
    )(*args)


def strip_fold_start(place, sems, flat, first, size, got):
    half = size // 2
    return sems.copy(
        flat.at[pl.ds(pl.multiple_of(first + (1 - place.core) * half, 16), half)], got, place.sibling
    )


def strip_cross_start(place, sems, copy, flat, first, size, got, both, cross):
    copy.wait()
    half = size // 2
    own = flat[pl.ds(pl.multiple_of(first + place.core * half, 16), half)]
    both[...] = (own.astype(F32) + got[...].astype(F32)).astype(BF)
    return sems.copy(rows_of(both, 1 - place.x, half // 2), cross, place.partner)


def strip_share(place, copy, both, cross):
    copy.wait()
    own = rows_of(both, place.x, cross.shape[0])[...]
    return (own.astype(F32) + cross[...].astype(F32)).astype(BF)


def padded_share(ref, parts):
    share = jnp.concatenate(parts, axis=0)
    spare = ref.shape[0] - share.shape[0]
    if spare:
        share = jnp.concatenate([share, jnp.zeros((spare, 256), BF)], axis=0)
    ref[...] = share


def enc_bwd_kernel(
    count, xp, z1, z2, z3, z4, df, u2, u3, u4, b, dec, d_piece, l_both, t_half,
    d_total, l_total, t_total, early, late, grad_out,
    m1, m2, m3, s1, s2, s3, s4, yt, pk, dx, got, rows_out,
    l_slots, l_piece,
    e_fold, e_sum, e_cross, e_values, e_near, e_both, e_slots, e_piece,
    f_fold, f_sum, f_cross, f_values, f_slots, f_piece,
    remote, here,
):
    place = Place(count)
    near, core, x = place.near, place.core, place.x
    sems = Sems(remote, here)
    row_places = [lax.rem(place.row + k, count) for k in range(1, count)]
    row_devices = [(at, place.me) for at in row_places]
    cross_device = (place.near_device[0], place.partner[1])
    place.greet(place.others + row_devices + [cross_device])

    def home(ref):
        return rows_of(ref, near, ref.shape[0] // 2)

    def waits(copies):
        for one in copies:
            one.wait()

    l_far = far_start(place, sems, l_both, l_slots)
    t_own = sems.here(t_half, home(t_total))
    t_last = last_start(place, sems, t_half, t_total)

    zero_big(m1, 32)
    zero_big(m2, 16)
    zero_big(m3, 8)
    zero_small(s1, 32, 0)
    zero_small(s2, 16, 128)
    zero_small(s3, 8, 128)
    zero_small(s4, 4, 256)
    swap = exchange_16()
    z = z4[...].astype(F32)
    s = sig(z)
    s4[1:5, :, 256:1280] = (df[...].astype(F32) * (s * (1.0 + z * (1.0 - s)))).astype(BF)

    def back(z_ref, m, dst, pad):
        def emit(m0, odd, q, acc):
            for t in range(acc.shape[0]):
                h = 2 * (m0 + t) + odd
                zz = z_ref[h, :, 256 * q : 256 * q + 256].astype(F32)
                ss = sig(zz)
                mm = zz * ss
                dst[h + 1, :, pad + 256 * q : pad + 256 * q + 256] = (
                    acc[t] * (ss + mm * (1.0 - ss))
                ).astype(BF)
                m[m0 + t + odd, 1 - odd, :, 128 + 256 * q : 384 + 256 * q] = mm.astype(BF)

        return emit

    up(s4, u4, 4, 4, back(z3, m3, s3, 128))
    turn(s4, yt, 4, 256)
    pack(pk, 0, 1, 128, 256, grad_w(m3, yt, 4), False, swap, True)
    up(s3, u3, 8, 4, back(z2, m2, s2, 128))
    turn(s3, yt, 8, 128)
    pack(pk, 2048, 2, 64, 128, grad_w(m2, yt, 8), False, swap)
    e_copy = strip_fold_start(place, sems, pk, 0, 2560, e_fold)
    far_end(place, l_far, l_both, l_slots, l_piece)
    l_back = [back_part(place, sems, l_piece, home(l_total), part) for part in range(2)]
    e_copy = strip_cross_start(place, sems, e_copy, pk, 0, 2560, e_fold, e_sum, e_cross)
    up(s2, u2, 16, 4, back(z1, m1, s1, 0))
    padded_share(e_values, [dec[...], strip_share(place, e_copy, e_sum, e_cross)])
    e_copy = near_start(place, sems, e_values, e_near)

    def put(i0, acc):
        dx[pl.ds(i0, acc.shape[0])] = acc.astype(BF)

    outer_up(s1, b, put)
    strips = [
        sems.copy(dx.at[pl.ds(8 * device[1], 8)], got.at[place.me], device)
        for device in place.others
    ]
    got[place.me] = dx[pl.ds(8 * place.me, 8)]
    near_end(place, e_copy, e_values, e_near, e_both)
    e_far = far_start(place, sems, e_both, e_slots)
    waits(l_back[0])
    l_last = last_part(place, sems, home(l_total), l_piece.shape[0], 0)
    turn(s2, yt, 16, 128)
    pack(pk, 2560, 4, 32, 64, grad_w(m1, yt, 16), False, swap)
    far_end(place, e_far, e_both, e_slots, e_piece)
    e_out = early.at[core, x]
    e_back = back_start(place, sems, e_piece, home(e_out))
    waits(l_back[1])
    l_last = l_last + last_part(place, sems, home(l_total), l_piece.shape[0], 1)
    d_back = [back_part(place, sems, d_piece, home(d_total), part) for part in range(2)]
    turn(s1, yt, 32, 0)
    pack_outer(pk, 2688, outer_grad(xp, yt), False)
    f_copy = strip_fold_start(place, sems, pk, 2560, 256, f_fold)
    waits(e_back)
    e_last = [
        sems.copy(home(e_out), home(e_out), device)
        for device in (place.near_device, place.partner, cross_device)
    ]
    f_copy = strip_cross_start(place, sems, f_copy, pk, 2560, 256, f_fold, f_sum, f_cross)
    waits(strips)
    stores = []

    def turn_out(first, count_here):
        for i in range(first, first + count_here):
            slot = i % 2
            if i > 1:
                stores[i - 2].wait()
            block = jnp.concatenate([got[(k % 2) * 2 + k // 2, i] for k in range(4)], axis=0)
            flat = block.T.astype(F32)
            for p in range(2):
                for c in range(3):
                    rows_out[slot, c, p] = flat[64 * (3 * p + c) : 64 * (3 * p + c) + 64]
            stores.append(sems.here(rows_out.at[slot], grad_out.at[:, 2 * i : 2 * i + 2]))

    turn_out(0, 4)
    waits(d_back[0])
    d_last = last_part(place, sems, home(d_total), d_piece.shape[0], 0)
    padded_share(f_values, [strip_share(place, f_copy, f_sum, f_cross)])
    each = f_piece.shape[0]
    f_rows = [
        sems.copy(rows_of(f_values, at, each), f_slots.at[k], device)
        for k, (at, device) in enumerate(zip(row_places, row_devices))
    ]
    turn_out(4, 4)
    waits(f_rows)
    whole = rows_of(f_values, place.row, each)[...].astype(F32)
    for k in range(count - 1):
        whole = whole + f_slots[k].astype(F32)
    f_piece[...] = whole.astype(BF)
    f_out = rows_of(late.at[core, x], place.row, each)
    f_back = [sems.here(f_piece, f_out)]
    f_back = f_back + [sems.copy(f_piece, f_out, device) for device in row_devices]
    waits(d_back[1])
    d_last = d_last + last_part(place, sems, home(d_total), d_piece.shape[0], 1)
    waits(e_last)
    e_side = sems.copy(early.at[core], early.at[core], place.sibling)
    waits(f_back)
    f_cross_out = sems.copy(late.at[core, x], late.at[core, x], place.partner)
    f_cross_out.wait()
    f_side = sems.copy(late.at[core], late.at[core], place.sibling)
    waits(stores[-2:])
    t_own.wait()
    waits([t_last, e_side, f_side] + d_last + l_last)


def share_rows(rows, count):
    return rows + -rows % (16 * count)


def enc_bwd(maps, dec, d_piece, l_both, t_half):
    count = lax.axis_size("rows")
    half = count // 2
    dma = pltpu.SemaphoreType.DMA
    any_spec = pl.BlockSpec(memory_space=pl.ANY)
    head = 2 * l_both.shape[0]
    quarter = dec.shape[0]
    early = share_rows(quarter + 640, count)
    late = share_rows(64, count)

    def steps(rows):
        return [
            V((rows, 256)),
            V((rows // 2, 256)),
            V((rows // 2, 256)),
            V((half - 1, rows // count, 256)),
            V((rows // count, 256)),
        ]

    d_total, l_total, t_total, e_out, f_out, grad_out = pl.pallas_call(
        functools.partial(enc_bwd_kernel, count),
        out_shape=(
            S((head, 256)),
            S((head, 256)),
            S((2 * t_half.shape[0], 512)),
            S((2, 2, early, 256)),
            S((2, 2, late, 256)),
            S((3, 16, 64, 256), F32),
        ),
        in_specs=VM(len(maps) + 4),
        out_specs=tuple([any_spec] * 6),
        scratch_shapes=[
            big(32),
            big(16),
            big(8),
            small(32, 0),
            small(16, 128),
            small(8, 128),
            small(4, 256),
            V((1024, 32 * NF)),
            V((2816, 256)),
            V((32, NF, 384)),
            V((4, 8, NF, 384)),
            V((2, 3, 2, 64, 256), F32),
            *steps(head)[3:],
            V((1280, 256)),
            V((1280, 256)),
            V((640, 256)),
            *steps(early),
            V((128, 256)),
            V((128, 256)),
            V((64, 256)),
            V((late, 256)),
            V((count - 1, late // count, 256)),
            V((late // count, 256)),
            dma((2, 7 * (half - 1) + 4 * half + 2 * (count - 1) + 15)),
            dma((18,)),
        ],
        compiler_params=pltpu.CompilerParams(
            collective_id=2, has_side_effects=True, vmem_limit_bytes=60 * MIB
        ),
        cost_estimate=estimate(110),
        name="encode_back",
    )(*maps, dec, d_piece, l_both, t_half)
    return d_total, l_total, t_total, e_out, f_out, jnp.transpose(grad_out, (3, 0, 1, 2))


def unpack_kernel(
    layers, quarter, d_total, l_total, upper, lower, early, late,
    latent_out, head_out, down_out, up_out, project_out, qkv_out, embed_out, place_out, gain_out, *outs,
):
    kernels, scratch, sems = outs[:8], outs[8:-1], outs[-1]
    (
        latent_v, head_v, down_v, up_v, project_v, qkv_v, embed_v, place_v, gain_v, *kernel_v
    ) = scratch
    stores = []

    def store(src, dst):
        one = pltpu.make_async_copy(src, dst, sems.at[len(stores)])
        one.start()
        stores.append(one)

    for k in range(layers):
        src, base = (upper, LAYER_ROWS * (k - 1)) if k else (lower, 0)
        down_v[k] = src[base : base + 512].astype(F32)
        up_v[k] = src[base + 512 : base + 1024].astype(F32)
        project_v[k] = src[base + 1024 : base + 1152].astype(F32)
        for part in range(3):
            first = base + 1152 + 128 * part
            for b in range(4):
                qkv_v[k, part, 128 * b : 128 * b + 128] = src[
                    first : first + 128, 128 * b : 128 * b + 128
                ].astype(F32)
    embed_v[...] = lower[LAYER_ROWS : LAYER_ROWS + 256].astype(F32)
    place_v[...] = lower[LAYER_ROWS + 256 : LAYER_ROWS + 256 + NF].astype(F32)
    gain_v[...] = lower[LAYER_ROWS + 256 + NF : LAYER_ROWS + 256 + NF + 16].astype(F32)[: 2 * layers]
    for src, dst in (
        (down_v, down_out), (up_v, up_out), (project_v, project_out), (qkv_v, qkv_out),
        (embed_v, embed_out), (place_v, place_out), (gain_v, gain_out),
    ):
        store(src, dst)
    for b in range(16):
        rows = slice(256 * b, 256 * b + 256)
        head_v[:, rows] = d_total[rows].astype(F32)
        latent_v[rows] = l_total[rows].astype(F32)
    store(head_v, head_out)
    store(latent_v, latent_out)

    def piece(first, is_enc):
        if not is_enc:
            at, place = divmod(first, quarter)
            return early[at // 2, at % 2, place : place + 64].astype(F32)
        if first < 2560:
            at, place = divmod(first, 640)
            return early[at // 2, at % 2, quarter + place : quarter + place + 64].astype(F32)
        at = (first - 2560) // 64
        return late[at // 2, at % 2, 0:64].astype(F32)

    for is_enc in (False, True):
        outer, first, second, third = kernel_v[4:] if is_enc else kernel_v[:4]
        for r in range(0, 2048, 64):
            value = piece(r, is_enc)
            if is_enc:
                third[r : r + 64] = value[:, :128]
                third[2048 + r : 2048 + r + 64] = value[:, 128:]
            else:
                third[r : r + 64] = value
        for r in range(0, 512, 64):
            value = piece(2048 + r, is_enc)
            second[r : r + 64] = value[:, :128]
            second[512 + r : 512 + r + 64] = value[:, 128:]
        for r in range(0, 128, 64):
            value = piece(2560 + r, is_enc)
            for k in range(4):
                first[128 * k + r : 128 * k + r + 64] = value[:, 64 * k : 64 * k + 64]
        outer[...] = piece(2688, is_enc)[:48, :32]
        for src, dst in zip(kernel_v[4:] if is_enc else kernel_v[:4], kernels[4:] if is_enc else kernels[:4]):
            store(src, dst)
    for one in stores:
        one.wait()


def unpack(layers, quarter, *args):
    dma = pltpu.SemaphoreType.DMA
    any_spec = pl.BlockSpec(memory_space=pl.ANY)
    shapes = [
        (4096, 256),
        (256, 4096),
        (layers, 512, 512),
        (layers, 512, 512),
        (layers, 128, 512),
        (layers, 3, 512, 128),
        (256, 512),
        (NF, 512),
        (2 * layers, 512),
        (48, 32),
        (512, 64),
        (1024, 128),
        (2048, 256),
        (48, 32),
        (512, 64),
        (1024, 128),
        (4096, 128),
    ]
    return pl.pallas_call(
        functools.partial(unpack_kernel, layers, quarter),
        out_shape=tuple(S(shape, F32) for shape in shapes),
        in_specs=VM(len(args)),
        out_specs=tuple([any_spec] * len(shapes)),
        scratch_shapes=[V(shape, F32) for shape in shapes] + [dma((len(shapes),))],
        compiler_params=pltpu.CompilerParams(vmem_limit_bytes=56 * MIB),
        cost_estimate=estimate(12),
        name="unpack",
    )(*args)


def beside(value):
    return lax.ppermute(value, "strip", [(0, 1), (1, 0), (2, 3), (3, 2)])


def make_mask(segment_ids):
    places = jnp.arange(segment_ids.shape[1])
    causal = places[:, None] >= places[None, :]
    return causal[None] & (segment_ids[:, :, None] == segment_ids[:, None, :])


def shards(
    frames,
    segment_ids,
    encode_one,
    encode_two,
    encode_three,
    encode_four,
    latent_head,
    token_embed,
    positions,
    norm_gains,
    qkv_weight,
    out_weight,
    up_weight,
    down_weight,
    decode_head,
    decode_one,
    decode_two,
    decode_three,
    decode_four,
    token_cotangent,
    frame_cotangent,
):
    strip = lax.axis_index("strip")
    x, core = strip // 2, strip % 2
    layers = qkv_weight.shape[0]

    kernels = (encode_one, encode_two, encode_three, encode_four)
    dec_rows = decoder_rows((decode_one, decode_two, decode_three, decode_four))
    qkv = jnp.transpose(qkv_weight, (0, 2, 1, 3))
    shards_here = (token_embed, qkv, out_weight, up_weight, down_weight)
    pixels, enc_f, head_in, head_out, theirs, hints = start(
        frames, frame_cotangent, kernels, latent_head, decode_head, shards_here
    )
    enc_a, enc_b, enc_t, enc_u = enc_f[0], enc_f[1], enc_f[2:5], enc_f[5:8]
    embed, qkv, project, widen, narrow = zip(shards_here, theirs)
    z1, z2, z3, z4, feat = enc_fwd(pixels, enc_a, *enc_t)

    first = 2 * core

    def mine(array, size):
        own = lax.dynamic_slice_in_dim(array, (first + x) * size, size)
        other = lax.dynamic_slice_in_dim(array, (first + 1 - x) * size, size)
        return jnp.concatenate([own, other], axis=0)

    allowed = make_mask(mine(segment_ids, 1)).astype(F32)
    blank = jnp.zeros((NF, NF), F32)
    allowed = jnp.concatenate(
        [
            jnp.concatenate([allowed[0], blank], axis=1),
            jnp.concatenate([blank, allowed[1]], axis=1),
        ],
        axis=0,
    )
    (
        tokens, latent, chances, decoded, upper, lower, grad_latent, feat_got,
        latent_near, feat_near, got_near, *dec_f,
    ) = middle(
        layers,
        feat,
        *head_in,
        *head_out,
        *embed,
        positions,
        norm_gains.reshape(2 * layers, -1),
        allowed,
        mine(token_cotangent, NF),
        *qkv,
        *project,
        *widen,
        *narrow,
        *dec_rows,
    )
    dec_a, dec_b, dec_t, dec_u = dec_f[0], dec_f[1], dec_f[2:5], dec_f[5:8]
    tokens = jnp.where(
        x == 0, tokens, jnp.concatenate([tokens[NF:], tokens[:NF]], axis=0)
    )
    other_tokens = beside(tokens)
    tokens_out = jnp.where(
        core == 0,
        jnp.concatenate([tokens, other_tokens]),
        jnp.concatenate([other_tokens, tokens]),
    )

    g_decoded, dec_flat, recon, upper, _, lower = decode(
        hints, decoded, dec_u[2], dec_u[1], dec_u[0], dec_b, dec_a, *dec_t, upper, lower
    )
    recon = jnp.transpose(recon, (3, 0, 1, 2))
    g_feat, dec_share, d_piece, l_both, lower = latents_back(
        g_decoded, latent, latent_near, chances, grad_latent, feat, feat_got, feat_near, got_near,
        *head_in, *head_out, dec_flat, lower,
    )

    d_total, l_total, lower, early, late, frames_grad = enc_bwd(
        (pixels, z1, z2, z3, z4, g_feat, *enc_u, enc_b), dec_share, d_piece, l_both, lower
    )
    (
        g_latent_head, g_decode_head, g_down, g_up, g_out, g_qkv, g_embed, g_place, g_gain,
        d_four, d_three, d_two, d_one, e_one, e_two, e_three, e_four,
    ) = unpack(layers, dec_share.shape[0], d_total, l_total, upper, lower, early, late)

    def of_input(rows, count):
        return rows.reshape(count, 4, 4, -1).transpose(3, 0, 1, 2)

    def of_output(rows, count):
        return rows.reshape(count, 4, 4, -1).transpose(0, 3, 1, 2)

    return (
        tokens_out,
        recon,
        frames_grad,
        of_input(e_one, 3),
        of_input(e_two, 32),
        of_input(e_three, 64),
        of_output(e_four, 256),
        g_latent_head,
        g_embed,
        g_place,
        g_gain.reshape(norm_gains.shape),
        g_qkv.transpose(0, 2, 1, 3),
        g_out,
        g_up,
        g_down,
        g_decode_head,
        of_output(d_one, 128),
        of_output(d_two, 64),
        of_output(d_three, 32),
        of_output(d_four, 3),
    )


def solution(mesh):
    placed = (
        P("rows", None, "strip", None),
        P("rows", None),
        P(),
        P(),
        P(),
        P(),
        P(None, "strip"),
        P("strip", None),
        P(),
        P(),
        P(None, None, None, "strip"),
        P(None, "strip", None),
        P(None, None, "strip"),
        P(None, "strip", None),
        P("strip", None),
        P(),
        P(),
        P(),
        P(),
        P("rows", None),
        P("rows", None, "strip", None),
    )
    return jax.shard_map(
        shards,
        mesh=mesh,
        in_specs=placed,
        out_specs=(
            P("rows", None),
            P("rows", None, "strip", None),
            P("rows", None, "strip", None),
            P(),
            P(),
            P(),
            P(),
            P(None, "strip"),
            P("strip", None),
            P(),
            P(),
            P(None, None, None, "strip"),
            P(None, "strip", None),
            P(None, None, "strip"),
            P(None, "strip", None),
            P("strip", None),
            P(),
            P(),
            P(),
            P(),
        ),
        check_vma=False,
    )
```
